32 devices in a mesh: section: 2 (over y), dp: 16 (over z, x, core).
Axes of the slice: x: 2, y: 2, z: 4, core: 2. Of those that a mesh axis runs over, the one named last changes fastest.
Arguments:
- node_input: bfloat16 [32, 384, 128], P('dp', 'section'), may hold values from -6 to 6
- edge_input: bfloat16 [32, 384, 48, 128], P('dp', 'section'), may hold values from -6 to 6
- neighbors: int32 [32, 384, 48], P('dp'), may hold values from 0 to 383
- residue_mask: int32 [32, 384], P('dp'), may hold values 0 or 1
- decode_order: int32 [32, 384], P('dp'), may hold values from 0 to 383, each once within a row
- node_cotangent: bfloat16 [32, 384, 128], P('dp', 'section'), may hold values from -6 to 6
- edge_cotangent: bfloat16 [32, 384, 48, 128], P('dp', 'section'), may hold values from -6 to 6
- message_w1: bfloat16 [2, 384, 128], P('section'), may hold values from -0.3125 to 0.3125
- message_w2: bfloat16 [2, 128, 128], P('section'), may hold values from -0.5 to 0.5
- message_w3: bfloat16 [2, 128, 128], P('section'), may hold values from -2 to 2
- inner_w: bfloat16 [2, 128, 512], P('section'), may hold values from -0.5 to 0.5
- inner_bias: float32 [2, 512], P('section'), may hold values from -3 to 3
- outer_w: bfloat16 [2, 512, 128], P('section'), may hold values from -0.25 to 0.25
- update_w1: bfloat16 [2, 384, 128], P('section'), may hold values from -0.3125 to 0.3125
- update_w2: bfloat16 [2, 128, 128], P('section'), may hold values from -0.5 to 0.5
- update_w3: bfloat16 [2, 128, 128], P('section'), may hold values from -0.5 to 0.5
- biases: float32 [2, 10, 128], P('section'), may hold values from -3 to 3
- norm_gains: float32 [2, 3, 128], P('section'), may hold values from 0.5 to 1.5
Outputs:
- decoded_nodes: bfloat16 [32, 384, 128], P('dp', 'section')
- decoded_edges: bfloat16 [32, 384, 48, 128], P('dp', 'section')
- node_grad: bfloat16 [32, 384, 128], P('dp', 'section')
- edge_grad: bfloat16 [32, 384, 48, 128], P('dp', 'section')
- message_w1_grad: float32 [2, 384, 128], P('section')
- message_w2_grad: float32 [2, 128, 128], P('section')
- message_w3_grad: float32 [2, 128, 128], P('section')
- inner_w_grad: float32 [2, 128, 512], P('section')
- inner_bias_grad: float32 [2, 512], P('section')
- outer_w_grad: float32 [2, 512, 128], P('section')
- update_w1_grad: float32 [2, 384, 128], P('section')
- update_w2_grad: float32 [2, 128, 128], P('section')
- update_w3_grad: float32 [2, 128, 128], P('section')
- biases_grad: float32 [2, 10, 128], P('section')
- norm_gains_grad: float32 [2, 3, 128], P('section')
The draws below stay inside these ranges and needn't reach their ends.
Inputs may be any that keep to these rules, and one draw needn't show every extreme that they name: Each row of decode_order holds every step once.
All inputs are finite; a program needn't handle non-finite values. No bound on the sum of `residue_mask` on one device may be relied on, other than what follows from the above.
Results may differ from the reference program's by a relative error of at most 0.029.
Values may be sent and summed in bfloat16 or wider, within the bound.
A program may use at most 640 MiB of HBM per device.

```python
import jax
import jax.numpy as jnp
from jax import lax

H = 128
FF = 512
K = 48
LENGTH = 384
PROTEINS = 32


def plant(result, rng, smallest, high):
    place = [jax.random.randint(jax.random.fold_in(rng, axis), (), 0, length) for axis, length in enumerate(result.shape)]
    longest = result.shape.index(max(result.shape))
    neighbour = place[:longest] + [(place[longest] + 1) % result.shape[longest]] + place[longest + 1:]
    return result.at[tuple(place)].set(smallest).at[tuple(neighbour)].set(high)


def steps_of(own_key, extent, shards, smallest, largest):
    gain, own = 1.0, jax.random.fold_in(own_key, 6)
    for axis_at, blocks in shards:
        steps = jnp.exp(jax.random.uniform(jax.random.fold_in(own, axis_at), (blocks,), jnp.float32, smallest / len(shards), largest / len(shards)))
        gain = gain * jnp.repeat(steps, extent[axis_at] // blocks).reshape([-1 if axis == axis_at else 1 for axis in range(len(extent))])
    return gain


def bell_draw(rng, shape, scale, limit, shards=(), held_as=jnp.bfloat16):
    array = scale * jax.random.normal(rng, shape, jnp.float32)
    if shards:
        array = array * steps_of(rng, shape, shards, -0.22, 0.18)
    return jnp.clip(array, -limit, limit).astype(held_as)


def setup_inputs(seed: int = 0) -> dict:
    seeds = jax.random.split(jax.random.key(seed), 19)
    return {
        "node_input": bell_draw(seeds[0], (PROTEINS, LENGTH, H), 1.0, 6.0, ((0, 16), (1, 2))),
        "edge_input": bell_draw(seeds[1], (PROTEINS, LENGTH, K, H), 1.0, 6.0, ((0, 16), (1, 2))),
        "neighbors": plant(jax.random.randint(seeds[2], (PROTEINS, LENGTH, K), 0, LENGTH), jax.random.fold_in(seeds[2], 1), 0, LENGTH - 1).astype(jnp.int32),
        "residue_mask": plant((jax.random.randint(seeds[3], (PROTEINS, LENGTH), 0, 8) < 7).astype(jnp.int32), jax.random.fold_in(seeds[3], 1), 0, 1),
        "decode_order": jax.vmap(lambda own: jax.random.permutation(own, LENGTH))(jax.random.split(seeds[4], PROTEINS)).reshape((PROTEINS, LENGTH)).astype(jnp.int32),
        "node_cotangent": bell_draw(seeds[5], (PROTEINS, LENGTH, H), 1.0, 6.0, ((0, 16), (1, 2))),
        "edge_cotangent": bell_draw(seeds[6], (PROTEINS, LENGTH, K, H), 1.0, 6.0, ((0, 16), (1, 2))),
        "message_w1": bell_draw(seeds[7], (2, 3 * H, H), (3 * H) ** -0.5, 0.3125, ((0, 2),)),
        "message_w2": bell_draw(seeds[8], (2, H, H), H ** -0.5, 0.5, ((0, 2),)),
        "message_w3": bell_draw(seeds[9], (2, H, H), (H // 16) ** -0.5, 2.0, ((0, 2),)),
        "inner_w": bell_draw(seeds[10], (2, H, FF), H ** -0.5, 0.5, ((0, 2),)),
        "inner_bias": bell_draw(seeds[11], (2, FF), 0.5, 3.0, ((0, 2),), jnp.float32),
        "outer_w": bell_draw(seeds[12], (2, FF, H), FF ** -0.5, 0.25, ((0, 2),)),
        "update_w1": bell_draw(seeds[13], (2, 3 * H, H), (3 * H) ** -0.5, 0.3125, ((0, 2),)),
        "update_w2": bell_draw(seeds[14], (2, H, H), H ** -0.5, 0.5, ((0, 2),)),
        "update_w3": bell_draw(seeds[15], (2, H, H), H ** -0.5, 0.5, ((0, 2),)),
        "biases": bell_draw(seeds[16], (2, 10, H), 0.5, 3.0, ((0, 2),), jnp.float32),
        "norm_gains": jnp.clip(1.0 + 0.1 * jax.random.normal(seeds[17], (2, 3, H), jnp.float32), 0.5, 1.5),
    }


@jax.custom_vjp
def low(v):
    return lax.optimization_barrier(v.astype(jnp.bfloat16)).astype(jnp.float32)

@jax.custom_vjp
def low_back(v):
    return v

def low_keep(v):
    return (low(v), None)

def low_pass(kept, grad):
    return (grad,)

def back_keep(v):
    return (v, None)

def back_low(kept, grad):
    return (low(grad),)
low.defvjp(low_keep, low_pass)
low_back.defvjp(back_keep, back_low)

def gelu_act(values):
    return jax.nn.gelu(values, approximate=True)

def layer_norm(resid, norm_gain, norm_shift):
    centered = resid - lax.optimization_barrier(jnp.mean(resid, axis=-1, keepdims=True))
    spread_sq = lax.optimization_barrier(jnp.mean(centered * centered, axis=-1, keepdims=True))
    return centered * lax.rsqrt(spread_sq + 1e-05) * norm_gain + norm_shift

def product(left, right):
    return low_back(jnp.dot(left, right, precision=lax.Precision.HIGHEST))

def mpnn_layer(weights, node_rows, edge_rows, neighbor_ids, attend, live_mask):
    weight_one, weight_two, weight_three, inner_weight, inner_offset, outer_weight, edge_one, edge_two, edge_three, bias_rows, gain_rows = weights
    feature_width = node_rows.shape[1]

    def assemble(features):
        local_rows = jnp.broadcast_to(features[:, None, :], edge_rows.shape)
        joined = jnp.concatenate([local_rows, edge_rows, features[neighbor_ids]], axis=-1)
        return low(joined.reshape(-1, 3 * feature_width))

    def perceptron(joined, first_w, second_w, third_w, offset):
        act_one = low(gelu_act(product(joined, first_w) + bias_rows[offset]))
        act_two = low(gelu_act(product(act_one, second_w) + bias_rows[offset + 1]))
        return product(act_two, third_w) + bias_rows[offset + 2]
    message = perceptron(assemble(node_rows), weight_one, weight_two, weight_three, 0)
    update = lax.optimization_barrier(jnp.sum(attend[:, :, None] * message.reshape(edge_rows.shape), axis=1)) / 30.0
    normed_one = layer_norm(node_rows + update, gain_rows[0], bias_rows[7])
    hidden = low(gelu_act(product(low(normed_one), inner_weight) + inner_offset))
    resid_two = normed_one + (product(hidden, outer_weight) + bias_rows[3])
    node_out = low(layer_norm(resid_two, gain_rows[1], bias_rows[8]) * live_mask[:, None])
    edge_message = perceptron(assemble(node_out), edge_one, edge_two, edge_three, 4)
    edge_out = layer_norm(edge_rows + edge_message.reshape(edge_rows.shape), gain_rows[2], bias_rows[9])
    return (node_out, edge_out)

def protein_pass(params, node_rows, edge_rows, neighbor_ids, live_mask, order_row):
    encoder = tuple((tensor[0] for tensor in params))
    decoder = tuple((tensor[1] for tensor in params))
    live_near = live_mask[neighbor_ids]
    earlier = (order_row[neighbor_ids] < order_row[:, None]).astype(jnp.float32)
    enc_nodes, enc_edges = mpnn_layer(encoder, node_rows, edge_rows, neighbor_ids, live_near, live_mask)
    dec_in_nodes = low_back(enc_nodes)
    dec_in_edges = low_back(low(enc_edges))
    return mpnn_layer(decoder, dec_in_nodes, dec_in_edges, neighbor_ids, live_near * earlier, live_mask)

def reference(node_input, edge_input, neighbors, residue_mask, decode_order, node_cotangent, edge_cotangent, message_w1, message_w2, message_w3, inner_w, inner_bias, outer_w, update_w1, update_w2, update_w3, biases, norm_gains):
    params = tuple((tensor.astype(jnp.float32) for tensor in (message_w1, message_w2, message_w3, inner_w, inner_bias, outer_w, update_w1, update_w2, update_w3, biases, norm_gains)))

    def step_one(totals, items):
        node_rows, edge_rows, neighbor_ids, mask_row, order_row, cot_nodes, cot_edges = items
        live_mask = mask_row.astype(jnp.float32)

        def forward(weights, nodes_in, edges_in):
            return protein_pass(weights, nodes_in, edges_in, neighbor_ids, live_mask, order_row)
        outputs, pull = jax.vjp(forward, params, node_rows.astype(jnp.float32), edge_rows.astype(jnp.float32))
        grad_params, grad_nodes, grad_edges = pull((cot_nodes.astype(jnp.float32), cot_edges.astype(jnp.float32)))
        totals = jax.tree.map(lambda first_term, second_term: first_term + second_term, totals, grad_params)
        return (totals, (outputs[0].astype(jnp.bfloat16), outputs[1].astype(jnp.bfloat16), grad_nodes.astype(jnp.bfloat16), grad_edges.astype(jnp.bfloat16)))
    zeros_start = tuple((jnp.zeros(tensor.shape, jnp.float32) for tensor in params))
    totals, stacked = lax.scan(step_one, zeros_start, (node_input, edge_input, neighbors, residue_mask, decode_order, node_cotangent, edge_cotangent))
    return (stacked[0], stacked[1], stacked[2], stacked[3], totals[0], totals[1], totals[2], totals[3], totals[4], totals[5], totals[6], totals[7], totals[8], totals[9], totals[10])
```

```python
import types

import jax
import jax.numpy as jnp
import numpy as np
from jax import lax
from jax.experimental import pallas as pl
from jax.experimental.pallas import tpu as pltpu
from jax.sharding import PartitionSpec as P

BF = jnp.bfloat16
F32 = jnp.float32
C1 = 0.7978845608
C2 = C1 * 0.044715
EPS = 1e-5
BLOCK_RES = 32
EXTRA = 16
SMALL = 32
MESH = pl.DeviceIdType.MESH


def mm(a, b, ca=1, cb=0):
    return lax.dot_general(a, b, (((ca,), (cb,)), ((), ())), preferred_element_type=F32)


def mm_exact(a, b, ca=1, cb=0):
    return lax.dot_general(
        a, b, (((ca,), (cb,)), ((), ())), precision=lax.Precision.HIGHEST, preferred_element_type=F32
    )


def gelu_pair(x):
    x2 = x * x
    t = jnp.tanh(x * (x2 * C2 + C1)).astype(BF)
    h = BF(0.5) * t + BF(0.5)
    g = x.astype(BF) * h
    d = h + (g * (BF(1.0) - h)) * (x2.astype(BF) * BF(6 * C2) + BF(2 * C1))
    return g, d


def gelu_pair_wide(x):
    x2 = x * x
    h = 0.5 * jnp.tanh(x * (x2 * C2 + C1)) + 0.5
    g = x * h
    d = h + (g * (1.0 - h)) * (x2 * (6 * C2) + 2 * C1)
    return g, d


def lane_sum(x):
    total = x[:, :128]
    for at in range(128, x.shape[1], 128):
        total = total + x[:, at : at + 128]
    return total


def to_row(acc):
    return mm_exact(jnp.ones((8, acc.shape[1]), F32), acc, 1, 1)[0:1]


def norm_rows(r):
    c = r - jnp.mean(r, axis=-1, keepdims=True)
    rs = lax.rsqrt(jnp.mean(c * c, axis=-1, keepdims=True) + EPS)
    return c * rs, rs


def norm_back_rows(dxh, xh, rs):
    m1 = jnp.mean(dxh, axis=-1, keepdims=True)
    m2 = jnp.mean(dxh * xh, axis=-1, keepdims=True)
    return (dxh - m1 - xh * m2) * rs


def norm_back(dy, xh, rs, gain_col):
    dxh = dy * gain_col
    m1 = jnp.mean(dxh, axis=0, keepdims=True)
    m2 = jnp.mean(dxh * xh, axis=0, keepdims=True)
    return (dxh - m1 - xh * m2) * rs


class Phase:
    def __init__(self, dims, collective_id=None):
        self.grid = (dims.parts, dims.blocks)
        self.collective_id = collective_id
        self.ins, self.outs, self.temps = [], [], []

    def stream_spec(self, shape):
        rest = len(shape) - 2
        return pl.BlockSpec((1, 1) + tuple(shape[2:]), lambda p, b: (p, b) + (0,) * rest)

    def whole_spec(self, shape):
        rank = len(shape)
        return pl.BlockSpec(tuple(shape), lambda p, b: (0,) * rank)

    def stream(self, **arrays):
        self.ins += [(n, a, self.stream_spec(a.shape)) for n, a in arrays.items()]

    def whole(self, **arrays):
        self.ins += [(n, a, self.whole_spec(a.shape)) for n, a in arrays.items()]

    def raw(self, **arrays):
        self.ins += [(n, a, pl.BlockSpec(memory_space=pl.ANY)) for n, a in arrays.items()]

    def edges(self, dims, **arrays):
        spec = pl.BlockSpec((1, dims.res, dims.near, dims.feat), lambda p, b: (p, b, 0, 0))
        self.ins += [(n, a, spec) for n, a in arrays.items()]

    def out_edges(self, dims, **shapes):
        spec = pl.BlockSpec((1, dims.res, dims.near, dims.feat), lambda p, b: (p, b, 0, 0))
        self.outs += [(n, jax.ShapeDtypeStruct(s, BF), spec) for n, s in shapes.items()]

    def out_stream(self, dtype, **shapes):
        self.outs += [(n, jax.ShapeDtypeStruct(s, dtype), self.stream_spec(s)) for n, s in shapes.items()]

    def out_whole(self, dtype, **shapes):
        self.outs += [(n, jax.ShapeDtypeStruct(s, dtype), self.whole_spec(s)) for n, s in shapes.items()]

    def out_raw(self, dtype, **shapes):
        spec = pl.BlockSpec(memory_space=pl.ANY)
        self.outs += [(n, jax.ShapeDtypeStruct(s, dtype), spec) for n, s in shapes.items()]

    def temp(self, dtype, **shapes):
        self.temps += [(n, pltpu.VMEM(s, dtype)) for n, s in shapes.items()]

    def sems(self, **counts):
        self.temps += [(n, pltpu.SemaphoreType.DMA((c,))) for n, c in counts.items()]

    def call(self, name, body):
        names = [n for n, _, _ in self.ins] + [n for n, _, _ in self.outs] + [n for n, _ in self.temps]

        def kernel(*refs):
            body(types.SimpleNamespace(**dict(zip(names, refs))))

        results = pl.pallas_call(
            kernel,
            grid=self.grid,
            in_specs=[s for _, _, s in self.ins],
            out_specs=[s for _, _, s in self.outs],
            out_shape=[s for _, s, _ in self.outs],
            scratch_shapes=[s for _, s in self.temps],
            compiler_params=pltpu.CompilerParams(
                dimension_semantics=(pltpu.ARBITRARY,) * len(self.grid),
                vmem_limit_bytes=58 << 20,
                collective_id=self.collective_id,
                has_side_effects=self.collective_id is not None,
            ),
            name=name,
        )(*[a for _, a, _ in self.ins])
        return types.SimpleNamespace(**dict(zip([n for n, _, _ in self.outs], results)))


def other_section():
    return {AXIS_S: 1 - lax.axis_index(AXIS_S)}


AXIS_S = "section"
AXIS_D = "dp"


def greet_partner():
    barrier = pltpu.get_barrier_semaphore()
    pl.semaphore_signal(barrier, inc=1, device_id=other_section(), device_id_type=MESH)
    pl.semaphore_wait(barrier, 1)


def to_partner(src, dst, send, recv):
    return pltpu.make_async_remote_copy(
        src_ref=src, dst_ref=dst, send_sem=send, recv_sem=recv, device_id=other_section(), device_id_type=MESH
    )


def prepare(dims, idx_row, edge_input, sum_rows, node_input, weights):
    d = dims
    ph = Phase(d, 1)
    ph.stream(idx=idx_row)
    ph.edges(d, edge=edge_input)
    ph.whole(sums=sum_rows)
    ph.raw(nodes=node_input, **{W_IN + n: a for n, a in weights.items()})
    ph.out_stream(
        BF,
        tt=(d.parts, d.blocks, d.length + d.res, d.rows),
        tn=(d.parts, d.blocks, d.rows, d.length + 128),
        et=(d.parts, d.blocks, d.feat, d.rows),
    )
    ph.out_raw(BF, nodes_got=node_input.shape)
    for n, a in weights.items():
        ph.out_raw(a.dtype, **{n: (2,) + a.shape[1:]})
    count = len(weights)
    ph.sems(send=count + 1, recv=count + 1, local=count)

    def body(r):
        p, b = pl.program_id(0), pl.program_id(1)
        section = lax.axis_index(AXIS_S)

        def copies():
            jobs = [to_partner(r.nodes, r.nodes_got, r.send.at[count], r.recv.at[count])]
            for i, n in enumerate(weights):
                src, dst = getattr(r, W_IN + n), getattr(r, n)
                jobs.append(to_partner(src.at[0], dst.at[section], r.send.at[i], r.recv.at[i]))
                jobs.append(pltpu.make_async_copy(src.at[0], dst.at[section], r.local.at[i]))
            return jobs

        @pl.when((p == 0) & (b == 0))
        def _():
            greet_partner()
            for job in copies():
                job.start()

        idx = r.idx[0, 0] - section * d.half
        idx = jnp.where(idx < 0, idx + d.length, idx)
        at = lax.broadcasted_iota(jnp.int32, (d.length, d.rows), 0)
        table = (at == idx).astype(F32).astype(BF)
        r.tt[0, 0, : d.length, :] = table
        sums = r.sums[...]
        r.tt[0, 0, d.length :, :] = sums[: d.res]
        r.tn[0, 0, :, : d.length] = table.T
        r.tn[0, 0, :, d.length :] = sums.T
        r.et[0, 0] = r.edge[0].reshape(d.rows, d.feat).T

        @pl.when((p == d.parts - 1) & (b == d.blocks - 1))
        def _():
            for job in copies():
                job.wait()

    return ph.call("tables", body)


W_IN = "w_"


def weight_args(w, *names):
    return {n: getattr(w, n) for n in names}


def load_cols(r, layer, aux, cols):
    n_bias, n_gain = r.bias.shape[1], r.gain.shape[1]
    aux[...] = jnp.zeros(aux.shape, F32)
    aux[0:n_bias] = r.bias[layer]
    aux[n_bias : n_bias + n_gain] = r.gain[layer]
    cols[...] = aux[...].T


def put_table(d, lhs, at, n_cat, w1, n_blk, bias_col, first):
    @pl.when(first)
    def _():
        lhs[at : at + d.feat, : d.length] = mm(w1[2 * d.feat :, :].T, n_cat[...], 1, 1).astype(BF)

    own = mm(w1[0 : d.feat, :].T, n_blk, 1, 1) + bias_col
    lhs[at : at + d.feat, d.length :] = own.astype(BF)


def message_part(a1, w2t, b2, att):
    g1, d1 = gelu_pair(a1)
    a2 = mm(w2t, g1) + b2
    g2, d2 = gelu_pair(a2)
    attb = att.astype(BF)
    return g1, d1, g2 * attb, d2 * attb


def add_node_outs(ph, d):
    ph.out_whole(BF, node_out=(d.parts, d.half, d.feat))
    shape = (d.parts, d.half, d.feat)
    ph.out_whole(F32, r1=shape, ip=(d.parts, d.half, d.wide), r2=shape, big=shape, cnt=shape)


def node_step(d, r, p, b, g2m, att, rt):
    big = mm(rt, g2m, 1, 1)
    cnt = mm(rt, jnp.broadcast_to(att.astype(BF), (16, att.shape[1])), 1, 1)
    at = pl.ds(pl.multiple_of(b * d.res, d.res), d.res)
    r.big[p, at, :] = big
    r.cnt[p, at, :] = jnp.broadcast_to(cnt[:, 0:1], big.shape)


def node_forward(r, p, n_own, layer, aux):
    big = r.big[p]
    hi = big.astype(BF)
    lo = (big - hi.astype(F32)).astype(BF)
    w3 = r.mw3[layer]
    upd = (mm(hi, w3) + mm(lo, w3) + r.cnt[p] * aux[2:3]) / 30.0
    r1 = n_own.astype(F32) + upd
    xh1, _ = norm_rows(r1)
    normed = xh1 * aux[10:11] + aux[7:8]
    ip = mm(normed.astype(BF), r.inner[layer]) + r.inner_b[layer]
    hid = gelu_pair_wide(ip)[0].astype(BF)
    r2 = normed + (mm(hid, r.outer[layer]) + aux[3:4])
    xh2, _ = norm_rows(r2)
    out = ((xh2 * aux[11:12] + aux[8:9]) * r.mask[p]).astype(BF)
    r.node_out[p] = out
    r.r1[p] = r1
    r.ip[p] = ip
    r.r2[p] = r2
    return out


def node_backward(d, r, p, layer, aux, dn):
    r1, ip, r2, big, cnt = r.r1[p], r.ip[p], r.r2[p], r.big[p], r.cnt[p]
    xh1, rs1 = norm_rows(r1)
    normed = xh1 * aux[10:11] + aux[7:8]
    xh2, rs2 = norm_rows(r2)
    dy2 = dn * r.mask[p]
    dr2 = norm_back_rows(dy2 * aux[11:12], xh2, rs2)
    low_outer = dr2.astype(BF)
    hid, slope = gelu_pair_wide(ip)
    dip = mm(low_outer, r.outer[layer], 1, 1) * slope
    low_inner = dip.astype(BF)
    at = d.at_outer
    r.msg[at : at + d.wide] += mm(hid.astype(BF), low_outer, 0, 0)
    at = d.at_inner
    r.msg[at : at + d.wide] += mm(low_inner, normed.astype(BF), 0, 0)
    dnormed = dr2 + mm(low_inner, r.inner[layer], 1, 1)
    dr1 = norm_back_rows(dnormed * aux[10:11], xh1, rs1)
    du = dr1 / 30.0
    dub = du.astype(BF)
    r.msg[4 * d.feat : 5 * d.feat] += mm(big.astype(BF), dub, 0, 0)
    dib = jnp.sum(dip, axis=0, keepdims=True)
    rows = {
        2: jnp.sum(cnt * du, axis=0, keepdims=True),
        3: jnp.sum(dr2, axis=0, keepdims=True),
        7: jnp.sum(dnormed, axis=0, keepdims=True),
        8: jnp.sum(dy2, axis=0, keepdims=True),
        10: jnp.sum(dnormed * xh1, axis=0, keepdims=True),
        11: jnp.sum(dy2 * xh2, axis=0, keepdims=True),
    }
    for i in range(d.wide // d.feat):
        rows[16 + i] = dib[:, i * d.feat : (i + 1) * d.feat]
    for row, value in rows.items():
        r.msg[d.at_small + row : d.at_small + row + 1] += value
    r.dr1[...] = dr1
    r.dub[...] = dub


def encoder_message(d, st, n_own, n_got, consts):
    ph = Phase(d, 2)
    ph.whole(n_own=n_own, n_got=n_got, rt=consts.sums, mask=consts.mask)
    ph.stream(tt=st.tt, et=st.et, extra=consts.extra)
    ph.whole(**weight_args(st, *NODE_W, *MSG_W))
    act = (d.parts, d.blocks, d.feat, d.rows)
    ph.out_stream(BF, g1=act, d1=act, d2=act)
    ph.out_stream(F32, att=(d.parts, d.blocks, 1, d.rows))
    add_node_outs(ph, d)
    ph.out_raw(BF, got=(d.half, d.feat))
    sq = (d.feat, d.feat)
    ph.temp(BF, n_cat=(d.length, d.feat), lhs=(d.feat + EXTRA, d.length + d.res), w1bt=sq, w2t=sq)
    ph.temp(BF, leave=(d.half, d.feat))
    ph.temp(F32, aux=sq, cols=sq)
    ph.sems(send=1, recv=1)

    def body(r):
        p, b = pl.program_id(0), pl.program_id(1)
        first, last = b == 0, b == d.blocks - 1
        job = to_partner(r.leave, r.got, r.send.at[0], r.recv.at[0])

        @pl.when(first & (p == 0))
        def _():
            greet_partner()
            r.w1bt[...] = r.mw1[0, d.feat : 2 * d.feat, :].T
            r.w2t[...] = r.mw2[0].T
            load_cols(r, 0, r.aux, r.cols)

        @pl.when(first)
        def _():
            r.n_cat[: d.half] = r.n_own[p]
            r.n_cat[d.half :] = r.n_got[p]

        n_blk = r.n_own[p, pl.ds(pl.multiple_of(b * d.res, d.res), d.res), :]
        put_table(d, r.lhs, 0, r.n_cat, r.mw1.at[0], n_blk, r.cols[:, 0:1], first)
        r.lhs[d.feat :, :] = r.extra[0, 0]
        out = mm(r.lhs[...], r.tt[0, 0])
        a1 = out[: d.feat] + mm(r.w1bt[...], r.et[0, 0])
        att = out[d.feat : d.feat + 1]
        r.att[0, 0] = jnp.where(out[d.feat + 1 : d.feat + 2] < 0.0, 1.0, 0.0)
        r.g1[0, 0], r.d1[0, 0], g2m, r.d2[0, 0] = message_part(a1, r.w2t[...], r.cols[:, 1:2], att)
        node_step(d, r, p, b, g2m, att, r.rt[: d.res])

        @pl.when(last)
        def _():
            out = node_forward(r, p, r.n_own[p], 0, r.aux[...])

            @pl.when(p == 0)
            def _():
                r.leave[...] = out
                job.start()

            @pl.when(p == d.parts - 1)
            def _():
                job.wait()

    return ph.call("enc_message", body)


NODE_W = ("mw3", "inner", "inner_b", "outer", "bias", "gain")
MSG_W = ("mw1", "mw2")
UPD_W = ("uw1", "uw2", "uw3")


def update_forward(a1, edge_t, w2t, w3c, b5, b6c):
    g1, d1 = gelu_pair(a1)
    a2 = mm(w2t, g1) + b5
    g2, d2 = gelu_pair(a2)
    feat = g1.shape[0]
    cent = mm(w3c[:, :feat], g2) + mm(w3c[:, feat:], edge_t) + b6c
    var = jnp.mean(cent * cent, axis=0, keepdims=True)
    rs = lax.rsqrt(var + EPS)
    return g1, d1, g2, d2, cent * rs, rs


def centre_weights(w3, cols, w3c, b6c):
    feat = w3.shape[0]
    eye = lax.broadcasted_iota(jnp.int32, w3.shape, 0) == lax.broadcasted_iota(jnp.int32, w3.shape, 1)
    w3f = w3.astype(F32)
    w3c[:, :feat] = (w3f - jnp.mean(w3f, axis=1, keepdims=True)).T.astype(BF)
    w3c[:, feat:] = (eye.astype(F32) - 1.0 / feat).astype(BF)
    b6 = cols[:, 6:7]
    b6c[...] = jnp.broadcast_to(b6 - jnp.mean(b6, axis=0, keepdims=True), b6c.shape)


def encoder_update(d, st, fa, consts):
    ph = Phase(d, 3)
    ph.whole(n_own=fa.node_out, got_a=fa.got, rt=consts.sums, mask=consts.mask)
    ph.stream(tt=st.tt, et=st.et, att=fa.att)
    ph.whole(**weight_args(st, *NODE_W, *MSG_W, *UPD_W))
    act = (d.parts, d.blocks, d.feat, d.rows)
    ph.out_stream(BF, ug1=act, ud1=act, ug2=act, ud2=act, uxh=act, e2=act, g1=act, d1=act, d2=act)
    ph.out_stream(F32, urs=(d.parts, d.blocks, 1, d.rows))
    add_node_outs(ph, d)
    ph.out_whole(BF, got_in=(d.half, d.feat))
    ph.out_raw(BF, got=(d.parts, d.half, d.feat))
    sq = (d.feat, d.feat)
    ph.temp(BF, n_cat=(d.length, d.feat), lhs=(2 * d.feat, d.length + d.res))
    ph.temp(BF, uw1bt=sq, uw2t=sq, mw1bt=sq, mw2t=sq, w3c=(d.feat, 2 * d.feat))
    ph.temp(BF, leave=(d.parts, d.half, d.feat), lead=(d.half, d.feat), arrive=(d.half, d.feat))
    ph.temp(F32, w3c_b=sq, e_aux=sq, e_cols=sq, d_aux=sq, d_cols=sq)
    ph.sems(send=d.parts + 1, recv=d.parts + 1)

    def body(r):
        p, b = pl.program_id(0), pl.program_id(1)
        first, last = b == 0, b == d.blocks - 1
        early = to_partner(r.lead, r.arrive, r.send.at[d.parts], r.recv.at[d.parts])
        jobs = [to_partner(r.leave.at[i], r.got.at[i], r.send.at[i], r.recv.at[i]) for i in range(d.parts)]

        @pl.when(first & (p == 0))
        def _():
            greet_partner()
            r.lead[...] = r.n_own[d.parts - 1]
            early.start()
            r.uw1bt[...] = r.uw1[0, d.feat : 2 * d.feat, :].T
            r.uw2t[...] = r.uw2[0].T
            r.mw1bt[...] = r.mw1[1, d.feat : 2 * d.feat, :].T
            r.mw2t[...] = r.mw2[1].T
            load_cols(r, 0, r.e_aux, r.e_cols)
            load_cols(r, 1, r.d_aux, r.d_cols)
            centre_weights(r.uw3[0], r.e_cols[...], r.w3c, r.w3c_b)
            r.n_cat[d.half :] = r.got_a[...]

        @pl.when(first & (p == 1))
        def _():
            early.wait()
            r.n_cat[d.half :] = r.arrive[...]
            r.got_in[...] = r.arrive[...]

        @pl.when(first)
        def _():
            r.n_cat[: d.half] = r.n_own[p]

        n_blk = r.n_own[p, pl.ds(pl.multiple_of(b * d.res, d.res), d.res), :]
        put_table(d, r.lhs, 0, r.n_cat, r.uw1.at[0], n_blk, r.e_cols[:, 4:5], first)
        put_table(d, r.lhs, d.feat, r.n_cat, r.mw1.at[1], n_blk, r.d_cols[:, 0:1], first)
        out = mm(r.lhs[...], r.tt[0, 0])
        et = r.et[0, 0]
        a1 = out[: d.feat] + mm(r.uw1bt[...], et)
        g1, d1, g2, d2, xh, rs = update_forward(a1, et, r.uw2t[...], r.w3c, r.e_cols[:, 5:6], r.w3c_b[:, 0:1])
        r.ug1[0, 0], r.ud1[0, 0], r.ug2[0, 0], r.ud2[0, 0] = g1, d1, g2, d2
        r.uxh[0, 0] = xh.astype(BF)
        r.urs[0, 0] = rs
        e2 = (xh * r.e_cols[:, 12:13] + r.e_cols[:, 9:10]).astype(BF)
        r.e2[0, 0] = e2
        att = r.att[0, 0]
        a1 = out[d.feat :] + mm(r.mw1bt[...], e2)
        r.g1[0, 0], r.d1[0, 0], g2m, r.d2[0, 0] = message_part(a1, r.mw2t[...], r.d_cols[:, 1:2], att)
        node_step(d, r, p, b, g2m, att, r.rt[: d.res])

        @pl.when(last)
        def _():
            r.leave[p] = node_forward(r, p, r.n_own[p], 1, r.d_aux[...])
            for i in range(d.parts):

                @pl.when(p == i)
                def _(i=i):
                    jobs[i].start()

            @pl.when(p == d.parts - 1)
            def _():
                for job in jobs:
                    job.wait()

    return ph.call("enc_update", body)


def spread_nodes(d, acc, sumk, w1, n_cat, grad, grad_at):
    s = acc.astype(BF)
    sk = jnp.concatenate([x[:, : d.res] for x in sumk], axis=1)
    skb = sk.astype(BF)
    far = mm(s, w1[2 * d.feat :].T, 0, 0)
    own = mm(skb, w1[: d.feat].T, 0, 0)
    grad[grad_at + 2 * d.feat : grad_at + 3 * d.feat, :] += mm(n_cat, s, 0, 1)
    grad[grad_at : grad_at + d.feat, :] += mm(n_cat[: d.half], skb, 0, 1)
    return own + far[: d.half], far[d.half :], to_row(sk)


def update_backward(d, r, dr3, g1, d1, g2, d2, w2, w3, edge_t):
    dr3b = dr3.astype(BF)
    r.upd[4 * d.feat : 5 * d.feat] += mm(g2, dr3b, 1, 1)
    r.a_b6[...] += lane_sum(dr3)
    da2 = mm(w3, dr3b) * d2.astype(F32)
    r.a_b5[...] += lane_sum(da2)
    da2b = da2.astype(BF)
    r.upd[3 * d.feat : 4 * d.feat] += mm(g1, da2b, 1, 1)
    da1b = (mm(w2, da2b) * d1.astype(F32)).astype(BF)
    r.upd[d.feat : 2 * d.feat] += mm(edge_t, da1b, 1, 1)
    return da1b, dr3b


def update_small(d, r, b4):
    at = 5 * d.feat
    r.upd[at + 4 : at + 5] += b4

    @pl.when(pl.program_id(0) == d.parts - 1)
    def _():
        for row, acc in ((5, r.a_b5), (6, r.a_b6), (9, r.a_b9), (12, r.a_g2)):
            r.upd[at + row : at + row + 1] += to_row(acc[...])


def zero(*refs):
    for ref in refs:
        ref[...] = jnp.zeros(ref.shape, ref.dtype)


def decoder_update(d, st, fb, cot):
    ph = Phase(d)
    ph.whole(n_own=fb.node_out, n_got=fb.got)
    ph.stream(tt=st.tt, tn=st.tn, e2=fb.e2)
    ph.edges(d, cot=cot)
    ph.whole(**weight_args(st, *UPD_W, *AUX_W))
    ph.out_edges(d, decoded=cot.shape)
    act = (d.parts, d.blocks, d.feat, d.rows)
    ph.out_stream(BF, da1=act, dr3=act)
    ph.out_whole(F32, upd=(d.upd_rows, d.feat), dn_own=(d.parts, d.half, d.feat))
    ph.out_whole(BF, dn_far=(d.parts, d.half, d.feat))
    sq = (d.feat, d.feat)
    ph.temp(BF, n_cat=(d.length, d.feat), lhs=(d.feat, d.length + d.res), w1bt=sq, w2t=sq)
    ph.temp(BF, w3c=(d.feat, 2 * d.feat))
    ph.temp(F32, w3c_b=sq, aux=sq, cols=sq, a_b5=sq, a_b6=sq, a_b9=sq, a_g2=sq)
    ph.temp(F32, a_s=(d.feat, d.length), a_k=(d.blocks, d.feat, 128))

    def body(r):
        p, b = pl.program_id(0), pl.program_id(1)
        first, last = b == 0, b == d.blocks - 1

        @pl.when(first & (p == 0))
        def _():
            r.w1bt[...] = r.uw1[1, d.feat : 2 * d.feat, :].T
            r.w2t[...] = r.uw2[1].T
            load_cols(r, 1, r.aux, r.cols)
            centre_weights(r.uw3[1], r.cols[...], r.w3c, r.w3c_b)
            zero(r.upd, r.a_b5, r.a_b6, r.a_b9, r.a_g2)

        @pl.when(first)
        def _():
            r.n_cat[: d.half] = r.n_own[p]
            r.n_cat[d.half :] = r.n_got[p]
            zero(r.a_s)

        n_blk = r.n_own[p, pl.ds(pl.multiple_of(b * d.res, d.res), d.res), :]
        put_table(d, r.lhs, 0, r.n_cat, r.uw1.at[1], n_blk, r.cols[:, 4:5], first)
        e2 = r.e2[0, 0]
        a1 = mm(r.lhs[...], r.tt[0, 0]) + mm(r.w1bt[...], e2)
        g1, d1, g2, d2, xh, rs = update_forward(a1, e2, r.w2t[...], r.w3c, r.cols[:, 5:6], r.w3c_b[:, 0:1])
        y = (xh * r.cols[:, 12:13] + r.cols[:, 9:10]).astype(BF)
        r.decoded[0] = y.T.reshape(d.res, d.near, d.feat)
        dy = r.cot[0].reshape(d.rows, d.feat).T.astype(F32)
        r.a_b9[...] += lane_sum(dy)
        r.a_g2[...] += lane_sum(dy * xh)
        dr3 = norm_back(dy, xh, rs, r.cols[:, 12:13])
        da1b, dr3b = update_backward(d, r, dr3, g1, d1, g2, d2, r.uw2[1], r.uw3[1], e2)
        r.da1[0, 0] = da1b
        r.dr3[0, 0] = dr3b
        spread = mm(da1b, r.tn[0, 0])
        r.a_s[...] += spread[:, : d.length]
        r.a_k[b] = spread[:, d.length :]

        @pl.when(last)
        def _():
            own, far, b4 = spread_nodes(
                d, r.a_s[...], [r.a_k[i] for i in range(d.blocks)], r.uw1[1], r.n_cat[...], r.upd, 0
            )
            r.dn_own[p] = own
            r.dn_far[p] = far.astype(BF)
            update_small(d, r, b4)

    return ph.call("dec_update", body)


AUX_W = ("bias", "gain")


def message_backward(d, r, b, layer, d2m, g1, d1, edge_t):
    at = pl.ds(pl.multiple_of(b * d.res, d.res), d.res)
    v = mm(r.mw3[layer], r.dub[at, :], 1, 1).astype(BF)
    da2 = mm(v, r.rt[: d.res]) * d2m.astype(F32)
    r.a_b1[...] += lane_sum(da2)
    da2b = da2.astype(BF)
    r.msg[3 * d.feat : 4 * d.feat] += mm(g1, da2b, 1, 1)
    da1b = (mm(r.mw2[layer], da2b) * d1.astype(F32)).astype(BF)
    r.msg[d.feat : 2 * d.feat] += mm(edge_t, da1b, 1, 1)
    return da1b


def message_small(d, r, b0):
    at = d.at_small
    r.msg[at : at + 1] += b0

    @pl.when(pl.program_id(0) == d.parts - 1)
    def _():
        r.msg[at + 1 : at + 2] += to_row(r.a_b1[...])


def middle_backward(d, st, fa, fb, fd, cot_n, consts):
    ph = Phase(d, 4)
    ph.whole(cot_n=cot_n, dn_a=fd.dn_own, dn_far_in=fd.dn_far, n_own=fa.node_out, got_a=fa.got, got_b=fb.got_in)
    ph.whole(mask=consts.mask, rt=consts.sums, r1=fb.r1, ip=fb.ip, r2=fb.r2, big=fb.big, cnt=fb.cnt)
    ph.stream(tn=st.tn, et=st.et, ug1=fb.ug1, ud1=fb.ud1, ug2=fb.ug2, ud2=fb.ud2, uxh=fb.uxh, urs=fb.urs)
    ph.stream(e2=fb.e2, g1=fb.g1, d1=fb.d1, d2=fb.d2, dec_da1=fd.da1, dec_dr3=fd.dr3)
    ph.whole(**weight_args(st, *NODE_W, *MSG_W, *UPD_W))
    act = (d.parts, d.blocks, d.feat, d.rows)
    ph.out_stream(BF, da1=act, dr3=act)
    ph.out_whole(F32, msg=(d.msg_rows, d.feat), upd=(d.upd_rows, d.feat), dn_own=(d.parts, d.half, d.feat))
    ph.out_raw(BF, got=(d.parts, d.half, d.feat))
    sq = (d.feat, d.feat)
    ph.temp(BF, n_cat=(d.length, d.feat), dub=(d.half, d.feat), back=(d.feat, 2 * d.feat))
    ph.temp(BF, both=(2 * d.feat, d.rows), leave=(d.parts, d.half, d.feat), arrive=(d.parts, d.half, d.feat))
    ph.temp(F32, dr1=(d.half, d.feat), e_aux=sq, e_cols=sq, d_aux=sq, d_cols=sq)
    ph.temp(F32, a_b1=sq, a_b5=sq, a_b6=sq, a_b9=sq, a_g2=sq)
    ph.temp(F32, a_s=(2 * d.feat, d.length), a_k=(d.blocks, 2 * d.feat, 128))
    ph.sems(send=2 * d.parts, recv=2 * d.parts)

    def body(r):
        p, b = pl.program_id(0), pl.program_id(1)
        first, last = b == 0, b == d.blocks - 1
        n = d.parts
        early = [to_partner(r.dn_far_in.at[i], r.arrive.at[i], r.send.at[n + i], r.recv.at[n + i]) for i in range(n)]
        jobs = [to_partner(r.leave.at[i], r.got.at[i], r.send.at[i], r.recv.at[i]) for i in range(n)]

        @pl.when(first & (p == 0))
        def _():
            greet_partner()
            for job in early:
                job.start()
            load_cols(r, 0, r.e_aux, r.e_cols)
            load_cols(r, 1, r.d_aux, r.d_cols)
            r.back[:, : d.feat] = r.mw1[1, d.feat : 2 * d.feat, :]
            r.back[:, d.feat :] = r.uw1[1, d.feat : 2 * d.feat, :]
            zero(r.msg, r.upd, r.a_b1, r.a_b5, r.a_b6, r.a_b9, r.a_g2)
            r.n_cat[d.half :] = r.got_a[...]

        @pl.when(first & (p == 1))
        def _():
            r.n_cat[d.half :] = r.got_b[...]

        for i in range(n):

            @pl.when(first & (p == i))
            def _(i=i):
                early[i].wait()

        @pl.when(first)
        def _():
            r.n_cat[: d.half] = r.n_own[p]
            zero(r.a_s)
            dn = r.cot_n[p].astype(F32) + r.dn_a[p] + r.arrive[p].astype(F32)
            node_backward(d, r, p, 1, r.d_aux[...], dn)

        e2 = r.e2[0, 0]
        da1m = message_backward(d, r, b, 1, r.d2[0, 0], r.g1[0, 0], r.d1[0, 0], e2)
        de = mm(r.back[:, : d.feat], da1m) + mm(r.back[:, d.feat :], r.dec_da1[0, 0])
        dy = (de + r.dec_dr3[0, 0].astype(F32)).astype(BF).astype(F32)
        xh = r.uxh[0, 0].astype(F32)
        r.a_b9[...] += lane_sum(dy)
        r.a_g2[...] += lane_sum(dy * xh)
        dr3 = norm_back(dy, xh, r.urs[0, 0], r.e_cols[:, 12:13])
        da1u, dr3b = update_backward(
            d, r, dr3, r.ug1[0, 0], r.ud1[0, 0], r.ug2[0, 0], r.ud2[0, 0], r.uw2[0], r.uw3[0], r.et[0, 0]
        )
        r.da1[0, 0] = da1u
        r.dr3[0, 0] = dr3b
        r.both[: d.feat] = da1m
        r.both[d.feat :] = da1u
        spread = mm(r.both[...], r.tn[0, 0])
        r.a_s[...] += spread[:, : d.length]
        r.a_k[b] = spread[:, d.length :]

        @pl.when(last)
        def _():
            n_cat = r.n_cat[...]
            a_k = [r.a_k[i] for i in range(d.blocks)]
            own_m, far_m, b0 = spread_nodes(
                d, r.a_s[: d.feat], [x[: d.feat] for x in a_k], r.mw1[1], n_cat, r.msg, 0
            )
            own_u, far_u, b4 = spread_nodes(
                d, r.a_s[d.feat :], [x[d.feat :] for x in a_k], r.uw1[0], n_cat, r.upd, 0
            )
            r.dn_own[p] = own_m + own_u + r.dr1[...]
            r.leave[p] = (far_m + far_u).astype(BF)
            for i in range(n):

                @pl.when(p == i)
                def _(i=i):
                    jobs[i].start()

            message_small(d, r, b0)
            update_small(d, r, b4)

            @pl.when(p == n - 1)
            def _():
                for job in jobs:
                    job.wait()

    return ph.call("dec_message_back", body)


def encoder_message_back(d, st, fa, fe, n_own, n_got, shape, consts):
    ph = Phase(d)
    ph.whole(dn_a=fe.dn_own, dn_b=fe.got, n_own=n_own, n_got=n_got)
    ph.whole(mask=consts.mask, rt=consts.sums, r1=fa.r1, ip=fa.ip, r2=fa.r2, big=fa.big, cnt=fa.cnt)
    ph.stream(tn=st.tn, et=st.et, g1=fa.g1, d1=fa.d1, d2=fa.d2, up_da1=fe.da1, up_dr3=fe.dr3)
    ph.whole(uw1=st.uw1, **weight_args(st, *NODE_W, *MSG_W))
    ph.out_edges(d, edge_grad=shape)
    ph.out_whole(F32, msg=(d.msg_rows, d.feat), dn_own=(d.parts, d.half, d.feat))
    ph.out_whole(BF, dn_far=(d.parts, d.half, d.feat))
    sq = (d.feat, d.feat)
    ph.temp(BF, n_cat=(d.length, d.feat), dub=(d.half, d.feat), back=(d.feat, 2 * d.feat))
    ph.temp(F32, dr1=(d.half, d.feat), aux=sq, cols=sq, a_b1=sq)
    ph.temp(F32, a_s=(d.feat, d.length), a_k=(d.blocks, d.feat, 128))

    def body(r):
        p, b = pl.program_id(0), pl.program_id(1)
        first, last = b == 0, b == d.blocks - 1

        @pl.when(first & (p == 0))
        def _():
            load_cols(r, 0, r.aux, r.cols)
            r.back[:, : d.feat] = r.mw1[0, d.feat : 2 * d.feat, :]
            r.back[:, d.feat :] = r.uw1[0, d.feat : 2 * d.feat, :]
            zero(r.msg, r.a_b1)

        @pl.when(first)
        def _():
            r.n_cat[: d.half] = r.n_own[p]
            r.n_cat[d.half :] = r.n_got[p]
            zero(r.a_s)
            node_backward(d, r, p, 0, r.aux[...], r.dn_a[p] + r.dn_b[p].astype(F32))

        da1m = message_backward(d, r, b, 0, r.d2[0, 0], r.g1[0, 0], r.d1[0, 0], r.et[0, 0])
        de = mm(r.back[:, : d.feat], da1m) + mm(r.back[:, d.feat :], r.up_da1[0, 0])
        de = (de + r.up_dr3[0, 0].astype(F32)).astype(BF)
        r.edge_grad[0] = de.T.reshape(d.res, d.near, d.feat)
        spread = mm(da1m, r.tn[0, 0])
        r.a_s[...] += spread[:, : d.length]
        r.a_k[b] = spread[:, d.length :]

        @pl.when(last)
        def _():
            own, far, b0 = spread_nodes(
                d, r.a_s[...], [r.a_k[i] for i in range(d.blocks)], r.mw1[0], r.n_cat[...], r.msg, 0
            )
            r.dn_own[p] = own + r.dr1[...]
            r.dn_far[p] = far.astype(BF)
            message_small(d, r, b0)

    return ph.call("enc_message_back", body)


def reduce_grads(d, enc_msg, enc_upd, dec_msg, dec_upd, dn_far):
    devices = d.devices
    bits = devices.bit_length() - 1
    unit = 16 * devices
    rows = -(-(d.msg_rows + d.upd_rows) // unit) * unit
    feat = d.feat
    sizes = [rows >> (i + 1) for i in range(bits)]

    def kernel(em, eu, dm, du, far, res, got, acc, *rest):
        halves = rest[: 2 * bits]
        sec_send, sec_recv, gathered, send, recv = rest[2 * bits :]
        section, me = lax.axis_index(AXIS_S), lax.axis_index(AXIS_D)

        def dp_peer(bit):
            flag = lax.rem(me // (1 << bit), 2)
            return {AXIS_D: me + (1 - 2 * flag) * (1 << bit)}, flag

        barrier = pltpu.get_barrier_semaphore()
        pl.semaphore_signal(barrier, inc=1, device_id=other_section(), device_id_type=MESH)
        for bit in range(bits):
            pl.semaphore_signal(barrier, inc=1, device_id=dp_peer(bit)[0], device_id_type=MESH)
        pl.semaphore_wait(barrier, bits + 1)

        def remote(src, dst, at, peer):
            return pltpu.make_async_remote_copy(
                src_ref=src, dst_ref=dst, send_sem=send.at[at], recv_sem=recv.at[at],
                device_id=peer, device_id_type=MESH,
            )

        nodes = remote(far, got, 0, other_section())
        nodes.start()
        m, u = d.msg_rows, d.upd_rows
        for layer, (msg, upd) in enumerate(((em, eu), (dm, du))):
            acc[layer, :m] = msg[...]
            acc[layer, m : m + u] = upd[...]
            if rows > m + u:
                acc[layer, m + u :] = jnp.zeros((rows - m - u, feat), F32)

        start = 0
        for step in range(bits):
            peer, flag = dp_peer(step)
            size = sizes[step]
            keep = pl.multiple_of(start + flag * size, 16)
            give = pl.multiple_of(start + (1 - flag) * size, 16)
            out, into = halves[2 * step], halves[2 * step + 1]
            if step == 0:
                out[...] = acc[:, pl.ds(give, size), :].astype(BF)
            else:
                out[...] = acc[section, pl.ds(give, size), :].astype(BF)
            job = remote(out, into, 1 + step, peer)
            job.start()
            job.wait()
            if step == 0:
                acc[:, pl.ds(keep, size), :] += into[...].astype(F32)
                sec_send[...] = acc[1 - section, pl.ds(keep, size), :].astype(BF)
                job = remote(sec_send, sec_recv, 1 + bits, other_section())
                job.start()
                job.wait()
                acc[section, pl.ds(keep, size), :] += sec_recv[...].astype(F32)
            else:
                acc[section, pl.ds(keep, size), :] += into[...].astype(F32)
            start = keep
        if bits == 0:
            sec_send[...] = acc[1 - section].astype(BF)
            job = remote(sec_send, sec_recv, 1 + bits, other_section())
            job.start()
            job.wait()
            acc[section] += sec_recv[...].astype(F32)
        size = sizes[-1] if bits else rows
        gathered[pl.ds(pl.multiple_of(start, 16), size), :] = acc[section, pl.ds(pl.multiple_of(start, 16), size), :].astype(BF)
        for step in reversed(range(bits)):
            peer, flag = dp_peer(step)
            size = sizes[step]
            part = gathered.at[pl.ds(pl.multiple_of(start, 16), size), :]
            job = remote(part, part, 2 + bits + step, peer)
            job.start()
            job.wait()
            start = start - flag * size
        res[...] = gathered[...]
        nodes.wait()

    vm = pl.BlockSpec(memory_space=pltpu.VMEM)
    scratch = [pltpu.VMEM((2, rows, feat), F32)]
    for step in range(bits):
        shape = (2, sizes[0], feat) if step == 0 else (sizes[step], feat)
        scratch += [pltpu.VMEM(shape, BF)] * 2
    across = sizes[0] if bits else rows
    scratch += [pltpu.VMEM((across, feat), BF)] * 2 + [pltpu.VMEM((rows, feat), BF)]
    scratch += [pltpu.SemaphoreType.DMA((2 * bits + 2,))] * 2
    return pl.pallas_call(
        kernel,
        in_specs=[vm] * 5,
        out_specs=[vm, pl.BlockSpec(memory_space=pl.ANY)],
        out_shape=[
            jax.ShapeDtypeStruct((rows, feat), BF),
            jax.ShapeDtypeStruct(dn_far.shape, BF),
        ],
        scratch_shapes=scratch,
        compiler_params=pltpu.CompilerParams(vmem_limit_bytes=58 << 20, collective_id=5, has_side_effects=True),
        name="reduce",
    )(enc_msg, enc_upd, dec_msg, dec_upd, dn_far)


def unpack(d, total, dn_own, dn_got, n_bias, n_gain):
    f = d.feat
    m = d.msg_rows
    shapes = [(1, 3 * f, f), (1, f, f), (1, f, f), (1, f, d.wide), (1, 1, d.wide), (1, d.wide, f)]
    shapes += [(1, 3 * f, f), (1, f, f), (1, f, f), (1, n_bias, f), (1, n_gain, f)]

    def kernel(t, own, got, node, mw1, mw2, mw3, inner, inner_b, outer, uw1, uw2, uw3, bias, gain):
        node[...] = (own[...] + got[...].astype(F32)).astype(BF)
        for ref, at in ((mw1, 0), (mw2, 3 * f), (mw3, 4 * f), (outer, d.at_outer)):
            ref[0] = t[at : at + ref.shape[1], :].astype(F32)
        for ref, at in ((uw1, m), (uw2, m + 3 * f), (uw3, m + 4 * f)):
            ref[0] = t[at : at + ref.shape[1], :].astype(F32)
        inner[0] = t[d.at_inner : d.at_inner + d.wide, :].astype(F32).T
        small = t[d.at_small : d.at_small + SMALL, :].astype(F32)
        other = t[m + 5 * f : m + 5 * f + SMALL, :].astype(F32)
        both = small + other
        bias[0] = both[:n_bias]
        gain[0] = both[n_bias : n_bias + n_gain]
        for i in range(d.wide // f):
            inner_b[0, :, i * f : (i + 1) * f] = small[16 + i : 17 + i]

    vm = pl.BlockSpec(memory_space=pltpu.VMEM)
    out = [jax.ShapeDtypeStruct(dn_own.shape, BF)] + [jax.ShapeDtypeStruct(s, F32) for s in shapes]
    return pl.pallas_call(kernel, in_specs=[vm] * 3, out_specs=[vm] * len(out), out_shape=out, name="unpack")(
        total, dn_own, dn_got
    )


def per_device(
    node_input,
    edge_input,
    neighbors,
    residue_mask,
    decode_order,
    node_cotangent,
    edge_cotangent,
    message_w1,
    message_w2,
    message_w3,
    inner_w,
    inner_bias,
    outer_w,
    update_w1,
    update_w2,
    update_w3,
    biases,
    norm_gains,
):
    section = lax.axis_index(AXIS_S)
    is_first = section == 0
    parts, half, near, feat = edge_input.shape
    length = neighbors.shape[1]
    wide = inner_w.shape[2]
    res = BLOCK_RES
    rows = res * near
    blocks = half // res
    at_outer = 5 * feat
    at_inner = at_outer + wide
    at_small = at_inner + wide
    d = types.SimpleNamespace(
        parts=parts, half=half, near=near, feat=feat, length=length, wide=wide, res=res, rows=rows, blocks=blocks,
        at_outer=at_outer, at_inner=at_inner, at_small=at_small, msg_rows=at_small + SMALL,
        upd_rows=5 * feat + SMALL, devices=lax.axis_size(AXIS_D),
    )
    weights = dict(
        mw1=message_w1, mw2=message_w2, mw3=message_w3, inner=inner_w, inner_b=inner_bias[:, None, :], outer=outer_w,
        uw1=update_w1, uw2=update_w2, uw3=update_w3, bias=biases, gain=norm_gains,
    )
    own_ids = lax.dynamic_slice_in_dim(neighbors, section * half, half, 1)
    idx_row = own_ids.reshape(parts, blocks, 1, rows)
    sums = np.zeros((128, rows), np.float32)
    sums[np.arange(rows) // near, np.arange(rows)] = 1.0
    sums = jnp.asarray(sums, BF)
    st = prepare(d, idx_row, edge_input, sums, node_input, weights)

    def own_first(x):
        return jnp.where(is_first, x, jnp.roll(x, half, axis=1))

    live = own_first(residue_mask)
    order = own_first(decode_order)
    centre = length // 2
    code = jnp.where(live == 1, order - centre, centre)
    own_code = (order[:, :half] - centre).reshape(parts, blocks, 1, res)
    lead = (parts, blocks, 1, length)
    top = jnp.pad(jnp.broadcast_to(live[:, None, None, :], lead), ((0, 0), (0, 0), (0, 0), (0, res)))
    second = jnp.concatenate([jnp.broadcast_to(code[:, None, None, :], lead), -own_code], axis=3)
    extra = jnp.concatenate([top, second, jnp.zeros((parts, blocks, EXTRA - 2, length + res), top.dtype)], axis=2)
    mask = jnp.broadcast_to(live[:, :half, None].astype(F32), (parts, half, feat))
    consts = types.SimpleNamespace(extra=extra.astype(BF), sums=sums, mask=mask)

    fa = encoder_message(d, st, node_input, st.nodes_got, consts)
    fb = encoder_update(d, st, fa, consts)
    fd = decoder_update(d, st, fb, edge_cotangent)
    fe = middle_backward(d, st, fa, fb, fd, node_cotangent, consts)
    ff = encoder_message_back(d, st, fa, fe, node_input, st.nodes_got, edge_input.shape, consts)
    total, got = reduce_grads(d, ff.msg, fe.upd, fe.msg, fd.upd, ff.dn_far)
    node_grad, mw1, mw2, mw3, inner, inner_b, outer, uw1, uw2, uw3, bias, gain = unpack(
        d, total, ff.dn_own, got, biases.shape[1], norm_gains.shape[1]
    )
    return (
        fb.node_out, fd.decoded, node_grad, ff.edge_grad, mw1, mw2, mw3, inner, inner_b[:, 0], outer,
        uw1, uw2, uw3, bias, gain,
    )


def solution(mesh):
    def split(*axes):
        return P(*axes)

    by_part = split(AXIS_D)
    by_half = split(AXIS_D, AXIS_S)
    by_layer = split(AXIS_S)
    in_specs = (by_half, by_half, by_part, by_part, by_part, by_half, by_half) + (by_layer,) * 11
    out_specs = (by_half,) * 4 + (by_layer,) * 11
    return jax.shard_map(per_device, mesh=mesh, in_specs=in_specs, out_specs=out_specs, check_vma=False)
```

```python
import types

import jax
import jax.numpy as jnp
import numpy as np
from jax import lax
from jax.experimental import pallas as pl
from jax.experimental.pallas import tpu as pltpu
from jax.sharding import PartitionSpec as P

BF = jnp.bfloat16
F32 = jnp.float32
C1 = 0.7978845608
C2 = C1 * 0.044715
EPS = 1e-5
BLOCK_RES = 64
EXTRA = 16
SMALL = 32
MESH = pl.DeviceIdType.MESH


def mm(a, b, ca=1, cb=0):
    return lax.dot_general(a, b, (((ca,), (cb,)), ((), ())), preferred_element_type=F32)


def mm_exact(a, b, ca=1, cb=0):
    return lax.dot_general(
        a, b, (((ca,), (cb,)), ((), ())), precision=lax.Precision.HIGHEST, preferred_element_type=F32
    )


def gelu_pair(x):
    x = x.astype(BF)
    w = x * x * BF(C2)
    h = jnp.tanh(x * (w + BF(C1))) + BF(1.0)
    g = x * h
    d = h + g * (BF(2.0) - h) * (w * BF(3.0) + BF(C1))
    return g, d


def gelu_pair_wide(x):
    x2 = x * x
    h = 0.5 * jnp.tanh(x * (x2 * C2 + C1)) + 0.5
    g = x * h
    d = h + (g * (1.0 - h)) * (x2 * (6 * C2) + 2 * C1)
    return g, d


def lane_sum(x):
    total = x[:, :128]
    for at in range(128, x.shape[1], 128):
        total = total + x[:, at : at + 128]
    return total


def to_row(acc):
    return mm_exact(jnp.ones((8, acc.shape[1]), F32), acc, 1, 1)[0:1]


def norm_rows(r):
    c = r - jnp.mean(r, axis=-1, keepdims=True)
    rs = lax.rsqrt(jnp.mean(c * c, axis=-1, keepdims=True) + EPS)
    return c * rs, rs


def norm_back_rows(dxh, xh, rs):
    m1 = jnp.mean(dxh, axis=-1, keepdims=True)
    m2 = jnp.mean(dxh * xh, axis=-1, keepdims=True)
    return (dxh - m1 - xh * m2) * rs


def norm_back(dy, xh, rs, gain_col):
    dxh = dy * gain_col
    m1 = jnp.mean(dxh, axis=0, keepdims=True)
    m2 = jnp.mean(dxh * xh, axis=0, keepdims=True)
    return (dxh - m1 - xh * m2) * rs


class Refs:
    def __init__(self, plain, slots, waits):
        self.__dict__.update(plain)
        self._slots, self._waits = slots, waits

    def __getattr__(self, name):
        slots = self.__dict__.get(SLOTS, {})
        if name not in slots:
            raise AttributeError(name)
        wait = self._waits.pop(name, None)
        if wait is not None:
            wait()
        return slots[name]


SLOTS = "_slots"


class Phase:
    def __init__(self, dims, collective_id=None):
        self.d = dims
        self.collective_id = collective_id
        self.ins, self.outs, self.temps, self.kinds = [], [], [], {}

    def whole_spec(self, shape):
        rank = len(shape)
        return pl.BlockSpec(tuple(shape), lambda p, b: (0,) * rank)

    def whole(self, **arrays):
        self.ins += [(n, a, self.whole_spec(a.shape)) for n, a in arrays.items()]

    def raw(self, **arrays):
        self.ins += [(n, a, pl.BlockSpec(memory_space=pl.ANY)) for n, a in arrays.items()]

    def stream(self, **arrays):
        self.raw(**arrays)
        self.kinds.update({n: (False, False, a.shape[2:], a.dtype) for n, a in arrays.items()})

    def edges(self, **arrays):
        self.raw(**arrays)
        block = (self.d.res, self.d.near, self.d.feat)
        self.kinds.update({n: (False, True, block, a.dtype) for n, a in arrays.items()})

    def out_whole(self, dtype, **shapes):
        self.outs += [(n, jax.ShapeDtypeStruct(s, dtype), self.whole_spec(s)) for n, s in shapes.items()]

    def out_raw(self, dtype, **shapes):
        spec = pl.BlockSpec(memory_space=pl.ANY)
        self.outs += [(n, jax.ShapeDtypeStruct(s, dtype), spec) for n, s in shapes.items()]

    def out_stream(self, dtype, **shapes):
        self.out_raw(dtype, **shapes)
        self.kinds.update({n: (True, False, s[2:], dtype) for n, s in shapes.items()})

    def out_edges(self, **shapes):
        self.out_raw(BF, **shapes)
        block = (self.d.res, self.d.near, self.d.feat)
        self.kinds.update({n: (True, True, block, BF) for n in shapes})

    def temp(self, dtype, **shapes):
        self.temps += [(n, pltpu.VMEM(s, dtype)) for n, s in shapes.items()]

    def sems(self, **counts):
        self.temps += [(n, pltpu.SemaphoreType.DMA((c,))) for n, c in counts.items()]

    def call(self, name, body):
        d = self.d
        names = [n for n, _, _ in self.ins] + [n for n, _, _ in self.outs] + [n for n, _ in self.temps]
        steps = d.parts * d.blocks
        buffers = [pltpu.VMEM((2,) + tuple(block), dtype) for _, _, block, dtype in self.kinds.values()]
        count = len(self.kinds)

        def kernel(*refs):
            refs, slots, sems = refs[: len(names)], refs[len(names) : len(names) + count], refs[len(names) + count :]
            plain = dict(zip(names, refs))
            step = pl.program_id(0) * d.blocks + pl.program_id(1)
            now = lax.rem(step, 2)

            def copy(i, n, at, slot):
                out, edges, _, _ = self.kinds[n]
                p, b = at // d.blocks, lax.rem(at, d.blocks)
                if edges:
                    far = plain[n].at[p, pl.ds(pl.multiple_of(b * d.res, d.res), d.res)]
                else:
                    far = plain[n].at[p, b]
                near = slots[i].at[slot]
                return pltpu.make_async_copy(*((near, far) if out else (far, near)), sems[i].at[slot])

            into = [(i, n) for i, n in enumerate(self.kinds) if not self.kinds[n][0]]
            outof = [(i, n) for i, n in enumerate(self.kinds) if self.kinds[n][0]]

            @pl.when(step == 0)
            def _():
                for i, n in into:
                    copy(i, n, step, now).start()

            @pl.when(step + 1 < steps)
            def _():
                for i, n in into:
                    copy(i, n, step + 1, 1 - now).start()

            @pl.when(step >= 2)
            def _():
                for i, n in outof:
                    copy(i, n, step - 2, now).wait()

            waits = {n: copy(i, n, step, now).wait for i, n in into}
            named = {n: slots[i].at[now] for i, n in enumerate(self.kinds)}
            body(Refs({n: x for n, x in plain.items() if n not in named}, named, waits))
            for wait in waits.values():
                wait()
            for i, n in outof:
                copy(i, n, step, now).start()

            @pl.when(step == steps - 1)
            def _():
                for i, n in outof:
                    if steps > 1:
                        copy(i, n, step - 1, 1 - now).wait()
                    copy(i, n, step, now).wait()

        results = pl.pallas_call(
            kernel,
            grid=(d.parts, d.blocks),
            in_specs=[s for _, _, s in self.ins],
            out_specs=[s for _, _, s in self.outs],
            out_shape=[s for _, s, _ in self.outs],
            scratch_shapes=[s for _, s in self.temps] + buffers + [pltpu.SemaphoreType.DMA((2,))] * count,
            compiler_params=pltpu.CompilerParams(
                dimension_semantics=(pltpu.ARBITRARY,) * 2,
                vmem_limit_bytes=60 << 20,
                collective_id=self.collective_id,
                has_side_effects=self.collective_id is not None,
            ),
            name=name,
        )(*[a for _, a, _ in self.ins])
        return types.SimpleNamespace(**dict(zip([n for n, _, _ in self.outs], results)))


def other_section():
    return {AXIS_S: 1 - lax.axis_index(AXIS_S)}


AXIS_S = "section"
AXIS_D = "dp"


def greet_partner():
    barrier = pltpu.get_barrier_semaphore()
    pl.semaphore_signal(barrier, inc=1, device_id=other_section(), device_id_type=MESH)
    pl.semaphore_wait(barrier, 1)


def to_partner(src, dst, send, recv):
    return pltpu.make_async_remote_copy(
        src_ref=src, dst_ref=dst, send_sem=send, recv_sem=recv, device_id=other_section(), device_id_type=MESH
    )


def put_one_hot(d, ref, at, idx):
    idx = idx.astype(jnp.int16)
    place = lax.broadcasted_iota(jnp.int16, (d.length, d.rows), 0)
    ref[at : at + d.length, :] = jnp.where(place == idx, jnp.ones((), BF), jnp.zeros((), BF))


def put_one_hot_rows(d, ref, idx):
    centre = d.length // 2
    idx = jnp.broadcast_to((idx - centre).astype(F32).astype(BF), (128, d.rows)).T
    place = lax.broadcasted_iota(jnp.int32, (d.rows, 128), 1)
    for at in range(0, d.length, 128):
        there = (place + (at - centre)).astype(F32).astype(BF)
        ref[:, at : at + 128] = jnp.where(idx == there, jnp.ones((), BF), jnp.zeros((), BF))


def weight_args(w, *names):
    return {n: getattr(w, n) for n in names}


def load_cols(r, layer, aux, cols):
    n_bias, n_gain = r.bias.shape[1], r.gain.shape[1]
    aux[...] = jnp.zeros(aux.shape, F32)
    for i in range(n_bias):
        aux[i : i + 1] = r.bias[layer, i]
    for i in range(n_gain):
        aux[n_bias + i : n_bias + i + 1] = r.gain[layer, i]
    cols[...] = aux[...].T


def put_table(d, lhs, at, left, n_cat, w1, n_blk, bias_col, first):
    @pl.when(first)
    def _():
        lhs[at : at + d.feat, left : left + d.length] = mm(w1[2 * d.feat :, :].T, n_cat[...], 1, 1).astype(BF)

    own = mm(w1[0 : d.feat, :].T, n_blk, 1, 1) + bias_col
    lhs[at : at + d.feat, left + d.length :] = own.astype(BF)


def message_part(a1, w2t, b2, att):
    g1, d1 = gelu_pair(a1)
    a2 = mm(w2t, g1) + b2
    g2, d2 = gelu_pair(a2)
    attb = att.astype(BF)
    return g1, d1, g2 * attb, d2 * attb


def add_node_outs(ph, d):
    ph.out_whole(BF, node_out=(d.parts, d.half, d.feat))
    shape = (d.parts, d.half, d.feat)
    ph.out_whole(F32, r1=shape, ip=(d.parts, d.half, d.wide), r2=shape, big=shape, cnt=shape)


def node_step(d, r, p, b, g2m, att, rt):
    big = mm(rt, g2m, 1, 1) * 0.5
    cnt = mm(rt, jnp.broadcast_to(att.astype(BF), (16, att.shape[1])), 1, 1)
    at = pl.ds(pl.multiple_of(b * d.res, d.res), d.res)
    r.big[p, at, :] = big
    r.cnt[p, at, :] = jnp.broadcast_to(cnt[:, 0:1], big.shape)


def node_forward(r, p, n_own, layer, aux):
    big = r.big[p]
    hi = big.astype(BF)
    lo = (big - hi.astype(F32)).astype(BF)
    w3 = r.mw3[layer]
    upd = (mm(hi, w3) + mm(lo, w3) + r.cnt[p] * aux[2:3]) / 30.0
    r1 = n_own.astype(F32) + upd
    xh1, _ = norm_rows(r1)
    normed = xh1 * aux[10:11] + aux[7:8]
    ip = mm(normed.astype(BF), r.inner[layer]) + r.inner_b[layer]
    hid = gelu_pair_wide(ip)[0].astype(BF)
    r2 = normed + (mm(hid, r.outer[layer]) + aux[3:4])
    xh2, _ = norm_rows(r2)
    out = ((xh2 * aux[11:12] + aux[8:9]) * r.mask[p]).astype(BF)
    r.node_out[p] = out
    r.r1[p] = r1
    r.ip[p] = ip
    r.r2[p] = r2
    return out


def node_backward(d, r, p, layer, aux, dn):
    r1, ip, r2, big, cnt = r.r1[p], r.ip[p], r.r2[p], r.big[p], r.cnt[p]
    xh1, rs1 = norm_rows(r1)
    normed = xh1 * aux[10:11] + aux[7:8]
    xh2, rs2 = norm_rows(r2)
    dy2 = dn * r.mask[p]
    dr2 = norm_back_rows(dy2 * aux[11:12], xh2, rs2)
    low_outer = dr2.astype(BF)
    hid, slope = gelu_pair_wide(ip)
    dip = mm(low_outer, r.outer[layer], 1, 1) * slope
    low_inner = dip.astype(BF)
    at = d.at_outer
    r.msg[at : at + d.wide] += mm(hid.astype(BF), low_outer, 0, 0)
    at = d.at_inner
    r.msg[at : at + d.wide] += mm(low_inner, normed.astype(BF), 0, 0)
    dnormed = dr2 + mm(low_inner, r.inner[layer], 1, 1)
    dr1 = norm_back_rows(dnormed * aux[10:11], xh1, rs1)
    du = dr1 / 30.0
    dub = du.astype(BF)
    r.msg[4 * d.feat : 5 * d.feat] += mm(big.astype(BF), dub, 0, 0)
    dib = jnp.sum(dip, axis=0, keepdims=True)
    rows = {
        2: jnp.sum(cnt * du, axis=0, keepdims=True),
        3: jnp.sum(dr2, axis=0, keepdims=True),
        7: jnp.sum(dnormed, axis=0, keepdims=True),
        8: jnp.sum(dy2, axis=0, keepdims=True),
        10: jnp.sum(dnormed * xh1, axis=0, keepdims=True),
        11: jnp.sum(dy2 * xh2, axis=0, keepdims=True),
    }
    for i in range(d.wide // d.feat):
        rows[16 + i] = dib[:, i * d.feat : (i + 1) * d.feat]
    for row, value in rows.items():
        r.msg[d.at_small + row : d.at_small + row + 1] += value
    r.dr1[...] = dr1
    r.dub[...] = dub


def encoder_message(d, edge_input, node_input, weights, consts):
    ph = Phase(d, 2)
    ph.whole(n_own=node_input, idx=consts.idx, rt=consts.sums, mask=consts.mask, extra=consts.extra)
    ph.edges(edge=edge_input)
    names = tuple(weights)
    own = {W_IN + n: a for n, a in weights.items()}
    ph.raw(**own)
    act = (d.parts, d.blocks, d.feat, d.rows)
    ph.out_stream(BF, g1=with_ones(d), d1=act, d2=act)
    ph.out_whole(F32, att=(d.parts, d.blocks, 1, d.rows))
    add_node_outs(ph, d)
    ph.out_raw(BF, got=(d.half, d.feat), nodes_got=node_input.shape)
    for n, a in weights.items():
        ph.out_raw(a.dtype, **{W_OUT + n: (2,) + a.shape})
        ph.temp(a.dtype, **{n: (2,) + a.shape})
    sq = (d.feat, d.feat)
    wide = d.feat + d.length + d.res
    ph.temp(BF, n_cat=(d.length, d.feat), lhs=(d.feat + EXTRA, wide), w2t=sq, tt=(wide, d.rows))
    ph.temp(BF, leave=(d.half, d.feat), arrive=node_input.shape)
    ph.temp(F32, aux=sq, cols=sq)
    count = len(names)
    ph.sems(send=count + 2, recv=count + 2, local=count, back=2 * count + 1)

    def body(r):
        p, b = pl.program_id(0), pl.program_id(1)
        first, last = b == 0, b == d.blocks - 1
        section = lax.axis_index(AXIS_S)
        job = to_partner(r.leave, r.got, r.send.at[count], r.recv.at[count])
        nodes = to_partner(r.n_own, r.arrive, r.send.at[count + 1], r.recv.at[count + 1])

        def swaps(group):
            out = []
            for n in group:
                i = names.index(n)
                dst = getattr(r, n).at[section]
                out.append(to_partner(getattr(r, W_IN + n), dst, r.send.at[i], r.recv.at[i]))
            return out

        def own_copies():
            return [
                pltpu.make_async_copy(getattr(r, W_IN + n), getattr(r, n).at[section], r.local.at[i])
                for i, n in enumerate(names)
            ]

        def returns():
            out = [pltpu.make_async_copy(r.arrive, r.nodes_got, r.back.at[2 * count])]
            for i, n in enumerate(names):
                src, dst = getattr(r, n), getattr(r, W_OUT + n)
                for layer in range(2):
                    sem = r.back.at[2 * i + layer]
                    out.append(pltpu.make_async_copy(src.at[layer], dst.at[layer], sem))
            return out

        begin = first & (p == 0)
        middle = (p == 1) & (b == 1)
        at_end = last & (p == d.parts - 1)

        @pl.when(begin)
        def _():
            greet_partner()
            nodes.start()
            for item in swaps(GROUP_ONE) + own_copies():
                item.start()
            r.tt[d.feat + d.length :, :] = r.rt[: d.res]

        put_one_hot(d, r.tt, d.feat, r.idx[p, b])
        r.tt[: d.feat, :] = r.edge[...].reshape(d.rows, d.feat).T

        @pl.when(begin)
        def _():
            nodes.wait()
            for item in swaps(GROUP_ONE) + own_copies():
                item.wait()
            for item in swaps(GROUP_TWO):
                item.start()
            r.lhs[: d.feat, : d.feat] = r.mw1[0, d.feat : 2 * d.feat, :].T
            r.lhs[d.feat :, : d.feat] = jnp.zeros((EXTRA, d.feat), BF)
            r.w2t[...] = half_of(r.mw2[0]).T
            load_cols(r, 0, r.aux, r.cols)

        @pl.when(first)
        def _():
            r.n_cat[: d.half] = r.n_own[p]
            r.n_cat[d.half :] = r.arrive[p]

        n_blk = r.n_own[p, pl.ds(pl.multiple_of(b * d.res, d.res), d.res), :]
        put_table(d, r.lhs, 0, d.feat, r.n_cat, r.mw1.at[0], n_blk, r.cols[:, 0:1], first)
        r.lhs[d.feat :, d.feat :] = r.extra[p, b]
        out = mm(r.lhs[...], r.tt[...])
        att = out[d.feat : d.feat + 1]
        r.att[p, b] = jnp.where(out[d.feat + 1 : d.feat + 2] < 0.0, 1.0, 0.0)
        g1, r.d1[...], g2m, r.d2[...] = message_part(out[: d.feat], r.w2t[...], r.cols[:, 1:2], att)
        put_ones(r.g1, g1)
        node_step(d, r, p, b, g2m, att, r.rt[: d.res])

        @pl.when(middle)
        def _():
            for item in swaps(GROUP_TWO):
                item.wait()
            for item in swaps(GROUP_THREE):
                item.start()
            r.leave[...] = node_forward(r, 0, r.n_own[0], 0, r.aux[...])
            job.start()

        @pl.when(at_end)
        def _():
            node_forward(r, d.parts - 1, r.n_own[d.parts - 1], 0, r.aux[...])
            for item in swaps(GROUP_THREE):
                item.wait()
            for item in returns():
                item.start()
            for item in returns():
                item.wait()
            job.wait()

    return ph.call("enc_message", body)


W_IN, W_OUT = "i_", "o_"
GROUP_ONE = ("mw1", "mw2", "bias", "gain")
GROUP_TWO = ("mw3", "inner", "inner_b", "outer")
GROUP_THREE = ("uw1", "uw2", "uw3")
NODE_W = ("mw3", "inner", "inner_b", "outer", "bias", "gain")
MSG_W = ("mw1", "mw2")
UPD_W = ("uw1", "uw2", "uw3")


def with_ones(d):
    return (d.parts, d.blocks, d.feat + 16, d.rows)


def put_ones(ref, g):
    feat, rows = g.shape
    ref[:feat] = g
    ref[feat:] = jnp.ones((16, rows), BF)


def half_of(w):
    return w * BF(0.5)


def update_forward(d, a1, w2t, w3c, b5, b6c, pair, cols):
    f = d.feat
    g1, d1 = gelu_pair(a1)
    a2 = mm(w2t, g1) + b5
    g2, d2 = gelu_pair(a2)
    pair[f : 2 * f] = g2
    cent = mm(w3c[...], pair[: 2 * f]) + b6c
    var = jnp.mean(cent * cent, axis=0, keepdims=True)
    rs = lax.rsqrt(var + EPS)
    xh = cent.astype(BF) * rs.astype(BF)
    y = xh * cols[:, 12:13].astype(BF) + cols[:, 9:10].astype(BF)
    return g1, d1, g2, d2, xh, rs, y


def centre_weights(w3, cols, w3c, b6c):
    feat = w3.shape[0]
    eye = lax.broadcasted_iota(jnp.int32, w3.shape, 0) == lax.broadcasted_iota(jnp.int32, w3.shape, 1)
    w3f = w3.astype(F32)
    w3c[:, feat:] = (0.5 * (w3f - jnp.mean(w3f, axis=1, keepdims=True))).T.astype(BF)
    w3c[:, :feat] = (eye.astype(F32) - 1.0 / feat).astype(BF)
    b6 = cols[:, 6:7]
    b6c[...] = jnp.broadcast_to(b6 - jnp.mean(b6, axis=0, keepdims=True), b6c.shape)


def encoder_update(d, edge_input, st, fa, consts):
    ph = Phase(d, 3)
    ph.whole(n_own=fa.node_out, got_a=fa.got, idx=consts.idx, rt=consts.sums, mask=consts.mask, att=fa.att)
    ph.edges(edge=edge_input)
    ph.whole(**weight_args(st, *NODE_W, *MSG_W, *UPD_W))
    act = (d.parts, d.blocks, d.feat, d.rows)
    tall = with_ones(d)
    ph.out_stream(BF, ug1=tall, ud1=act, ug2=tall, ud2=act, uxh=act, e2=act, g1=tall, d1=act, d2=act)
    ph.out_whole(F32, urs=(d.parts, d.blocks, 1, d.rows))
    add_node_outs(ph, d)
    ph.out_whole(BF, got_in=(d.half, d.feat))
    ph.out_raw(BF, got=(d.parts, d.half, d.feat))
    sq = (d.feat, d.feat)
    wide = d.feat + d.length + d.res
    ph.temp(BF, n_cat=(d.length, d.feat), lhs=(2 * d.feat, wide), tt=(wide, d.rows))
    ph.temp(BF, uw2t=sq, mw1bt=sq, mw2t=sq, w3c=(d.feat, 2 * d.feat), pair=(2 * d.feat, d.rows))
    ph.temp(BF, leave=(d.parts, d.half, d.feat), lead=(d.half, d.feat), arrive=(d.half, d.feat))
    ph.temp(F32, w3c_b=sq, e_aux=sq, e_cols=sq, d_aux=sq, d_cols=sq)
    ph.sems(send=d.parts + 1, recv=d.parts + 1)

    def body(r):
        p, b = pl.program_id(0), pl.program_id(1)
        first, last = b == 0, b == d.blocks - 1
        early = to_partner(r.lead, r.arrive, r.send.at[d.parts], r.recv.at[d.parts])
        jobs = [to_partner(r.leave.at[i], r.got.at[i], r.send.at[i], r.recv.at[i]) for i in range(d.parts)]

        @pl.when(first & (p == 0))
        def _():
            greet_partner()
            r.lead[...] = r.n_own[d.parts - 1]
            early.start()
            r.tt[d.feat + d.length :, :] = r.rt[: d.res]
            r.lhs[: d.feat, : d.feat] = r.uw1[0, d.feat : 2 * d.feat, :].T
            r.lhs[d.feat :, : d.feat] = jnp.zeros((d.feat, d.feat), BF)
            r.uw2t[...] = half_of(r.uw2[0]).T
            r.mw1bt[...] = r.mw1[1, d.feat : 2 * d.feat, :].T
            r.mw2t[...] = half_of(r.mw2[1]).T
            load_cols(r, 0, r.e_aux, r.e_cols)
            load_cols(r, 1, r.d_aux, r.d_cols)
            centre_weights(r.uw3[0], r.e_cols[...], r.w3c, r.w3c_b)
            r.n_cat[d.half :] = r.got_a[...]

        @pl.when(first & (p == 1))
        def _():
            early.wait()
            r.n_cat[d.half :] = r.arrive[...]
            r.got_in[...] = r.arrive[...]

        @pl.when(first)
        def _():
            r.n_cat[: d.half] = r.n_own[p]

        n_blk = r.n_own[p, pl.ds(pl.multiple_of(b * d.res, d.res), d.res), :]
        put_table(d, r.lhs, 0, d.feat, r.n_cat, r.uw1.at[0], n_blk, r.e_cols[:, 4:5], first)
        put_table(d, r.lhs, d.feat, d.feat, r.n_cat, r.mw1.at[1], n_blk, r.d_cols[:, 0:1], first)
        put_one_hot(d, r.tt, d.feat, r.idx[p, b])
        edge_t = r.edge[...].reshape(d.rows, d.feat).T
        r.tt[: d.feat, :] = edge_t
        r.pair[: d.feat] = edge_t
        out = mm(r.lhs[...], r.tt[...])
        g1, d1, g2, d2, xh, rs, e2 = update_forward(
            d, out[: d.feat], r.uw2t[...], r.w3c, r.e_cols[:, 5:6], r.w3c_b[:, 0:1], r.pair, r.e_cols
        )
        put_ones(r.ug1, g1)
        put_ones(r.ug2, g2)
        r.ud1[...], r.ud2[...], r.uxh[...], r.urs[p, b], r.e2[...] = d1, d2, xh, rs, e2
        att = r.att[p, b]
        a1 = out[d.feat :] + mm(r.mw1bt[...], e2)
        g1, r.d1[...], g2m, r.d2[...] = message_part(a1, r.mw2t[...], r.d_cols[:, 1:2], att)
        put_ones(r.g1, g1)
        node_step(d, r, p, b, g2m, att, r.rt[: d.res])

        @pl.when(last)
        def _():
            r.leave[p] = node_forward(r, p, r.n_own[p], 1, r.d_aux[...])
            for i in range(d.parts):

                @pl.when(p == i)
                def _(i=i):
                    jobs[i].start()

            @pl.when(p == d.parts - 1)
            def _():
                for job in jobs:
                    job.wait()

    return ph.call("enc_update", body)


def spread_nodes(d, acc, sumk, w1, n_cat, grad, grad_at):
    s = acc.astype(BF)
    sk = jnp.concatenate([x[:, : d.res] for x in sumk], axis=1)
    skb = sk.astype(BF)
    far = mm(s, w1[2 * d.feat :].T, 0, 0)
    own = mm(skb, w1[: d.feat].T, 0, 0)
    grad[grad_at + 2 * d.feat : grad_at + 3 * d.feat, :] += mm(n_cat, s, 0, 1)
    grad[grad_at : grad_at + d.feat, :] += mm(n_cat[: d.half], skb, 0, 1)
    return own + far[: d.half], far[d.half :], to_row(sk)


def lane_total(x):
    size = x.shape[1] // 4
    x = (x[:, :size] + x[:, size : 2 * size]) + (x[:, 2 * size : 3 * size] + x[:, 3 * size :])
    return lane_sum(x.astype(F32))


def norm_backward(d, r, dy, xh, rs, gain_mat):
    r.a_b9[...] += lane_total(dy)
    r.a_g2[...] += lane_total(dy * xh)
    z = mm(gain_mat, dy).astype(BF)
    m2 = jnp.mean((z * xh).astype(F32), axis=0, keepdims=True)
    return (z - xh * m2.astype(BF)) * rs.astype(BF)


def gain_matrix(cols):
    feat = cols.shape[0]
    shape = (feat, feat)
    eye = lax.broadcasted_iota(jnp.int32, shape, 0) == lax.broadcasted_iota(jnp.int32, shape, 1)
    scaled = jnp.where(eye, jnp.broadcast_to(cols[:, 12:13], shape), 0.0)
    return (scaled - jnp.mean(scaled, axis=0, keepdims=True)).astype(BF)


def update_backward(d, r, dr3, g1, d1, g2, d2, w2, w3, da1):
    r.a_w3[...] += mm(g2, dr3, 1, 1)
    da2 = mm(w3, dr3).astype(BF) * d2
    r.a_w2[...] += mm(g1, da2, 1, 1)
    da1[...] = mm(w2, da2).astype(BF) * d1


def update_small(d, r, b4):
    f = d.feat
    at = 5 * f
    r.upd[at + 4 : at + 5] += b4

    @pl.when(pl.program_id(0) == d.parts - 1)
    def _():
        r.upd[3 * f : 4 * f] = 0.5 * r.a_w2[:f]
        r.upd[4 * f : 5 * f] = 0.5 * r.a_w3[:f]
        r.upd[at + 5 : at + 6] = r.a_w2[f : f + 1]
        r.upd[at + 6 : at + 7] = r.a_w3[f : f + 1]
        r.upd[at + 9 : at + 10] = to_row(r.a_b9[...])
        r.upd[at + 12 : at + 13] = to_row(r.a_g2[...])


def zero(*refs):
    for ref in refs:
        ref[...] = jnp.zeros(ref.shape, ref.dtype)


def decoder_update(d, st, fb, cot, consts):
    ph = Phase(d)
    ph.whole(n_own=fb.node_out, n_got=fb.got, idx=consts.idx, rt=consts.sums)
    ph.stream(e2=fb.e2)
    ph.edges(cot=cot)
    ph.whole(**weight_args(st, *UPD_W, *AUX_W))
    ph.out_edges(decoded=cot.shape)
    ph.out_stream(BF, part=(d.parts, d.blocks, d.feat, d.rows))
    ph.out_whole(F32, upd=(d.upd_rows, d.feat), dn_own=(d.parts, d.half, d.feat))
    ph.out_whole(BF, dn_far=(d.parts, d.half, d.feat))
    sq = (d.feat, d.feat)
    ph.temp(BF, n_cat=(d.length, d.feat), lhs=(d.feat, d.length + d.res), w1bt=sq, w2t=sq, w2h=sq, w3h=sq)
    ph.temp(BF, tt=(d.length + d.res, d.rows), tn=(d.rows, d.length + 128), da1=(d.feat, d.rows))
    ph.temp(BF, w3c=(d.feat, 2 * d.feat), gain_mat=sq, pair=(2 * d.feat + 16, d.rows), one=(d.feat + 16, d.rows))
    tall = (d.feat + 16, d.feat)
    ph.temp(F32, w3c_b=sq, aux=sq, cols=sq, a_w2=tall, a_w3=tall, a_b9=sq, a_g2=sq)
    ph.temp(F32, a_s=(d.feat, d.length), a_k=(d.blocks, d.feat, 128))

    def body(r):
        p, b = pl.program_id(0), pl.program_id(1)
        first, last = b == 0, b == d.blocks - 1

        @pl.when(first & (p == 0))
        def _():
            r.w1bt[...] = r.uw1[1, d.feat : 2 * d.feat, :].T
            r.w2h[...] = half_of(r.uw2[1])
            r.w2t[...] = r.w2h[...].T
            r.w3h[...] = half_of(r.uw3[1])
            load_cols(r, 1, r.aux, r.cols)
            centre_weights(r.uw3[1], r.cols[...], r.w3c, r.w3c_b)
            r.gain_mat[...] = gain_matrix(r.cols[...])
            zero(r.upd, r.a_w2, r.a_w3, r.a_b9, r.a_g2)
            r.pair[2 * d.feat :] = jnp.ones((16, d.rows), BF)
            r.one[d.feat :] = jnp.ones((16, d.rows), BF)
            r.tt[d.length :, :] = r.rt[: d.res]
            r.tn[:, d.length :] = r.rt[...].T

        @pl.when(first)
        def _():
            r.n_cat[: d.half] = r.n_own[p]
            r.n_cat[d.half :] = r.n_got[p]
            zero(r.a_s)

        n_blk = r.n_own[p, pl.ds(pl.multiple_of(b * d.res, d.res), d.res), :]
        put_table(d, r.lhs, 0, 0, r.n_cat, r.uw1.at[1], n_blk, r.cols[:, 4:5], first)
        f = d.feat
        idx = r.idx[p, b]
        put_one_hot(d, r.tt, 0, idx)
        put_one_hot_rows(d, r.tn, idx)
        e2 = r.e2[...]
        r.pair[:f] = e2
        a1 = mm(r.lhs[...], r.tt[...]) + mm(r.w1bt[...], e2)
        g1, d1, _, d2, xh, rs, y = update_forward(
            d, a1, r.w2t[...], r.w3c, r.cols[:, 5:6], r.w3c_b[:, 0:1], r.pair, r.cols
        )
        r.one[:f] = g1
        r.decoded[...] = y.T.reshape(d.res, d.near, f)
        dy = r.cot[...].reshape(d.rows, f).T
        dr3 = norm_backward(d, r, dy, xh, rs, r.gain_mat[...])
        update_backward(d, r, dr3, r.one[...], d1, r.pair[f:], d2, r.w2h[...], r.w3h[...], r.da1)
        r.upd[f : 2 * f] += mm(e2, r.da1[...], 1, 1)
        r.part[...] = (mm(r.uw1[1, f : 2 * f, :], r.da1[...]) + dr3.astype(F32)).astype(BF)
        spread = mm(r.da1[...], r.tn[...])
        r.a_s[...] += spread[:, : d.length]
        r.a_k[b] = spread[:, d.length :]

        @pl.when(last)
        def _():
            own, far, b4 = spread_nodes(
                d, r.a_s[...], [r.a_k[i] for i in range(d.blocks)], r.uw1[1], r.n_cat[...], r.upd, 0
            )
            r.dn_own[p] = own
            r.dn_far[p] = far.astype(BF)
            update_small(d, r, b4)

    return ph.call("dec_update", body)


AUX_W = ("bias", "gain")


def message_backward(d, r, b, layer, da1):
    at = pl.ds(pl.multiple_of(b * d.res, d.res), d.res)
    v = (mm(r.mw3[layer], r.dub[at, :], 1, 1) * 0.5).astype(BF)
    da2 = mm(v, r.rt[: d.res]).astype(BF) * r.d2[...]
    r.m_w2[...] += mm(r.g1[...], da2, 1, 1)
    da1[...] = mm(r.mw2h[...], da2).astype(BF) * r.d1[...]


def message_small(d, r, b0):
    f = d.feat
    at = d.at_small
    r.msg[at : at + 1] += b0

    @pl.when(pl.program_id(0) == d.parts - 1)
    def _():
        r.msg[3 * f : 4 * f] = 0.5 * r.m_w2[:f]
        r.msg[at + 1 : at + 2] = r.m_w2[f : f + 1]


def middle_backward(d, edge_input, st, fa, fb, fd, cot_n, consts):
    ph = Phase(d, 4)
    ph.whole(cot_n=cot_n, dn_a=fd.dn_own, dn_far_in=fd.dn_far, n_own=fa.node_out, got_a=fa.got, got_b=fb.got_in)
    ph.whole(mask=consts.mask, rt=consts.sums, r1=fb.r1, ip=fb.ip, r2=fb.r2, big=fb.big, cnt=fb.cnt)
    ph.whole(urs=fb.urs, idx=consts.idx)
    ph.stream(d2=fb.d2, g1=fb.g1, d1=fb.d1, e2=fb.e2, dec_part=fd.part, uxh=fb.uxh)
    ph.stream(ug2=fb.ug2, ud2=fb.ud2, ug1=fb.ug1, ud1=fb.ud1)
    ph.edges(edge=edge_input)
    ph.whole(**weight_args(st, *NODE_W, *MSG_W, *UPD_W))
    ph.out_stream(BF, part=(d.parts, d.blocks, d.feat, d.rows))
    ph.out_whole(F32, msg=(d.msg_rows, d.feat), upd=(d.upd_rows, d.feat), dn_own=(d.parts, d.half, d.feat))
    ph.out_raw(BF, got=(d.parts, d.half, d.feat))
    sq = (d.feat, d.feat)
    ph.temp(BF, n_cat=(d.length, d.feat), dub=(d.half, d.feat), tn=(d.rows, d.length + 128))
    ph.temp(BF, both=(2 * d.feat, d.rows), w2h=sq, w3h=sq, mw2h=sq, gain_mat=sq)
    ph.temp(BF, leave=(d.parts, d.half, d.feat), arrive=(d.parts, d.half, d.feat))
    ph.temp(F32, dr1=(d.half, d.feat), e_aux=sq, e_cols=sq, d_aux=sq, d_cols=sq)
    tall = (d.feat + 16, d.feat)
    ph.temp(F32, m_w2=tall, a_w2=tall, a_w3=tall, a_b9=sq, a_g2=sq, a_w1=sq)
    ph.temp(F32, a_s=(2 * d.feat, d.length), a_k=(d.blocks, 2 * d.feat, 128))
    ph.sems(send=2 * d.parts, recv=2 * d.parts)

    def body(r):
        p, b = pl.program_id(0), pl.program_id(1)
        first, last = b == 0, b == d.blocks - 1
        n = d.parts
        early = [to_partner(r.dn_far_in.at[i], r.arrive.at[i], r.send.at[n + i], r.recv.at[n + i]) for i in range(n)]
        jobs = [to_partner(r.leave.at[i], r.got.at[i], r.send.at[i], r.recv.at[i]) for i in range(n)]

        @pl.when(first & (p == 0))
        def _():
            greet_partner()
            for job in early:
                job.start()
            load_cols(r, 0, r.e_aux, r.e_cols)
            load_cols(r, 1, r.d_aux, r.d_cols)
            r.tn[:, d.length :] = r.rt[...].T
            r.w2h[...] = half_of(r.uw2[0])
            r.w3h[...] = half_of(r.uw3[0])
            r.mw2h[...] = half_of(r.mw2[1])
            r.gain_mat[...] = gain_matrix(r.e_cols[...])
            zero(r.msg, r.upd, r.m_w2, r.a_w2, r.a_w3, r.a_b9, r.a_g2, r.a_w1)
            r.n_cat[d.half :] = r.got_a[...]

        @pl.when(first & (p == 1))
        def _():
            r.n_cat[d.half :] = r.got_b[...]

        for i in range(n):

            @pl.when(first & (p == i))
            def _(i=i):
                early[i].wait()

        @pl.when(first)
        def _():
            r.n_cat[: d.half] = r.n_own[p]
            zero(r.a_s)
            dn = r.cot_n[p].astype(F32) + r.dn_a[p] + r.arrive[p].astype(F32)
            node_backward(d, r, p, 1, r.d_aux[...], dn)

        f = d.feat
        put_one_hot_rows(d, r.tn, r.idx[p, b])
        message_backward(d, r, b, 1, r.both.at[:f])
        r.msg[f : 2 * f] += mm(r.e2[...], r.both[:f], 1, 1)
        de = mm(r.mw1[1, f : 2 * f, :], r.both[:f])
        dy = (de + r.dec_part[...].astype(F32)).astype(BF)
        dr3 = norm_backward(d, r, dy, r.uxh[...], r.urs[p, b], r.gain_mat[...])
        update_backward(
            d, r, dr3, r.ug1[...], r.ud1[...], r.ug2[...], r.ud2[...], r.w2h[...], r.w3h[...], r.both.at[f:]
        )
        r.a_w1[...] += mm(r.both[f:], r.edge[...].reshape(d.rows, f))
        r.part[...] = (mm(r.uw1[0, f : 2 * f, :], r.both[f:]) + dr3.astype(F32)).astype(BF)
        spread = mm(r.both[...], r.tn[...])
        r.a_s[...] += spread[:, : d.length]
        r.a_k[b] = spread[:, d.length :]

        @pl.when(last)
        def _():
            n_cat = r.n_cat[...]
            a_k = [r.a_k[i] for i in range(d.blocks)]
            own_m, far_m, b0 = spread_nodes(
                d, r.a_s[: d.feat], [x[: d.feat] for x in a_k], r.mw1[1], n_cat, r.msg, 0
            )
            own_u, far_u, b4 = spread_nodes(
                d, r.a_s[d.feat :], [x[d.feat :] for x in a_k], r.uw1[0], n_cat, r.upd, 0
            )
            r.dn_own[p] = own_m + own_u + r.dr1[...]
            r.leave[p] = (far_m + far_u).astype(BF)
            for i in range(n):

                @pl.when(p == i)
                def _(i=i):
                    jobs[i].start()

            message_small(d, r, b0)
            update_small(d, r, b4)

            @pl.when(p == n - 1)
            def _():
                r.upd[d.feat : 2 * d.feat] = r.a_w1[...].T
                for job in jobs:
                    job.wait()

    return ph.call("dec_message_back", body)


def encoder_message_back(d, edge_input, st, fa, fe, n_own, n_got, consts):
    ph = Phase(d)
    ph.whole(dn_a=fe.dn_own, dn_b=fe.got, n_own=n_own, n_got=n_got)
    ph.whole(mask=consts.mask, rt=consts.sums, r1=fa.r1, ip=fa.ip, r2=fa.r2, big=fa.big, cnt=fa.cnt)
    ph.whole(idx=consts.idx)
    ph.stream(d2=fa.d2, g1=fa.g1, d1=fa.d1, up_part=fe.part)
    ph.edges(edge=edge_input)
    ph.whole(**weight_args(st, *NODE_W, *MSG_W))
    ph.out_edges(edge_grad=edge_input.shape)
    ph.out_whole(F32, msg=(d.msg_rows, d.feat), dn_own=(d.parts, d.half, d.feat))
    ph.out_whole(BF, dn_far=(d.parts, d.half, d.feat))
    sq = (d.feat, d.feat)
    ph.temp(BF, n_cat=(d.length, d.feat), dub=(d.half, d.feat), tn=(d.rows, d.length + 128))
    ph.temp(BF, da1=(d.feat, d.rows), mw2h=sq)
    ph.temp(F32, dr1=(d.half, d.feat), aux=sq, cols=sq, a_w1=sq, m_w2=(d.feat + 16, d.feat))
    ph.temp(F32, a_s=(d.feat, d.length), a_k=(d.blocks, d.feat, 128))

    def body(r):
        p, b = pl.program_id(0), pl.program_id(1)
        first, last = b == 0, b == d.blocks - 1

        @pl.when(first & (p == 0))
        def _():
            load_cols(r, 0, r.aux, r.cols)
            r.tn[:, d.length :] = r.rt[...].T
            r.mw2h[...] = half_of(r.mw2[0])
            zero(r.msg, r.m_w2, r.a_w1)

        @pl.when(first)
        def _():
            r.n_cat[: d.half] = r.n_own[p]
            r.n_cat[d.half :] = r.n_got[p]
            zero(r.a_s)
            node_backward(d, r, p, 0, r.aux[...], r.dn_a[p] + r.dn_b[p].astype(F32))

        f = d.feat
        put_one_hot_rows(d, r.tn, r.idx[p, b])
        message_backward(d, r, b, 0, r.da1)
        r.a_w1[...] += mm(r.da1[...], r.edge[...].reshape(d.rows, f))
        de = mm(r.mw1[0, f : 2 * f, :], r.da1[...])
        de = (de + r.up_part[...].astype(F32)).astype(BF)
        r.edge_grad[...] = de.T.reshape(d.res, d.near, f)
        spread = mm(r.da1[...], r.tn[...])
        r.a_s[...] += spread[:, : d.length]
        r.a_k[b] = spread[:, d.length :]

        @pl.when(last)
        def _():
            own, far, b0 = spread_nodes(
                d, r.a_s[...], [r.a_k[i] for i in range(d.blocks)], r.mw1[0], r.n_cat[...], r.msg, 0
            )
            r.dn_own[p] = own + r.dr1[...]
            r.dn_far[p] = far.astype(BF)
            message_small(d, r, b0)

            @pl.when(p == d.parts - 1)
            def _():
                r.msg[d.feat : 2 * d.feat] = r.a_w1[...].T

    return ph.call("enc_message_back", body)


def reduce_grads(d, enc_msg, enc_upd, dec_msg, dec_upd, dn_far):
    devices = d.devices
    bits = devices.bit_length() - 1
    unit = 16 * devices
    feat = d.feat
    need = -(-(d.msg_rows + d.upd_rows) // unit)
    shares = [need // 3 + (1 if need % 3 > i else 0) for i in range(3)]
    groups = [unit * share for share in shares if share]
    rows = sum(groups)
    bases = [sum(groups[:i]) for i in range(len(groups))]
    across = -1
    dims = [across] + list(range(1, bits))
    turn = min(3, len(dims))
    orders = []
    for g in range(len(groups)):
        head = dims[:turn]
        head = head[g % turn :] + head[: g % turn]
        orders.append(([0] if bits else []) + head + dims[turn:])
    stages = len(orders[0])
    plans = []
    for g, order in enumerate(orders):
        size, both, plan = groups[g], True, []
        for dim in order:
            if dim == across:
                both = False
                plan.append((dim, size, False))
            else:
                size //= 2
                plan.append((dim, size, both))
        plans.append(plan)
    turns = len(groups) * stages

    def kernel(em, eu, dm, du, far, res, got, acc, gathered, *rest):
        buffers, (send, recv) = rest[: 2 * turns], rest[2 * turns :]
        section, me = lax.axis_index(AXIS_S), lax.axis_index(AXIS_D)

        def flag(bit):
            return lax.rem(me // (1 << bit), 2)

        def peer(dim):
            if dim == across:
                return other_section()
            return {AXIS_D: me + (1 - 2 * flag(dim)) * (1 << dim)}

        barrier = pltpu.get_barrier_semaphore()
        for dim in [across] + list(range(bits)):
            pl.semaphore_signal(barrier, inc=1, device_id=peer(dim), device_id_type=MESH)
        pl.semaphore_wait(barrier, bits + 1)

        def remote(src, dst, at, dim):
            return pltpu.make_async_remote_copy(
                src_ref=src, dst_ref=dst, send_sem=send.at[at], recv_sem=recv.at[at],
                device_id=peer(dim), device_id_type=MESH,
            )

        nodes = remote(far, got, 2 * turns, across)
        nodes.start()
        m, u = d.msg_rows, d.upd_rows
        for layer, (msg, upd) in enumerate(((em, eu), (dm, du))):
            acc[layer, :m] = msg[...]
            acc[layer, m : m + u] = upd[...]
            if rows > m + u:
                acc[layer, m + u :] = jnp.zeros((rows - m - u, feat), F32)

        def span(start, size):
            return pl.ds(pl.multiple_of(start, 16), size)

        starts = list(bases)
        for k in range(stages):
            jobs, spans = [], []
            for g, plan in enumerate(plans):
                dim, size, both = plan[k]
                at = g * stages + k
                out, into = buffers[2 * at], buffers[2 * at + 1]
                if dim == across:
                    keep = span(starts[g], size)
                    out[...] = acc[1 - section, keep, :].astype(BF)
                else:
                    side = flag(dim)
                    keep = span(starts[g] + side * size, size)
                    give = span(starts[g] + (1 - side) * size, size)
                    if both:
                        out[...] = acc[:, give, :].astype(BF)
                    else:
                        out[...] = acc[section, give, :].astype(BF)
                    starts[g] = starts[g] + side * size
                job = remote(out, into, at, dim)
                job.start()
                jobs.append(job)
                spans.append(keep)
            for g, plan in enumerate(plans):
                dim, size, both = plan[k]
                jobs[g].wait()
                into = buffers[2 * (g * stages + k) + 1]
                if both:
                    acc[:, spans[g], :] += into[...].astype(F32)
                else:
                    acc[section, spans[g], :] += into[...].astype(F32)
        sizes = [plan[-1][1] for plan in plans]
        for g in range(len(groups)):
            keep = span(starts[g], sizes[g])
            gathered[keep, :] = acc[section, keep, :].astype(BF)
        backs = [[step for step in reversed(plan) if step[0] != across] for plan in plans]
        for k in range(bits):
            jobs = []
            for g, back in enumerate(backs):
                dim, size, _ = back[k]
                part = gathered.at[span(starts[g], size), :]
                job = remote(part, part, turns + g * bits + k, dim)
                job.start()
                jobs.append(job)
                starts[g] = starts[g] - flag(dim) * size
            for job in jobs:
                job.wait()
        res[...] = gathered[...]
        nodes.wait()

    vm = pl.BlockSpec(memory_space=pltpu.VMEM)
    scratch = [pltpu.VMEM((2, rows, feat), F32), pltpu.VMEM((rows, feat), BF)]
    for plan in plans:
        for _, size, both in plan:
            scratch += [pltpu.VMEM((2, size, feat) if both else (size, feat), BF)] * 2
    scratch += [pltpu.SemaphoreType.DMA((2 * turns + 1,))] * 2
    return pl.pallas_call(
        kernel,
        in_specs=[vm] * 5,
        out_specs=[vm, pl.BlockSpec(memory_space=pl.ANY)],
        out_shape=[
            jax.ShapeDtypeStruct((rows, feat), BF),
            jax.ShapeDtypeStruct(dn_far.shape, BF),
        ],
        scratch_shapes=scratch,
        compiler_params=pltpu.CompilerParams(vmem_limit_bytes=58 << 20, collective_id=5, has_side_effects=True),
        name="reduce",
    )(enc_msg, enc_upd, dec_msg, dec_upd, dn_far)


def unpack(d, total, dn_own, dn_got, n_bias, n_gain):
    f = d.feat
    m = d.msg_rows
    shapes = [(1, 3 * f, f), (1, f, f), (1, f, f), (1, f, d.wide), (1, 1, d.wide), (1, d.wide, f)]
    shapes += [(1, 3 * f, f), (1, f, f), (1, f, f), (n_bias, 1, f), (n_gain, 1, f)]

    def kernel(t, own, got, node, mw1, mw2, mw3, inner, inner_b, outer, uw1, uw2, uw3, bias, gain):
        node[...] = (own[...] + got[...].astype(F32)).astype(BF)
        for ref, at in ((mw1, 0), (mw2, 3 * f), (mw3, 4 * f), (outer, d.at_outer)):
            ref[0] = t[at : at + ref.shape[1], :].astype(F32)
        for ref, at in ((uw1, m), (uw2, m + 3 * f), (uw3, m + 4 * f)):
            ref[0] = t[at : at + ref.shape[1], :].astype(F32)
        inner[0] = t[d.at_inner : d.at_inner + d.wide, :].astype(F32).T
        small = t[d.at_small : d.at_small + SMALL, :].astype(F32)
        other = t[m + 5 * f : m + 5 * f + SMALL, :].astype(F32)
        both = small + other
        for i in range(n_bias):
            bias[i] = both[i : i + 1]
        for i in range(n_gain):
            gain[i] = both[n_bias + i : n_bias + i + 1]
        for i in range(d.wide // f):
            inner_b[0, :, i * f : (i + 1) * f] = small[16 + i : 17 + i]

    vm = pl.BlockSpec(memory_space=pltpu.VMEM)
    out = [jax.ShapeDtypeStruct(dn_own.shape, BF)] + [jax.ShapeDtypeStruct(s, F32) for s in shapes]
    return pl.pallas_call(kernel, in_specs=[vm] * 3, out_specs=[vm] * len(out), out_shape=out, name="unpack")(
        total, dn_own, dn_got
    )


def per_device(
    node_input,
    edge_input,
    neighbors,
    residue_mask,
    decode_order,
    node_cotangent,
    edge_cotangent,
    message_w1,
    message_w2,
    message_w3,
    inner_w,
    inner_bias,
    outer_w,
    update_w1,
    update_w2,
    update_w3,
    biases,
    norm_gains,
):
    section = lax.axis_index(AXIS_S)
    is_first = section == 0
    parts, half, near, feat = edge_input.shape
    length = neighbors.shape[1]
    wide = inner_w.shape[2]
    res = BLOCK_RES
    rows = res * near
    blocks = half // res
    at_outer = 5 * feat
    at_inner = at_outer + wide
    at_small = at_inner + wide
    d = types.SimpleNamespace(
        parts=parts, half=half, near=near, feat=feat, length=length, wide=wide, res=res, rows=rows, blocks=blocks,
        at_outer=at_outer, at_inner=at_inner, at_small=at_small, msg_rows=at_small + SMALL,
        upd_rows=5 * feat + SMALL, devices=lax.axis_size(AXIS_D),
    )
    weights = dict(
        mw1=message_w1[0], mw2=message_w2[0], mw3=message_w3[0], inner=inner_w[0], inner_b=inner_bias, outer=outer_w[0],
        uw1=update_w1[0], uw2=update_w2[0], uw3=update_w3[0],
        bias=biases.transpose(1, 0, 2), gain=norm_gains.transpose(1, 0, 2),
    )
    own_ids = lax.dynamic_slice_in_dim(neighbors, section * half, half, 1) - section * half
    idx_row = jnp.where(own_ids < 0, own_ids + length, own_ids).reshape(parts, blocks, 1, rows)
    sums = np.zeros((128, rows), np.float32)
    sums[np.arange(rows) // near, np.arange(rows)] = 1.0
    sums = jnp.asarray(sums, BF)

    def own_first(x):
        return jnp.where(is_first, x, jnp.roll(x, half, axis=1))

    live = own_first(residue_mask)
    order = own_first(decode_order)
    centre = length // 2
    code = jnp.where(live == 1, order - centre, centre)
    own_code = (order[:, :half] - centre).reshape(parts, blocks, 1, res)
    lead = (parts, blocks, 1, length)
    top = jnp.pad(jnp.broadcast_to(live[:, None, None, :], lead), ((0, 0), (0, 0), (0, 0), (0, res)))
    second = jnp.concatenate([jnp.broadcast_to(code[:, None, None, :], lead), -own_code], axis=3)
    extra = jnp.concatenate([top, second, jnp.zeros((parts, blocks, EXTRA - 2, length + res), top.dtype)], axis=2)
    mask = jnp.broadcast_to(live[:, :half, None].astype(F32), (parts, half, feat))
    consts = types.SimpleNamespace(extra=extra.astype(BF), sums=sums, mask=mask, idx=idx_row)

    fa = encoder_message(d, edge_input, node_input, weights, consts)
    st = types.SimpleNamespace(**{n: getattr(fa, W_OUT + n) for n in weights})
    fb = encoder_update(d, edge_input, st, fa, consts)
    fd = decoder_update(d, st, fb, edge_cotangent, consts)
    fe = middle_backward(d, edge_input, st, fa, fb, fd, node_cotangent, consts)
    ff = encoder_message_back(d, edge_input, st, fa, fe, node_input, fa.nodes_got, consts)
    total, got = reduce_grads(d, ff.msg, fe.upd, fe.msg, fd.upd, ff.dn_far)
    node_grad, mw1, mw2, mw3, inner, inner_b, outer, uw1, uw2, uw3, bias, gain = unpack(
        d, total, ff.dn_own, got, biases.shape[1], norm_gains.shape[1]
    )
    return (
        fb.node_out, fd.decoded, node_grad, ff.edge_grad, mw1, mw2, mw3, inner, inner_b[:, 0], outer,
        uw1, uw2, uw3, bias.transpose(1, 0, 2), gain.transpose(1, 0, 2),
    )


def solution(mesh):
    def split(*axes):
        return P(*axes)

    by_part = split(AXIS_D)
    by_half = split(AXIS_D, AXIS_S)
    by_layer = split(AXIS_S)
    in_specs = (by_half, by_half, by_part, by_part, by_part, by_half, by_half) + (by_layer,) * 11
    out_specs = (by_half,) * 4 + (by_layer,) * 11
    return jax.shard_map(per_device, mesh=mesh, in_specs=in_specs, out_specs=out_specs, check_vma=False)
```

```python
import types

import jax
import jax.numpy as jnp
import numpy as np
from jax import lax
from jax.experimental import pallas as pl
from jax.experimental.pallas import tpu as pltpu
from jax.sharding import PartitionSpec as P

BF = jnp.bfloat16
F32 = jnp.float32
C1 = 0.7978845608
C2 = C1 * 0.044715
EPS = 1e-5
BLOCK_RES = 64
EXTRA = 16
SMALL = 32
MESH = pl.DeviceIdType.MESH


def mm(a, b, ca=1, cb=0):
    return lax.dot_general(a, b, (((ca,), (cb,)), ((), ())), preferred_element_type=F32)


def mm_exact(a, b, ca=1, cb=0):
    return lax.dot_general(
        a, b, (((ca,), (cb,)), ((), ())), precision=lax.Precision.HIGHEST, preferred_element_type=F32
    )


def gelu_pair(x):
    x = x.astype(BF)
    w = x * x * BF(C2)
    h = jnp.tanh(x * (w + BF(C1))) + BF(1.0)
    g = x * h
    d = h + g * (BF(2.0) - h) * (w * BF(3.0) + BF(C1))
    return g, d


def gelu_pair_wide(x):
    x2 = x * x
    h = 0.5 * jnp.tanh(x * (x2 * C2 + C1)) + 0.5
    g = x * h
    d = h + (g * (1.0 - h)) * (x2 * (6 * C2) + 2 * C1)
    return g, d


def lane_sum(x):
    total = x[:, :128]
    for at in range(128, x.shape[1], 128):
        total = total + x[:, at : at + 128]
    return total


def to_row(acc):
    return mm_exact(jnp.ones((8, acc.shape[1]), F32), acc, 1, 1)[0:1]


def norm_rows(r):
    c = r - jnp.mean(r, axis=-1, keepdims=True)
    rs = lax.rsqrt(jnp.mean(c * c, axis=-1, keepdims=True) + EPS)
    return c * rs, rs


def norm_back_rows(dxh, xh, rs):
    m1 = jnp.mean(dxh, axis=-1, keepdims=True)
    m2 = jnp.mean(dxh * xh, axis=-1, keepdims=True)
    return (dxh - m1 - xh * m2) * rs


def norm_back(dy, xh, rs, gain_col):
    dxh = dy * gain_col
    m1 = jnp.mean(dxh, axis=0, keepdims=True)
    m2 = jnp.mean(dxh * xh, axis=0, keepdims=True)
    return (dxh - m1 - xh * m2) * rs


class Phase:
    def __init__(self, dims, collective_id=None):
        self.d = dims
        self.collective_id = collective_id
        self.ins, self.outs, self.temps, self.kinds = [], [], [], {}

    def whole_spec(self, shape):
        rank = len(shape)
        return pl.BlockSpec(tuple(shape), lambda p, b: (0,) * rank)

    def whole(self, **arrays):
        self.ins += [(n, a, self.whole_spec(a.shape)) for n, a in arrays.items()]

    def raw(self, **arrays):
        self.ins += [(n, a, pl.BlockSpec(memory_space=pl.ANY)) for n, a in arrays.items()]

    def stream(self, **arrays):
        self.raw(**arrays)
        self.kinds.update({n: (False, False, a.shape[2:], a.dtype) for n, a in arrays.items()})

    def edges(self, **arrays):
        self.raw(**arrays)
        block = (self.d.res, self.d.near, self.d.feat)
        self.kinds.update({n: (False, True, block, a.dtype) for n, a in arrays.items()})

    def out_whole(self, dtype, **shapes):
        self.outs += [(n, jax.ShapeDtypeStruct(s, dtype), self.whole_spec(s)) for n, s in shapes.items()]

    def out_raw(self, dtype, **shapes):
        spec = pl.BlockSpec(memory_space=pl.ANY)
        self.outs += [(n, jax.ShapeDtypeStruct(s, dtype), spec) for n, s in shapes.items()]

    def out_stream(self, dtype, **shapes):
        self.out_raw(dtype, **shapes)
        self.kinds.update({n: (True, False, s[2:], dtype) for n, s in shapes.items()})

    def out_edges(self, **shapes):
        self.out_raw(BF, **shapes)
        block = (self.d.res, self.d.near, self.d.feat)
        self.kinds.update({n: (True, True, block, BF) for n in shapes})

    def temp(self, dtype, **shapes):
        self.temps += [(n, pltpu.VMEM(s, dtype)) for n, s in shapes.items()]

    def sems(self, **counts):
        self.temps += [(n, pltpu.SemaphoreType.DMA((c,))) for n, c in counts.items()]

    def call(self, name, body):
        d = self.d
        names = [n for n, _, _ in self.ins] + [n for n, _, _ in self.outs] + [n for n, _ in self.temps]
        steps = d.parts * d.blocks
        buffers = [pltpu.VMEM((2,) + tuple(block), dtype) for _, _, block, dtype in self.kinds.values()]
        count = len(self.kinds)

        def kernel(*refs):
            refs, slots, sems = refs[: len(names)], refs[len(names) : len(names) + count], refs[len(names) + count :]
            plain = dict(zip(names, refs))
            step = pl.program_id(0) * d.blocks + pl.program_id(1)
            now = lax.rem(step, 2)

            def copy(i, n, at, slot):
                out, edges, _, _ = self.kinds[n]
                p, b = at // d.blocks, lax.rem(at, d.blocks)
                if edges:
                    far = plain[n].at[p, pl.ds(pl.multiple_of(b * d.res, d.res), d.res)]
                else:
                    far = plain[n].at[p, b]
                near = slots[i].at[slot]
                return pltpu.make_async_copy(*((near, far) if out else (far, near)), sems[i].at[slot])

            into = [(i, n) for i, n in enumerate(self.kinds) if not self.kinds[n][0]]
            outof = [(i, n) for i, n in enumerate(self.kinds) if self.kinds[n][0]]

            @pl.when(step == 0)
            def _():
                for i, n in into:
                    copy(i, n, step, now).start()

            @pl.when(step + 1 < steps)
            def _():
                for i, n in into:
                    copy(i, n, step + 1, 1 - now).start()

            @pl.when(step >= 2)
            def _():
                for i, n in outof:
                    copy(i, n, step - 2, now).wait()

            def ready():
                for i, n in into:
                    copy(i, n, step, now).wait()

            plain_or_slot = dict(plain, ready=ready)
            plain_or_slot.update({n: slots[i].at[now] for i, n in enumerate(self.kinds)})
            body(types.SimpleNamespace(**plain_or_slot))
            for i, n in outof:
                copy(i, n, step, now).start()

            @pl.when(step == steps - 1)
            def _():
                for i, n in outof:
                    if steps > 1:
                        copy(i, n, step - 1, 1 - now).wait()
                    copy(i, n, step, now).wait()

        results = pl.pallas_call(
            kernel,
            grid=(d.parts, d.blocks),
            in_specs=[s for _, _, s in self.ins],
            out_specs=[s for _, _, s in self.outs],
            out_shape=[s for _, s, _ in self.outs],
            scratch_shapes=[s for _, s in self.temps] + buffers + [pltpu.SemaphoreType.DMA((2,))] * count,
            compiler_params=pltpu.CompilerParams(
                dimension_semantics=(pltpu.ARBITRARY,) * 2,
                vmem_limit_bytes=60 << 20,
                collective_id=self.collective_id,
                has_side_effects=self.collective_id is not None,
            ),
            name=name,
        )(*[a for _, a, _ in self.ins])
        return types.SimpleNamespace(**dict(zip([n for n, _, _ in self.outs], results)))


def other_section():
    return {AXIS_S: 1 - lax.axis_index(AXIS_S)}


AXIS_S = "section"
AXIS_D = "dp"


def greet_partner():
    barrier = pltpu.get_barrier_semaphore()
    pl.semaphore_signal(barrier, inc=1, device_id=other_section(), device_id_type=MESH)
    pl.semaphore_wait(barrier, 1)


def to_partner(src, dst, send, recv):
    return pltpu.make_async_remote_copy(
        src_ref=src, dst_ref=dst, send_sem=send, recv_sem=recv, device_id=other_section(), device_id_type=MESH
    )


def put_one_hot(d, ref, at, idx):
    idx = idx.astype(jnp.int16)
    place = lax.broadcasted_iota(jnp.int16, (d.length, d.rows), 0)
    ref[at : at + d.length, :] = jnp.where(place == idx, jnp.ones((), BF), jnp.zeros((), BF))


def put_one_hot_rows(d, ref, idx):
    centre = d.length // 2
    idx = jnp.broadcast_to((idx - centre).astype(F32).astype(BF), (128, d.rows)).T
    place = lax.broadcasted_iota(jnp.int32, (d.rows, 128), 1)
    for at in range(0, d.length, 128):
        there = (place + (at - centre)).astype(F32).astype(BF)
        ref[:, at : at + 128] = jnp.where(idx == there, jnp.ones((), BF), jnp.zeros((), BF))


def weight_args(w, *names):
    return {n: getattr(w, n) for n in names}


def load_cols(r, layer, aux, cols):
    n_bias, n_gain = r.bias.shape[1], r.gain.shape[1]
    aux[...] = jnp.zeros(aux.shape, F32)
    for i in range(n_bias):
        aux[i : i + 1] = r.bias[layer, i]
    for i in range(n_gain):
        aux[n_bias + i : n_bias + i + 1] = r.gain[layer, i]
    cols[...] = aux[...].T


def put_table(d, lhs, at, left, n_cat, w1):
    lhs[at : at + d.feat, left : left + d.length] = mm(w1[2 * d.feat :, :].T, n_cat[...], 1, 1).astype(BF)


def put_own(d, lhs, at, left, w1, n_blk, bias_col):
    own = mm(w1[0 : d.feat, :].T, n_blk, 1, 1) + bias_col
    lhs[at : at + d.feat, left + d.length :] = own.astype(BF)


def message_part(a1, w2t, b2, att):
    g1, d1 = gelu_pair(a1)
    a2 = mm(w2t, g1) + b2
    g2, d2 = gelu_pair(a2)
    attb = att.astype(BF)
    return g1, d1, g2 * attb, d2 * attb


def add_node_outs(ph, d):
    ph.out_whole(BF, node_out=(d.parts, d.half, d.feat))
    shape = (d.parts, d.half, d.feat)
    ph.out_whole(F32, r1=shape, ip=(d.parts, d.half, d.wide), r2=shape, big=shape, cnt=shape)


def node_step(d, r, p, b, g2m, att, rt):
    big = mm(rt, g2m, 1, 1) * 0.5
    cnt = mm(rt, jnp.broadcast_to(att.astype(BF), (16, att.shape[1])), 1, 1)
    at = pl.ds(pl.multiple_of(b * d.res, d.res), d.res)
    r.big[p, at, :] = big
    r.cnt[p, at, :] = jnp.broadcast_to(cnt[:, 0:1], big.shape)


def node_forward(r, p, n_own, layer, aux):
    big = r.big[p]
    hi = big.astype(BF)
    lo = (big - hi.astype(F32)).astype(BF)
    w3 = r.mw3[layer]
    upd = (mm(hi, w3) + mm(lo, w3) + r.cnt[p] * aux[2:3]) / 30.0
    r1 = n_own.astype(F32) + upd
    xh1, _ = norm_rows(r1)
    normed = xh1 * aux[10:11] + aux[7:8]
    ip = mm(normed.astype(BF), r.inner[layer]) + r.inner_b[layer]
    hid = gelu_pair_wide(ip)[0].astype(BF)
    r2 = normed + (mm(hid, r.outer[layer]) + aux[3:4])
    xh2, _ = norm_rows(r2)
    out = ((xh2 * aux[11:12] + aux[8:9]) * r.mask[p]).astype(BF)
    r.node_out[p] = out
    r.r1[p] = r1
    r.ip[p] = ip
    r.r2[p] = r2
    return out


def node_backward(d, r, p, layer, aux, dn):
    r1, ip, r2, big, cnt = r.r1[p], r.ip[p], r.r2[p], r.big[p], r.cnt[p]
    xh1, rs1 = norm_rows(r1)
    normed = xh1 * aux[10:11] + aux[7:8]
    xh2, rs2 = norm_rows(r2)
    dy2 = dn * r.mask[p]
    dr2 = norm_back_rows(dy2 * aux[11:12], xh2, rs2)
    low_outer = dr2.astype(BF)
    hid, slope = gelu_pair_wide(ip)
    dip = mm(low_outer, r.outer[layer], 1, 1) * slope
    low_inner = dip.astype(BF)
    at = d.at_outer
    r.msg[at : at + d.wide] += mm(hid.astype(BF), low_outer, 0, 0)
    at = d.at_inner
    r.msg[at : at + d.wide] += mm(low_inner, normed.astype(BF), 0, 0)
    dnormed = dr2 + mm(low_inner, r.inner[layer], 1, 1)
    dr1 = norm_back_rows(dnormed * aux[10:11], xh1, rs1)
    du = dr1 / 30.0
    dub = du.astype(BF)
    r.msg[4 * d.feat : 5 * d.feat] += mm(big.astype(BF), dub, 0, 0)
    dib = jnp.sum(dip, axis=0, keepdims=True)
    rows = {
        2: jnp.sum(cnt * du, axis=0, keepdims=True),
        3: jnp.sum(dr2, axis=0, keepdims=True),
        7: jnp.sum(dnormed, axis=0, keepdims=True),
        8: jnp.sum(dy2, axis=0, keepdims=True),
        10: jnp.sum(dnormed * xh1, axis=0, keepdims=True),
        11: jnp.sum(dy2 * xh2, axis=0, keepdims=True),
    }
    for i in range(d.wide // d.feat):
        rows[16 + i] = dib[:, i * d.feat : (i + 1) * d.feat]
    for row, value in rows.items():
        r.msg[d.at_small + row : d.at_small + row + 1] += value
    r.dr1[...] = dr1
    r.dub[...] = dub


def encoder_message(d, edge_input, node_input, weights, consts):
    ph = Phase(d, 2)
    ph.whole(n_own=node_input, idx=consts.idx, rt=consts.sums, mask=consts.mask, extra=consts.extra)
    ph.edges(edge=edge_input)
    names = tuple(weights)
    own = {W_IN + n: a for n, a in weights.items()}
    ph.raw(**own)
    act = (d.parts, d.blocks, d.feat, d.rows)
    ph.out_stream(BF, g1=with_ones(d), d1=act, d2=act)
    ph.out_whole(F32, att=(d.parts, d.blocks, 1, d.rows))
    add_node_outs(ph, d)
    ph.out_raw(BF, got=(d.half, d.feat), nodes_got=node_input.shape)
    for n, a in weights.items():
        ph.out_raw(a.dtype, **{W_OUT + n: (2,) + a.shape})
        ph.temp(a.dtype, **{n: (2,) + a.shape})
    sq = (d.feat, d.feat)
    wide = d.feat + d.length + d.res
    ph.temp(BF, n_cat=(d.length, d.feat), lhs=(d.feat + EXTRA, wide), w2t=sq, tt=(wide, d.rows))
    ph.temp(BF, leave=(d.half, d.feat), arrive=node_input.shape)
    ph.temp(F32, aux=sq, cols=sq)
    count = len(names)
    ph.sems(send=count + 2, recv=count + 2, local=count, back=2 * count + 1)

    def body(r):
        p, b = pl.program_id(0), pl.program_id(1)
        first, last = b == 0, b == d.blocks - 1
        section = lax.axis_index(AXIS_S)
        job = to_partner(r.leave, r.got, r.send.at[count], r.recv.at[count])
        nodes = to_partner(r.n_own, r.arrive, r.send.at[count + 1], r.recv.at[count + 1])

        def swaps(group):
            out = []
            for n in group:
                i = names.index(n)
                dst = getattr(r, n).at[section]
                out.append(to_partner(getattr(r, W_IN + n), dst, r.send.at[i], r.recv.at[i]))
            return out

        def own_copies():
            return [
                pltpu.make_async_copy(getattr(r, W_IN + n), getattr(r, n).at[section], r.local.at[i])
                for i, n in enumerate(names)
            ]

        def returns():
            out = [pltpu.make_async_copy(r.arrive, r.nodes_got, r.back.at[2 * count])]
            for i, n in enumerate(names):
                src, dst = getattr(r, n), getattr(r, W_OUT + n)
                for layer in range(2):
                    sem = r.back.at[2 * i + layer]
                    out.append(pltpu.make_async_copy(src.at[layer], dst.at[layer], sem))
            return out

        begin = first & (p == 0)
        middle = (p == 1) & (b == 1)
        at_end = last & (p == d.parts - 1)

        @pl.when(begin)
        def _():
            greet_partner()
            nodes.start()
            for item in swaps(GROUP_ONE) + own_copies():
                item.start()
            r.tt[d.feat + d.length :, :] = r.rt[: d.res]

        @pl.when(begin)
        def _():
            nodes.wait()
            for item in swaps(GROUP_ONE) + own_copies():
                item.wait()
            for item in swaps(GROUP_TWO):
                item.start()
            r.lhs[: d.feat, : d.feat] = r.mw1[0, d.feat : 2 * d.feat, :].T
            r.lhs[d.feat :, : d.feat] = jnp.zeros((EXTRA, d.feat), BF)
            r.w2t[...] = half_of(r.mw2[0]).T
            load_cols(r, 0, r.aux, r.cols)

        @pl.when(first)
        def _():
            r.n_cat[: d.half] = r.n_own[p]
            r.n_cat[d.half :] = r.arrive[p]
            put_table(d, r.lhs, 0, d.feat, r.n_cat, r.mw1.at[0])

        n_blk = r.n_own[p, pl.ds(pl.multiple_of(b * d.res, d.res), d.res), :]
        r.ready()
        put_one_hot(d, r.tt, d.feat, r.idx[p, b])
        r.tt[: d.feat, :] = r.edge[...].reshape(d.rows, d.feat).T
        put_own(d, r.lhs, 0, d.feat, r.mw1.at[0], n_blk, r.cols[:, 0:1])
        r.lhs[d.feat :, d.feat :] = r.extra[p, b]
        out = mm(r.lhs[...], r.tt[...])
        att = out[d.feat : d.feat + 1]
        r.att[p, b] = jnp.where(out[d.feat + 1 : d.feat + 2] < 0.0, 1.0, 0.0)
        g1, r.d1[...], g2m, r.d2[...] = message_part(out[: d.feat], r.w2t[...], r.cols[:, 1:2], att)
        put_ones(r.g1, g1)
        node_step(d, r, p, b, g2m, att, r.rt[: d.res])

        @pl.when(middle)
        def _():
            for item in swaps(GROUP_TWO):
                item.wait()
            for item in swaps(GROUP_THREE):
                item.start()
            r.leave[...] = node_forward(r, 0, r.n_own[0], 0, r.aux[...])
            job.start()

        @pl.when(at_end)
        def _():
            node_forward(r, d.parts - 1, r.n_own[d.parts - 1], 0, r.aux[...])
            for item in swaps(GROUP_THREE):
                item.wait()
            for item in returns():
                item.start()
            for item in returns():
                item.wait()
            job.wait()

    return ph.call("enc_message", body)


W_IN, W_OUT = "i_", "o_"
GROUP_ONE = ("mw1", "mw2", "bias", "gain")
GROUP_TWO = ("mw3", "inner", "inner_b", "outer")
GROUP_THREE = ("uw1", "uw2", "uw3")
NODE_W = ("mw3", "inner", "inner_b", "outer", "bias", "gain")
MSG_W = ("mw1", "mw2")
UPD_W = ("uw1", "uw2", "uw3")


def with_ones(d):
    return (d.parts, d.blocks, d.feat + 16, d.rows)


def put_ones(ref, g):
    feat, rows = g.shape
    ref[:feat] = g
    ref[feat:] = jnp.ones((16, rows), BF)


def half_of(w):
    return w * BF(0.5)


def update_forward(d, a1, w2t, w3c, b5, b6c, pair, cols):
    f = d.feat
    g1, d1 = gelu_pair(a1)
    a2 = mm(w2t, g1) + b5
    g2, d2 = gelu_pair(a2)
    pair[f : 2 * f] = g2
    cent = mm(w3c[...], pair[: 2 * f]) + b6c
    var = jnp.mean(cent * cent, axis=0, keepdims=True)
    rs = lax.rsqrt(var + EPS)
    xh = cent.astype(BF) * rs.astype(BF)
    y = xh * cols[:, 12:13].astype(BF) + cols[:, 9:10].astype(BF)
    return g1, d1, g2, d2, xh, rs, y


def centre_weights(w3, cols, w3c, b6c):
    feat = w3.shape[0]
    eye = lax.broadcasted_iota(jnp.int32, w3.shape, 0) == lax.broadcasted_iota(jnp.int32, w3.shape, 1)
    w3f = w3.astype(F32)
    w3c[:, feat:] = (0.5 * (w3f - jnp.mean(w3f, axis=1, keepdims=True))).T.astype(BF)
    w3c[:, :feat] = (eye.astype(F32) - 1.0 / feat).astype(BF)
    b6 = cols[:, 6:7]
    b6c[...] = jnp.broadcast_to(b6 - jnp.mean(b6, axis=0, keepdims=True), b6c.shape)


def encoder_update(d, edge_input, st, fa, consts):
    ph = Phase(d, 3)
    ph.whole(n_own=fa.node_out, got_a=fa.got, idx=consts.idx, rt=consts.sums, mask=consts.mask, att=fa.att)
    ph.edges(edge=edge_input)
    ph.whole(**weight_args(st, *NODE_W, *MSG_W, *UPD_W))
    act = (d.parts, d.blocks, d.feat, d.rows)
    tall = with_ones(d)
    ph.out_stream(BF, ug1=tall, ud1=act, ug2=tall, ud2=act, uxh=act, e2=act, g1=tall, d1=act, d2=act)
    ph.out_whole(F32, urs=(d.parts, d.blocks, 1, d.rows))
    add_node_outs(ph, d)
    ph.out_whole(BF, got_in=(d.half, d.feat))
    ph.out_raw(BF, got=(d.parts, d.half, d.feat))
    sq = (d.feat, d.feat)
    wide = d.feat + d.length + d.res
    ph.temp(BF, n_cat=(d.length, d.feat), lhs=(2 * d.feat, wide), tt=(wide, d.rows))
    ph.temp(BF, uw2t=sq, mw1bt=sq, mw2t=sq, w3c=(d.feat, 2 * d.feat), pair=(2 * d.feat, d.rows))
    ph.temp(BF, leave=(d.parts, d.half, d.feat), lead=(d.half, d.feat), arrive=(d.half, d.feat))
    ph.temp(F32, w3c_b=sq, e_aux=sq, e_cols=sq, d_aux=sq, d_cols=sq)
    ph.sems(send=d.parts + 1, recv=d.parts + 1)

    def body(r):
        p, b = pl.program_id(0), pl.program_id(1)
        first, last = b == 0, b == d.blocks - 1
        early = to_partner(r.lead, r.arrive, r.send.at[d.parts], r.recv.at[d.parts])
        jobs = [to_partner(r.leave.at[i], r.got.at[i], r.send.at[i], r.recv.at[i]) for i in range(d.parts)]

        @pl.when(first & (p == 0))
        def _():
            greet_partner()
            r.lead[...] = r.n_own[d.parts - 1]
            early.start()
            r.tt[d.feat + d.length :, :] = r.rt[: d.res]
            r.lhs[: d.feat, : d.feat] = r.uw1[0, d.feat : 2 * d.feat, :].T
            r.lhs[d.feat :, : d.feat] = jnp.zeros((d.feat, d.feat), BF)
            r.uw2t[...] = half_of(r.uw2[0]).T
            r.mw1bt[...] = r.mw1[1, d.feat : 2 * d.feat, :].T
            r.mw2t[...] = half_of(r.mw2[1]).T
            load_cols(r, 0, r.e_aux, r.e_cols)
            load_cols(r, 1, r.d_aux, r.d_cols)
            centre_weights(r.uw3[0], r.e_cols[...], r.w3c, r.w3c_b)
            r.n_cat[d.half :] = r.got_a[...]

        @pl.when(first & (p == 1))
        def _():
            early.wait()
            r.n_cat[d.half :] = r.arrive[...]
            r.got_in[...] = r.arrive[...]

        @pl.when(first)
        def _():
            r.n_cat[: d.half] = r.n_own[p]
            put_table(d, r.lhs, 0, d.feat, r.n_cat, r.uw1.at[0])
            put_table(d, r.lhs, d.feat, d.feat, r.n_cat, r.mw1.at[1])

        r.ready()
        n_blk = r.n_own[p, pl.ds(pl.multiple_of(b * d.res, d.res), d.res), :]
        put_own(d, r.lhs, 0, d.feat, r.uw1.at[0], n_blk, r.e_cols[:, 4:5])
        put_own(d, r.lhs, d.feat, d.feat, r.mw1.at[1], n_blk, r.d_cols[:, 0:1])
        put_one_hot(d, r.tt, d.feat, r.idx[p, b])
        edge_t = r.edge[...].reshape(d.rows, d.feat).T
        r.tt[: d.feat, :] = edge_t
        r.pair[: d.feat] = edge_t
        out = mm(r.lhs[...], r.tt[...])
        g1, d1, g2, d2, xh, rs, e2 = update_forward(
            d, out[: d.feat], r.uw2t[...], r.w3c, r.e_cols[:, 5:6], r.w3c_b[:, 0:1], r.pair, r.e_cols
        )
        put_ones(r.ug1, g1)
        put_ones(r.ug2, g2)
        r.ud1[...], r.ud2[...], r.uxh[...], r.urs[p, b], r.e2[...] = d1, d2, xh, rs, e2
        att = r.att[p, b]
        a1 = out[d.feat :] + mm(r.mw1bt[...], e2)
        g1, r.d1[...], g2m, r.d2[...] = message_part(a1, r.mw2t[...], r.d_cols[:, 1:2], att)
        put_ones(r.g1, g1)
        node_step(d, r, p, b, g2m, att, r.rt[: d.res])

        @pl.when(last)
        def _():
            r.leave[p] = node_forward(r, p, r.n_own[p], 1, r.d_aux[...])
            for i in range(d.parts):

                @pl.when(p == i)
                def _(i=i):
                    jobs[i].start()

            @pl.when(p == d.parts - 1)
            def _():
                for job in jobs:
                    job.wait()

    return ph.call("enc_update", body)


def spread_nodes(d, acc, sumk, w1, n_cat, grad, grad_at):
    s = acc.astype(BF)
    sk = jnp.concatenate([x[:, : d.res] for x in sumk], axis=1)
    skb = sk.astype(BF)
    far = mm(s, w1[2 * d.feat :].T, 0, 0)
    own = mm(skb, w1[: d.feat].T, 0, 0)
    grad[grad_at + 2 * d.feat : grad_at + 3 * d.feat, :] += mm(n_cat, s, 0, 1)
    grad[grad_at : grad_at + d.feat, :] += mm(n_cat[: d.half], skb, 0, 1)
    return own + far[: d.half], far[d.half :], to_row(sk)


def lane_total(x):
    size = x.shape[1] // 4
    x = (x[:, :size] + x[:, size : 2 * size]) + (x[:, 2 * size : 3 * size] + x[:, 3 * size :])
    return lane_sum(x.astype(F32))


def norm_backward(d, r, dy, xh, rs, gain_mat):
    r.a_b9[...] += lane_total(dy)
    r.a_g2[...] += lane_total(dy * xh)
    z = mm(gain_mat, dy).astype(BF)
    m2 = jnp.mean((z * xh).astype(F32), axis=0, keepdims=True)
    return (z - xh * m2.astype(BF)) * rs.astype(BF)


def gain_matrix(cols):
    feat = cols.shape[0]
    shape = (feat, feat)
    eye = lax.broadcasted_iota(jnp.int32, shape, 0) == lax.broadcasted_iota(jnp.int32, shape, 1)
    scaled = jnp.where(eye, jnp.broadcast_to(cols[:, 12:13], shape), 0.0)
    return (scaled - jnp.mean(scaled, axis=0, keepdims=True)).astype(BF)


def update_backward(d, r, dr3, g1, d1, g2, d2, w2, w3, da1):
    r.a_w3[...] += mm(g2, dr3, 1, 1)
    da2 = mm(w3, dr3).astype(BF) * d2
    r.a_w2[...] += mm(g1, da2, 1, 1)
    da1[...] = mm(w2, da2).astype(BF) * d1


def update_small(d, r, b4):
    f = d.feat
    at = 5 * f
    r.upd[at + 4 : at + 5] += b4

    @pl.when(pl.program_id(0) == d.parts - 1)
    def _():
        r.upd[3 * f : 4 * f] = 0.5 * r.a_w2[:f]
        r.upd[4 * f : 5 * f] = 0.5 * r.a_w3[:f]
        r.upd[at + 5 : at + 6] = r.a_w2[f : f + 1]
        r.upd[at + 6 : at + 7] = r.a_w3[f : f + 1]
        r.upd[at + 9 : at + 10] = to_row(r.a_b9[...])
        r.upd[at + 12 : at + 13] = to_row(r.a_g2[...])


def zero(*refs):
    for ref in refs:
        ref[...] = jnp.zeros(ref.shape, ref.dtype)


def decoder_update(d, st, fb, cot, consts):
    ph = Phase(d)
    ph.whole(n_own=fb.node_out, n_got=fb.got, idx=consts.idx, rt=consts.sums)
    ph.stream(e2=fb.e2)
    ph.edges(cot=cot)
    ph.whole(**weight_args(st, *UPD_W, *AUX_W))
    ph.out_edges(decoded=cot.shape)
    ph.out_stream(BF, part=(d.parts, d.blocks, d.feat, d.rows))
    ph.out_whole(F32, upd=(d.upd_rows, d.feat), dn_own=(d.parts, d.half, d.feat))
    ph.out_whole(BF, dn_far=(d.parts, d.half, d.feat))
    sq = (d.feat, d.feat)
    ph.temp(BF, n_cat=(d.length, d.feat), lhs=(d.feat, d.length + d.res), w1bt=sq, w2t=sq, w2h=sq, w3h=sq)
    ph.temp(BF, tt=(d.length + d.res, d.rows), tn=(d.rows, d.length + 128), da1=(d.feat, d.rows))
    ph.temp(BF, w3c=(d.feat, 2 * d.feat), gain_mat=sq, pair=(2 * d.feat + 16, d.rows), one=(d.feat + 16, d.rows))
    tall = (d.feat + 16, d.feat)
    ph.temp(F32, w3c_b=sq, aux=sq, cols=sq, a_w2=tall, a_w3=tall, a_b9=sq, a_g2=sq)
    ph.temp(F32, a_s=(d.feat, d.length), a_k=(d.blocks, d.feat, 128))

    def body(r):
        p, b = pl.program_id(0), pl.program_id(1)
        first, last = b == 0, b == d.blocks - 1

        @pl.when(first & (p == 0))
        def _():
            r.w1bt[...] = r.uw1[1, d.feat : 2 * d.feat, :].T
            r.w2h[...] = half_of(r.uw2[1])
            r.w2t[...] = r.w2h[...].T
            r.w3h[...] = half_of(r.uw3[1])
            load_cols(r, 1, r.aux, r.cols)
            centre_weights(r.uw3[1], r.cols[...], r.w3c, r.w3c_b)
            r.gain_mat[...] = gain_matrix(r.cols[...])
            zero(r.upd, r.a_w2, r.a_w3, r.a_b9, r.a_g2)
            r.pair[2 * d.feat :] = jnp.ones((16, d.rows), BF)
            r.one[d.feat :] = jnp.ones((16, d.rows), BF)
            r.tt[d.length :, :] = r.rt[: d.res]
            r.tn[:, d.length :] = r.rt[...].T

        @pl.when(first)
        def _():
            r.n_cat[: d.half] = r.n_own[p]
            r.n_cat[d.half :] = r.n_got[p]
            put_table(d, r.lhs, 0, 0, r.n_cat, r.uw1.at[1])
            zero(r.a_s)

        r.ready()
        f = d.feat
        n_blk = r.n_own[p, pl.ds(pl.multiple_of(b * d.res, d.res), d.res), :]
        put_own(d, r.lhs, 0, 0, r.uw1.at[1], n_blk, r.cols[:, 4:5])
        idx = r.idx[p, b]
        put_one_hot(d, r.tt, 0, idx)
        put_one_hot_rows(d, r.tn, idx)
        e2 = r.e2[...]
        r.pair[:f] = e2
        a1 = mm(r.lhs[...], r.tt[...]) + mm(r.w1bt[...], e2)
        g1, d1, _, d2, xh, rs, y = update_forward(
            d, a1, r.w2t[...], r.w3c, r.cols[:, 5:6], r.w3c_b[:, 0:1], r.pair, r.cols
        )
        r.one[:f] = g1
        r.decoded[...] = y.T.reshape(d.res, d.near, f)
        dy = r.cot[...].reshape(d.rows, f).T
        dr3 = norm_backward(d, r, dy, xh, rs, r.gain_mat[...])
        update_backward(d, r, dr3, r.one[...], d1, r.pair[f:], d2, r.w2h[...], r.w3h[...], r.da1)
        r.upd[f : 2 * f] += mm(e2, r.da1[...], 1, 1)
        r.part[...] = (mm(r.uw1[1, f : 2 * f, :], r.da1[...]) + dr3.astype(F32)).astype(BF)
        spread = mm(r.da1[...], r.tn[...])
        r.a_s[...] += spread[:, : d.length]
        r.a_k[b] = spread[:, d.length :]

        @pl.when(last)
        def _():
            own, far, b4 = spread_nodes(
                d, r.a_s[...], [r.a_k[i] for i in range(d.blocks)], r.uw1[1], r.n_cat[...], r.upd, 0
            )
            r.dn_own[p] = own
            r.dn_far[p] = far.astype(BF)
            update_small(d, r, b4)

    return ph.call("dec_update", body)


AUX_W = ("bias", "gain")


def message_backward(d, r, b, layer, da1):
    at = pl.ds(pl.multiple_of(b * d.res, d.res), d.res)
    v = (mm(r.mw3[layer], r.dub[at, :], 1, 1) * 0.5).astype(BF)
    da2 = mm(v, r.rt[: d.res]).astype(BF) * r.d2[...]
    r.m_w2[...] += mm(r.g1[...], da2, 1, 1)
    da1[...] = mm(r.mw2h[...], da2).astype(BF) * r.d1[...]


def message_small(d, r, b0):
    f = d.feat
    at = d.at_small
    r.msg[at : at + 1] += b0

    @pl.when(pl.program_id(0) == d.parts - 1)
    def _():
        r.msg[3 * f : 4 * f] = 0.5 * r.m_w2[:f]
        r.msg[at + 1 : at + 2] = r.m_w2[f : f + 1]


def middle_backward(d, edge_input, st, fa, fb, fd, cot_n, consts):
    ph = Phase(d, 4)
    ph.whole(cot_n=cot_n, dn_a=fd.dn_own, dn_far_in=fd.dn_far, n_own=fa.node_out, got_a=fa.got, got_b=fb.got_in)
    ph.whole(mask=consts.mask, rt=consts.sums, r1=fb.r1, ip=fb.ip, r2=fb.r2, big=fb.big, cnt=fb.cnt)
    ph.whole(urs=fb.urs, idx=consts.idx)
    ph.stream(d2=fb.d2, g1=fb.g1, d1=fb.d1, e2=fb.e2, dec_part=fd.part, uxh=fb.uxh)
    ph.stream(ug2=fb.ug2, ud2=fb.ud2, ug1=fb.ug1, ud1=fb.ud1)
    ph.edges(edge=edge_input)
    ph.whole(**weight_args(st, *NODE_W, *MSG_W, *UPD_W))
    ph.out_stream(BF, part=(d.parts, d.blocks, d.feat, d.rows))
    ph.out_whole(F32, msg=(d.msg_rows, d.feat), upd=(d.upd_rows, d.feat), dn_own=(d.parts, d.half, d.feat))
    ph.out_raw(BF, got=(d.parts, d.half, d.feat))
    sq = (d.feat, d.feat)
    ph.temp(BF, n_cat=(d.length, d.feat), dub=(d.half, d.feat), tn=(d.rows, d.length + 128))
    ph.temp(BF, both=(2 * d.feat, d.rows), w2h=sq, w3h=sq, mw2h=sq, gain_mat=sq)
    ph.temp(BF, leave=(d.parts, d.half, d.feat), arrive=(d.parts, d.half, d.feat))
    ph.temp(F32, dr1=(d.half, d.feat), e_aux=sq, e_cols=sq, d_aux=sq, d_cols=sq)
    tall = (d.feat + 16, d.feat)
    ph.temp(F32, m_w2=tall, a_w2=tall, a_w3=tall, a_b9=sq, a_g2=sq, a_w1=sq)
    ph.temp(F32, a_s=(2 * d.feat, d.length), a_k=(d.blocks, 2 * d.feat, 128))
    ph.sems(send=2 * d.parts, recv=2 * d.parts)

    def body(r):
        p, b = pl.program_id(0), pl.program_id(1)
        first, last = b == 0, b == d.blocks - 1
        n = d.parts
        early = [to_partner(r.dn_far_in.at[i], r.arrive.at[i], r.send.at[n + i], r.recv.at[n + i]) for i in range(n)]
        jobs = [to_partner(r.leave.at[i], r.got.at[i], r.send.at[i], r.recv.at[i]) for i in range(n)]

        @pl.when(first & (p == 0))
        def _():
            greet_partner()
            for job in early:
                job.start()
            load_cols(r, 0, r.e_aux, r.e_cols)
            load_cols(r, 1, r.d_aux, r.d_cols)
            r.tn[:, d.length :] = r.rt[...].T
            r.w2h[...] = half_of(r.uw2[0])
            r.w3h[...] = half_of(r.uw3[0])
            r.mw2h[...] = half_of(r.mw2[1])
            r.gain_mat[...] = gain_matrix(r.e_cols[...])
            zero(r.msg, r.upd, r.m_w2, r.a_w2, r.a_w3, r.a_b9, r.a_g2, r.a_w1)
            r.n_cat[d.half :] = r.got_a[...]

        @pl.when(first & (p == 1))
        def _():
            r.n_cat[d.half :] = r.got_b[...]

        for i in range(n):

            @pl.when(first & (p == i))
            def _(i=i):
                early[i].wait()

        @pl.when(first)
        def _():
            r.n_cat[: d.half] = r.n_own[p]
            zero(r.a_s)
            dn = r.cot_n[p].astype(F32) + r.dn_a[p] + r.arrive[p].astype(F32)
            node_backward(d, r, p, 1, r.d_aux[...], dn)

        f = d.feat
        r.ready()
        put_one_hot_rows(d, r.tn, r.idx[p, b])
        message_backward(d, r, b, 1, r.both.at[:f])
        r.msg[f : 2 * f] += mm(r.e2[...], r.both[:f], 1, 1)
        de = mm(r.mw1[1, f : 2 * f, :], r.both[:f])
        dy = (de + r.dec_part[...].astype(F32)).astype(BF)
        dr3 = norm_backward(d, r, dy, r.uxh[...], r.urs[p, b], r.gain_mat[...])
        update_backward(
            d, r, dr3, r.ug1[...], r.ud1[...], r.ug2[...], r.ud2[...], r.w2h[...], r.w3h[...], r.both.at[f:]
        )
        r.a_w1[...] += mm(r.both[f:], r.edge[...].reshape(d.rows, f))
        r.part[...] = (mm(r.uw1[0, f : 2 * f, :], r.both[f:]) + dr3.astype(F32)).astype(BF)
        spread = mm(r.both[...], r.tn[...])
        r.a_s[...] += spread[:, : d.length]
        r.a_k[b] = spread[:, d.length :]

        @pl.when(last)
        def _():
            n_cat = r.n_cat[...]
            a_k = [r.a_k[i] for i in range(d.blocks)]
            own_m, far_m, b0 = spread_nodes(
                d, r.a_s[: d.feat], [x[: d.feat] for x in a_k], r.mw1[1], n_cat, r.msg, 0
            )
            own_u, far_u, b4 = spread_nodes(
                d, r.a_s[d.feat :], [x[d.feat :] for x in a_k], r.uw1[0], n_cat, r.upd, 0
            )
            r.dn_own[p] = own_m + own_u + r.dr1[...]
            r.leave[p] = (far_m + far_u).astype(BF)
            for i in range(n):

                @pl.when(p == i)
                def _(i=i):
                    jobs[i].start()

            message_small(d, r, b0)
            update_small(d, r, b4)

            @pl.when(p == n - 1)
            def _():
                r.upd[d.feat : 2 * d.feat] = r.a_w1[...].T
                for job in jobs:
                    job.wait()

    return ph.call("dec_message_back", body)


def encoder_message_back(d, edge_input, st, fa, fe, n_own, n_got, consts):
    ph = Phase(d)
    ph.whole(dn_a=fe.dn_own, dn_b=fe.got, n_own=n_own, n_got=n_got)
    ph.whole(mask=consts.mask, rt=consts.sums, r1=fa.r1, ip=fa.ip, r2=fa.r2, big=fa.big, cnt=fa.cnt)
    ph.whole(idx=consts.idx)
    ph.stream(d2=fa.d2, g1=fa.g1, d1=fa.d1, up_part=fe.part)
    ph.edges(edge=edge_input)
    ph.whole(**weight_args(st, *NODE_W, *MSG_W))
    ph.out_edges(edge_grad=edge_input.shape)
    ph.out_whole(F32, msg=(d.msg_rows, d.feat), dn_own=(d.parts, d.half, d.feat))
    ph.out_whole(BF, dn_far=(d.parts, d.half, d.feat))
    sq = (d.feat, d.feat)
    ph.temp(BF, n_cat=(d.length, d.feat), dub=(d.half, d.feat), tn=(d.rows, d.length + 128))
    ph.temp(BF, da1=(d.feat, d.rows), mw2h=sq)
    ph.temp(F32, dr1=(d.half, d.feat), aux=sq, cols=sq, a_w1=sq, m_w2=(d.feat + 16, d.feat))
    ph.temp(F32, a_s=(d.feat, d.length), a_k=(d.blocks, d.feat, 128))

    def body(r):
        p, b = pl.program_id(0), pl.program_id(1)
        first, last = b == 0, b == d.blocks - 1

        @pl.when(first & (p == 0))
        def _():
            load_cols(r, 0, r.aux, r.cols)
            r.tn[:, d.length :] = r.rt[...].T
            r.mw2h[...] = half_of(r.mw2[0])
            zero(r.msg, r.m_w2, r.a_w1)

        @pl.when(first)
        def _():
            r.n_cat[: d.half] = r.n_own[p]
            r.n_cat[d.half :] = r.n_got[p]
            zero(r.a_s)
            node_backward(d, r, p, 0, r.aux[...], r.dn_a[p] + r.dn_b[p].astype(F32))

        f = d.feat
        r.ready()
        put_one_hot_rows(d, r.tn, r.idx[p, b])
        message_backward(d, r, b, 0, r.da1)
        r.a_w1[...] += mm(r.da1[...], r.edge[...].reshape(d.rows, f))
        de = mm(r.mw1[0, f : 2 * f, :], r.da1[...])
        de = (de + r.up_part[...].astype(F32)).astype(BF)
        r.edge_grad[...] = de.T.reshape(d.res, d.near, f)
        spread = mm(r.da1[...], r.tn[...])
        r.a_s[...] += spread[:, : d.length]
        r.a_k[b] = spread[:, d.length :]

        @pl.when(last)
        def _():
            own, far, b0 = spread_nodes(
                d, r.a_s[...], [r.a_k[i] for i in range(d.blocks)], r.mw1[0], r.n_cat[...], r.msg, 0
            )
            r.dn_own[p] = own + r.dr1[...]
            r.dn_far[p] = far.astype(BF)
            message_small(d, r, b0)

            @pl.when(p == d.parts - 1)
            def _():
                r.msg[d.feat : 2 * d.feat] = r.a_w1[...].T

    return ph.call("enc_message_back", body)


def reduce_grads(d, enc_msg, enc_upd, dec_msg, dec_upd, dn_far):
    devices = d.devices
    bits = devices.bit_length() - 1
    unit = 16 * devices
    feat = d.feat
    need = -(-(d.msg_rows + d.upd_rows) // unit)
    shares = [need // 3 + (1 if need % 3 > i else 0) for i in range(3)]
    groups = [unit * share for share in shares if share]
    rows = sum(groups)
    bases = [sum(groups[:i]) for i in range(len(groups))]
    across = -1
    dims = [across] + list(range(1, bits))
    turn = min(3, len(dims))
    orders = []
    for g in range(len(groups)):
        head = dims[:turn]
        head = head[g % turn :] + head[: g % turn]
        orders.append(([0] if bits else []) + head + dims[turn:])
    stages = len(orders[0])
    plans = []
    for g, order in enumerate(orders):
        size, both, plan = groups[g], True, []
        for dim in order:
            if dim == across:
                both = False
                plan.append((dim, size, False))
            else:
                size //= 2
                plan.append((dim, size, both))
        plans.append(plan)
    turns = len(groups) * stages

    def kernel(em, eu, dm, du, far, res, got, acc, gathered, *rest):
        buffers, (send, recv) = rest[: 2 * turns], rest[2 * turns :]
        section, me = lax.axis_index(AXIS_S), lax.axis_index(AXIS_D)

        def flag(bit):
            return lax.rem(me // (1 << bit), 2)

        def peer(dim):
            if dim == across:
                return other_section()
            return {AXIS_D: me + (1 - 2 * flag(dim)) * (1 << dim)}

        barrier = pltpu.get_barrier_semaphore()
        for dim in [across] + list(range(bits)):
            pl.semaphore_signal(barrier, inc=1, device_id=peer(dim), device_id_type=MESH)
        pl.semaphore_wait(barrier, bits + 1)

        def remote(src, dst, at, dim):
            return pltpu.make_async_remote_copy(
                src_ref=src, dst_ref=dst, send_sem=send.at[at], recv_sem=recv.at[at],
                device_id=peer(dim), device_id_type=MESH,
            )

        nodes = remote(far, got, 2 * turns, across)
        nodes.start()
        m, u = d.msg_rows, d.upd_rows
        for layer, (msg, upd) in enumerate(((em, eu), (dm, du))):
            acc[layer, :m] = msg[...]
            acc[layer, m : m + u] = upd[...]
            if rows > m + u:
                acc[layer, m + u :] = jnp.zeros((rows - m - u, feat), F32)

        def span(start, size):
            return pl.ds(pl.multiple_of(start, 16), size)

        starts = list(bases)
        for k in range(stages):
            jobs, spans = [], []
            for g, plan in enumerate(plans):
                dim, size, both = plan[k]
                at = g * stages + k
                out, into = buffers[2 * at], buffers[2 * at + 1]
                if dim == across:
                    keep = span(starts[g], size)
                    out[...] = acc[1 - section, keep, :].astype(BF)
                else:
                    side = flag(dim)
                    keep = span(starts[g] + side * size, size)
                    give = span(starts[g] + (1 - side) * size, size)
                    if both:
                        out[...] = acc[:, give, :].astype(BF)
                    else:
                        out[...] = acc[section, give, :].astype(BF)
                    starts[g] = starts[g] + side * size
                job = remote(out, into, at, dim)
                job.start()
                jobs.append(job)
                spans.append(keep)
            for g, plan in enumerate(plans):
                dim, size, both = plan[k]
                jobs[g].wait()
                into = buffers[2 * (g * stages + k) + 1]
                if both:
                    acc[:, spans[g], :] += into[...].astype(F32)
                else:
                    acc[section, spans[g], :] += into[...].astype(F32)
        sizes = [plan[-1][1] for plan in plans]
        for g in range(len(groups)):
            keep = span(starts[g], sizes[g])
            gathered[keep, :] = acc[section, keep, :].astype(BF)
        backs = [[step for step in reversed(plan) if step[0] != across] for plan in plans]
        for k in range(bits):
            jobs = []
            for g, back in enumerate(backs):
                dim, size, _ = back[k]
                part = gathered.at[span(starts[g], size), :]
                job = remote(part, part, turns + g * bits + k, dim)
                job.start()
                jobs.append(job)
                starts[g] = starts[g] - flag(dim) * size
            for job in jobs:
                job.wait()
        res[...] = gathered[...]
        nodes.wait()

    vm = pl.BlockSpec(memory_space=pltpu.VMEM)
    scratch = [pltpu.VMEM((2, rows, feat), F32), pltpu.VMEM((rows, feat), BF)]
    for plan in plans:
        for _, size, both in plan:
            scratch += [pltpu.VMEM((2, size, feat) if both else (size, feat), BF)] * 2
    scratch += [pltpu.SemaphoreType.DMA((2 * turns + 1,))] * 2
    return pl.pallas_call(
        kernel,
        in_specs=[vm] * 5,
        out_specs=[vm, pl.BlockSpec(memory_space=pl.ANY)],
        out_shape=[
            jax.ShapeDtypeStruct((rows, feat), BF),
            jax.ShapeDtypeStruct(dn_far.shape, BF),
        ],
        scratch_shapes=scratch,
        compiler_params=pltpu.CompilerParams(vmem_limit_bytes=58 << 20, collective_id=5, has_side_effects=True),
        name="reduce",
    )(enc_msg, enc_upd, dec_msg, dec_upd, dn_far)


def unpack(d, total, dn_own, dn_got, n_bias, n_gain):
    f = d.feat
    m = d.msg_rows
    shapes = [(1, 3 * f, f), (1, f, f), (1, f, f), (1, f, d.wide), (1, 1, d.wide), (1, d.wide, f)]
    shapes += [(1, 3 * f, f), (1, f, f), (1, f, f), (n_bias, 1, f), (n_gain, 1, f)]

    def kernel(t, own, got, node, mw1, mw2, mw3, inner, inner_b, outer, uw1, uw2, uw3, bias, gain):
        node[...] = (own[...] + got[...].astype(F32)).astype(BF)
        for ref, at in ((mw1, 0), (mw2, 3 * f), (mw3, 4 * f), (outer, d.at_outer)):
            ref[0] = t[at : at + ref.shape[1], :].astype(F32)
        for ref, at in ((uw1, m), (uw2, m + 3 * f), (uw3, m + 4 * f)):
            ref[0] = t[at : at + ref.shape[1], :].astype(F32)
        inner[0] = t[d.at_inner : d.at_inner + d.wide, :].astype(F32).T
        small = t[d.at_small : d.at_small + SMALL, :].astype(F32)
        other = t[m + 5 * f : m + 5 * f + SMALL, :].astype(F32)
        both = small + other
        for i in range(n_bias):
            bias[i] = both[i : i + 1]
        for i in range(n_gain):
            gain[i] = both[n_bias + i : n_bias + i + 1]
        for i in range(d.wide // f):
            inner_b[0, :, i * f : (i + 1) * f] = small[16 + i : 17 + i]

    vm = pl.BlockSpec(memory_space=pltpu.VMEM)
    out = [jax.ShapeDtypeStruct(dn_own.shape, BF)] + [jax.ShapeDtypeStruct(s, F32) for s in shapes]
    return pl.pallas_call(kernel, in_specs=[vm] * 3, out_specs=[vm] * len(out), out_shape=out, name="unpack")(
        total, dn_own, dn_got
    )


def per_device(
    node_input,
    edge_input,
    neighbors,
    residue_mask,
    decode_order,
    node_cotangent,
    edge_cotangent,
    message_w1,
    message_w2,
    message_w3,
    inner_w,
    inner_bias,
    outer_w,
    update_w1,
    update_w2,
    update_w3,
    biases,
    norm_gains,
):
    section = lax.axis_index(AXIS_S)
    is_first = section == 0
    parts, half, near, feat = edge_input.shape
    length = neighbors.shape[1]
    wide = inner_w.shape[2]
    res = BLOCK_RES
    rows = res * near
    blocks = half // res
    at_outer = 5 * feat
    at_inner = at_outer + wide
    at_small = at_inner + wide
    d = types.SimpleNamespace(
        parts=parts, half=half, near=near, feat=feat, length=length, wide=wide, res=res, rows=rows, blocks=blocks,
        at_outer=at_outer, at_inner=at_inner, at_small=at_small, msg_rows=at_small + SMALL,
        upd_rows=5 * feat + SMALL, devices=lax.axis_size(AXIS_D),
    )
    weights = dict(
        mw1=message_w1[0], mw2=message_w2[0], mw3=message_w3[0], inner=inner_w[0], inner_b=inner_bias, outer=outer_w[0],
        uw1=update_w1[0], uw2=update_w2[0], uw3=update_w3[0],
        bias=biases.transpose(1, 0, 2), gain=norm_gains.transpose(1, 0, 2),
    )
    own_ids = lax.dynamic_slice_in_dim(neighbors, section * half, half, 1) - section * half
    idx_row = jnp.where(own_ids < 0, own_ids + length, own_ids).reshape(parts, blocks, 1, rows)
    sums = np.zeros((128, rows), np.float32)
    sums[np.arange(rows) // near, np.arange(rows)] = 1.0
    sums = jnp.asarray(sums, BF)

    def own_first(x):
        return jnp.where(is_first, x, jnp.roll(x, half, axis=1))

    live = own_first(residue_mask)
    order = own_first(decode_order)
    centre = length // 2
    code = jnp.where(live == 1, order - centre, centre)
    own_code = (order[:, :half] - centre).reshape(parts, blocks, 1, res)
    lead = (parts, blocks, 1, length)
    top = jnp.pad(jnp.broadcast_to(live[:, None, None, :], lead), ((0, 0), (0, 0), (0, 0), (0, res)))
    second = jnp.concatenate([jnp.broadcast_to(code[:, None, None, :], lead), -own_code], axis=3)
    extra = jnp.concatenate([top, second, jnp.zeros((parts, blocks, EXTRA - 2, length + res), top.dtype)], axis=2)
    mask = jnp.broadcast_to(live[:, :half, None].astype(F32), (parts, half, feat))
    consts = types.SimpleNamespace(extra=extra.astype(BF), sums=sums, mask=mask, idx=idx_row)

    fa = encoder_message(d, edge_input, node_input, weights, consts)
    st = types.SimpleNamespace(**{n: getattr(fa, W_OUT + n) for n in weights})
    fb = encoder_update(d, edge_input, st, fa, consts)
    fd = decoder_update(d, st, fb, edge_cotangent, consts)
    fe = middle_backward(d, edge_input, st, fa, fb, fd, node_cotangent, consts)
    ff = encoder_message_back(d, edge_input, st, fa, fe, node_input, fa.nodes_got, consts)
    total, got = reduce_grads(d, ff.msg, fe.upd, fe.msg, fd.upd, ff.dn_far)
    node_grad, mw1, mw2, mw3, inner, inner_b, outer, uw1, uw2, uw3, bias, gain = unpack(
        d, total, ff.dn_own, got, biases.shape[1], norm_gains.shape[1]
    )
    return (
        fb.node_out, fd.decoded, node_grad, ff.edge_grad, mw1, mw2, mw3, inner, inner_b[:, 0], outer,
        uw1, uw2, uw3, bias.transpose(1, 0, 2), gain.transpose(1, 0, 2),
    )


def solution(mesh):
    def split(*axes):
        return P(*axes)

    by_part = split(AXIS_D)
    by_half = split(AXIS_D, AXIS_S)
    by_layer = split(AXIS_S)
    in_specs = (by_half, by_half, by_part, by_part, by_part, by_half, by_half) + (by_layer,) * 11
    out_specs = (by_half,) * 4 + (by_layer,) * 11
    return jax.shard_map(per_device, mesh=mesh, in_specs=in_specs, out_specs=out_specs, check_vma=False)
```

```python
import types

import jax
import jax.numpy as jnp
import numpy as np
from jax import lax
from jax.experimental import pallas as pl
from jax.experimental.pallas import tpu as pltpu
from jax.sharding import PartitionSpec as P

BF = jnp.bfloat16
F32 = jnp.float32
C1 = 0.7978845608
C2 = C1 * 0.044715
EPS = 1e-5
BLOCK_RES = 64
EXTRA = 16
SMALL = 32
MESH = pl.DeviceIdType.MESH


def mm(a, b, ca=1, cb=0):
    return lax.dot_general(a, b, (((ca,), (cb,)), ((), ())), preferred_element_type=F32)


def mm_exact(a, b, ca=1, cb=0):
    return lax.dot_general(
        a, b, (((ca,), (cb,)), ((), ())), precision=lax.Precision.HIGHEST, preferred_element_type=F32
    )


def gelu_pair(x):
    x = x.astype(BF)
    w = x * x * BF(C2)
    h = jnp.tanh(x * (w + BF(C1))) + BF(1.0)
    g = x * h
    d = h + g * (BF(2.0) - h) * (w * BF(3.0) + BF(C1))
    return g, d


def gelu_pair_wide(x):
    x2 = x * x
    h = 0.5 * jnp.tanh(x * (x2 * C2 + C1)) + 0.5
    g = x * h
    d = h + (g * (1.0 - h)) * (x2 * (6 * C2) + 2 * C1)
    return g, d


def lane_sum(x):
    total = x[:, :128]
    for at in range(128, x.shape[1], 128):
        total = total + x[:, at : at + 128]
    return total


def to_row(acc):
    return mm_exact(jnp.ones((8, acc.shape[1]), F32), acc, 1, 1)[0:1]


def norm_rows(r):
    c = r - jnp.mean(r, axis=-1, keepdims=True)
    rs = lax.rsqrt(jnp.mean(c * c, axis=-1, keepdims=True) + EPS)
    return c * rs, rs


def norm_back_rows(dxh, xh, rs):
    m1 = jnp.mean(dxh, axis=-1, keepdims=True)
    m2 = jnp.mean(dxh * xh, axis=-1, keepdims=True)
    return (dxh - m1 - xh * m2) * rs


def norm_back(dy, xh, rs, gain_col):
    dxh = dy * gain_col
    m1 = jnp.mean(dxh, axis=0, keepdims=True)
    m2 = jnp.mean(dxh * xh, axis=0, keepdims=True)
    return (dxh - m1 - xh * m2) * rs


class Phase:
    def __init__(self, dims, collective_id=None):
        self.d = dims
        self.collective_id = collective_id
        self.ins, self.outs, self.temps, self.kinds = [], [], [], {}

    def whole_spec(self, shape):
        rank = len(shape)
        return pl.BlockSpec(tuple(shape), lambda p, b: (0,) * rank)

    def whole(self, **arrays):
        self.ins += [(n, a, self.whole_spec(a.shape)) for n, a in arrays.items()]

    def raw(self, **arrays):
        self.ins += [(n, a, pl.BlockSpec(memory_space=pl.ANY)) for n, a in arrays.items()]

    def stream(self, **arrays):
        self.raw(**arrays)
        self.kinds.update({n: (False, False, a.shape[2:], a.dtype) for n, a in arrays.items()})

    def stream_top(self, rows, **arrays):
        self.raw(**arrays)
        self.kinds.update({n: (False, False, (rows,) + a.shape[3:], a.dtype) for n, a in arrays.items()})

    def edges(self, **arrays):
        self.raw(**arrays)
        block = (self.d.res, self.d.near, self.d.feat)
        self.kinds.update({n: (False, True, block, a.dtype) for n, a in arrays.items()})

    def out_whole(self, dtype, **shapes):
        self.outs += [(n, jax.ShapeDtypeStruct(s, dtype), self.whole_spec(s)) for n, s in shapes.items()]

    def out_raw(self, dtype, **shapes):
        spec = pl.BlockSpec(memory_space=pl.ANY)
        self.outs += [(n, jax.ShapeDtypeStruct(s, dtype), spec) for n, s in shapes.items()]

    def out_stream(self, dtype, **shapes):
        self.out_raw(dtype, **shapes)
        self.kinds.update({n: (True, False, s[2:], dtype) for n, s in shapes.items()})

    def out_edges(self, **shapes):
        self.out_raw(BF, **shapes)
        block = (self.d.res, self.d.near, self.d.feat)
        self.kinds.update({n: (True, True, block, BF) for n in shapes})

    def temp(self, dtype, **shapes):
        self.temps += [(n, pltpu.VMEM(s, dtype)) for n, s in shapes.items()]

    def sems(self, **counts):
        self.temps += [(n, pltpu.SemaphoreType.DMA((c,))) for n, c in counts.items()]

    def call(self, name, body):
        d = self.d
        names = [n for n, _, _ in self.ins] + [n for n, _, _ in self.outs] + [n for n, _ in self.temps]
        steps = d.parts * d.blocks
        buffers = [pltpu.VMEM((2,) + tuple(block), dtype) for _, _, block, dtype in self.kinds.values()]
        count = len(self.kinds)

        def kernel(*refs):
            refs, slots, sems = refs[: len(names)], refs[len(names) : len(names) + count], refs[len(names) + count :]
            plain = dict(zip(names, refs))
            step = pl.program_id(0) * d.blocks + pl.program_id(1)
            now = lax.rem(step, 2)

            def copy(i, n, at, slot):
                out, edges, block, _ = self.kinds[n]
                p, b = at // d.blocks, lax.rem(at, d.blocks)
                if edges:
                    far = plain[n].at[p, pl.ds(pl.multiple_of(b * d.res, d.res), d.res)]
                elif block[0] < plain[n].shape[2]:
                    far = plain[n].at[p, b, pl.ds(0, block[0])]
                else:
                    far = plain[n].at[p, b]
                near = slots[i].at[slot]
                return pltpu.make_async_copy(*((near, far) if out else (far, near)), sems[i].at[slot])

            into = [(i, n) for i, n in enumerate(self.kinds) if not self.kinds[n][0]]
            outof = [(i, n) for i, n in enumerate(self.kinds) if self.kinds[n][0]]

            @pl.when(step == 0)
            def _():
                for i, n in into:
                    copy(i, n, step, now).start()

            @pl.when(step + 1 < steps)
            def _():
                for i, n in into:
                    copy(i, n, step + 1, 1 - now).start()

            @pl.when(step >= 2)
            def _():
                for i, n in outof:
                    copy(i, n, step - 2, now).wait()

            def ready():
                for i, n in into:
                    copy(i, n, step, now).wait()

            def flush():
                for i, n in outof:
                    copy(i, n, step, now).start()

            plain_or_slot = dict(plain, ready=ready, flush=flush)
            plain_or_slot.update({n: slots[i].at[now] for i, n in enumerate(self.kinds)})
            body(types.SimpleNamespace(**plain_or_slot))

            @pl.when(step == steps - 1)
            def _():
                for i, n in outof:
                    if steps > 1:
                        copy(i, n, step - 1, 1 - now).wait()
                    copy(i, n, step, now).wait()

        results = pl.pallas_call(
            kernel,
            grid=(d.parts, d.blocks),
            in_specs=[s for _, _, s in self.ins],
            out_specs=[s for _, _, s in self.outs],
            out_shape=[s for _, s, _ in self.outs],
            scratch_shapes=[s for _, s in self.temps] + buffers + [pltpu.SemaphoreType.DMA((2,))] * count,
            compiler_params=pltpu.CompilerParams(
                dimension_semantics=(pltpu.ARBITRARY,) * 2,
                vmem_limit_bytes=60 << 20,
                collective_id=self.collective_id,
                has_side_effects=self.collective_id is not None,
            ),
            name=name,
        )(*[a for _, a, _ in self.ins])
        return types.SimpleNamespace(**dict(zip([n for n, _, _ in self.outs], results)))


def other_section():
    return {AXIS_S: 1 - lax.axis_index(AXIS_S)}


AXIS_S = "section"
AXIS_D = "dp"


def greet_partner():
    barrier = pltpu.get_barrier_semaphore()
    pl.semaphore_signal(barrier, inc=1, device_id=other_section(), device_id_type=MESH)
    pl.semaphore_wait(barrier, 1)


def to_partner(src, dst, send, recv):
    return pltpu.make_async_remote_copy(
        src_ref=src, dst_ref=dst, send_sem=send, recv_sem=recv, device_id=other_section(), device_id_type=MESH
    )


def put_one_hot(d, ref, at, idx):
    idx = idx.astype(jnp.int16)
    place = lax.broadcasted_iota(jnp.int16, (d.length, d.rows), 0)
    ref[at : at + d.length, :] = jnp.where(place == idx, jnp.ones((), BF), jnp.zeros((), BF))


def put_one_hot_rows(d, ref, idx):
    centre = d.length // 2
    idx = jnp.broadcast_to((idx - centre).astype(F32).astype(BF), (128, d.rows)).T
    place = lax.broadcasted_iota(jnp.int32, (d.rows, 128), 1)
    for at in range(0, d.length, 128):
        there = (place + (at - centre)).astype(F32).astype(BF)
        ref[:, at : at + 128] = jnp.where(idx == there, jnp.ones((), BF), jnp.zeros((), BF))


def weight_args(w, *names):
    return {n: getattr(w, n) for n in names}


def load_cols(r, layer, aux, cols):
    n_bias, n_gain = r.bias.shape[1], r.gain.shape[1]
    aux[...] = jnp.zeros(aux.shape, F32)
    for i in range(n_bias):
        aux[i : i + 1] = r.bias[layer, i]
    for i in range(n_gain):
        aux[n_bias + i : n_bias + i + 1] = r.gain[layer, i]
    cols[...] = aux[...].T


def put_table(d, lhs, at, left, n_cat, w1):
    lhs[at : at + d.feat, left : left + d.length] = mm(w1[2 * d.feat :, :].T, n_cat[...], 1, 1).astype(BF)


def put_own(d, lhs, at, left, w1, n_blk, bias_col):
    own = mm(w1[0 : d.feat, :].T, n_blk, 1, 1) + bias_col
    lhs[at : at + d.feat, left + d.length :] = own.astype(BF)


def message_part(a1, w2t, b2, att, kept):
    g1, d1 = gelu_pair(a1)
    a2 = mm(w2t, g1) + b2
    g2, d2 = gelu_pair(a2)
    attb = att.astype(BF)
    feat, rows = g2.shape
    kept[:feat] = g2 * attb
    kept[feat:] = jnp.broadcast_to(attb, (16, rows))
    return g1, d1, d2 * attb


def add_node_outs(ph, d):
    ph.out_whole(BF, node_out=(d.parts, d.half, d.feat))
    shape = (d.parts, d.half, d.feat)
    ph.out_whole(F32, r1=shape, ip=(d.parts, d.half, d.wide), r2=shape, big=shape, cnt=shape)


def node_step(d, r, p, b):
    sums = mm(r.rt[: d.res], r.kept[...], 1, 1)
    at = pl.ds(pl.multiple_of(b * d.res, d.res), d.res)
    r.big[p, at, :] = sums[:, : d.feat] * 0.5
    r.cnt[p, at, :] = jnp.broadcast_to(sums[:, d.feat : d.feat + 1], (d.res, d.feat))


def node_forward(r, p, n_own, layer, aux):
    big = r.big[p]
    hi = big.astype(BF)
    lo = (big - hi.astype(F32)).astype(BF)
    w3 = r.mw3[layer]
    upd = (mm(hi, w3) + mm(lo, w3) + r.cnt[p] * aux[2:3]) / 30.0
    r1 = n_own.astype(F32) + upd
    xh1, _ = norm_rows(r1)
    normed = xh1 * aux[10:11] + aux[7:8]
    ip = mm(normed.astype(BF), r.inner[layer]) + r.inner_b[layer]
    hid = gelu_pair_wide(ip)[0].astype(BF)
    r2 = normed + (mm(hid, r.outer[layer]) + aux[3:4])
    xh2, _ = norm_rows(r2)
    out = ((xh2 * aux[11:12] + aux[8:9]) * r.mask[p]).astype(BF)
    r.node_out[p] = out
    r.r1[p] = r1
    r.ip[p] = ip
    r.r2[p] = r2
    return out


def node_backward(d, r, p, layer, aux, dn):
    r1, ip, r2, big, cnt = r.r1[p], r.ip[p], r.r2[p], r.big[p], r.cnt[p]
    xh1, rs1 = norm_rows(r1)
    normed = xh1 * aux[10:11] + aux[7:8]
    xh2, rs2 = norm_rows(r2)
    dy2 = dn * r.mask[p]
    dr2 = norm_back_rows(dy2 * aux[11:12], xh2, rs2)
    low_outer = dr2.astype(BF)
    hid, slope = gelu_pair_wide(ip)
    dip = mm(low_outer, r.outer[layer], 1, 1) * slope
    low_inner = dip.astype(BF)
    at = d.at_outer
    r.msg[at : at + d.wide] += mm(hid.astype(BF), low_outer, 0, 0)
    at = d.at_inner
    r.msg[at : at + d.wide] += mm(low_inner, normed.astype(BF), 0, 0)
    dnormed = dr2 + mm(low_inner, r.inner[layer], 1, 1)
    dr1 = norm_back_rows(dnormed * aux[10:11], xh1, rs1)
    du = dr1 / 30.0
    dub = du.astype(BF)
    r.msg[4 * d.feat : 5 * d.feat] += mm(big.astype(BF), dub, 0, 0)
    dib = jnp.sum(dip, axis=0, keepdims=True)
    rows = {
        2: jnp.sum(cnt * du, axis=0, keepdims=True),
        3: jnp.sum(dr2, axis=0, keepdims=True),
        7: jnp.sum(dnormed, axis=0, keepdims=True),
        8: jnp.sum(dy2, axis=0, keepdims=True),
        10: jnp.sum(dnormed * xh1, axis=0, keepdims=True),
        11: jnp.sum(dy2 * xh2, axis=0, keepdims=True),
    }
    for i in range(d.wide // d.feat):
        rows[16 + i] = dib[:, i * d.feat : (i + 1) * d.feat]
    for row, value in rows.items():
        r.msg[d.at_small + row : d.at_small + row + 1] += value
    r.dr1[...] = dr1
    r.dub[...] = dub


def own_first(d, row):
    row = row.astype(F32)
    if row.shape[0] == 1:
        row = jnp.broadcast_to(row, (8, d.length))
    return jnp.where(lax.axis_index(AXIS_S) == 0, row, pltpu.roll(row, d.half, 1))


def put_positions(d, r):
    section = lax.axis_index(AXIS_S)
    centre = d.length // 2
    line = lax.broadcasted_iota(jnp.int32, (8, d.length), 0)
    for p in range(d.parts):
        live = own_first(d, r.live[p : p + 1, :])
        order = own_first(d, r.order[p : p + 1, :]) - centre
        code = jnp.where(live > 0.5, order, float(centre))
        r.codes[p, :8] = jnp.where(line == 0, live, jnp.where(line == 1, code, 0.0)).astype(BF)
        r.codes[p, 8:] = jnp.zeros((EXTRA - 8, d.length), BF)
        ids = own_first(d, r.near[p]) - float(d.half) * section.astype(F32)
        ids = jnp.where(ids < 0.0, ids + float(d.length), ids) - float(centre)
        r.mask[p] = jnp.broadcast_to(live[0:1], (d.feat, d.length)).T[: d.half]
        for b in range(d.blocks):
            own = pltpu.roll(order, (d.length - b * d.res) % d.length, 1) if b else order
            r.owns[p, b, :8] = jnp.where(line == 1, -own, 0.0)[:, : d.res].astype(BF)
            r.owns[p, b, 8:] = jnp.zeros((EXTRA - 8, d.res), BF)
            block = pltpu.roll(ids, (d.length - b * d.res) % d.length, 1) if b else ids
            spread = mm(block[:, : d.res].astype(BF), r.rt[: d.res])
            row = jnp.sum(spread * r.pick[...].astype(F32), axis=0, keepdims=True)
            r.idx[p, b] = row.astype(jnp.int32) + centre


def encoder_message(d, edge_input, node_input, neighbors, residue_mask, decode_order, weights, consts):
    ph = Phase(d, 2)
    ph.whole(n_own=node_input, rt=consts.sums, pick=consts.pick, near=neighbors, live=residue_mask, order=decode_order)
    ph.out_whole(jnp.int32, idx=(d.parts, d.blocks, 1, d.rows))
    ph.out_whole(F32, mask=(d.parts, d.half, d.feat))
    ph.temp(BF, codes=(d.parts, EXTRA, d.length), owns=(d.parts, d.blocks, EXTRA, d.res))
    ph.edges(edge=edge_input)
    names = tuple(weights)
    own = {W_IN + n: a for n, a in weights.items()}
    ph.raw(**own)
    act = (d.parts, d.blocks, d.feat, d.rows)
    ph.out_stream(BF, g1=with_ones(d), d1=act, d2=act)
    ph.out_whole(F32, att=(d.parts, d.blocks, 1, d.rows))
    add_node_outs(ph, d)
    ph.out_raw(BF, got=(d.half, d.feat), nodes_got=node_input.shape)
    for n, a in weights.items():
        ph.out_raw(a.dtype, **{W_OUT + n: (2,) + a.shape})
        ph.temp(a.dtype, **{n: (2,) + a.shape})
    sq = (d.feat, d.feat)
    wide = d.feat + d.length + d.res
    ph.temp(BF, n_cat=(d.length, d.feat), lhs=(d.feat + EXTRA, wide), w2t=sq, tt=(wide, d.rows))
    ph.temp(BF, leave=(d.half, d.feat), arrive=node_input.shape, kept=(d.feat + 16, d.rows))
    ph.temp(F32, aux=sq, cols=sq)
    count = len(names)
    ph.sems(send=count + 2, recv=count + 2, local=count, back=2 * count + 1)

    def body(r):
        p, b = pl.program_id(0), pl.program_id(1)
        first, last = b == 0, b == d.blocks - 1
        section = lax.axis_index(AXIS_S)
        job = to_partner(r.leave, r.got, r.send.at[count], r.recv.at[count])
        nodes = to_partner(r.n_own, r.arrive, r.send.at[count + 1], r.recv.at[count + 1])

        def swaps(group):
            out = []
            for n in group:
                i = names.index(n)
                dst = getattr(r, n).at[section]
                out.append(to_partner(getattr(r, W_IN + n), dst, r.send.at[i], r.recv.at[i]))
            return out

        def own_copies():
            return [
                pltpu.make_async_copy(getattr(r, W_IN + n), getattr(r, n).at[section], r.local.at[i])
                for i, n in enumerate(names)
            ]

        def returns(group):
            out = [pltpu.make_async_copy(r.arrive, r.nodes_got, r.back.at[2 * count])] if group == GROUP_ONE else []
            for n in group:
                i = names.index(n)
                src, dst = getattr(r, n), getattr(r, W_OUT + n)
                for layer in range(2):
                    sem = r.back.at[2 * i + layer]
                    out.append(pltpu.make_async_copy(src.at[layer], dst.at[layer], sem))
            return out

        begin = first & (p == 0)
        middle = (p == 1) & (b == 1)
        at_end = last & (p == d.parts - 1)

        @pl.when(begin)
        def _():
            greet_partner()
            nodes.start()
            for item in swaps(GROUP_ONE) + own_copies():
                item.start()
            r.tt[d.feat + d.length :, :] = r.rt[: d.res]
            put_positions(d, r)
            nodes.wait()
            for item in swaps(GROUP_ONE) + own_copies():
                item.wait()
            for item in swaps(GROUP_TWO):
                item.start()
            r.lhs[: d.feat, : d.feat] = r.mw1[0, d.feat : 2 * d.feat, :].T
            r.lhs[d.feat :, : d.feat] = jnp.zeros((EXTRA, d.feat), BF)
            r.w2t[...] = half_of(r.mw2[0]).T
            load_cols(r, 0, r.aux, r.cols)

        @pl.when(first)
        def _():
            r.n_cat[: d.half] = r.n_own[p]
            r.n_cat[d.half :] = r.arrive[p]
            put_table(d, r.lhs, 0, d.feat, r.n_cat, r.mw1.at[0])

        n_blk = r.n_own[p, pl.ds(pl.multiple_of(b * d.res, d.res), d.res), :]
        r.ready()
        put_one_hot(d, r.tt, d.feat, r.idx[p, b])
        r.tt[: d.feat, :] = r.edge[...].reshape(d.rows, d.feat).T
        put_own(d, r.lhs, 0, d.feat, r.mw1.at[0], n_blk, r.cols[:, 0:1])
        r.lhs[d.feat :, d.feat : d.feat + d.length] = r.codes[p]
        r.lhs[d.feat :, d.feat + d.length :] = r.owns[p, b]
        out = mm(r.lhs[...], r.tt[...])
        att = out[d.feat : d.feat + 1]
        r.att[p, b] = jnp.where(out[d.feat + 1 : d.feat + 2] < 0.0, 1.0, 0.0)
        g1, r.d1[...], r.d2[...] = message_part(out[: d.feat], r.w2t[...], r.cols[:, 1:2], att, r.kept)
        put_ones(r.g1, g1)
        node_step(d, r, p, b)
        r.flush()

        @pl.when(middle)
        def _():
            for item in swaps(GROUP_TWO):
                item.wait()
            for item in swaps(GROUP_THREE) + returns(GROUP_ONE) + returns(GROUP_TWO):
                item.start()
            r.leave[...] = node_forward(r, 0, r.n_own[0], 0, r.aux[...])
            job.start()

        @pl.when(at_end)
        def _():
            for item in swaps(GROUP_THREE):
                item.wait()
            for item in returns(GROUP_THREE):
                item.start()
            node_forward(r, d.parts - 1, r.n_own[d.parts - 1], 0, r.aux[...])
            for item in returns(GROUP_ONE) + returns(GROUP_TWO) + returns(GROUP_THREE):
                item.wait()
            job.wait()

    return ph.call("enc_message", body)


W_IN, W_OUT = "i_", "o_"
GROUP_ONE = ("mw1", "mw2", "bias", "gain")
GROUP_TWO = ("mw3", "inner", "inner_b", "outer")
GROUP_THREE = ("uw1", "uw2", "uw3")
NODE_W = ("mw3", "inner", "inner_b", "outer", "bias", "gain")
MSG_W = ("mw1", "mw2")
UPD_W = ("uw1", "uw2", "uw3")


def with_ones(d):
    return (d.parts, d.blocks, d.feat + 16, d.rows)


def put_ones(ref, g):
    feat, rows = g.shape
    ref[:feat] = g
    ref[feat:] = jnp.ones((16, rows), BF)


def half_of(w):
    return w * BF(0.5)


def update_forward(d, a1, w2t, w3c, b5, b6c, pair, cols):
    f = d.feat
    g1, d1 = gelu_pair(a1)
    a2 = mm(w2t, g1) + b5
    g2, d2 = gelu_pair(a2)
    pair[f : 2 * f] = g2
    cent = mm(w3c[...], pair[: 2 * f]) + b6c
    var = jnp.mean(cent * cent, axis=0, keepdims=True)
    rs = lax.rsqrt(var + EPS)
    xh = cent.astype(BF) * rs.astype(BF)
    y = xh * cols[:, 12:13].astype(BF) + cols[:, 9:10].astype(BF)
    return g1, d1, g2, d2, xh, rs, y


def centre_weights(w3, cols, w3c, b6c):
    feat = w3.shape[0]
    eye = lax.broadcasted_iota(jnp.int32, w3.shape, 0) == lax.broadcasted_iota(jnp.int32, w3.shape, 1)
    w3f = w3.astype(F32)
    w3c[:, feat:] = (0.5 * (w3f - jnp.mean(w3f, axis=1, keepdims=True))).T.astype(BF)
    w3c[:, :feat] = (eye.astype(F32) - 1.0 / feat).astype(BF)
    b6 = cols[:, 6:7]
    b6c[...] = jnp.broadcast_to(b6 - jnp.mean(b6, axis=0, keepdims=True), b6c.shape)


def encoder_update(d, edge_input, st, fa, consts):
    ph = Phase(d, 3)
    ph.whole(n_own=fa.node_out, got_a=fa.got, idx=consts.idx, rt=consts.sums, mask=consts.mask, att=fa.att)
    ph.edges(edge=edge_input)
    ph.whole(**weight_args(st, *NODE_W, *MSG_W, *UPD_W))
    act = (d.parts, d.blocks, d.feat, d.rows)
    two = (d.parts, d.blocks, 2 * d.feat + 16, d.rows)
    ph.out_stream(BF, ugs=two, ud1=act, ud2=act, uxh=act, e2g=two, d1=act, d2=act)
    ph.out_whole(F32, urs=(d.parts, d.blocks, 1, d.rows))
    add_node_outs(ph, d)
    ph.out_whole(BF, got_in=(d.half, d.feat))
    ph.out_raw(BF, got=(d.parts, d.half, d.feat))
    sq = (d.feat, d.feat)
    wide = d.feat + d.length + d.res
    ph.temp(BF, n_cat=(d.length, d.feat), lhs=(2 * d.feat, wide), tt=(wide, d.rows))
    ph.temp(BF, uw2t=sq, mw1bt=sq, mw2t=sq, w3c=(d.feat, 2 * d.feat), pair=(2 * d.feat, d.rows))
    ph.temp(BF, kept=(d.feat + 16, d.rows), leave=(d.parts, d.half, d.feat), lead=(d.half, d.feat), arrive=(d.half, d.feat))
    ph.temp(F32, w3c_b=sq, e_aux=sq, e_cols=sq, d_aux=sq, d_cols=sq)
    ph.sems(send=d.parts + 1, recv=d.parts + 1)

    def body(r):
        p, b = pl.program_id(0), pl.program_id(1)
        first, last = b == 0, b == d.blocks - 1
        early = to_partner(r.lead, r.arrive, r.send.at[d.parts], r.recv.at[d.parts])
        jobs = [to_partner(r.leave.at[i], r.got.at[i], r.send.at[i], r.recv.at[i]) for i in range(d.parts)]

        @pl.when(first & (p == 0))
        def _():
            greet_partner()
            r.lead[...] = r.n_own[d.parts - 1]
            early.start()
            r.tt[d.feat + d.length :, :] = r.rt[: d.res]
            r.lhs[: d.feat, : d.feat] = r.uw1[0, d.feat : 2 * d.feat, :].T
            r.lhs[d.feat :, : d.feat] = jnp.zeros((d.feat, d.feat), BF)
            r.uw2t[...] = half_of(r.uw2[0]).T
            r.mw1bt[...] = r.mw1[1, d.feat : 2 * d.feat, :].T
            r.mw2t[...] = half_of(r.mw2[1]).T
            load_cols(r, 0, r.e_aux, r.e_cols)
            load_cols(r, 1, r.d_aux, r.d_cols)
            centre_weights(r.uw3[0], r.e_cols[...], r.w3c, r.w3c_b)
            r.n_cat[d.half :] = r.got_a[...]

        @pl.when(first & (p == 1))
        def _():
            early.wait()
            r.n_cat[d.half :] = r.arrive[...]
            r.got_in[...] = r.arrive[...]

        @pl.when(first)
        def _():
            r.n_cat[: d.half] = r.n_own[p]
            put_table(d, r.lhs, 0, d.feat, r.n_cat, r.uw1.at[0])
            put_table(d, r.lhs, d.feat, d.feat, r.n_cat, r.mw1.at[1])

        r.ready()
        n_blk = r.n_own[p, pl.ds(pl.multiple_of(b * d.res, d.res), d.res), :]
        put_own(d, r.lhs, 0, d.feat, r.uw1.at[0], n_blk, r.e_cols[:, 4:5])
        put_own(d, r.lhs, d.feat, d.feat, r.mw1.at[1], n_blk, r.d_cols[:, 0:1])
        put_one_hot(d, r.tt, d.feat, r.idx[p, b])
        edge_t = r.edge[...].reshape(d.rows, d.feat).T
        r.tt[: d.feat, :] = edge_t
        r.pair[: d.feat] = edge_t
        out = mm(r.lhs[...], r.tt[...])
        g1, d1, g2, d2, xh, rs, e2 = update_forward(
            d, out[: d.feat], r.uw2t[...], r.w3c, r.e_cols[:, 5:6], r.w3c_b[:, 0:1], r.pair, r.e_cols
        )
        f = d.feat
        r.ugs[:f] = g2
        put_ones(r.ugs.at[f:], g1)
        r.ud1[...], r.ud2[...], r.uxh[...], r.urs[p, b], r.e2g[:f] = d1, d2, xh, rs, e2
        att = r.att[p, b]
        a1 = out[d.feat :] + mm(r.mw1bt[...], e2)
        g1, r.d1[...], r.d2[...] = message_part(a1, r.mw2t[...], r.d_cols[:, 1:2], att, r.kept)
        put_ones(r.e2g.at[f:], g1)
        node_step(d, r, p, b)
        r.flush()

        @pl.when(last)
        def _():
            r.leave[p] = node_forward(r, p, r.n_own[p], 1, r.d_aux[...])
            for i in range(d.parts):

                @pl.when(p == i)
                def _(i=i):
                    jobs[i].start()

            @pl.when(p == d.parts - 1)
            def _():
                for job in jobs:
                    job.wait()

    return ph.call("enc_update", body)


def spread_nodes(d, acc, sumk, w1, n_cat, grad, grad_at):
    s = acc.astype(BF)
    sk = jnp.concatenate([x[:, : d.res] for x in sumk], axis=1)
    skb = sk.astype(BF)
    far = mm(s, w1[2 * d.feat :].T, 0, 0)
    own = mm(skb, w1[: d.feat].T, 0, 0)
    grad[grad_at + 2 * d.feat : grad_at + 3 * d.feat, :] += mm(n_cat, s, 0, 1)
    grad[grad_at : grad_at + d.feat, :] += mm(n_cat[: d.half], skb, 0, 1)
    return own + far[: d.half], far[d.half :], to_row(sk)


def lane_total(x):
    size = x.shape[1] // 4
    x = (x[:, :size] + x[:, size : 2 * size]) + (x[:, 2 * size : 3 * size] + x[:, 3 * size :])
    return lane_sum(x.astype(F32))


def norm_backward(d, r, dy, xh, rs, gain_mat):
    r.a_b9[...] += lane_total(dy)
    r.a_g2[...] += lane_total(dy * xh)
    z = mm(gain_mat, dy).astype(BF)
    m2 = jnp.mean((z * xh).astype(F32), axis=0, keepdims=True)
    return (z - xh * m2.astype(BF)) * rs.astype(BF)


def gain_matrix(cols):
    feat = cols.shape[0]
    shape = (feat, feat)
    eye = lax.broadcasted_iota(jnp.int32, shape, 0) == lax.broadcasted_iota(jnp.int32, shape, 1)
    scaled = jnp.where(eye, jnp.broadcast_to(cols[:, 12:13], shape), 0.0)
    return (scaled - jnp.mean(scaled, axis=0, keepdims=True)).astype(BF)


def update_backward(d, r, dr3, gs, d1, d2, w2, w3, low, da1):
    f = d.feat
    low[:f] = dr3
    low[f:] = mm(w3, dr3).astype(BF) * d2
    r.a_w23[...] += mm(gs, low[...], 1, 1)
    da1[...] = mm(w2, low[f:]).astype(BF) * d1


def update_small(d, r, b4):
    f = d.feat
    at = 5 * f
    r.upd[at + 4 : at + 5] += b4

    @pl.when(pl.program_id(0) == d.parts - 1)
    def _():
        r.upd[3 * f : 4 * f] = 0.5 * r.a_w23[f : 2 * f, f:]
        r.upd[4 * f : 5 * f] = 0.5 * r.a_w23[:f, :f]
        r.upd[at + 5 : at + 6] = r.a_w23[2 * f : 2 * f + 1, f:]
        r.upd[at + 6 : at + 7] = r.a_w23[2 * f : 2 * f + 1, :f]
        r.upd[at + 9 : at + 10] = to_row(r.a_b9[...])
        r.upd[at + 12 : at + 13] = to_row(r.a_g2[...])


def zero(*refs):
    for ref in refs:
        ref[...] = jnp.zeros(ref.shape, ref.dtype)


def decoder_update(d, st, fb, cot, consts):
    ph = Phase(d)
    ph.whole(n_own=fb.node_out, n_got=fb.got, idx=consts.idx, rt=consts.sums)
    ph.stream_top(d.feat, e2=fb.e2g)
    ph.edges(cot=cot)
    ph.whole(**weight_args(st, *UPD_W, *AUX_W))
    ph.out_edges(decoded=cot.shape)
    ph.out_stream(BF, part=(d.parts, d.blocks, d.feat, d.rows))
    ph.out_whole(F32, upd=(d.upd_rows, d.feat), dn_own=(d.parts, d.half, d.feat))
    ph.out_whole(BF, dn_far=(d.parts, d.half, d.feat), nodes=(d.parts, d.half, d.feat))
    sq = (d.feat, d.feat)
    ph.temp(BF, n_cat=(d.length, d.feat), lhs=(d.feat, d.length + d.res), w1bt=sq, w2t=sq, w2h=sq, w3h=sq)
    ph.temp(BF, tt=(d.length + d.res, d.rows), tn=(d.rows, d.length + 128), da1=(d.feat, d.rows))
    ph.temp(BF, w3c=(d.feat, 2 * d.feat), gain_mat=sq, pair=(3 * d.feat + 16, d.rows), low=(2 * d.feat, d.rows))
    ph.temp(F32, w3c_b=sq, aux=sq, cols=sq, a_w23=(2 * d.feat + 16, 2 * d.feat), a_b9=sq, a_g2=sq)
    ph.temp(F32, a_s=(d.feat, d.length), a_k=(d.blocks, d.feat, 128))

    def body(r):
        p, b = pl.program_id(0), pl.program_id(1)
        first, last = b == 0, b == d.blocks - 1

        @pl.when(first & (p == 0))
        def _():
            r.nodes[...] = r.n_own[...]
            r.w1bt[...] = r.uw1[1, d.feat : 2 * d.feat, :].T
            r.w2h[...] = half_of(r.uw2[1])
            r.w2t[...] = r.w2h[...].T
            r.w3h[...] = half_of(r.uw3[1])
            load_cols(r, 1, r.aux, r.cols)
            centre_weights(r.uw3[1], r.cols[...], r.w3c, r.w3c_b)
            r.gain_mat[...] = gain_matrix(r.cols[...])
            zero(r.upd, r.a_w23, r.a_b9, r.a_g2)
            r.pair[3 * d.feat :] = jnp.ones((16, d.rows), BF)
            r.tt[d.length :, :] = r.rt[: d.res]
            r.tn[:, d.length :] = r.rt[...].T

        @pl.when(first)
        def _():
            r.n_cat[: d.half] = r.n_own[p]
            r.n_cat[d.half :] = r.n_got[p]
            put_table(d, r.lhs, 0, 0, r.n_cat, r.uw1.at[1])
            zero(r.a_s)

        r.ready()
        f = d.feat
        n_blk = r.n_own[p, pl.ds(pl.multiple_of(b * d.res, d.res), d.res), :]
        put_own(d, r.lhs, 0, 0, r.uw1.at[1], n_blk, r.cols[:, 4:5])
        idx = r.idx[p, b]
        put_one_hot(d, r.tt, 0, idx)
        put_one_hot_rows(d, r.tn, idx)
        e2 = r.e2[...]
        r.pair[:f] = e2
        a1 = mm(r.lhs[...], r.tt[...]) + mm(r.w1bt[...], e2)
        g1, d1, _, d2, xh, rs, y = update_forward(
            d, a1, r.w2t[...], r.w3c, r.cols[:, 5:6], r.w3c_b[:, 0:1], r.pair, r.cols
        )
        r.pair[2 * f : 3 * f] = g1
        r.decoded[...] = y.T.reshape(d.res, d.near, f)
        dy = r.cot[...].reshape(d.rows, f).T
        dr3 = norm_backward(d, r, dy, xh, rs, r.gain_mat[...])
        update_backward(d, r, dr3, r.pair[f:], d1, d2, r.w2h[...], r.w3h[...], r.low, r.da1)
        r.upd[f : 2 * f] += mm(e2, r.da1[...], 1, 1)
        r.part[...] = (mm(r.uw1[1, f : 2 * f, :], r.da1[...]) + dr3.astype(F32)).astype(BF)
        spread = mm(r.da1[...], r.tn[...])
        r.a_s[...] += spread[:, : d.length]
        r.a_k[b] = spread[:, d.length :]
        r.flush()

        @pl.when(last)
        def _():
            own, far, b4 = spread_nodes(
                d, r.a_s[...], [r.a_k[i] for i in range(d.blocks)], r.uw1[1], r.n_cat[...], r.upd, 0
            )
            r.dn_own[p] = own
            r.dn_far[p] = far.astype(BF)
            update_small(d, r, b4)

    return ph.call("dec_update", body)


AUX_W = ("bias", "gain")


def message_backward(d, r, b, layer, low):
    at = pl.ds(pl.multiple_of(b * d.res, d.res), d.res)
    v = (mm(r.mw3[layer], r.dub[at, :], 1, 1) * 0.5).astype(BF)
    f = d.feat
    low[:f] = mm(v, r.rt[: d.res]).astype(BF) * r.d2[...]
    low[f:] = mm(r.mw2h[...], low[:f]).astype(BF) * r.d1[...]


def message_small(d, r, b0):
    r.msg[d.at_small : d.at_small + 1] += b0


def middle_backward(d, edge_input, st, fa, fb, fd, cot_n, consts):
    ph = Phase(d, 4)
    ph.whole(cot_n=cot_n, dn_a=fd.dn_own, dn_far_in=fd.dn_far, n_own=fa.node_out, got_a=fa.got, got_b=fb.got_in)
    ph.whole(mask=consts.mask, rt=consts.sums, r1=fb.r1, ip=fb.ip, r2=fb.r2, big=fb.big, cnt=fb.cnt)
    ph.whole(urs=fb.urs, idx=consts.idx)
    ph.stream(d2=fb.d2, d1=fb.d1, e2g=fb.e2g, dec_part=fd.part, uxh=fb.uxh, ugs=fb.ugs, ud2=fb.ud2, ud1=fb.ud1)
    ph.edges(edge=edge_input)
    ph.whole(**weight_args(st, *NODE_W, *MSG_W, *UPD_W))
    ph.out_stream(BF, part=(d.parts, d.blocks, d.feat, d.rows))
    ph.out_whole(F32, msg=(d.msg_rows, d.feat), upd=(d.upd_rows, d.feat), dn_own=(d.parts, d.half, d.feat))
    ph.out_raw(BF, got=(d.parts, d.half, d.feat))
    sq = (d.feat, d.feat)
    ph.temp(BF, n_cat=(d.length, d.feat), dub=(d.half, d.feat), tn=(d.rows, d.length + 128))
    ph.temp(BF, tri=(3 * d.feat, d.rows), low=(2 * d.feat, d.rows), w2h=sq, w3h=sq, mw2h=sq, gain_mat=sq)
    ph.temp(BF, leave=(d.parts, d.half, d.feat), arrive=(d.parts, d.half, d.feat))
    ph.temp(F32, dr1=(d.half, d.feat), e_aux=sq, e_cols=sq, d_aux=sq, d_cols=sq)
    tall = (2 * d.feat + 16, 2 * d.feat)
    ph.temp(F32, m_w12=tall, a_w23=tall, a_b9=sq, a_g2=sq, a_w1=sq)
    ph.temp(F32, a_s=(2 * d.feat, d.length), a_k=(d.blocks, 2 * d.feat, 128))
    ph.sems(send=2 * d.parts, recv=2 * d.parts)

    def body(r):
        p, b = pl.program_id(0), pl.program_id(1)
        first, last = b == 0, b == d.blocks - 1
        n = d.parts
        early = [to_partner(r.dn_far_in.at[i], r.arrive.at[i], r.send.at[n + i], r.recv.at[n + i]) for i in range(n)]
        jobs = [to_partner(r.leave.at[i], r.got.at[i], r.send.at[i], r.recv.at[i]) for i in range(n)]

        @pl.when(first & (p == 0))
        def _():
            greet_partner()
            for job in early:
                job.start()
            load_cols(r, 0, r.e_aux, r.e_cols)
            load_cols(r, 1, r.d_aux, r.d_cols)
            r.tn[:, d.length :] = r.rt[...].T
            r.w2h[...] = half_of(r.uw2[0])
            r.w3h[...] = half_of(r.uw3[0])
            r.mw2h[...] = half_of(r.mw2[1])
            r.gain_mat[...] = gain_matrix(r.e_cols[...])
            zero(r.msg, r.upd, r.m_w12, r.a_w23, r.a_b9, r.a_g2, r.a_w1)
            r.n_cat[d.half :] = r.got_a[...]

        @pl.when(first & (p == 1))
        def _():
            r.n_cat[d.half :] = r.got_b[...]

        for i in range(n):

            @pl.when(first & (p == i))
            def _(i=i):
                early[i].wait()

        @pl.when(first)
        def _():
            r.n_cat[: d.half] = r.n_own[p]
            zero(r.a_s)
            dn = r.cot_n[p].astype(F32) + r.dn_a[p] + r.arrive[p].astype(F32)
            node_backward(d, r, p, 1, r.d_aux[...], dn)

        f = d.feat
        r.ready()
        put_one_hot_rows(d, r.tn, r.idx[p, b])
        message_backward(d, r, b, 1, r.tri.at[: 2 * f])
        r.m_w12[...] += mm(r.e2g[...], r.tri[: 2 * f], 1, 1)
        de = mm(r.mw1[1, f : 2 * f, :], r.tri[f : 2 * f])
        dy = (de + r.dec_part[...].astype(F32)).astype(BF)
        dr3 = norm_backward(d, r, dy, r.uxh[...], r.urs[p, b], r.gain_mat[...])
        da1 = r.tri.at[2 * f :]
        update_backward(d, r, dr3, r.ugs[...], r.ud1[...], r.ud2[...], r.w2h[...], r.w3h[...], r.low, da1)
        r.a_w1[...] += mm(da1[...], r.edge[...].reshape(d.rows, f))
        r.part[...] = (mm(r.uw1[0, f : 2 * f, :], da1[...]) + dr3.astype(F32)).astype(BF)
        spread = mm(r.tri[f:], r.tn[...])
        r.a_s[...] += spread[:, : d.length]
        r.a_k[b] = spread[:, d.length :]
        r.flush()

        @pl.when(last)
        def _():
            n_cat = r.n_cat[...]
            a_k = [r.a_k[i] for i in range(d.blocks)]
            own_m, far_m, b0 = spread_nodes(
                d, r.a_s[: d.feat], [x[: d.feat] for x in a_k], r.mw1[1], n_cat, r.msg, 0
            )
            own_u, far_u, b4 = spread_nodes(
                d, r.a_s[d.feat :], [x[d.feat :] for x in a_k], r.uw1[0], n_cat, r.upd, 0
            )
            r.dn_own[p] = own_m + own_u + r.dr1[...]
            r.leave[p] = (far_m + far_u).astype(BF)
            for i in range(n):

                @pl.when(p == i)
                def _(i=i):
                    jobs[i].start()

            message_small(d, r, b0)
            update_small(d, r, b4)

            @pl.when(p == n - 1)
            def _():
                f, at = d.feat, d.at_small
                r.upd[f : 2 * f] = r.a_w1[...].T
                r.msg[f : 2 * f] = r.m_w12[:f, f:]
                r.msg[3 * f : 4 * f] = 0.5 * r.m_w12[f : 2 * f, :f]
                r.msg[at + 1 : at + 2] = r.m_w12[2 * f : 2 * f + 1, :f]
                for job in jobs:
                    job.wait()

    return ph.call("dec_message_back", body)


def encoder_message_back(d, edge_input, st, fa, fe, n_own, n_got, consts):
    ph = Phase(d)
    ph.whole(dn_a=fe.dn_own, dn_b=fe.got, n_own=n_own, n_got=n_got)
    ph.whole(mask=consts.mask, rt=consts.sums, r1=fa.r1, ip=fa.ip, r2=fa.r2, big=fa.big, cnt=fa.cnt)
    ph.whole(idx=consts.idx)
    ph.stream(d2=fa.d2, g1=fa.g1, d1=fa.d1, up_part=fe.part)
    ph.edges(edge=edge_input)
    ph.whole(**weight_args(st, *NODE_W, *MSG_W))
    ph.out_edges(edge_grad=edge_input.shape)
    ph.out_whole(F32, msg=(d.msg_rows, d.feat), dn_own=(d.parts, d.half, d.feat))
    ph.out_whole(BF, dn_far=(d.parts, d.half, d.feat))
    sq = (d.feat, d.feat)
    ph.temp(BF, n_cat=(d.length, d.feat), dub=(d.half, d.feat), tn=(d.rows, d.length + 128))
    ph.temp(BF, low=(2 * d.feat, d.rows), mw2h=sq)
    ph.temp(F32, dr1=(d.half, d.feat), aux=sq, cols=sq, a_w1=sq, m_w2=(d.feat + 16, d.feat))
    ph.temp(F32, a_s=(d.feat, d.length), a_k=(d.blocks, d.feat, 128))

    def body(r):
        p, b = pl.program_id(0), pl.program_id(1)
        first, last = b == 0, b == d.blocks - 1

        @pl.when(first & (p == 0))
        def _():
            load_cols(r, 0, r.aux, r.cols)
            r.tn[:, d.length :] = r.rt[...].T
            r.mw2h[...] = half_of(r.mw2[0])
            zero(r.msg, r.m_w2, r.a_w1)

        @pl.when(first)
        def _():
            r.n_cat[: d.half] = r.n_own[p]
            r.n_cat[d.half :] = r.n_got[p]
            zero(r.a_s)
            node_backward(d, r, p, 0, r.aux[...], r.dn_a[p] + r.dn_b[p].astype(F32))

        f = d.feat
        r.ready()
        put_one_hot_rows(d, r.tn, r.idx[p, b])
        message_backward(d, r, b, 0, r.low)
        da1 = r.low.at[f:]
        r.m_w2[...] += mm(r.g1[...], r.low[:f], 1, 1)
        r.a_w1[...] += mm(da1[...], r.edge[...].reshape(d.rows, f))
        de = mm(r.mw1[0, f : 2 * f, :], da1[...])
        de = (de + r.up_part[...].astype(F32)).astype(BF)
        r.edge_grad[...] = de.T.reshape(d.res, d.near, f)
        spread = mm(da1[...], r.tn[...])
        r.a_s[...] += spread[:, : d.length]
        r.a_k[b] = spread[:, d.length :]
        r.flush()

        @pl.when(last)
        def _():
            own, far, b0 = spread_nodes(
                d, r.a_s[...], [r.a_k[i] for i in range(d.blocks)], r.mw1[0], r.n_cat[...], r.msg, 0
            )
            r.dn_own[p] = own + r.dr1[...]
            r.dn_far[p] = far.astype(BF)
            message_small(d, r, b0)

            @pl.when(p == d.parts - 1)
            def _():
                f, at = d.feat, d.at_small
                r.msg[f : 2 * f] = r.a_w1[...].T
                r.msg[3 * f : 4 * f] = 0.5 * r.m_w2[:f]
                r.msg[at + 1 : at + 2] = r.m_w2[f : f + 1]

    return ph.call("enc_message_back", body)


def reduce_grads(d, enc_msg, enc_upd, dec_msg, dec_upd, dn_far):
    devices = d.devices
    bits = devices.bit_length() - 1
    unit = 16 * devices
    feat = d.feat
    need = -(-(d.msg_rows + d.upd_rows) // unit)
    shares = [need // 3 + (1 if need % 3 > i else 0) for i in range(3)]
    groups = [unit * share for share in shares if share]
    rows = sum(groups)
    bases = [sum(groups[:i]) for i in range(len(groups))]
    across = -1
    dims = [across] + list(range(1, bits))
    turn = min(3, len(dims))
    orders = []
    for g in range(len(groups)):
        head = dims[:turn]
        head = head[g % turn :] + head[: g % turn]
        orders.append(([0] if bits else []) + head + dims[turn:])
    stages = len(orders[0])
    plans = []
    for g, order in enumerate(orders):
        size, both, plan = groups[g], True, []
        for dim in order:
            if dim == across:
                both = False
                plan.append((dim, size, False))
            else:
                size //= 2
                plan.append((dim, size, both))
        plans.append(plan)
    turns = len(groups) * stages

    def kernel(em, eu, dm, du, far, res, got, acc, gathered, *rest):
        buffers, (send, recv) = rest[: 2 * turns], rest[2 * turns :]
        section, me = lax.axis_index(AXIS_S), lax.axis_index(AXIS_D)

        def flag(bit):
            return lax.rem(me // (1 << bit), 2)

        def peer(dim):
            if dim == across:
                return other_section()
            return {AXIS_D: me + (1 - 2 * flag(dim)) * (1 << dim)}

        barrier = pltpu.get_barrier_semaphore()
        for dim in [across] + list(range(bits)):
            pl.semaphore_signal(barrier, inc=1, device_id=peer(dim), device_id_type=MESH)
        pl.semaphore_wait(barrier, bits + 1)

        def remote(src, dst, at, dim):
            return pltpu.make_async_remote_copy(
                src_ref=src, dst_ref=dst, send_sem=send.at[at], recv_sem=recv.at[at],
                device_id=peer(dim), device_id_type=MESH,
            )

        nodes = remote(far, got, 2 * turns, across)
        nodes.start()
        m, u = d.msg_rows, d.upd_rows
        for layer, (msg, upd) in enumerate(((em, eu), (dm, du))):
            acc[layer, :m] = msg[...]
            acc[layer, m : m + u] = upd[...]
            if rows > m + u:
                acc[layer, m + u :] = jnp.zeros((rows - m - u, feat), F32)

        def span(start, size):
            return pl.ds(pl.multiple_of(start, 16), size)

        starts = list(bases)
        for k in range(stages):
            jobs, spans = [], []
            for g, plan in enumerate(plans):
                dim, size, both = plan[k]
                at = g * stages + k
                out, into = buffers[2 * at], buffers[2 * at + 1]
                if dim == across:
                    keep = span(starts[g], size)
                    out[...] = acc[1 - section, keep, :].astype(BF)
                else:
                    side = flag(dim)
                    keep = span(starts[g] + side * size, size)
                    give = span(starts[g] + (1 - side) * size, size)
                    if both:
                        out[...] = acc[:, give, :].astype(BF)
                    else:
                        out[...] = acc[section, give, :].astype(BF)
                    starts[g] = starts[g] + side * size
                job = remote(out, into, at, dim)
                job.start()
                jobs.append(job)
                spans.append(keep)
            for g, plan in enumerate(plans):
                dim, size, both = plan[k]
                jobs[g].wait()
                into = buffers[2 * (g * stages + k) + 1]
                if both:
                    acc[:, spans[g], :] += into[...].astype(F32)
                else:
                    acc[section, spans[g], :] += into[...].astype(F32)
        sizes = [plan[-1][1] for plan in plans]
        for g in range(len(groups)):
            keep = span(starts[g], sizes[g])
            gathered[keep, :] = acc[section, keep, :].astype(BF)
        backs = [[step for step in reversed(plan) if step[0] != across] for plan in plans]
        for k in range(bits):
            jobs = []
            for g, back in enumerate(backs):
                dim, size, _ = back[k]
                part = gathered.at[span(starts[g], size), :]
                job = remote(part, part, turns + g * bits + k, dim)
                job.start()
                jobs.append(job)
                starts[g] = starts[g] - flag(dim) * size
            for job in jobs:
                job.wait()
        res[...] = gathered[...]
        nodes.wait()

    vm = pl.BlockSpec(memory_space=pltpu.VMEM)
    scratch = [pltpu.VMEM((2, rows, feat), F32), pltpu.VMEM((rows, feat), BF)]
    for plan in plans:
        for _, size, both in plan:
            scratch += [pltpu.VMEM((2, size, feat) if both else (size, feat), BF)] * 2
    scratch += [pltpu.SemaphoreType.DMA((2 * turns + 1,))] * 2
    return pl.pallas_call(
        kernel,
        in_specs=[vm] * 5,
        out_specs=[vm, pl.BlockSpec(memory_space=pl.ANY)],
        out_shape=[
            jax.ShapeDtypeStruct((rows, feat), BF),
            jax.ShapeDtypeStruct(dn_far.shape, BF),
        ],
        scratch_shapes=scratch,
        compiler_params=pltpu.CompilerParams(vmem_limit_bytes=58 << 20, collective_id=5, has_side_effects=True),
        name="reduce",
    )(enc_msg, enc_upd, dec_msg, dec_upd, dn_far)


def unpack(d, total, dn_own, dn_got, n_bias, n_gain):
    f = d.feat
    m = d.msg_rows
    shapes = [(1, 3 * f, f), (1, f, f), (1, f, f), (1, f, d.wide), (1, 1, d.wide), (1, d.wide, f)]
    shapes += [(1, 3 * f, f), (1, f, f), (1, f, f), (n_bias, 1, f), (n_gain, 1, f)]

    def kernel(t, own, got, node, mw1, mw2, mw3, inner, inner_b, outer, uw1, uw2, uw3, bias, gain):
        node[...] = (own[...] + got[...].astype(F32)).astype(BF)
        for ref, at in ((mw1, 0), (mw2, 3 * f), (mw3, 4 * f), (outer, d.at_outer)):
            ref[0] = t[at : at + ref.shape[1], :].astype(F32)
        for ref, at in ((uw1, m), (uw2, m + 3 * f), (uw3, m + 4 * f)):
            ref[0] = t[at : at + ref.shape[1], :].astype(F32)
        inner[0] = t[d.at_inner : d.at_inner + d.wide, :].astype(F32).T
        small = t[d.at_small : d.at_small + SMALL, :].astype(F32)
        other = t[m + 5 * f : m + 5 * f + SMALL, :].astype(F32)
        both = small + other
        for i in range(n_bias):
            bias[i] = both[i : i + 1]
        for i in range(n_gain):
            gain[i] = both[n_bias + i : n_bias + i + 1]
        for i in range(d.wide // f):
            inner_b[0, :, i * f : (i + 1) * f] = small[16 + i : 17 + i]

    vm = pl.BlockSpec(memory_space=pltpu.VMEM)
    out = [jax.ShapeDtypeStruct(dn_own.shape, BF)] + [jax.ShapeDtypeStruct(s, F32) for s in shapes]
    return pl.pallas_call(kernel, in_specs=[vm] * 3, out_specs=[vm] * len(out), out_shape=out, name="unpack")(
        total, dn_own, dn_got
    )


def per_device(
    node_input,
    edge_input,
    neighbors,
    residue_mask,
    decode_order,
    node_cotangent,
    edge_cotangent,
    message_w1,
    message_w2,
    message_w3,
    inner_w,
    inner_bias,
    outer_w,
    update_w1,
    update_w2,
    update_w3,
    biases,
    norm_gains,
):
    parts, half, near, feat = edge_input.shape
    length = neighbors.shape[1]
    wide = inner_w.shape[2]
    res = BLOCK_RES
    rows = res * near
    blocks = half // res
    at_outer = 5 * feat
    at_inner = at_outer + wide
    at_small = at_inner + wide
    d = types.SimpleNamespace(
        parts=parts, half=half, near=near, feat=feat, length=length, wide=wide, res=res, rows=rows, blocks=blocks,
        at_outer=at_outer, at_inner=at_inner, at_small=at_small, msg_rows=at_small + SMALL,
        upd_rows=5 * feat + SMALL, devices=lax.axis_size(AXIS_D),
    )
    weights = dict(
        mw1=message_w1[0], mw2=message_w2[0], mw3=message_w3[0], inner=inner_w[0], inner_b=inner_bias, outer=outer_w[0],
        uw1=update_w1[0], uw2=update_w2[0], uw3=update_w3[0],
        bias=biases.transpose(1, 0, 2), gain=norm_gains.transpose(1, 0, 2),
    )
    sums = np.zeros((128, rows), np.float32)
    sums[np.arange(rows) // near, np.arange(rows)] = 1.0
    pick = (np.arange(rows)[None, :] % near == np.arange(near)[:, None]).astype(np.float32)
    consts = types.SimpleNamespace(sums=jnp.asarray(sums, BF), pick=jnp.asarray(pick, BF))
    fa = encoder_message(
        d, edge_input, node_input, neighbors.transpose(0, 2, 1), residue_mask, decode_order, weights, consts
    )
    consts.idx, consts.mask = fa.idx, fa.mask
    st = types.SimpleNamespace(**{n: getattr(fa, W_OUT + n) for n in weights})
    fb = encoder_update(d, edge_input, st, fa, consts)
    fd = decoder_update(d, st, fb, edge_cotangent, consts)
    fe = middle_backward(d, edge_input, st, fa, fb, fd, node_cotangent, consts)
    ff = encoder_message_back(d, edge_input, st, fa, fe, node_input, fa.nodes_got, consts)
    total, got = reduce_grads(d, ff.msg, fe.upd, fe.msg, fd.upd, ff.dn_far)
    node_grad, mw1, mw2, mw3, inner, inner_b, outer, uw1, uw2, uw3, bias, gain = unpack(
        d, total, ff.dn_own, got, biases.shape[1], norm_gains.shape[1]
    )
    return (
        fd.nodes, fd.decoded, node_grad, ff.edge_grad, mw1, mw2, mw3, inner, inner_b[:, 0], outer,
        uw1, uw2, uw3, bias.transpose(1, 0, 2), gain.transpose(1, 0, 2),
    )


def solution(mesh):
    def split(*axes):
        return P(*axes)

    by_part = split(AXIS_D)
    by_half = split(AXIS_D, AXIS_S)
    by_layer = split(AXIS_S)
    in_specs = (by_half, by_half, by_part, by_part, by_part, by_half, by_half) + (by_layer,) * 11
    out_specs = (by_half,) * 4 + (by_layer,) * 11
    return jax.shard_map(per_device, mesh=mesh, in_specs=in_specs, out_specs=out_specs, check_vma=False)
```

```python
import types

import jax
import jax.numpy as jnp
import numpy as np
from jax import lax
from jax.experimental import pallas as pl
from jax.experimental.pallas import tpu as pltpu
from jax.sharding import PartitionSpec as P

BF = jnp.bfloat16
F32 = jnp.float32
C1 = 0.7978845608
C2 = C1 * 0.044715
EPS = 1e-5
BLOCK_RES = 64
EXTRA = 16
SMALL = 32
MESH = pl.DeviceIdType.MESH


def mm(a, b, ca=1, cb=0):
    return lax.dot_general(a, b, (((ca,), (cb,)), ((), ())), preferred_element_type=F32)


def mm_exact(a, b, ca=1, cb=0):
    return lax.dot_general(
        a, b, (((ca,), (cb,)), ((), ())), precision=lax.Precision.HIGHEST, preferred_element_type=F32
    )


def gelu_pair(x):
    x = x.astype(BF)
    w = x * x * BF(C2)
    h = jnp.tanh(x * (w + BF(C1))) + BF(1.0)
    g = x * h
    d = h + g * (BF(2.0) - h) * (w * BF(3.0) + BF(C1))
    return g, d


def gelu_pair_wide(x):
    x2 = x * x
    h = 0.5 * jnp.tanh(x * (x2 * C2 + C1)) + 0.5
    g = x * h
    d = h + (g * (1.0 - h)) * (x2 * (6 * C2) + 2 * C1)
    return g, d


def lane_sum(x):
    total = x[:, :128]
    for at in range(128, x.shape[1], 128):
        total = total + x[:, at : at + 128]
    return total


def to_row(acc):
    return mm_exact(jnp.ones((8, acc.shape[1]), F32), acc, 1, 1)[0:1]


def norm_rows(r):
    c = r - jnp.mean(r, axis=-1, keepdims=True)
    rs = lax.rsqrt(jnp.mean(c * c, axis=-1, keepdims=True) + EPS)
    return c * rs, rs


def norm_back_rows(dxh, xh, rs):
    m1 = jnp.mean(dxh, axis=-1, keepdims=True)
    m2 = jnp.mean(dxh * xh, axis=-1, keepdims=True)
    return (dxh - m1 - xh * m2) * rs


def norm_back(dy, xh, rs, gain_col):
    dxh = dy * gain_col
    m1 = jnp.mean(dxh, axis=0, keepdims=True)
    m2 = jnp.mean(dxh * xh, axis=0, keepdims=True)
    return (dxh - m1 - xh * m2) * rs


class Phase:
    def __init__(self, dims, collective_id=None):
        self.d = dims
        self.collective_id = collective_id
        self.ins, self.outs, self.temps, self.kinds, self.wholes = [], [], [], {}, {}

    def whole_spec(self, shape):
        rank = len(shape)
        return pl.BlockSpec(tuple(shape), lambda p, b: (0,) * rank)

    def whole(self, **arrays):
        self.raw(**arrays)
        self.wholes.update({n: pltpu.VMEM(a.shape, a.dtype) for n, a in arrays.items()})

    def raw(self, **arrays):
        self.ins += [(n, a, pl.BlockSpec(memory_space=pl.ANY)) for n, a in arrays.items()]

    def stream(self, **arrays):
        self.raw(**arrays)
        self.kinds.update({n: (False, False, a.shape[2:], a.dtype) for n, a in arrays.items()})

    def stream_top(self, rows, **arrays):
        self.raw(**arrays)
        self.kinds.update({n: (False, False, (rows,) + a.shape[3:], a.dtype) for n, a in arrays.items()})

    def edges(self, **arrays):
        self.raw(**arrays)
        block = (self.d.res, self.d.near, self.d.feat)
        self.kinds.update({n: (False, True, block, a.dtype) for n, a in arrays.items()})

    def out_whole(self, dtype, **shapes):
        self.outs += [(n, jax.ShapeDtypeStruct(s, dtype), self.whole_spec(s)) for n, s in shapes.items()]

    def out_raw(self, dtype, **shapes):
        spec = pl.BlockSpec(memory_space=pl.ANY)
        self.outs += [(n, jax.ShapeDtypeStruct(s, dtype), spec) for n, s in shapes.items()]

    def out_stream(self, dtype, **shapes):
        self.out_raw(dtype, **shapes)
        self.kinds.update({n: (True, False, s[2:], dtype) for n, s in shapes.items()})

    def out_edges(self, **shapes):
        self.out_raw(BF, **shapes)
        block = (self.d.res, self.d.near, self.d.feat)
        self.kinds.update({n: (True, True, block, BF) for n in shapes})

    def temp(self, dtype, **shapes):
        self.temps += [(n, pltpu.VMEM(s, dtype)) for n, s in shapes.items()]

    def sems(self, **counts):
        self.temps += [(n, pltpu.SemaphoreType.DMA((c,))) for n, c in counts.items()]

    def call(self, name, body):
        d = self.d
        names = [n for n, _, _ in self.ins] + [n for n, _, _ in self.outs] + [n for n, _ in self.temps]
        steps = d.parts * d.blocks
        buffers = [pltpu.VMEM((2,) + tuple(block), dtype) for _, _, block, dtype in self.kinds.values()]
        count = len(self.kinds)

        def kernel(*refs):
            refs, rest = refs[: len(names)], refs[len(names) :]
            slots, sems, kept = rest[:count], rest[count : 2 * count], rest[2 * count : -1]
            plain = dict(zip(names, refs))
            step = pl.program_id(0) * d.blocks + pl.program_id(1)
            now = lax.rem(step, 2)

            def copy(i, n, at, slot):
                out, edges, block, _ = self.kinds[n]
                p, b = at // d.blocks, lax.rem(at, d.blocks)
                if edges:
                    far = plain[n].at[p, pl.ds(pl.multiple_of(b * d.res, d.res), d.res)]
                elif block[0] < plain[n].shape[2]:
                    far = plain[n].at[p, b, pl.ds(0, block[0])]
                else:
                    far = plain[n].at[p, b]
                near = slots[i].at[slot]
                return pltpu.make_async_copy(*((near, far) if out else (far, near)), sems[i].at[slot])

            into = [(i, n) for i, n in enumerate(self.kinds) if not self.kinds[n][0]]
            outof = [(i, n) for i, n in enumerate(self.kinds) if self.kinds[n][0]]

            def loads():
                return [
                    pltpu.make_async_copy(plain[n], kept[i], rest[-1].at[i]) for i, n in enumerate(self.wholes)
                ]

            def load():
                for item in loads():
                    item.wait()

            @pl.when(step == 0)
            def _():
                for item in loads():
                    item.start()
                for i, n in into:
                    copy(i, n, step, now).start()

            @pl.when(step + 1 < steps)
            def _():
                for i, n in into:
                    copy(i, n, step + 1, 1 - now).start()

            @pl.when(step >= 2)
            def _():
                for i, n in outof:
                    copy(i, n, step - 2, now).wait()

            def ready():
                for i, n in into:
                    copy(i, n, step, now).wait()

            def flush():
                for i, n in outof:
                    copy(i, n, step, now).start()

            plain_or_slot = dict(plain, ready=ready, flush=flush, load=load)
            plain_or_slot.update(zip(self.wholes, kept))
            plain_or_slot.update({n: slots[i].at[now] for i, n in enumerate(self.kinds)})
            body(types.SimpleNamespace(**plain_or_slot))

            @pl.when(step == steps - 1)
            def _():
                for i, n in outof:
                    if steps > 1:
                        copy(i, n, step - 1, 1 - now).wait()
                    copy(i, n, step, now).wait()

        results = pl.pallas_call(
            kernel,
            grid=(d.parts, d.blocks),
            in_specs=[s for _, _, s in self.ins],
            out_specs=[s for _, _, s in self.outs],
            out_shape=[s for _, s, _ in self.outs],
            scratch_shapes=[s for _, s in self.temps] + buffers
            + [pltpu.SemaphoreType.DMA((2,))] * count
            + list(self.wholes.values())
            + [pltpu.SemaphoreType.DMA((len(self.wholes),))],
            compiler_params=pltpu.CompilerParams(
                dimension_semantics=(pltpu.ARBITRARY,) * 2,
                vmem_limit_bytes=60 << 20,
                collective_id=self.collective_id,
                has_side_effects=self.collective_id is not None,
            ),
            name=name,
        )(*[a for _, a, _ in self.ins])
        return types.SimpleNamespace(**dict(zip([n for n, _, _ in self.outs], results)))


def other_section():
    return {AXIS_S: 1 - lax.axis_index(AXIS_S)}


AXIS_S = "section"
AXIS_D = "dp"


def greet_partner():
    barrier = pltpu.get_barrier_semaphore()
    pl.semaphore_signal(barrier, inc=1, device_id=other_section(), device_id_type=MESH)
    pl.semaphore_wait(barrier, 1)


def to_partner(src, dst, send, recv):
    return pltpu.make_async_remote_copy(
        src_ref=src, dst_ref=dst, send_sem=send, recv_sem=recv, device_id=other_section(), device_id_type=MESH
    )


def put_one_hot(d, ref, at, idx):
    idx = idx.astype(jnp.int16)
    place = lax.broadcasted_iota(jnp.int16, (d.length, d.rows), 0)
    ref[at : at + d.length, :] = jnp.where(place == idx, jnp.ones((), BF), jnp.zeros((), BF))


def put_one_hot_rows(d, ref, idx):
    centre = d.length // 2
    idx = jnp.broadcast_to((idx - centre).astype(F32).astype(BF), (128, d.rows)).T
    place = lax.broadcasted_iota(jnp.int32, (d.rows, 128), 1)
    for at in range(0, d.length, 128):
        there = (place + (at - centre)).astype(F32).astype(BF)
        ref[:, at : at + 128] = jnp.where(idx == there, jnp.ones((), BF), jnp.zeros((), BF))


def weight_args(w, *names):
    return {n: getattr(w, n) for n in names}


def load_cols(r, layer, aux, cols):
    n_bias, n_gain = r.bias.shape[1], r.gain.shape[1]
    aux[...] = jnp.zeros(aux.shape, F32)
    for i in range(n_bias):
        aux[i : i + 1] = r.bias[layer, i]
    for i in range(n_gain):
        aux[n_bias + i : n_bias + i + 1] = r.gain[layer, i]
    cols[...] = aux[...].T


def put_table(d, lhs, at, left, n_cat, w1):
    lhs[at : at + d.feat, left : left + d.length] = mm(w1[2 * d.feat :, :].T, n_cat[...], 1, 1).astype(BF)


def put_own(d, lhs, at, left, w1, n_blk, bias_col):
    own = mm(w1[0 : d.feat, :].T, n_blk, 1, 1) + bias_col
    lhs[at : at + d.feat, left + d.length :] = own.astype(BF)


def message_part(a1, w2t, b2, att, kept):
    g1, d1 = gelu_pair(a1)
    a2 = mm(w2t, g1) + b2
    g2, d2 = gelu_pair(a2)
    attb = att.astype(BF)
    feat, rows = g2.shape
    kept[:feat] = g2 * attb
    kept[feat:] = jnp.broadcast_to(attb, (16, rows))
    return g1, d1, d2 * attb


def add_node_outs(ph, d):
    ph.out_whole(BF, node_out=(d.parts, d.half, d.feat))
    shape = (d.parts, d.half, d.feat)
    ph.out_whole(F32, r1=shape, ip=(d.parts, d.half, d.wide), r2=shape, big=shape, cnt=shape)


def node_step(d, r, p, b):
    sums = mm(r.rt[: d.res], r.kept[...], 1, 1)
    at = pl.ds(pl.multiple_of(b * d.res, d.res), d.res)
    r.big[p, at, :] = sums[:, : d.feat] * 0.5
    r.cnt[p, at, :] = jnp.broadcast_to(sums[:, d.feat : d.feat + 1], (d.res, d.feat))


def node_forward(r, p, n_own, layer, aux):
    big = r.big[p]
    hi = big.astype(BF)
    lo = (big - hi.astype(F32)).astype(BF)
    w3 = r.mw3[layer]
    upd = (mm(hi, w3) + mm(lo, w3) + r.cnt[p] * aux[2:3]) / 30.0
    r1 = n_own.astype(F32) + upd
    xh1, _ = norm_rows(r1)
    normed = xh1 * aux[10:11] + aux[7:8]
    ip = mm(normed.astype(BF), r.inner[layer]) + r.inner_b[layer]
    hid = gelu_pair_wide(ip)[0].astype(BF)
    r2 = normed + (mm(hid, r.outer[layer]) + aux[3:4])
    xh2, _ = norm_rows(r2)
    out = ((xh2 * aux[11:12] + aux[8:9]) * r.mask[p]).astype(BF)
    r.node_out[p] = out
    r.r1[p] = r1
    r.ip[p] = ip
    r.r2[p] = r2
    return out


def node_backward(d, r, p, layer, aux, dn):
    def rows_of(ref):
        return ref[...].reshape(-1, ref.shape[2]) if p is None else ref[p]

    r1, ip, r2, big, cnt = rows_of(r.r1), rows_of(r.ip), rows_of(r.r2), rows_of(r.big), rows_of(r.cnt)
    xh1, rs1 = norm_rows(r1)
    normed = xh1 * aux[10:11] + aux[7:8]
    xh2, rs2 = norm_rows(r2)
    dy2 = dn * rows_of(r.mask)
    dr2 = norm_back_rows(dy2 * aux[11:12], xh2, rs2)
    low_outer = dr2.astype(BF)
    hid, slope = gelu_pair_wide(ip)
    dip = mm(low_outer, r.outer[layer], 1, 1) * slope
    low_inner = dip.astype(BF)
    at = d.at_outer
    r.msg[at : at + d.wide] += mm(hid.astype(BF), low_outer, 0, 0)
    at = d.at_inner
    r.msg[at : at + d.wide] += mm(low_inner, normed.astype(BF), 0, 0)
    dnormed = dr2 + mm(low_inner, r.inner[layer], 1, 1)
    dr1 = norm_back_rows(dnormed * aux[10:11], xh1, rs1)
    du = dr1 / 30.0
    dub = du.astype(BF)
    r.msg[4 * d.feat : 5 * d.feat] += mm(big.astype(BF), dub, 0, 0)
    dib = jnp.sum(dip, axis=0, keepdims=True)
    rows = {
        2: jnp.sum(cnt * du, axis=0, keepdims=True),
        3: jnp.sum(dr2, axis=0, keepdims=True),
        7: jnp.sum(dnormed, axis=0, keepdims=True),
        8: jnp.sum(dy2, axis=0, keepdims=True),
        10: jnp.sum(dnormed * xh1, axis=0, keepdims=True),
        11: jnp.sum(dy2 * xh2, axis=0, keepdims=True),
    }
    for i in range(d.wide // d.feat):
        rows[16 + i] = dib[:, i * d.feat : (i + 1) * d.feat]
    for row, value in rows.items():
        r.msg[d.at_small + row : d.at_small + row + 1] += value
    if p is None:
        r.dr1[...] = dr1.reshape(r.dr1.shape)
        r.dub[...] = dub.reshape(r.dub.shape)
    else:
        r.dr1[p] = dr1
        r.dub[p] = dub


def own_first(d, row):
    row = row.astype(F32)
    if row.shape[0] == 1:
        row = jnp.broadcast_to(row, (8, d.length))
    return jnp.where(lax.axis_index(AXIS_S) == 0, row, pltpu.roll(row, d.half, 1))


def put_positions(d, r):
    section = lax.axis_index(AXIS_S)
    centre = d.length // 2
    line = lax.broadcasted_iota(jnp.int32, (8, d.length), 0)
    for p in range(d.parts):
        live = own_first(d, r.live[p : p + 1, :])
        order = own_first(d, r.order[p : p + 1, :]) - centre
        code = jnp.where(live > 0.5, order, float(centre))
        r.codes[p, :8] = jnp.where(line == 0, live, jnp.where(line == 1, code, 0.0)).astype(BF)
        r.codes[p, 8:] = jnp.zeros((EXTRA - 8, d.length), BF)
        ids = own_first(d, r.near[p]) - float(d.half) * section.astype(F32)
        ids = jnp.where(ids < 0.0, ids + float(d.length), ids) - float(centre)
        r.mask[p] = jnp.broadcast_to(live[0:1], (d.feat, d.length)).T[: d.half]
        for b in range(d.blocks):
            own = pltpu.roll(order, (d.length - b * d.res) % d.length, 1) if b else order
            r.owns[p, b, :8] = jnp.where(line == 1, -own, 0.0)[:, : d.res].astype(BF)
            r.owns[p, b, 8:] = jnp.zeros((EXTRA - 8, d.res), BF)
            block = pltpu.roll(ids, (d.length - b * d.res) % d.length, 1) if b else ids
            spread = mm(block[:, : d.res].astype(BF), r.rt[: d.res])
            row = jnp.sum(spread * r.pick[...].astype(F32), axis=0, keepdims=True)
            r.idx[p, b] = row.astype(jnp.int32) + centre


def encoder_message(d, edge_input, node_input, neighbors, residue_mask, decode_order, weights, consts):
    ph = Phase(d, 2)
    ph.raw(n_far=node_input)
    ph.whole(n_own=node_input, rt=consts.sums, pick=consts.pick, near=neighbors, live=residue_mask, order=decode_order)
    ph.out_whole(jnp.int32, idx=(d.parts, d.blocks, 1, d.rows))
    ph.out_whole(F32, mask=(d.parts, d.half, d.feat))
    ph.temp(BF, codes=(d.parts, EXTRA, d.length), owns=(d.parts, d.blocks, EXTRA, d.res))
    ph.edges(edge=edge_input)
    names = tuple(weights)
    own = {W_IN + n: a for n, a in weights.items()}
    ph.raw(**own)
    act = (d.parts, d.blocks, d.feat, d.rows)
    ph.out_stream(BF, g1=with_ones(d), d1=act, d2=act)
    ph.out_whole(F32, att=(d.parts, d.blocks, 1, d.rows))
    add_node_outs(ph, d)
    ph.out_raw(BF, got=(d.half, d.feat), nodes_got=node_input.shape)
    for n, a in weights.items():
        ph.out_raw(a.dtype, **{W_OUT + n: (2,) + a.shape})
        ph.temp(a.dtype, **{n: (2,) + a.shape})
    sq = (d.feat, d.feat)
    wide = d.feat + d.length + d.res
    ph.temp(BF, n_cat=(d.length, d.feat), lhs=(d.feat + EXTRA, wide), w2t=sq, tt=(wide, d.rows))
    ph.temp(BF, leave=(d.half, d.feat), arrive=node_input.shape, kept=(d.feat + 16, d.rows))
    ph.temp(F32, aux=sq, cols=sq)
    count = len(names)
    ph.sems(send=count + 2, recv=count + 2, local=count, back=2 * count + 1)

    def body(r):
        p, b = pl.program_id(0), pl.program_id(1)
        first, last = b == 0, b == d.blocks - 1
        section = lax.axis_index(AXIS_S)
        job = to_partner(r.leave, r.got, r.send.at[count], r.recv.at[count])
        nodes = to_partner(r.n_far, r.arrive, r.send.at[count + 1], r.recv.at[count + 1])

        def swaps(group):
            out = []
            for n in group:
                i = names.index(n)
                dst = getattr(r, n).at[section]
                out.append(to_partner(getattr(r, W_IN + n), dst, r.send.at[i], r.recv.at[i]))
            return out

        def own_copies():
            return [
                pltpu.make_async_copy(getattr(r, W_IN + n), getattr(r, n).at[section], r.local.at[i])
                for i, n in enumerate(names)
            ]

        def returns(group):
            out = [pltpu.make_async_copy(r.arrive, r.nodes_got, r.back.at[2 * count])] if group == GROUP_ONE else []
            for n in group:
                i = names.index(n)
                src, dst = getattr(r, n), getattr(r, W_OUT + n)
                for layer in range(2):
                    sem = r.back.at[2 * i + layer]
                    out.append(pltpu.make_async_copy(src.at[layer], dst.at[layer], sem))
            return out

        begin = first & (p == 0)
        middle = (p == 1) & (b == 1)
        at_end = last & (p == d.parts - 1)

        @pl.when(begin)
        def _():
            greet_partner()
            nodes.start()
            for item in swaps(GROUP_ONE) + own_copies():
                item.start()
            r.load()
            r.tt[d.feat + d.length :, :] = r.rt[: d.res]
            put_positions(d, r)
            nodes.wait()
            for item in swaps(GROUP_ONE) + own_copies():
                item.wait()
            for item in swaps(GROUP_TWO):
                item.start()
            r.lhs[: d.feat, : d.feat] = r.mw1[0, d.feat : 2 * d.feat, :].T
            r.lhs[d.feat :, : d.feat] = jnp.zeros((EXTRA, d.feat), BF)
            r.w2t[...] = half_of(r.mw2[0]).T
            load_cols(r, 0, r.aux, r.cols)

        @pl.when(first)
        def _():
            r.n_cat[: d.half] = r.n_own[p]
            r.n_cat[d.half :] = r.arrive[p]
            put_table(d, r.lhs, 0, d.feat, r.n_cat, r.mw1.at[0])

        n_blk = r.n_own[p, pl.ds(pl.multiple_of(b * d.res, d.res), d.res), :]
        r.ready()
        put_one_hot(d, r.tt, d.feat, r.idx[p, b])
        r.tt[: d.feat, :] = r.edge[...].reshape(d.rows, d.feat).T
        put_own(d, r.lhs, 0, d.feat, r.mw1.at[0], n_blk, r.cols[:, 0:1])
        r.lhs[d.feat :, d.feat : d.feat + d.length] = r.codes[p]
        r.lhs[d.feat :, d.feat + d.length :] = r.owns[p, b]
        out = mm(r.lhs[...], r.tt[...])
        att = out[d.feat : d.feat + 1]
        r.att[p, b] = jnp.where(out[d.feat + 1 : d.feat + 2] < 0.0, 1.0, 0.0)
        g1, r.d1[...], r.d2[...] = message_part(out[: d.feat], r.w2t[...], r.cols[:, 1:2], att, r.kept)
        put_ones(r.g1, g1)
        node_step(d, r, p, b)
        r.flush()

        @pl.when(middle)
        def _():
            for item in swaps(GROUP_TWO):
                item.wait()
            for item in swaps(GROUP_THREE) + returns(GROUP_ONE) + returns(GROUP_TWO):
                item.start()
            r.leave[...] = node_forward(r, 0, r.n_own[0], 0, r.aux[...])
            job.start()

        @pl.when(at_end)
        def _():
            for item in swaps(GROUP_THREE):
                item.wait()
            for item in returns(GROUP_THREE):
                item.start()
            node_forward(r, d.parts - 1, r.n_own[d.parts - 1], 0, r.aux[...])
            for item in returns(GROUP_ONE) + returns(GROUP_TWO) + returns(GROUP_THREE):
                item.wait()
            job.wait()

    return ph.call("enc_message", body)


W_IN, W_OUT = "i_", "o_"
GROUP_ONE = ("mw1", "mw2", "bias", "gain")
GROUP_TWO = ("mw3", "inner", "inner_b", "outer")
GROUP_THREE = ("uw1", "uw2", "uw3")
NODE_W = ("mw3", "inner", "inner_b", "outer", "bias", "gain")
MSG_W = ("mw1", "mw2")
UPD_W = ("uw1", "uw2", "uw3")


def with_ones(d):
    return (d.parts, d.blocks, d.feat + 16, d.rows)


def put_ones(ref, g):
    feat, rows = g.shape
    ref[:feat] = g
    ref[feat:] = jnp.ones((16, rows), BF)


def half_of(w):
    return w * BF(0.5)


def update_forward(d, a1, w2t, w3c, b5, b6c, pair, cols):
    f = d.feat
    g1, d1 = gelu_pair(a1)
    a2 = mm(w2t, g1) + b5
    g2, d2 = gelu_pair(a2)
    pair[f : 2 * f] = g2
    cent = mm(w3c[...], pair[: 2 * f]) + b6c
    var = jnp.mean(cent * cent, axis=0, keepdims=True)
    rs = lax.rsqrt(var + EPS)
    xh = cent.astype(BF) * rs.astype(BF)
    y = xh * cols[:, 12:13].astype(BF) + cols[:, 9:10].astype(BF)
    return g1, d1, g2, d2, xh, rs, y


def centre_weights(w3, cols, w3c, b6c):
    feat = w3.shape[0]
    eye = lax.broadcasted_iota(jnp.int32, w3.shape, 0) == lax.broadcasted_iota(jnp.int32, w3.shape, 1)
    w3f = w3.astype(F32)
    w3c[:, feat:] = (0.5 * (w3f - jnp.mean(w3f, axis=1, keepdims=True))).T.astype(BF)
    w3c[:, :feat] = (eye.astype(F32) - 1.0 / feat).astype(BF)
    b6 = cols[:, 6:7]
    b6c[...] = jnp.broadcast_to(b6 - jnp.mean(b6, axis=0, keepdims=True), b6c.shape)


def encoder_update(d, edge_input, st, fa, consts):
    ph = Phase(d, 3)
    ph.raw(n_far=fa.node_out)
    ph.whole(n_own=fa.node_out, got_a=fa.got, idx=consts.idx, rt=consts.sums, mask=consts.mask, att=fa.att)
    ph.edges(edge=edge_input)
    ph.whole(**weight_args(st, *NODE_W, *MSG_W, *UPD_W))
    act = (d.parts, d.blocks, d.feat, d.rows)
    two = (d.parts, d.blocks, 2 * d.feat + 16, d.rows)
    ph.out_stream(BF, ugs=two, ud1=act, ud2=act, uxh=act, e2g=two, d1=act, d2=act)
    ph.out_whole(F32, urs=(d.parts, d.blocks, 1, d.rows))
    add_node_outs(ph, d)
    ph.out_whole(BF, got_in=(d.half, d.feat))
    ph.out_raw(BF, got=(d.parts, d.half, d.feat))
    sq = (d.feat, d.feat)
    wide = d.feat + d.length + d.res
    ph.temp(BF, n_cat=(d.length, d.feat), lhs=(2 * d.feat, wide), tt=(wide, d.rows))
    ph.temp(BF, uw2t=sq, mw1bt=sq, mw2t=sq, w3c=(d.feat, 2 * d.feat), pair=(2 * d.feat, d.rows))
    ph.temp(BF, kept=(d.feat + 16, d.rows), leave=(d.parts, d.half, d.feat), arrive=(d.half, d.feat))
    ph.temp(F32, w3c_b=sq, e_aux=sq, e_cols=sq, d_aux=sq, d_cols=sq)
    ph.sems(send=d.parts + 1, recv=d.parts + 1)

    def body(r):
        p, b = pl.program_id(0), pl.program_id(1)
        first, last = b == 0, b == d.blocks - 1
        early = to_partner(r.n_far.at[d.parts - 1], r.arrive, r.send.at[d.parts], r.recv.at[d.parts])
        jobs = [to_partner(r.leave.at[i], r.got.at[i], r.send.at[i], r.recv.at[i]) for i in range(d.parts)]

        @pl.when(first & (p == 0))
        def _():
            greet_partner()
            early.start()
            r.load()
            r.tt[d.feat + d.length :, :] = r.rt[: d.res]
            r.lhs[: d.feat, : d.feat] = r.uw1[0, d.feat : 2 * d.feat, :].T
            r.lhs[d.feat :, : d.feat] = jnp.zeros((d.feat, d.feat), BF)
            r.uw2t[...] = half_of(r.uw2[0]).T
            r.mw1bt[...] = r.mw1[1, d.feat : 2 * d.feat, :].T
            r.mw2t[...] = half_of(r.mw2[1]).T
            load_cols(r, 0, r.e_aux, r.e_cols)
            load_cols(r, 1, r.d_aux, r.d_cols)
            centre_weights(r.uw3[0], r.e_cols[...], r.w3c, r.w3c_b)
            r.n_cat[d.half :] = r.got_a[...]

        @pl.when(first & (p == 1))
        def _():
            early.wait()
            r.n_cat[d.half :] = r.arrive[...]
            r.got_in[...] = r.arrive[...]

        @pl.when(first)
        def _():
            r.n_cat[: d.half] = r.n_own[p]
            put_table(d, r.lhs, 0, d.feat, r.n_cat, r.uw1.at[0])
            put_table(d, r.lhs, d.feat, d.feat, r.n_cat, r.mw1.at[1])

        r.ready()
        n_blk = r.n_own[p, pl.ds(pl.multiple_of(b * d.res, d.res), d.res), :]
        put_own(d, r.lhs, 0, d.feat, r.uw1.at[0], n_blk, r.e_cols[:, 4:5])
        put_own(d, r.lhs, d.feat, d.feat, r.mw1.at[1], n_blk, r.d_cols[:, 0:1])
        put_one_hot(d, r.tt, d.feat, r.idx[p, b])
        edge_t = r.edge[...].reshape(d.rows, d.feat).T
        r.tt[: d.feat, :] = edge_t
        r.pair[: d.feat] = edge_t
        out = mm(r.lhs[...], r.tt[...])
        g1, d1, g2, d2, xh, rs, e2 = update_forward(
            d, out[: d.feat], r.uw2t[...], r.w3c, r.e_cols[:, 5:6], r.w3c_b[:, 0:1], r.pair, r.e_cols
        )
        f = d.feat
        r.ugs[:f] = g2
        put_ones(r.ugs.at[f:], g1)
        r.ud1[...], r.ud2[...], r.uxh[...], r.urs[p, b], r.e2g[:f] = d1, d2, xh, rs, e2
        att = r.att[p, b]
        a1 = out[d.feat :] + mm(r.mw1bt[...], e2)
        g1, r.d1[...], r.d2[...] = message_part(a1, r.mw2t[...], r.d_cols[:, 1:2], att, r.kept)
        put_ones(r.e2g.at[f:], g1)
        node_step(d, r, p, b)
        r.flush()

        @pl.when(last)
        def _():
            r.leave[p] = node_forward(r, p, r.n_own[p], 1, r.d_aux[...])
            for i in range(d.parts):

                @pl.when(p == i)
                def _(i=i):
                    jobs[i].start()

            @pl.when(p == d.parts - 1)
            def _():
                for job in jobs:
                    job.wait()

    return ph.call("enc_update", body)


def spread_nodes(d, acc, sumk, w1, n_cat, grad, grad_at):
    s = acc.astype(BF)
    sk = jnp.concatenate([x[:, : d.res] for x in sumk], axis=1)
    skb = sk.astype(BF)
    far = mm(s, w1[2 * d.feat :].T, 0, 0)
    own = mm(skb, w1[: d.feat].T, 0, 0)
    grad[grad_at + 2 * d.feat : grad_at + 3 * d.feat, :] += mm(n_cat, s, 0, 1)
    grad[grad_at : grad_at + d.feat, :] += mm(n_cat[: d.half], skb, 0, 1)
    return own + far[: d.half], far[d.half :], to_row(sk)


def lane_total(x):
    size = x.shape[1] // 4
    x = (x[:, :size] + x[:, size : 2 * size]) + (x[:, 2 * size : 3 * size] + x[:, 3 * size :])
    return lane_sum(x.astype(F32))


def norm_backward(d, r, dy, xh, rs, gain_mat):
    r.a_b9[...] += lane_total(dy)
    r.a_g2[...] += lane_total(dy * xh)
    z = mm(gain_mat, dy).astype(BF)
    m2 = jnp.mean((z * xh).astype(F32), axis=0, keepdims=True)
    return (z - xh * m2.astype(BF)) * rs.astype(BF)


def gain_matrix(cols):
    feat = cols.shape[0]
    shape = (feat, feat)
    eye = lax.broadcasted_iota(jnp.int32, shape, 0) == lax.broadcasted_iota(jnp.int32, shape, 1)
    scaled = jnp.where(eye, jnp.broadcast_to(cols[:, 12:13], shape), 0.0)
    return (scaled - jnp.mean(scaled, axis=0, keepdims=True)).astype(BF)


def update_backward(d, r, dr3, gs, d1, d2, w2, w3, low, da1):
    f = d.feat
    low[:f] = dr3
    low[f:] = mm(w3, dr3).astype(BF) * d2
    r.a_w23[...] += mm(gs, low[...], 1, 1)
    da1[...] = mm(w2, low[f:]).astype(BF) * d1


def update_small(d, r, b4):
    f = d.feat
    at = 5 * f
    r.upd[at + 4 : at + 5] += b4

    @pl.when(pl.program_id(0) == d.parts - 1)
    def _():
        r.upd[3 * f : 4 * f] = 0.5 * r.a_w23[f : 2 * f, f:]
        r.upd[4 * f : 5 * f] = 0.5 * r.a_w23[:f, :f]
        r.upd[at + 5 : at + 6] = r.a_w23[2 * f : 2 * f + 1, f:]
        r.upd[at + 6 : at + 7] = r.a_w23[2 * f : 2 * f + 1, :f]
        r.upd[at + 9 : at + 10] = to_row(r.a_b9[...])
        r.upd[at + 12 : at + 13] = to_row(r.a_g2[...])


def zero(*refs):
    for ref in refs:
        ref[...] = jnp.zeros(ref.shape, ref.dtype)


def decoder_update(d, st, fb, cot, consts):
    ph = Phase(d)
    ph.whole(n_own=fb.node_out, n_got=fb.got, idx=consts.idx, rt=consts.sums)
    ph.stream_top(d.feat, e2=fb.e2g)
    ph.edges(cot=cot)
    ph.whole(**weight_args(st, *UPD_W, *AUX_W))
    ph.out_edges(decoded=cot.shape)
    ph.out_stream(BF, part=(d.parts, d.blocks, d.feat, d.rows))
    ph.out_whole(F32, upd=(d.upd_rows, d.feat), dn_own=(d.parts, d.half, d.feat))
    ph.out_whole(BF, dn_far=(d.parts, d.half, d.feat), nodes=(d.parts, d.half, d.feat))
    sq = (d.feat, d.feat)
    wide = d.length + d.res
    ph.temp(BF, n_cat=(d.length, d.feat), lhs=(d.feat, wide), w1bt=sq, w2t=sq, w2h=sq, w3h=sq)
    ph.temp(BF, tt=(wide, d.rows), tn=(d.rows, d.length + 128), da1=(d.feat, d.rows))
    ph.temp(BF, w3c=(d.feat, 2 * d.feat), gain_mat=sq, pair=(3 * d.feat + 16, d.rows), low=(2 * d.feat, d.rows))
    ph.temp(F32, w3c_b=sq, aux=sq, cols=sq, a_w23=(2 * d.feat + 16, 2 * d.feat), a_b9=sq, a_g2=sq)
    ph.temp(F32, a_s=(d.feat, d.length), a_k=(d.blocks, d.feat, 128))

    def body(r):
        p, b = pl.program_id(0), pl.program_id(1)
        first, last = b == 0, b == d.blocks - 1

        @pl.when(first & (p == 0))
        def _():
            r.load()
            r.nodes[...] = r.n_own[...]
            r.w1bt[...] = r.uw1[1, d.feat : 2 * d.feat, :].T
            r.w2h[...] = half_of(r.uw2[1])
            r.w2t[...] = r.w2h[...].T
            r.w3h[...] = half_of(r.uw3[1])
            load_cols(r, 1, r.aux, r.cols)
            centre_weights(r.uw3[1], r.cols[...], r.w3c, r.w3c_b)
            r.gain_mat[...] = gain_matrix(r.cols[...])
            zero(r.upd, r.a_w23, r.a_b9, r.a_g2)
            r.pair[3 * d.feat :] = jnp.ones((16, d.rows), BF)
            r.tt[d.length :, :] = r.rt[: d.res]
            r.tn[:, d.length :] = r.rt[...].T

        @pl.when(first)
        def _():
            r.n_cat[: d.half] = r.n_own[p]
            r.n_cat[d.half :] = r.n_got[p]
            put_table(d, r.lhs, 0, 0, r.n_cat, r.uw1.at[1])
            zero(r.a_s)

        r.ready()
        f = d.feat
        n_blk = r.n_own[p, pl.ds(pl.multiple_of(b * d.res, d.res), d.res), :]
        put_own(d, r.lhs, 0, 0, r.uw1.at[1], n_blk, r.cols[:, 4:5])
        idx = r.idx[p, b]
        put_one_hot(d, r.tt, 0, idx)
        put_one_hot_rows(d, r.tn, idx)
        e2 = r.e2[...]
        r.pair[:f] = e2
        a1 = mm(r.lhs[...], r.tt[...]) + mm(r.w1bt[...], e2)
        g1, d1, _, d2, xh, rs, y = update_forward(
            d, a1, r.w2t[...], r.w3c, r.cols[:, 5:6], r.w3c_b[:, 0:1], r.pair, r.cols
        )
        r.pair[2 * f : 3 * f] = g1
        r.decoded[...] = y.T.reshape(d.res, d.near, f)
        dy = r.cot[...].reshape(d.rows, f).T
        dr3 = norm_backward(d, r, dy, xh, rs, r.gain_mat[...])
        update_backward(d, r, dr3, r.pair[f:], d1, d2, r.w2h[...], r.w3h[...], r.low, r.da1)
        r.upd[f : 2 * f] += mm(e2, r.da1[...], 1, 1)
        r.part[...] = (mm(r.uw1[1, f : 2 * f, :], r.da1[...]) + dr3.astype(F32)).astype(BF)
        spread = mm(r.da1[...], r.tn[...])
        r.a_s[...] += spread[:, : d.length]
        r.a_k[b] = spread[:, d.length :]
        r.flush()

        @pl.when(last)
        def _():
            own, far, b4 = spread_nodes(
                d, r.a_s[...], [r.a_k[i] for i in range(d.blocks)], r.uw1[1], r.n_cat[...], r.upd, 0
            )
            r.dn_own[p] = own
            r.dn_far[p] = far.astype(BF)
            update_small(d, r, b4)

    return ph.call("dec_update", body)


AUX_W = ("bias", "gain")


def message_backward(d, r, b, layer, low):
    at = pl.ds(pl.multiple_of(b * d.res, d.res), d.res)
    v = (mm(r.mw3[layer], r.dub[pl.program_id(0), at, :], 1, 1) * 0.5).astype(BF)
    f = d.feat
    low[:f] = mm(v, r.rt[: d.res]).astype(BF) * r.d2[...]
    low[f:] = mm(r.mw2h[...], low[:f]).astype(BF) * r.d1[...]


def message_small(d, r, b0):
    r.msg[d.at_small : d.at_small + 1] += b0


def middle_backward(d, edge_input, st, fa, fb, fd, cot_n, consts):
    ph = Phase(d, 4)
    ph.raw(dn_far_in=fd.dn_far)
    ph.whole(cot_n=cot_n, dn_a=fd.dn_own, n_own=fa.node_out, got_a=fa.got, got_b=fb.got_in)
    ph.whole(mask=consts.mask, rt=consts.sums, r1=fb.r1, ip=fb.ip, r2=fb.r2, big=fb.big, cnt=fb.cnt)
    ph.whole(urs=fb.urs, idx=consts.idx)
    ph.stream(d2=fb.d2, d1=fb.d1, e2g=fb.e2g, dec_part=fd.part, uxh=fb.uxh, ugs=fb.ugs, ud2=fb.ud2, ud1=fb.ud1)
    ph.edges(edge=edge_input)
    ph.whole(**weight_args(st, *NODE_W, *MSG_W, *UPD_W))
    ph.out_stream(BF, part=(d.parts, d.blocks, d.feat, d.rows))
    ph.out_whole(F32, msg=(d.msg_rows, d.feat), upd=(d.upd_rows, d.feat), dn_own=(d.parts, d.half, d.feat))
    ph.out_raw(BF, got=(d.parts, d.half, d.feat))
    sq = (d.feat, d.feat)
    ph.temp(BF, n_cat=(d.length, d.feat), dub=(d.parts, d.half, d.feat), tt=(d.length + d.res, d.rows))
    ph.temp(BF, tri=(3 * d.feat, d.rows), low=(2 * d.feat, d.rows), w2h=sq, w3h=sq, mw2h=sq, gain_mat=sq)
    ph.temp(BF, leave=(d.parts, d.half, d.feat), arrive=(d.parts, d.half, d.feat))
    ph.temp(F32, dr1=(d.parts, d.half, d.feat), e_aux=sq, e_cols=sq, d_aux=sq, d_cols=sq)
    tall = (2 * d.feat + 16, 2 * d.feat)
    ph.temp(F32, m_w12=tall, a_w23=tall, a_b9=sq, a_g2=sq, a_w1=sq)
    ph.temp(F32, a_s=(2 * d.feat, d.length), a_k=(d.blocks, 2 * d.feat, 128))
    ph.sems(send=2 * d.parts, recv=2 * d.parts)

    def body(r):
        p, b = pl.program_id(0), pl.program_id(1)
        first, last = b == 0, b == d.blocks - 1
        n = d.parts
        early = [to_partner(r.dn_far_in.at[i], r.arrive.at[i], r.send.at[n + i], r.recv.at[n + i]) for i in range(n)]
        jobs = [to_partner(r.leave.at[i], r.got.at[i], r.send.at[i], r.recv.at[i]) for i in range(n)]

        @pl.when(first & (p == 0))
        def _():
            greet_partner()
            for job in early:
                job.start()
            r.load()
            load_cols(r, 0, r.e_aux, r.e_cols)
            load_cols(r, 1, r.d_aux, r.d_cols)
            r.tt[d.length :, :] = r.rt[: d.res]
            r.w2h[...] = half_of(r.uw2[0])
            r.w3h[...] = half_of(r.uw3[0])
            r.mw2h[...] = half_of(r.mw2[1])
            r.gain_mat[...] = gain_matrix(r.e_cols[...])
            zero(r.msg, r.upd, r.m_w12, r.a_w23, r.a_b9, r.a_g2, r.a_w1)
            r.n_cat[d.half :] = r.got_a[...]

        @pl.when(first & (p == 1))
        def _():
            r.n_cat[d.half :] = r.got_b[...]

        for i in range(n):

            @pl.when(first & (p == i))
            def _(i=i):
                early[i].wait()

        @pl.when(first)
        def _():
            r.n_cat[: d.half] = r.n_own[p]
            zero(r.a_s)
            dn = r.cot_n[p].astype(F32) + r.dn_a[p] + r.arrive[p].astype(F32)
            node_backward(d, r, p, 1, r.d_aux[...], dn)

        f = d.feat
        r.ready()
        put_one_hot(d, r.tt, 0, r.idx[p, b])
        message_backward(d, r, b, 1, r.tri.at[: 2 * f])
        r.m_w12[...] += mm(r.e2g[...], r.tri[: 2 * f], 1, 1)
        de = mm(r.mw1[1, f : 2 * f, :], r.tri[f : 2 * f])
        dy = (de + r.dec_part[...].astype(F32)).astype(BF)
        dr3 = norm_backward(d, r, dy, r.uxh[...], r.urs[p, b], r.gain_mat[...])
        da1 = r.tri.at[2 * f :]
        update_backward(d, r, dr3, r.ugs[...], r.ud1[...], r.ud2[...], r.w2h[...], r.w3h[...], r.low, da1)
        r.a_w1[...] += mm(da1[...], r.edge[...].reshape(d.rows, f))
        r.part[...] = (mm(r.uw1[0, f : 2 * f, :], da1[...]) + dr3.astype(F32)).astype(BF)
        spread = mm(r.tri[f:], r.tt[...], 1, 1)
        r.a_s[...] += spread[:, : d.length]
        r.a_k[b, :, : d.res] = spread[:, d.length :]
        r.flush()

        @pl.when(last)
        def _():
            n_cat = r.n_cat[...]
            a_k = [r.a_k[i] for i in range(d.blocks)]
            own_m, far_m, b0 = spread_nodes(
                d, r.a_s[: d.feat], [x[: d.feat] for x in a_k], r.mw1[1], n_cat, r.msg, 0
            )
            own_u, far_u, b4 = spread_nodes(
                d, r.a_s[d.feat :], [x[d.feat :] for x in a_k], r.uw1[0], n_cat, r.upd, 0
            )
            r.dn_own[p] = own_m + own_u + r.dr1[p]
            r.leave[p] = (far_m + far_u).astype(BF)
            for i in range(n):

                @pl.when(p == i)
                def _(i=i):
                    jobs[i].start()

            message_small(d, r, b0)
            update_small(d, r, b4)

            @pl.when(p == n - 1)
            def _():
                f, at = d.feat, d.at_small
                r.upd[f : 2 * f] = r.a_w1[...].T
                r.msg[f : 2 * f] = r.m_w12[:f, f:]
                r.msg[3 * f : 4 * f] = 0.5 * r.m_w12[f : 2 * f, :f]
                r.msg[at + 1 : at + 2] = r.m_w12[2 * f : 2 * f + 1, :f]
                for job in jobs:
                    job.wait()

    return ph.call("dec_message_back", body)


def encoder_message_back(d, edge_input, st, fa, fe, n_own, n_got, consts):
    ph = Phase(d)
    ph.whole(dn_a=fe.dn_own, dn_b=fe.got, n_own=n_own, n_got=n_got)
    ph.whole(mask=consts.mask, rt=consts.sums, r1=fa.r1, ip=fa.ip, r2=fa.r2, big=fa.big, cnt=fa.cnt)
    ph.whole(idx=consts.idx)
    ph.stream(d2=fa.d2, g1=fa.g1, d1=fa.d1, up_part=fe.part)
    ph.edges(edge=edge_input)
    ph.whole(**weight_args(st, *NODE_W, *MSG_W))
    ph.out_edges(edge_grad=edge_input.shape)
    ph.out_whole(F32, msg=(d.msg_rows, d.feat), dn_own=(d.parts, d.half, d.feat))
    ph.out_whole(BF, dn_far=(d.parts, d.half, d.feat))
    sq = (d.feat, d.feat)
    ph.temp(BF, n_cat=(d.length, d.feat), dub=(d.parts, d.half, d.feat), tn=(d.rows, d.length + 128))
    ph.temp(BF, low=(2 * d.feat, d.rows), mw2h=sq)
    ph.temp(F32, dr1=(d.parts, d.half, d.feat), aux=sq, cols=sq, a_w1=sq, m_w2=(d.feat + 16, d.feat))
    ph.temp(F32, a_s=(d.feat, d.length), a_k=(d.blocks, d.feat, 128))

    def body(r):
        p, b = pl.program_id(0), pl.program_id(1)
        first, last = b == 0, b == d.blocks - 1

        @pl.when(first & (p == 0))
        def _():
            r.load()
            load_cols(r, 0, r.aux, r.cols)
            r.tn[:, d.length :] = r.rt[...].T
            r.mw2h[...] = half_of(r.mw2[0])
            zero(r.msg, r.m_w2, r.a_w1)
            dn = r.dn_a[...] + r.dn_b[...].astype(F32)
            node_backward(d, r, None, 0, r.aux[...], dn.reshape(-1, d.feat))

        @pl.when(first)
        def _():
            r.n_cat[: d.half] = r.n_own[p]
            r.n_cat[d.half :] = r.n_got[p]
            zero(r.a_s)

        f = d.feat
        r.ready()
        put_one_hot_rows(d, r.tn, r.idx[p, b])
        message_backward(d, r, b, 0, r.low)
        da1 = r.low.at[f:]
        r.m_w2[...] += mm(r.g1[...], r.low[:f], 1, 1)
        r.a_w1[...] += mm(da1[...], r.edge[...].reshape(d.rows, f))
        de = mm(r.mw1[0, f : 2 * f, :], da1[...])
        de = (de + r.up_part[...].astype(F32)).astype(BF)
        r.edge_grad[...] = de.T.reshape(d.res, d.near, f)
        spread = mm(da1[...], r.tn[...])
        r.a_s[...] += spread[:, : d.length]
        r.a_k[b] = spread[:, d.length :]
        r.flush()

        @pl.when(last)
        def _():
            own, far, b0 = spread_nodes(
                d, r.a_s[...], [r.a_k[i] for i in range(d.blocks)], r.mw1[0], r.n_cat[...], r.msg, 0
            )
            r.dn_own[p] = own + r.dr1[p]
            r.dn_far[p] = far.astype(BF)
            message_small(d, r, b0)

            @pl.when(p == d.parts - 1)
            def _():
                f, at = d.feat, d.at_small
                r.msg[f : 2 * f] = r.a_w1[...].T
                r.msg[3 * f : 4 * f] = 0.5 * r.m_w2[:f]
                r.msg[at + 1 : at + 2] = r.m_w2[f : f + 1]

    return ph.call("enc_message_back", body)


class Reducer:
    def __init__(self, devices, feat, shares):
        self.feat = feat
        self.bits = bits = devices.bit_length() - 1
        self.groups = [16 * devices * share for share in shares]
        self.rows = sum(self.groups)
        self.bases = [sum(self.groups[:i]) for i in range(len(shares))]
        pairs, top = [], bits
        while top > 1:
            low = max(1, top - 2)
            pairs.insert(0, (low, top - low))
            top = low
        dims = [ACROSS] + pairs
        turn = min(3, len(dims))
        self.plans = []
        for g, size in enumerate(self.groups):
            head = dims[:turn]
            order = ([(0, 1)] if bits else []) + head[g % turn :] + head[: g % turn] + dims[turn:]
            both, plan = True, []
            for dim in order:
                if dim == ACROSS:
                    both = False
                else:
                    size >>= dim[1]
                plan.append((dim, size, both))
            self.plans.append(plan)
        self.backs = [[step for step in reversed(plan) if step[0] != ACROSS] for plan in self.plans]
        self.halving = len(self.plans[0])
        self.stages = self.halving + len(self.backs[0])
        self.dims = ([(0, 1)] if bits else []) + dims
        self.sem_at, self.buffer_at, self.shapes = {}, {}, []
        for g, plan in enumerate(self.plans):
            for k, (dim, size, both) in enumerate(plan):
                for o in self.offsets(dim):
                    self.sem_at[(g, k, o)] = len(self.sem_at)
                    self.buffer_at[(g, k, o)] = len(self.shapes)
                    self.shapes += [(2, size, feat) if both else (size, feat)] * 2
            for k, (dim, _, _) in enumerate(self.backs[g]):
                for o in self.offsets(dim):
                    self.sem_at[(g, self.halving + k, o)] = len(self.sem_at)

    def scratch(self):
        temps = [pltpu.VMEM((2, self.rows, self.feat), F32), pltpu.VMEM((self.rows, self.feat), BF)]
        temps += [pltpu.VMEM(shape, BF) for shape in self.shapes]
        return temps + [pltpu.SemaphoreType.DMA((len(self.sem_at),))] * 2

    def bind(self, refs):
        self.acc, self.gathered = refs[:2]
        self.buffers, (self.send, self.recv) = refs[2:-2], refs[-2:]

    def offsets(self, dim):
        return range(1, 2 if dim == ACROSS else 1 << dim[1])

    def code(self, dim):
        return lax.rem(lax.axis_index(AXIS_D) // (1 << dim[0]), 1 << dim[1])

    def peer(self, dim, o):
        if dim == ACROSS:
            return other_section()
        code = self.code(dim)
        other = lax.rem(code + o, 1 << dim[1])
        return {AXIS_D: lax.axis_index(AXIS_D) + (other - code) * (1 << dim[0])}

    def greet(self):
        barrier = pltpu.get_barrier_semaphore()
        count = 0
        for dim in self.dims:
            for o in self.offsets(dim):
                pl.semaphore_signal(barrier, inc=1, device_id=self.peer(dim, o), device_id_type=MESH)
                count += 1
        pl.semaphore_wait(barrier, count)

    def begin(self, g, k):
        start = self.bases[g]
        for dim, size, _ in self.plans[g][:k]:
            if dim != ACROSS:
                start = start + self.code(dim) * size
        return start

    def span(self, start, size):
        return pl.ds(pl.multiple_of(start, 16), size)

    def job(self, src, dst, key, dim):
        at = self.sem_at[key]
        return pltpu.make_async_remote_copy(
            src_ref=src, dst_ref=dst, send_sem=self.send.at[at], recv_sem=self.recv.at[at],
            device_id=self.peer(dim, key[2]), device_id_type=MESH,
        )

    def jobs(self, g, k):
        plan = self.plans[g]
        if k < self.halving:
            out = []
            for o in self.offsets(plan[k][0]):
                at = self.buffer_at[(g, k, o)]
                out.append(self.job(self.buffers[at], self.buffers[at + 1], (g, k, o), plan[k][0]))
            return out
        dim, size, _ = self.backs[g][k - self.halving]
        start = self.begin(g, [step[0] for step in plan].index(dim) + 1)
        part = self.gathered.at[self.span(start, size), :]
        return [self.job(part, part, (g, k, o), dim) for o in self.offsets(dim)]

    def start(self, g, k):
        section = lax.axis_index(AXIS_S)
        plan = self.plans[g]
        if k < self.halving:
            dim, size, both = plan[k]
            start = self.begin(g, k)
            for o in self.offsets(dim):
                out = self.buffers[self.buffer_at[(g, k, o)]]
                if dim == ACROSS:
                    out[...] = self.acc[1 - section, self.span(start, size), :].astype(BF)
                    continue
                give = self.span(start + lax.rem(self.code(dim) + o, 1 << dim[1]) * size, size)
                if both:
                    out[...] = self.acc[:, give, :].astype(BF)
                else:
                    out[...] = self.acc[section, give, :].astype(BF)
        elif k == self.halving:
            keep = self.span(self.begin(g, self.halving), plan[-1][1])
            self.gathered[keep, :] = self.acc[section, keep, :].astype(BF)
        for job in self.jobs(g, k):
            job.start()

    def finish(self, g, k):
        section = lax.axis_index(AXIS_S)
        for job in self.jobs(g, k):
            job.wait()
        if k >= self.halving:
            return
        dim, size, both = self.plans[g][k]
        keep = self.span(self.begin(g, k + 1), size)
        for o in self.offsets(dim):
            into = self.buffers[self.buffer_at[(g, k, o)] + 1]
            if both:
                self.acc[:, keep, :] += into[...].astype(F32)
            else:
                self.acc[section, keep, :] += into[...].astype(F32)

    def run(self):
        count = len(self.plans)
        for g in range(count):
            self.start(g, 0)
        for k in range(self.stages):
            for g in range(count):
                self.finish(g, k)
                if k + 1 < self.stages:
                    self.start(g, k + 1)
        if self.stages == self.halving:
            self.gathered[...] = self.acc[lax.axis_index(AXIS_S)].astype(BF)


ACROSS = (-1, 0)


def reduce_grads(d, enc_msg, enc_upd, dec_msg, dec_upd, dn_far):
    m, u = d.msg_rows, d.upd_rows
    units = -(-(m + u) // (16 * d.devices))
    red = Reducer(d.devices, d.feat, [2] * (units // 2) + [1] * (units % 2))

    def kernel(em, eu, dm, du, far, res, got, far_sems, *refs):
        red.bind(refs)
        red.greet()
        nodes = to_partner(far, got, far_sems.at[0], far_sems.at[1])
        nodes.start()
        for layer, (msg, upd) in enumerate(((em, eu), (dm, du))):
            red.acc[layer, :m] = msg[...]
            red.acc[layer, m : m + u] = upd[...]
            if red.rows > m + u:
                red.acc[layer, m + u :] = jnp.zeros((red.rows - m - u, d.feat), F32)
        red.run()
        res[...] = red.gathered[...]
        nodes.wait()

    vm = pl.BlockSpec(memory_space=pltpu.VMEM)
    return pl.pallas_call(
        kernel,
        in_specs=[vm] * 5,
        out_specs=[vm, pl.BlockSpec(memory_space=pl.ANY)],
        out_shape=[jax.ShapeDtypeStruct((red.rows, d.feat), BF), jax.ShapeDtypeStruct(dn_far.shape, BF)],
        scratch_shapes=[pltpu.SemaphoreType.DMA((2,))] + red.scratch(),
        compiler_params=pltpu.CompilerParams(vmem_limit_bytes=58 << 20, collective_id=5, has_side_effects=True),
        name="reduce",
    )(enc_msg, enc_upd, dec_msg, dec_upd, dn_far)


def unpack(d, total, dn_own, dn_got, n_bias, n_gain):
    f = d.feat
    m = d.msg_rows
    shapes = [(1, 3 * f, f), (1, f, f), (1, f, f), (1, f, d.wide), (1, 1, d.wide), (1, d.wide, f)]
    shapes += [(1, 3 * f, f), (1, f, f), (1, f, f), (n_bias, 1, f), (n_gain, 1, f)]

    def kernel(t, own, got, node, mw1, mw2, mw3, inner, inner_b, outer, uw1, uw2, uw3, bias, gain):
        node[...] = (own[...] + got[...].astype(F32)).astype(BF)
        for ref, at in ((mw1, 0), (mw2, 3 * f), (mw3, 4 * f), (outer, d.at_outer)):
            ref[0] = t[at : at + ref.shape[1], :].astype(F32)
        for ref, at in ((uw1, m), (uw2, m + 3 * f), (uw3, m + 4 * f)):
            ref[0] = t[at : at + ref.shape[1], :].astype(F32)
        inner[0] = t[d.at_inner : d.at_inner + d.wide, :].astype(F32).T
        small = t[d.at_small : d.at_small + SMALL, :].astype(F32)
        other = t[m + 5 * f : m + 5 * f + SMALL, :].astype(F32)
        both = small + other
        for i in range(n_bias):
            bias[i] = both[i : i + 1]
        for i in range(n_gain):
            gain[i] = both[n_bias + i : n_bias + i + 1]
        for i in range(d.wide // f):
            inner_b[0, :, i * f : (i + 1) * f] = small[16 + i : 17 + i]

    vm = pl.BlockSpec(memory_space=pltpu.VMEM)
    out = [jax.ShapeDtypeStruct(dn_own.shape, BF)] + [jax.ShapeDtypeStruct(s, F32) for s in shapes]
    return pl.pallas_call(kernel, in_specs=[vm] * 3, out_specs=[vm] * len(out), out_shape=out, name="unpack")(
        total, dn_own, dn_got
    )


def per_device(
    node_input,
    edge_input,
    neighbors,
    residue_mask,
    decode_order,
    node_cotangent,
    edge_cotangent,
    message_w1,
    message_w2,
    message_w3,
    inner_w,
    inner_bias,
    outer_w,
    update_w1,
    update_w2,
    update_w3,
    biases,
    norm_gains,
):
    parts, half, near, feat = edge_input.shape
    length = neighbors.shape[1]
    wide = inner_w.shape[2]
    res = BLOCK_RES
    rows = res * near
    blocks = half // res
    at_outer = 5 * feat
    at_inner = at_outer + wide
    at_small = at_inner + wide
    d = types.SimpleNamespace(
        parts=parts, half=half, near=near, feat=feat, length=length, wide=wide, res=res, rows=rows, blocks=blocks,
        at_outer=at_outer, at_inner=at_inner, at_small=at_small, msg_rows=at_small + SMALL,
        upd_rows=5 * feat + SMALL, devices=lax.axis_size(AXIS_D),
    )
    weights = dict(
        mw1=message_w1[0], mw2=message_w2[0], mw3=message_w3[0], inner=inner_w[0], inner_b=inner_bias, outer=outer_w[0],
        uw1=update_w1[0], uw2=update_w2[0], uw3=update_w3[0],
        bias=biases.transpose(1, 0, 2), gain=norm_gains.transpose(1, 0, 2),
    )
    sums = np.zeros((128, rows), np.float32)
    sums[np.arange(rows) // near, np.arange(rows)] = 1.0
    pick = (np.arange(rows)[None, :] % near == np.arange(near)[:, None]).astype(np.float32)
    consts = types.SimpleNamespace(sums=jnp.asarray(sums, BF), pick=jnp.asarray(pick, BF))
    fa = encoder_message(
        d, edge_input, node_input, neighbors.transpose(0, 2, 1), residue_mask, decode_order, weights, consts
    )
    consts.idx, consts.mask = fa.idx, fa.mask
    st = types.SimpleNamespace(**{n: getattr(fa, W_OUT + n) for n in weights})
    fb = encoder_update(d, edge_input, st, fa, consts)
    fd = decoder_update(d, st, fb, edge_cotangent, consts)
    fe = middle_backward(d, edge_input, st, fa, fb, fd, node_cotangent, consts)
    ff = encoder_message_back(d, edge_input, st, fa, fe, node_input, fa.nodes_got, consts)
    total, got = reduce_grads(d, ff.msg, fe.upd, fe.msg, fd.upd, ff.dn_far)
    node_grad, mw1, mw2, mw3, inner, inner_b, outer, uw1, uw2, uw3, bias, gain = unpack(
        d, total, ff.dn_own, got, biases.shape[1], norm_gains.shape[1]
    )
    return (
        fd.nodes, fd.decoded, node_grad, ff.edge_grad, mw1, mw2, mw3, inner, inner_b[:, 0], outer,
        uw1, uw2, uw3, bias.transpose(1, 0, 2), gain.transpose(1, 0, 2),
    )


def solution(mesh):
    def split(*axes):
        return P(*axes)

    by_part = split(AXIS_D)
    by_half = split(AXIS_D, AXIS_S)
    by_layer = split(AXIS_S)
    in_specs = (by_half, by_half, by_part, by_part, by_part, by_half, by_half) + (by_layer,) * 11
    out_specs = (by_half,) * 4 + (by_layer,) * 11
    return jax.shard_map(per_device, mesh=mesh, in_specs=in_specs, out_specs=out_specs, check_vma=False)
```

```python
import types

import jax
import jax.numpy as jnp
import numpy as np
from jax import lax
from jax.experimental import pallas as pl
from jax.experimental.pallas import tpu as pltpu
from jax.sharding import PartitionSpec as P

BF = jnp.bfloat16
F32 = jnp.float32
C1 = 0.7978845608
C2 = C1 * 0.044715
EPS = 1e-5
BLOCK_RES = 64
EXTRA = 16
SMALL = 32
MESH = pl.DeviceIdType.MESH


def mm(a, b, ca=1, cb=0):
    return lax.dot_general(a, b, (((ca,), (cb,)), ((), ())), preferred_element_type=F32)


def mm_exact(a, b, ca=1, cb=0):
    return lax.dot_general(
        a, b, (((ca,), (cb,)), ((), ())), precision=lax.Precision.HIGHEST, preferred_element_type=F32
    )


def gelu_pair(x):
    x = x.astype(BF)
    w = x * x * BF(C2)
    h = jnp.tanh(x * (w + BF(C1))) + BF(1.0)
    g = x * h
    d = h + g * (BF(2.0) - h) * (w * BF(3.0) + BF(C1))
    return g, d


def gelu_pair_wide(x):
    x2 = x * x
    h = 0.5 * jnp.tanh(x * (x2 * C2 + C1)) + 0.5
    g = x * h
    d = h + (g * (1.0 - h)) * (x2 * (6 * C2) + 2 * C1)
    return g, d


def lane_sum(x):
    total = x[:, :128]
    for at in range(128, x.shape[1], 128):
        total = total + x[:, at : at + 128]
    return total


def to_row(acc):
    return mm_exact(jnp.ones((8, acc.shape[1]), F32), acc, 1, 1)[0:1]


def norm_rows(r):
    c = r - jnp.mean(r, axis=-1, keepdims=True)
    rs = lax.rsqrt(jnp.mean(c * c, axis=-1, keepdims=True) + EPS)
    return c * rs, rs


def norm_back_rows(dxh, xh, rs):
    m1 = jnp.mean(dxh, axis=-1, keepdims=True)
    m2 = jnp.mean(dxh * xh, axis=-1, keepdims=True)
    return (dxh - m1 - xh * m2) * rs


def norm_back(dy, xh, rs, gain_col):
    dxh = dy * gain_col
    m1 = jnp.mean(dxh, axis=0, keepdims=True)
    m2 = jnp.mean(dxh * xh, axis=0, keepdims=True)
    return (dxh - m1 - xh * m2) * rs


class Phase:
    def __init__(self, dims, collective_id=None):
        self.d = dims
        self.collective_id = collective_id
        self.ins, self.outs, self.temps, self.kinds, self.wholes, self.later = [], [], [], {}, {}, ()

    def whole_spec(self, shape):
        rank = len(shape)
        return pl.BlockSpec(tuple(shape), lambda p, b: (0,) * rank)

    def whole(self, **arrays):
        self.raw(**arrays)
        self.wholes.update({n: pltpu.VMEM(a.shape, a.dtype) for n, a in arrays.items()})

    def raw(self, **arrays):
        self.ins += [(n, a, pl.BlockSpec(memory_space=pl.ANY)) for n, a in arrays.items()]

    def stream(self, **arrays):
        self.raw(**arrays)
        self.kinds.update({n: (False, False, a.shape[2:], a.dtype) for n, a in arrays.items()})

    def stream_top(self, rows, **arrays):
        self.raw(**arrays)
        self.kinds.update({n: (False, False, (rows,) + a.shape[3:], a.dtype) for n, a in arrays.items()})

    def edges(self, **arrays):
        self.raw(**arrays)
        block = (self.d.res, self.d.near, self.d.feat)
        self.kinds.update({n: (False, True, block, a.dtype) for n, a in arrays.items()})

    def out_whole(self, dtype, **shapes):
        self.outs += [(n, jax.ShapeDtypeStruct(s, dtype), self.whole_spec(s)) for n, s in shapes.items()]

    def out_raw(self, dtype, **shapes):
        spec = pl.BlockSpec(memory_space=pl.ANY)
        self.outs += [(n, jax.ShapeDtypeStruct(s, dtype), spec) for n, s in shapes.items()]

    def out_stream(self, dtype, **shapes):
        self.out_raw(dtype, **shapes)
        self.kinds.update({n: (True, False, s[2:], dtype) for n, s in shapes.items()})

    def out_edges(self, **shapes):
        self.out_raw(BF, **shapes)
        block = (self.d.res, self.d.near, self.d.feat)
        self.kinds.update({n: (True, True, block, BF) for n in shapes})

    def temp(self, dtype, **shapes):
        self.temps += [(n, pltpu.VMEM(s, dtype)) for n, s in shapes.items()]

    def sems(self, **counts):
        self.temps += [(n, pltpu.SemaphoreType.DMA((c,))) for n, c in counts.items()]

    def call(self, name, body):
        d = self.d
        names = [n for n, _, _ in self.ins] + [n for n, _, _ in self.outs] + [n for n, _ in self.temps]
        steps = d.parts * d.blocks
        buffers = [pltpu.VMEM((2,) + tuple(block), dtype) for _, _, block, dtype in self.kinds.values()]
        count = len(self.kinds)

        def kernel(*refs):
            refs, rest = refs[: len(names)], refs[len(names) :]
            slots, sems, kept = rest[:count], rest[count : 2 * count], rest[2 * count : -1]
            plain = dict(zip(names, refs))
            step = pl.program_id(0) * d.blocks + pl.program_id(1)
            now = lax.rem(step, 2)

            def copy(i, n, at, slot):
                out, edges, block, _ = self.kinds[n]
                p, b = at // d.blocks, lax.rem(at, d.blocks)
                if edges:
                    far = plain[n].at[p, pl.ds(pl.multiple_of(b * d.res, d.res), d.res)]
                elif block[0] < plain[n].shape[2]:
                    far = plain[n].at[p, b, pl.ds(0, block[0])]
                else:
                    far = plain[n].at[p, b]
                near = slots[i].at[slot]
                return pltpu.make_async_copy(*((near, far) if out else (far, near)), sems[i].at[slot])

            into = [(i, n) for i, n in enumerate(self.kinds) if not self.kinds[n][0]]
            outof = [(i, n) for i, n in enumerate(self.kinds) if self.kinds[n][0]]

            def loads():
                return [
                    pltpu.make_async_copy(plain[n], kept[i], rest[-1].at[i]) for i, n in enumerate(self.wholes)
                ]

            def load(*later):
                for item, n in zip(loads(), self.wholes):
                    if (n in later) if later else (n not in self.later):
                        item.wait()

            @pl.when(step == 0)
            def _():
                for item in loads():
                    item.start()
                for i, n in into:
                    copy(i, n, step, now).start()

            @pl.when(step + 1 < steps)
            def _():
                for i, n in into:
                    copy(i, n, step + 1, 1 - now).start()

            @pl.when(step >= 2)
            def _():
                for i, n in outof:
                    copy(i, n, step - 2, now).wait()

            def ready():
                for i, n in into:
                    copy(i, n, step, now).wait()

            def flush():
                for i, n in outof:
                    copy(i, n, step, now).start()

            plain_or_slot = dict(plain, ready=ready, flush=flush, load=load)
            plain_or_slot.update(zip(self.wholes, kept))
            plain_or_slot.update({n: slots[i].at[now] for i, n in enumerate(self.kinds)})
            body(types.SimpleNamespace(**plain_or_slot))

            @pl.when(step == steps - 1)
            def _():
                for i, n in outof:
                    if steps > 1:
                        copy(i, n, step - 1, 1 - now).wait()
                    copy(i, n, step, now).wait()

        results = pl.pallas_call(
            kernel,
            grid=(d.parts, d.blocks),
            in_specs=[s for _, _, s in self.ins],
            out_specs=[s for _, _, s in self.outs],
            out_shape=[s for _, s, _ in self.outs],
            scratch_shapes=[s for _, s in self.temps] + buffers
            + [pltpu.SemaphoreType.DMA((2,))] * count
            + list(self.wholes.values())
            + [pltpu.SemaphoreType.DMA((len(self.wholes),))],
            compiler_params=pltpu.CompilerParams(
                dimension_semantics=(pltpu.ARBITRARY,) * 2,
                vmem_limit_bytes=60 << 20,
                collective_id=self.collective_id,
                has_side_effects=self.collective_id is not None,
            ),
            name=name,
        )(*[a for _, a, _ in self.ins])
        return types.SimpleNamespace(**dict(zip([n for n, _, _ in self.outs], results)))


def other_section():
    return {AXIS_S: 1 - lax.axis_index(AXIS_S)}


AXIS_S = "section"
AXIS_D = "dp"


def greet_partner():
    barrier = pltpu.get_barrier_semaphore()
    pl.semaphore_signal(barrier, inc=1, device_id=other_section(), device_id_type=MESH)
    pl.semaphore_wait(barrier, 1)


def to_partner(src, dst, send, recv):
    return pltpu.make_async_remote_copy(
        src_ref=src, dst_ref=dst, send_sem=send, recv_sem=recv, device_id=other_section(), device_id_type=MESH
    )


def put_one_hot(d, ref, at, idx):
    idx = idx.astype(jnp.int16)
    place = lax.broadcasted_iota(jnp.int16, (d.length, d.rows), 0)
    ref[at : at + d.length, :] = jnp.where(place == idx, jnp.ones((), BF), jnp.zeros((), BF))


def put_one_hot_rows(d, ref, idx):
    centre = d.length // 2
    idx = jnp.broadcast_to((idx - centre).astype(F32).astype(BF), (128, d.rows)).T
    place = lax.broadcasted_iota(jnp.int32, (d.rows, 128), 1)
    for at in range(0, d.length, 128):
        there = (place + (at - centre)).astype(F32).astype(BF)
        ref[:, at : at + 128] = jnp.where(idx == there, jnp.ones((), BF), jnp.zeros((), BF))


def weight_args(w, *names):
    return {n: getattr(w, n) for n in names}


def load_cols(r, layer, aux, cols):
    n_bias, n_gain = r.bias.shape[1], r.gain.shape[1]
    aux[...] = jnp.zeros(aux.shape, F32)
    for i in range(n_bias):
        aux[i : i + 1] = r.bias[layer, i]
    for i in range(n_gain):
        aux[n_bias + i : n_bias + i + 1] = r.gain[layer, i]
    cols[...] = aux[...].T


def put_table(d, lhs, at, left, n_cat, w1):
    lhs[at : at + d.feat, left : left + d.length] = mm(w1[2 * d.feat :, :].T, n_cat[...], 1, 1).astype(BF)


def put_own(d, lhs, at, left, w1, n_blk, bias_col):
    own = mm(w1[0 : d.feat, :].T, n_blk, 1, 1) + bias_col
    lhs[at : at + d.feat, left + d.length :] = own.astype(BF)


def message_part(a1, w2t, b2, att, kept):
    g1, d1 = gelu_pair(a1)
    a2 = mm(w2t, g1) + b2
    g2, d2 = gelu_pair(a2)
    attb = att.astype(BF)
    feat, rows = g2.shape
    kept[:feat] = g2 * attb
    kept[feat:] = jnp.broadcast_to(attb, (16, rows))
    return g1, d1, d2 * attb


def add_node_outs(ph, d):
    ph.out_whole(BF, node_out=(d.parts, d.half, d.feat))
    shape = (d.parts, d.half, d.feat)
    ph.out_whole(F32, r1=shape, ip=(d.parts, d.half, d.wide), r2=shape, big=shape, cnt=shape)


def node_step(d, r, p, b):
    sums = mm(r.rt[: d.res], r.kept[...], 1, 1)
    at = pl.ds(pl.multiple_of(b * d.res, d.res), d.res)
    r.big[p, at, :] = sums[:, : d.feat] * 0.5
    r.cnt[p, at, :] = jnp.broadcast_to(sums[:, d.feat : d.feat + 1], (d.res, d.feat))


def node_forward(r, p, n_own, layer, aux):
    big = r.big[p]
    hi = big.astype(BF)
    lo = (big - hi.astype(F32)).astype(BF)
    w3 = r.mw3[layer]
    upd = (mm(hi, w3) + mm(lo, w3) + r.cnt[p] * aux[2:3]) / 30.0
    r1 = n_own.astype(F32) + upd
    xh1, _ = norm_rows(r1)
    normed = xh1 * aux[10:11] + aux[7:8]
    ip = mm(normed.astype(BF), r.inner[layer]) + r.inner_b[layer]
    hid = gelu_pair_wide(ip)[0].astype(BF)
    r2 = normed + (mm(hid, r.outer[layer]) + aux[3:4])
    xh2, _ = norm_rows(r2)
    out = ((xh2 * aux[11:12] + aux[8:9]) * r.mask[p]).astype(BF)
    r.node_out[p] = out
    r.r1[p] = r1
    r.ip[p] = ip
    r.r2[p] = r2
    return out


def node_backward(d, r, p, layer, aux, dn):
    def rows_of(ref):
        return ref[...].reshape(-1, ref.shape[2]) if p is None else ref[p]

    r1, ip, r2, big, cnt = rows_of(r.r1), rows_of(r.ip), rows_of(r.r2), rows_of(r.big), rows_of(r.cnt)
    xh1, rs1 = norm_rows(r1)
    normed = xh1 * aux[10:11] + aux[7:8]
    xh2, rs2 = norm_rows(r2)
    dy2 = dn * rows_of(r.mask)
    dr2 = norm_back_rows(dy2 * aux[11:12], xh2, rs2)
    low_outer = dr2.astype(BF)
    hid, slope = gelu_pair_wide(ip)
    dip = mm(low_outer, r.outer[layer], 1, 1) * slope
    low_inner = dip.astype(BF)
    at = d.at_outer
    r.msg[at : at + d.wide] += mm(hid.astype(BF), low_outer, 0, 0)
    at = d.at_inner
    r.msg[at : at + d.wide] += mm(low_inner, normed.astype(BF), 0, 0)
    dnormed = dr2 + mm(low_inner, r.inner[layer], 1, 1)
    dr1 = norm_back_rows(dnormed * aux[10:11], xh1, rs1)
    du = dr1 / 30.0
    dub = du.astype(BF)
    r.msg[4 * d.feat : 5 * d.feat] += mm(big.astype(BF), dub, 0, 0)
    dib = jnp.sum(dip, axis=0, keepdims=True)
    rows = {
        2: jnp.sum(cnt * du, axis=0, keepdims=True),
        3: jnp.sum(dr2, axis=0, keepdims=True),
        7: jnp.sum(dnormed, axis=0, keepdims=True),
        8: jnp.sum(dy2, axis=0, keepdims=True),
        10: jnp.sum(dnormed * xh1, axis=0, keepdims=True),
        11: jnp.sum(dy2 * xh2, axis=0, keepdims=True),
    }
    for i in range(d.wide // d.feat):
        rows[16 + i] = dib[:, i * d.feat : (i + 1) * d.feat]
    for row, value in rows.items():
        r.msg[d.at_small + row : d.at_small + row + 1] += value
    if p is None:
        r.dr1[...] = dr1.reshape(r.dr1.shape)
        r.dub[...] = dub.reshape(r.dub.shape)
    else:
        r.dr1[p] = dr1
        r.dub[p] = dub


def own_first(d, row):
    row = row.astype(F32)
    if row.shape[0] == 1:
        row = jnp.broadcast_to(row, (8, d.length))
    return jnp.where(lax.axis_index(AXIS_S) == 0, row, pltpu.roll(row, d.half, 1))


def put_positions(d, r):
    section = lax.axis_index(AXIS_S)
    centre = d.length // 2
    line = lax.broadcasted_iota(jnp.int32, (8, d.length), 0)
    for p in range(d.parts):
        live = own_first(d, r.live[p : p + 1, :])
        order = own_first(d, r.order[p : p + 1, :]) - centre
        code = jnp.where(live > 0.5, order, float(centre))
        r.codes[p, :8] = jnp.where(line == 0, live, jnp.where(line == 1, code, 0.0)).astype(BF)
        r.codes[p, 8:] = jnp.zeros((EXTRA - 8, d.length), BF)
        ids = own_first(d, r.near[p]) - float(d.half) * section.astype(F32)
        ids = jnp.where(ids < 0.0, ids + float(d.length), ids) - float(centre)
        r.mask[p] = jnp.broadcast_to(live[0:1], (d.feat, d.length)).T[: d.half]
        for b in range(d.blocks):
            own = pltpu.roll(order, (d.length - b * d.res) % d.length, 1) if b else order
            r.owns[p, b, :8] = jnp.where(line == 1, -own, 0.0)[:, : d.res].astype(BF)
            r.owns[p, b, 8:] = jnp.zeros((EXTRA - 8, d.res), BF)
            block = pltpu.roll(ids, (d.length - b * d.res) % d.length, 1) if b else ids
            spread = mm(block[:, : d.res].astype(BF), r.rt[: d.res])
            row = jnp.sum(spread * r.pick[...].astype(F32), axis=0, keepdims=True)
            r.idx[p, b] = row.astype(jnp.int32) + centre


def encoder_message(d, edge_input, node_input, neighbors, residue_mask, decode_order, weights, consts):
    ph = Phase(d, 2)
    ph.raw(n_far=node_input)
    ph.whole(n_own=node_input, rt=consts.sums, pick=consts.pick, near=neighbors, live=residue_mask, order=decode_order)
    ph.whole(edge=edge_input)
    ph.later = (EDGE,)
    ph.out_whole(jnp.int32, idx=(d.parts, d.blocks, 1, d.rows))
    ph.out_whole(F32, mask=(d.parts, d.half, d.feat))
    ph.temp(BF, codes=(d.parts, EXTRA, d.length), owns=(d.parts, d.blocks, EXTRA, d.res))
    names = tuple(weights)
    own = {W_IN + n: a for n, a in weights.items()}
    ph.raw(**own)
    act = (d.parts, d.blocks, d.feat, d.rows)
    ph.out_stream(BF, g1=with_ones(d), d1=act, d2=act)
    ph.out_whole(F32, att=(d.parts, d.blocks, 1, d.rows))
    add_node_outs(ph, d)
    ph.out_raw(BF, got=(d.half, d.feat), nodes_got=node_input.shape)
    for n, a in weights.items():
        ph.out_raw(a.dtype, **{W_OUT + n: (2,) + a.shape})
        ph.temp(a.dtype, **{n: (2,) + a.shape})
    sq = (d.feat, d.feat)
    wide = d.feat + d.length + d.res
    ph.temp(BF, n_cat=(d.length, d.feat), lhs=(d.feat + EXTRA, wide), w2t=sq, tt=(d.parts * d.blocks, wide, d.rows))
    ph.temp(BF, leave=(d.half, d.feat), arrive=node_input.shape, kept=(d.feat + 16, d.rows))
    ph.temp(F32, aux=sq, cols=sq)
    count = len(names)
    ph.sems(send=count + 2, recv=count + 2, local=count, back=2 * count + 1)

    def body(r):
        p, b = pl.program_id(0), pl.program_id(1)
        first, last = b == 0, b == d.blocks - 1
        section = lax.axis_index(AXIS_S)
        job = to_partner(r.leave, r.got, r.send.at[count], r.recv.at[count])
        nodes = to_partner(r.n_far, r.arrive, r.send.at[count + 1], r.recv.at[count + 1])

        def swaps(group):
            out = []
            for n in group:
                i = names.index(n)
                dst = getattr(r, n).at[section]
                out.append(to_partner(getattr(r, W_IN + n), dst, r.send.at[i], r.recv.at[i]))
            return out

        def own_copies():
            return [
                pltpu.make_async_copy(getattr(r, W_IN + n), getattr(r, n).at[section], r.local.at[i])
                for i, n in enumerate(names)
            ]

        def returns(group):
            out = [pltpu.make_async_copy(r.arrive, r.nodes_got, r.back.at[2 * count])] if group == GROUP_ONE else []
            for n in group:
                i = names.index(n)
                src, dst = getattr(r, n), getattr(r, W_OUT + n)
                for layer in range(2):
                    sem = r.back.at[2 * i + layer]
                    out.append(pltpu.make_async_copy(src.at[layer], dst.at[layer], sem))
            return out

        begin = first & (p == 0)
        middle = (p == 1) & (b == 1)
        at_end = last & (p == d.parts - 1)

        @pl.when(begin)
        def _():
            greet_partner()
            nodes.start()
            for item in swaps(GROUP_ONE) + own_copies():
                item.start()
            r.load()
            put_positions(d, r)
            r.load(EDGE)
            for q in range(d.parts):

                @pl.loop(0, d.blocks)
                def _(c, q=q):
                    table = r.tt.at[q * d.blocks + c]
                    put_one_hot(d, table, d.feat, r.idx[q, c])
                    table[d.feat + d.length :, :] = r.rt[: d.res]
                    own = r.edge[q, pl.ds(pl.multiple_of(c * d.res, d.res), d.res)]
                    table[: d.feat, :] = own.reshape(d.rows, d.feat).T

            nodes.wait()
            for item in swaps(GROUP_ONE) + own_copies():
                item.wait()
            for item in swaps(GROUP_TWO) + swaps(GROUP_THREE):
                item.start()
            r.lhs[: d.feat, : d.feat] = r.mw1[0, d.feat : 2 * d.feat, :].T
            r.lhs[d.feat :, : d.feat] = jnp.zeros((EXTRA, d.feat), BF)
            r.w2t[...] = half_of(r.mw2[0]).T
            load_cols(r, 0, r.aux, r.cols)

        @pl.when(first)
        def _():
            r.n_cat[: d.half] = r.n_own[p]
            r.n_cat[d.half :] = r.arrive[p]
            put_table(d, r.lhs, 0, d.feat, r.n_cat, r.mw1.at[0])

        n_blk = r.n_own[p, pl.ds(pl.multiple_of(b * d.res, d.res), d.res), :]
        r.ready()
        put_own(d, r.lhs, 0, d.feat, r.mw1.at[0], n_blk, r.cols[:, 0:1])
        r.lhs[d.feat :, d.feat : d.feat + d.length] = r.codes[p]
        r.lhs[d.feat :, d.feat + d.length :] = r.owns[p, b]
        out = mm(r.lhs[...], r.tt[p * d.blocks + b])
        att = out[d.feat : d.feat + 1]
        r.att[p, b] = jnp.where(out[d.feat + 1 : d.feat + 2] < 0.0, 1.0, 0.0)
        g1, r.d1[...], r.d2[...] = message_part(out[: d.feat], r.w2t[...], r.cols[:, 1:2], att, r.kept)
        put_ones(r.g1, g1)
        node_step(d, r, p, b)
        r.flush()

        @pl.when(middle)
        def _():
            for item in swaps(GROUP_TWO) + swaps(GROUP_THREE):
                item.wait()
            for item in returns(GROUP_ONE) + returns(GROUP_TWO) + returns(GROUP_THREE):
                item.start()
            r.leave[...] = node_forward(r, 0, r.n_own[0], 0, r.aux[...])
            job.start()

        @pl.when(at_end)
        def _():
            node_forward(r, d.parts - 1, r.n_own[d.parts - 1], 0, r.aux[...])
            for item in returns(GROUP_ONE) + returns(GROUP_TWO) + returns(GROUP_THREE):
                item.wait()
            job.wait()

    return ph.call("enc_message", body)


W_IN, W_OUT = "i_", "o_"
EDGE = "edge"
GROUP_ONE = ("mw1", "mw2", "bias", "gain")
GROUP_TWO = ("mw3", "inner", "inner_b", "outer")
GROUP_THREE = ("uw1", "uw2", "uw3")
NODE_W = ("mw3", "inner", "inner_b", "outer", "bias", "gain")
MSG_W = ("mw1", "mw2")
UPD_W = ("uw1", "uw2", "uw3")


def with_ones(d):
    return (d.parts, d.blocks, d.feat + 16, d.rows)


def put_ones(ref, g):
    feat, rows = g.shape
    ref[:feat] = g
    ref[feat:] = jnp.ones((16, rows), BF)


def half_of(w):
    return w * BF(0.5)


def update_forward(d, a1, w2t, w3c, b5, b6c, pair, cols):
    f = d.feat
    g1, d1 = gelu_pair(a1)
    a2 = mm(w2t, g1) + b5
    g2, d2 = gelu_pair(a2)
    pair[f : 2 * f] = g2
    cent = mm(w3c[...], pair[: 2 * f]) + b6c
    var = jnp.mean(cent * cent, axis=0, keepdims=True)
    rs = lax.rsqrt(var + EPS)
    xh = cent.astype(BF) * rs.astype(BF)
    y = xh * cols[:, 12:13].astype(BF) + cols[:, 9:10].astype(BF)
    return g1, d1, g2, d2, xh, rs, y


def centre_weights(w3, cols, w3c, b6c):
    feat = w3.shape[0]
    eye = lax.broadcasted_iota(jnp.int32, w3.shape, 0) == lax.broadcasted_iota(jnp.int32, w3.shape, 1)
    w3f = w3.astype(F32)
    w3c[:, feat:] = (0.5 * (w3f - jnp.mean(w3f, axis=1, keepdims=True))).T.astype(BF)
    w3c[:, :feat] = (eye.astype(F32) - 1.0 / feat).astype(BF)
    b6 = cols[:, 6:7]
    b6c[...] = jnp.broadcast_to(b6 - jnp.mean(b6, axis=0, keepdims=True), b6c.shape)


def encoder_update(d, edge_input, st, fa, consts):
    ph = Phase(d, 3)
    ph.raw(n_far=fa.node_out)
    ph.whole(n_own=fa.node_out, got_a=fa.got, idx=consts.idx, rt=consts.sums, mask=consts.mask, att=fa.att)
    ph.edges(edge=edge_input)
    ph.whole(**weight_args(st, *NODE_W, *MSG_W, *UPD_W))
    act = (d.parts, d.blocks, d.feat, d.rows)
    two = (d.parts, d.blocks, 2 * d.feat + 16, d.rows)
    ph.out_stream(BF, ugs=two, ud1=act, ud2=act, uxh=act, e2g=two, d1=act, d2=act)
    ph.out_whole(F32, urs=(d.parts, d.blocks, 1, d.rows))
    add_node_outs(ph, d)
    ph.out_whole(BF, got_in=(d.half, d.feat))
    ph.out_raw(BF, got=(d.parts, d.half, d.feat))
    sq = (d.feat, d.feat)
    wide = d.feat + d.length + d.res
    ph.temp(BF, n_cat=(d.length, d.feat), lhs=(2 * d.feat, wide), tt=(wide, d.rows))
    ph.temp(BF, uw2t=sq, mw2t=sq, w3c=(d.feat, 2 * d.feat), pair=(2 * d.feat, d.rows))
    ph.temp(BF, kept=(d.feat + 16, d.rows), leave=(d.parts, d.half, d.feat), arrive=(d.half, d.feat))
    ph.temp(F32, w3c_b=sq, e_aux=sq, e_cols=sq, d_aux=sq, d_cols=sq)
    ph.sems(send=d.parts + 1, recv=d.parts + 1)

    def body(r):
        p, b = pl.program_id(0), pl.program_id(1)
        first, last = b == 0, b == d.blocks - 1
        early = to_partner(r.n_far.at[d.parts - 1], r.arrive, r.send.at[d.parts], r.recv.at[d.parts])
        jobs = [to_partner(r.leave.at[i], r.got.at[i], r.send.at[i], r.recv.at[i]) for i in range(d.parts)]

        @pl.when(first & (p == 0))
        def _():
            greet_partner()
            early.start()
            r.load()
            r.tt[d.feat + d.length :, :] = r.rt[: d.res]
            r.lhs[: d.feat, : d.feat] = r.uw1[0, d.feat : 2 * d.feat, :].T
            r.lhs[d.feat :, : d.feat] = r.mw1[1, d.feat : 2 * d.feat, :].T
            r.uw2t[...] = half_of(r.uw2[0]).T
            r.mw2t[...] = half_of(r.mw2[1]).T
            load_cols(r, 0, r.e_aux, r.e_cols)
            load_cols(r, 1, r.d_aux, r.d_cols)
            centre_weights(r.uw3[0], r.e_cols[...], r.w3c, r.w3c_b)
            r.n_cat[d.half :] = r.got_a[...]

        @pl.when(first & (p == 1))
        def _():
            early.wait()
            r.n_cat[d.half :] = r.arrive[...]
            r.got_in[...] = r.arrive[...]

        @pl.when(first)
        def _():
            r.n_cat[: d.half] = r.n_own[p]
            put_table(d, r.lhs, 0, d.feat, r.n_cat, r.uw1.at[0])
            put_table(d, r.lhs, d.feat, d.feat, r.n_cat, r.mw1.at[1])

        r.ready()
        n_blk = r.n_own[p, pl.ds(pl.multiple_of(b * d.res, d.res), d.res), :]
        put_own(d, r.lhs, 0, d.feat, r.uw1.at[0], n_blk, r.e_cols[:, 4:5])
        put_own(d, r.lhs, d.feat, d.feat, r.mw1.at[1], n_blk, r.d_cols[:, 0:1])
        put_one_hot(d, r.tt, d.feat, r.idx[p, b])
        edge_t = r.edge[...].reshape(d.rows, d.feat).T
        r.tt[: d.feat, :] = edge_t
        r.pair[: d.feat] = edge_t
        g1, d1, g2, d2, xh, rs, e2 = update_forward(
            d, mm(r.lhs[: d.feat], r.tt[...]), r.uw2t[...], r.w3c, r.e_cols[:, 5:6], r.w3c_b[:, 0:1], r.pair, r.e_cols
        )
        f = d.feat
        r.ugs[:f] = g2
        put_ones(r.ugs.at[f:], g1)
        r.ud1[...], r.ud2[...], r.uxh[...], r.urs[p, b], r.e2g[:f] = d1, d2, xh, rs, e2
        att = r.att[p, b]
        r.tt[:f] = e2
        a1 = mm(r.lhs[f:], r.tt[...])
        g1, r.d1[...], r.d2[...] = message_part(a1, r.mw2t[...], r.d_cols[:, 1:2], att, r.kept)
        put_ones(r.e2g.at[f:], g1)
        node_step(d, r, p, b)
        r.flush()

        @pl.when(last)
        def _():
            r.leave[p] = node_forward(r, p, r.n_own[p], 1, r.d_aux[...])
            for i in range(d.parts):

                @pl.when(p == i)
                def _(i=i):
                    jobs[i].start()

            @pl.when(p == d.parts - 1)
            def _():
                for job in jobs:
                    job.wait()

    return ph.call("enc_update", body)


def spread_nodes(d, acc, sumk, w1, n_cat, grad, grad_at):
    s = acc.astype(BF)
    sk = jnp.concatenate([x[:, : d.res] for x in sumk], axis=1)
    skb = sk.astype(BF)
    far = mm(s, w1[2 * d.feat :].T, 0, 0)
    own = mm(skb, w1[: d.feat].T, 0, 0)
    grad[grad_at + 2 * d.feat : grad_at + 3 * d.feat, :] += mm(n_cat, s, 0, 1)
    grad[grad_at : grad_at + d.feat, :] += mm(n_cat[: d.half], skb, 0, 1)
    return own + far[: d.half], far[d.half :], to_row(sk)


def lane_total(x):
    size = x.shape[1] // 4
    x = (x[:, :size] + x[:, size : 2 * size]) + (x[:, 2 * size : 3 * size] + x[:, 3 * size :])
    return lane_sum(x.astype(F32))


def norm_backward(d, r, dy, xh, rs, gain_mat):
    r.a_b9[...] += lane_total(dy)
    r.a_g2[...] += lane_total(dy * xh)
    z = mm(gain_mat, dy).astype(BF)
    m2 = jnp.mean((z * xh).astype(F32), axis=0, keepdims=True)
    return (z - xh * m2.astype(BF)) * rs.astype(BF)


def gain_matrix(cols):
    feat = cols.shape[0]
    shape = (feat, feat)
    eye = lax.broadcasted_iota(jnp.int32, shape, 0) == lax.broadcasted_iota(jnp.int32, shape, 1)
    scaled = jnp.where(eye, jnp.broadcast_to(cols[:, 12:13], shape), 0.0)
    return (scaled - jnp.mean(scaled, axis=0, keepdims=True)).astype(BF)


def update_backward(d, r, dr3, gs, d1, d2, w2, w3, low, da1):
    f = d.feat
    low[:f] = dr3
    low[f:] = mm(w3, dr3).astype(BF) * d2
    r.a_w23[...] += mm(gs, low[...], 1, 1)
    da1[...] = mm(w2, low[f:]).astype(BF) * d1


def update_small(d, r, b4):
    f = d.feat
    at = 5 * f
    r.upd[at + 4 : at + 5] += b4

    @pl.when(pl.program_id(0) == d.parts - 1)
    def _():
        r.upd[3 * f : 4 * f] = 0.5 * r.a_w23[f : 2 * f, f:]
        r.upd[4 * f : 5 * f] = 0.5 * r.a_w23[:f, :f]
        r.upd[at + 5 : at + 6] = r.a_w23[2 * f : 2 * f + 1, f:]
        r.upd[at + 6 : at + 7] = r.a_w23[2 * f : 2 * f + 1, :f]
        r.upd[at + 9 : at + 10] = to_row(r.a_b9[...])
        r.upd[at + 12 : at + 13] = to_row(r.a_g2[...])


def zero(*refs):
    for ref in refs:
        ref[...] = jnp.zeros(ref.shape, ref.dtype)


def decoder_update(d, st, fb, cot, consts):
    ph = Phase(d)
    ph.whole(n_own=fb.node_out, n_got=fb.got, idx=consts.idx, rt=consts.sums)
    ph.stream_top(d.feat, e2=fb.e2g)
    ph.edges(cot=cot)
    ph.whole(**weight_args(st, *UPD_W, *AUX_W))
    ph.out_edges(decoded=cot.shape)
    ph.out_stream(BF, part=(d.parts, d.blocks, d.feat, d.rows))
    ph.out_whole(F32, upd=(d.upd_rows, d.feat), dn_own=(d.parts, d.half, d.feat))
    ph.out_whole(BF, dn_far=(d.parts, d.half, d.feat), nodes=(d.parts, d.half, d.feat))
    sq = (d.feat, d.feat)
    wide = d.length + d.res
    ph.temp(BF, n_cat=(d.length, d.feat), lhs=(d.feat, wide), w1bt=sq, w2t=sq, w2h=sq, w3h=sq)
    ph.temp(BF, tt=(wide, d.rows), tn=(d.rows, d.length + 128), da1=(d.feat, d.rows))
    ph.temp(BF, w3c=(d.feat, 2 * d.feat), gain_mat=sq, pair=(3 * d.feat + 16, d.rows), low=(2 * d.feat, d.rows))
    ph.temp(F32, w3c_b=sq, aux=sq, cols=sq, a_w23=(2 * d.feat + 16, 2 * d.feat), a_b9=sq, a_g2=sq)
    ph.temp(F32, a_s=(d.feat, d.length), a_k=(d.blocks, d.feat, 128))

    def body(r):
        p, b = pl.program_id(0), pl.program_id(1)
        first, last = b == 0, b == d.blocks - 1

        @pl.when(first & (p == 0))
        def _():
            r.load()
            r.nodes[...] = r.n_own[...]
            r.w1bt[...] = r.uw1[1, d.feat : 2 * d.feat, :].T
            r.w2h[...] = half_of(r.uw2[1])
            r.w2t[...] = r.w2h[...].T
            r.w3h[...] = half_of(r.uw3[1])
            load_cols(r, 1, r.aux, r.cols)
            centre_weights(r.uw3[1], r.cols[...], r.w3c, r.w3c_b)
            r.gain_mat[...] = gain_matrix(r.cols[...])
            zero(r.upd, r.a_w23, r.a_b9, r.a_g2)
            r.pair[3 * d.feat :] = jnp.ones((16, d.rows), BF)
            r.tt[d.length :, :] = r.rt[: d.res]
            r.tn[:, d.length :] = r.rt[...].T

        @pl.when(first)
        def _():
            r.n_cat[: d.half] = r.n_own[p]
            r.n_cat[d.half :] = r.n_got[p]
            put_table(d, r.lhs, 0, 0, r.n_cat, r.uw1.at[1])
            zero(r.a_s)

        r.ready()
        f = d.feat
        n_blk = r.n_own[p, pl.ds(pl.multiple_of(b * d.res, d.res), d.res), :]
        put_own(d, r.lhs, 0, 0, r.uw1.at[1], n_blk, r.cols[:, 4:5])
        idx = r.idx[p, b]
        put_one_hot(d, r.tt, 0, idx)
        put_one_hot_rows(d, r.tn, idx)
        e2 = r.e2[...]
        r.pair[:f] = e2
        a1 = mm(r.lhs[...], r.tt[...]) + mm(r.w1bt[...], e2)
        g1, d1, _, d2, xh, rs, y = update_forward(
            d, a1, r.w2t[...], r.w3c, r.cols[:, 5:6], r.w3c_b[:, 0:1], r.pair, r.cols
        )
        r.pair[2 * f : 3 * f] = g1
        r.decoded[...] = y.T.reshape(d.res, d.near, f)
        dy = r.cot[...].reshape(d.rows, f).T
        dr3 = norm_backward(d, r, dy, xh, rs, r.gain_mat[...])
        update_backward(d, r, dr3, r.pair[f:], d1, d2, r.w2h[...], r.w3h[...], r.low, r.da1)
        r.upd[f : 2 * f] += mm(e2, r.da1[...], 1, 1)
        r.part[...] = (mm(r.uw1[1, f : 2 * f, :], r.da1[...]) + dr3.astype(F32)).astype(BF)
        spread = mm(r.da1[...], r.tn[...])
        r.a_s[...] += spread[:, : d.length]
        r.a_k[b] = spread[:, d.length :]
        r.flush()

        @pl.when(last)
        def _():
            own, far, b4 = spread_nodes(
                d, r.a_s[...], [r.a_k[i] for i in range(d.blocks)], r.uw1[1], r.n_cat[...], r.upd, 0
            )
            r.dn_own[p] = own
            r.dn_far[p] = far.astype(BF)
            update_small(d, r, b4)

    return ph.call("dec_update", body)


AUX_W = ("bias", "gain")


def message_backward(d, r, b, layer, low):
    at = pl.ds(pl.multiple_of(b * d.res, d.res), d.res)
    v = (mm(r.mw3[layer], r.dub[pl.program_id(0), at, :], 1, 1) * 0.5).astype(BF)
    f = d.feat
    low[:f] = mm(v, r.rt[: d.res]).astype(BF) * r.d2[...]
    low[f:] = mm(r.mw2h[...], low[:f]).astype(BF) * r.d1[...]


def message_small(d, r, b0):
    r.msg[d.at_small : d.at_small + 1] += b0


def middle_backward(d, edge_input, st, fa, fb, fd, cot_n, consts):
    ph = Phase(d, 4)
    ph.raw(dn_far_in=fd.dn_far)
    ph.whole(cot_n=cot_n, dn_a=fd.dn_own, n_own=fa.node_out, got_a=fa.got, got_b=fb.got_in)
    ph.whole(mask=consts.mask, rt=consts.sums, r1=fb.r1, ip=fb.ip, r2=fb.r2, big=fb.big, cnt=fb.cnt)
    ph.whole(urs=fb.urs, idx=consts.idx)
    ph.stream(d2=fb.d2, d1=fb.d1, e2g=fb.e2g, dec_part=fd.part, uxh=fb.uxh, ugs=fb.ugs, ud2=fb.ud2, ud1=fb.ud1)
    ph.edges(edge=edge_input)
    ph.whole(**weight_args(st, *NODE_W, *MSG_W, *UPD_W))
    ph.out_stream(BF, part=(d.parts, d.blocks, d.feat, d.rows))
    ph.out_whole(F32, msg=(d.msg_rows, d.feat), upd=(d.upd_rows, d.feat), dn_own=(d.parts, d.half, d.feat))
    ph.out_raw(BF, got=(d.parts, d.half, d.feat))
    sq = (d.feat, d.feat)
    ph.temp(BF, n_cat=(d.length, d.feat), dub=(d.parts, d.half, d.feat), tt=(d.length + d.res, d.rows))
    ph.temp(BF, tri=(3 * d.feat, d.rows), low=(2 * d.feat, d.rows), w2h=sq, w3h=sq, mw2h=sq, gain_mat=sq)
    ph.temp(BF, leave=(d.parts, d.half, d.feat), arrive=(d.parts, d.half, d.feat))
    ph.temp(F32, dr1=(d.parts, d.half, d.feat), e_aux=sq, e_cols=sq, d_aux=sq, d_cols=sq)
    tall = (2 * d.feat + 16, 2 * d.feat)
    ph.temp(F32, m_w12=tall, a_w23=tall, a_b9=sq, a_g2=sq, a_w1=sq)
    ph.temp(F32, a_s=(2 * d.feat, d.length), a_k=(d.blocks, 2 * d.feat, 128))
    ph.sems(send=2 * d.parts, recv=2 * d.parts)

    def body(r):
        p, b = pl.program_id(0), pl.program_id(1)
        first, last = b == 0, b == d.blocks - 1
        n = d.parts
        early = [to_partner(r.dn_far_in.at[i], r.arrive.at[i], r.send.at[n + i], r.recv.at[n + i]) for i in range(n)]
        jobs = [to_partner(r.leave.at[i], r.got.at[i], r.send.at[i], r.recv.at[i]) for i in range(n)]

        @pl.when(first & (p == 0))
        def _():
            greet_partner()
            for job in early:
                job.start()
            r.load()
            load_cols(r, 0, r.e_aux, r.e_cols)
            load_cols(r, 1, r.d_aux, r.d_cols)
            r.tt[d.length :, :] = r.rt[: d.res]
            r.w2h[...] = half_of(r.uw2[0])
            r.w3h[...] = half_of(r.uw3[0])
            r.mw2h[...] = half_of(r.mw2[1])
            r.gain_mat[...] = gain_matrix(r.e_cols[...])
            zero(r.msg, r.upd, r.m_w12, r.a_w23, r.a_b9, r.a_g2, r.a_w1)
            r.n_cat[d.half :] = r.got_a[...]

        @pl.when(first & (p == 1))
        def _():
            r.n_cat[d.half :] = r.got_b[...]

        for i in range(n):

            @pl.when(first & (p == i))
            def _(i=i):
                early[i].wait()

        @pl.when(first)
        def _():
            r.n_cat[: d.half] = r.n_own[p]
            zero(r.a_s)
            dn = r.cot_n[p].astype(F32) + r.dn_a[p] + r.arrive[p].astype(F32)
            node_backward(d, r, p, 1, r.d_aux[...], dn)

        f = d.feat
        r.ready()
        put_one_hot(d, r.tt, 0, r.idx[p, b])
        message_backward(d, r, b, 1, r.tri.at[: 2 * f])
        r.m_w12[...] += mm(r.e2g[...], r.tri[: 2 * f], 1, 1)
        de = mm(r.mw1[1, f : 2 * f, :], r.tri[f : 2 * f])
        dy = (de + r.dec_part[...].astype(F32)).astype(BF)
        dr3 = norm_backward(d, r, dy, r.uxh[...], r.urs[p, b], r.gain_mat[...])
        da1 = r.tri.at[2 * f :]
        update_backward(d, r, dr3, r.ugs[...], r.ud1[...], r.ud2[...], r.w2h[...], r.w3h[...], r.low, da1)
        r.a_w1[...] += mm(da1[...], r.edge[...].reshape(d.rows, f))
        r.part[...] = (mm(r.uw1[0, f : 2 * f, :], da1[...]) + dr3.astype(F32)).astype(BF)
        spread = mm(r.tri[f:], r.tt[...], 1, 1)
        r.a_s[...] += spread[:, : d.length]
        r.a_k[b, :, : d.res] = spread[:, d.length :]
        r.flush()

        @pl.when(last)
        def _():
            n_cat = r.n_cat[...]
            a_k = [r.a_k[i] for i in range(d.blocks)]
            own_m, far_m, b0 = spread_nodes(
                d, r.a_s[: d.feat], [x[: d.feat] for x in a_k], r.mw1[1], n_cat, r.msg, 0
            )
            own_u, far_u, b4 = spread_nodes(
                d, r.a_s[d.feat :], [x[d.feat :] for x in a_k], r.uw1[0], n_cat, r.upd, 0
            )
            r.dn_own[p] = own_m + own_u + r.dr1[p]
            r.leave[p] = (far_m + far_u).astype(BF)
            for i in range(n):

                @pl.when(p == i)
                def _(i=i):
                    jobs[i].start()

            message_small(d, r, b0)
            update_small(d, r, b4)

            @pl.when(p == n - 1)
            def _():
                f, at = d.feat, d.at_small
                r.upd[f : 2 * f] = r.a_w1[...].T
                r.msg[f : 2 * f] = r.m_w12[:f, f:]
                r.msg[3 * f : 4 * f] = 0.5 * r.m_w12[f : 2 * f, :f]
                r.msg[at + 1 : at + 2] = r.m_w12[2 * f : 2 * f + 1, :f]
                for job in jobs:
                    job.wait()

    return ph.call("dec_message_back", body)


def encoder_message_back(d, edge_input, st, fa, fe, n_own, n_got, consts):
    ph = Phase(d)
    ph.whole(dn_a=fe.dn_own, dn_b=fe.got, n_own=n_own, n_got=n_got)
    ph.whole(mask=consts.mask, rt=consts.sums, r1=fa.r1, ip=fa.ip, r2=fa.r2, big=fa.big, cnt=fa.cnt)
    ph.whole(idx=consts.idx)
    ph.stream(d2=fa.d2, g1=fa.g1, d1=fa.d1, up_part=fe.part)
    ph.edges(edge=edge_input)
    ph.whole(**weight_args(st, *NODE_W, *MSG_W))
    ph.out_edges(edge_grad=edge_input.shape)
    ph.out_whole(F32, msg=(d.msg_rows, d.feat), dn_own=(d.parts, d.half, d.feat))
    ph.out_whole(BF, dn_far=(d.parts, d.half, d.feat))
    sq = (d.feat, d.feat)
    ph.temp(BF, n_cat=(d.length, d.feat), dub=(d.parts, d.half, d.feat), tn=(d.rows, d.length + 128))
    ph.temp(BF, low=(2 * d.feat, d.rows), mw2h=sq)
    ph.temp(F32, dr1=(d.parts, d.half, d.feat), aux=sq, cols=sq, a_w1=sq, m_w2=(d.feat + 16, d.feat))
    ph.temp(F32, a_s=(d.feat, d.length), a_k=(d.blocks, d.feat, 128))

    def body(r):
        p, b = pl.program_id(0), pl.program_id(1)
        first, last = b == 0, b == d.blocks - 1

        @pl.when(first & (p == 0))
        def _():
            r.load()
            load_cols(r, 0, r.aux, r.cols)
            r.tn[:, d.length :] = r.rt[...].T
            r.mw2h[...] = half_of(r.mw2[0])
            zero(r.msg, r.m_w2, r.a_w1)
            dn = r.dn_a[...] + r.dn_b[...].astype(F32)
            node_backward(d, r, None, 0, r.aux[...], dn.reshape(-1, d.feat))

        @pl.when(first)
        def _():
            r.n_cat[: d.half] = r.n_own[p]
            r.n_cat[d.half :] = r.n_got[p]
            zero(r.a_s)

        f = d.feat
        r.ready()
        put_one_hot_rows(d, r.tn, r.idx[p, b])
        message_backward(d, r, b, 0, r.low)
        da1 = r.low.at[f:]
        r.m_w2[...] += mm(r.g1[...], r.low[:f], 1, 1)
        r.a_w1[...] += mm(da1[...], r.edge[...].reshape(d.rows, f))
        de = mm(r.mw1[0, f : 2 * f, :], da1[...])
        de = (de + r.up_part[...].astype(F32)).astype(BF)
        r.edge_grad[...] = de.T.reshape(d.res, d.near, f)
        spread = mm(da1[...], r.tn[...])
        r.a_s[...] += spread[:, : d.length]
        r.a_k[b] = spread[:, d.length :]
        r.flush()

        @pl.when(last)
        def _():
            own, far, b0 = spread_nodes(
                d, r.a_s[...], [r.a_k[i] for i in range(d.blocks)], r.mw1[0], r.n_cat[...], r.msg, 0
            )
            r.dn_own[p] = own + r.dr1[p]
            r.dn_far[p] = far.astype(BF)
            message_small(d, r, b0)

            @pl.when(p == d.parts - 1)
            def _():
                f, at = d.feat, d.at_small
                r.msg[f : 2 * f] = r.a_w1[...].T
                r.msg[3 * f : 4 * f] = 0.5 * r.m_w2[:f]
                r.msg[at + 1 : at + 2] = r.m_w2[f : f + 1]

    return ph.call("enc_message_back", body)


class Reducer:
    def __init__(self, devices, feat, shares):
        self.feat = feat
        self.bits = bits = devices.bit_length() - 1
        self.groups = [16 * devices * share for share in shares]
        self.rows = sum(self.groups)
        self.bases = [sum(self.groups[:i]) for i in range(len(shares))]
        pairs, top = [], bits
        while top > 1:
            low = max(1, top - 2)
            pairs.insert(0, (low, top - low))
            top = low
        dims = [ACROSS] + pairs
        turn = min(3, len(dims))
        self.plans = []
        for g, size in enumerate(self.groups):
            head = dims[:turn]
            order = ([(0, 1)] if bits else []) + head[g % turn :] + head[: g % turn] + dims[turn:]
            both, plan = True, []
            for dim in order:
                if dim == ACROSS:
                    both = False
                else:
                    size >>= dim[1]
                plan.append((dim, size, both))
            self.plans.append(plan)
        self.backs = [[step for step in reversed(plan) if step[0] != ACROSS] for plan in self.plans]
        self.halving = len(self.plans[0])
        self.stages = self.halving + len(self.backs[0])
        self.dims = ([(0, 1)] if bits else []) + dims
        self.sem_at, self.buffer_at, self.shapes = {}, {}, []
        for g, plan in enumerate(self.plans):
            for k, (dim, size, both) in enumerate(plan):
                for o in self.offsets(dim):
                    self.sem_at[(g, k, o)] = len(self.sem_at)
                    self.buffer_at[(g, k, o)] = len(self.shapes)
                    self.shapes += [(2, size, feat) if both else (size, feat)] * 2
            for k, (dim, _, _) in enumerate(self.backs[g]):
                for o in self.offsets(dim):
                    self.sem_at[(g, self.halving + k, o)] = len(self.sem_at)

    def scratch(self):
        temps = [pltpu.VMEM((2, self.rows, self.feat), F32), pltpu.VMEM((self.rows, self.feat), BF)]
        temps += [pltpu.VMEM(shape, BF) for shape in self.shapes]
        return temps + [pltpu.SemaphoreType.DMA((len(self.sem_at),))] * 2

    def bind(self, refs):
        self.acc, self.gathered = refs[:2]
        self.buffers, (self.send, self.recv) = refs[2:-2], refs[-2:]

    def offsets(self, dim):
        return range(1, 2 if dim == ACROSS else 1 << dim[1])

    def code(self, dim):
        return lax.rem(lax.axis_index(AXIS_D) // (1 << dim[0]), 1 << dim[1])

    def peer(self, dim, o):
        if dim == ACROSS:
            return other_section()
        code = self.code(dim)
        other = lax.rem(code + o, 1 << dim[1])
        return {AXIS_D: lax.axis_index(AXIS_D) + (other - code) * (1 << dim[0])}

    def greet(self):
        barrier = pltpu.get_barrier_semaphore()
        count = 0
        for dim in self.dims:
            for o in self.offsets(dim):
                pl.semaphore_signal(barrier, inc=1, device_id=self.peer(dim, o), device_id_type=MESH)
                count += 1
        pl.semaphore_wait(barrier, count)

    def begin(self, g, k):
        start = self.bases[g]
        for dim, size, _ in self.plans[g][:k]:
            if dim != ACROSS:
                start = start + self.code(dim) * size
        return start

    def span(self, start, size):
        return pl.ds(pl.multiple_of(start, 16), size)

    def job(self, src, dst, key, dim):
        at = self.sem_at[key]
        return pltpu.make_async_remote_copy(
            src_ref=src, dst_ref=dst, send_sem=self.send.at[at], recv_sem=self.recv.at[at],
            device_id=self.peer(dim, key[2]), device_id_type=MESH,
        )

    def jobs(self, g, k):
        plan = self.plans[g]
        if k < self.halving:
            out = []
            for o in self.offsets(plan[k][0]):
                at = self.buffer_at[(g, k, o)]
                out.append(self.job(self.buffers[at], self.buffers[at + 1], (g, k, o), plan[k][0]))
            return out
        dim, size, _ = self.backs[g][k - self.halving]
        start = self.begin(g, [step[0] for step in plan].index(dim) + 1)
        part = self.gathered.at[self.span(start, size), :]
        return [self.job(part, part, (g, k, o), dim) for o in self.offsets(dim)]

    def start(self, g, k):
        section = lax.axis_index(AXIS_S)
        plan = self.plans[g]
        if k < self.halving:
            dim, size, both = plan[k]
            start = self.begin(g, k)
            for o in self.offsets(dim):
                out = self.buffers[self.buffer_at[(g, k, o)]]
                if dim == ACROSS:
                    out[...] = self.acc[1 - section, self.span(start, size), :].astype(BF)
                    continue
                give = self.span(start + lax.rem(self.code(dim) + o, 1 << dim[1]) * size, size)
                if both:
                    out[...] = self.acc[:, give, :].astype(BF)
                else:
                    out[...] = self.acc[section, give, :].astype(BF)
        elif k == self.halving:
            keep = self.span(self.begin(g, self.halving), plan[-1][1])
            self.gathered[keep, :] = self.acc[section, keep, :].astype(BF)
        for job in self.jobs(g, k):
            job.start()

    def finish(self, g, k):
        section = lax.axis_index(AXIS_S)
        for job in self.jobs(g, k):
            job.wait()
        if k >= self.halving:
            return
        dim, size, both = self.plans[g][k]
        keep = self.span(self.begin(g, k + 1), size)
        for o in self.offsets(dim):
            into = self.buffers[self.buffer_at[(g, k, o)] + 1]
            if both:
                self.acc[:, keep, :] += into[...].astype(F32)
            else:
                self.acc[section, keep, :] += into[...].astype(F32)

    def run(self):
        count = len(self.plans)
        for g in range(count):
            self.start(g, 0)
        for k in range(self.stages):
            for g in range(count):
                self.finish(g, k)
                if k + 1 < self.stages:
                    self.start(g, k + 1)
        if self.stages == self.halving:
            self.gathered[...] = self.acc[lax.axis_index(AXIS_S)].astype(BF)


ACROSS = (-1, 0)


def reduce_grads(d, enc_msg, enc_upd, dec_msg, dec_upd, dn_far):
    m, u = d.msg_rows, d.upd_rows
    units = -(-(m + u) // (16 * d.devices))
    red = Reducer(d.devices, d.feat, [2] * (units // 2) + [1] * (units % 2))

    def kernel(em, eu, dm, du, far, res, got, far_sems, load_sems, *refs):
        red.bind(refs)
        loads = []
        for layer, (msg, upd) in enumerate(((em, eu), (dm, du))):
            spots = (red.acc.at[layer, pl.ds(0, m)], red.acc.at[layer, pl.ds(m, u)])
            for i, (src, dst) in enumerate(zip((msg, upd), spots)):
                loads.append(pltpu.make_async_copy(src, dst, load_sems.at[2 * layer + i]))
        for item in loads:
            item.start()
        if red.rows > m + u:
            red.acc[:, m + u :] = jnp.zeros((2, red.rows - m - u, d.feat), F32)
        red.greet()
        nodes = to_partner(far, got, far_sems.at[0], far_sems.at[1])
        nodes.start()
        for item in loads:
            item.wait()
        red.run()
        res[...] = red.gathered[...]
        nodes.wait()

    vm, anywhere = pl.BlockSpec(memory_space=pltpu.VMEM), pl.BlockSpec(memory_space=pl.ANY)
    return pl.pallas_call(
        kernel,
        in_specs=[anywhere] * 5,
        out_specs=[vm, anywhere],
        out_shape=[jax.ShapeDtypeStruct((red.rows, d.feat), BF), jax.ShapeDtypeStruct(dn_far.shape, BF)],
        scratch_shapes=[pltpu.SemaphoreType.DMA((2,)), pltpu.SemaphoreType.DMA((4,))] + red.scratch(),
        compiler_params=pltpu.CompilerParams(vmem_limit_bytes=58 << 20, collective_id=5, has_side_effects=True),
        name="reduce",
    )(enc_msg, enc_upd, dec_msg, dec_upd, dn_far)


def unpack(d, total, dn_own, dn_got, n_bias, n_gain):
    f = d.feat
    m = d.msg_rows
    shapes = [(1, 3 * f, f), (1, f, f), (1, f, f), (1, f, d.wide), (1, 1, d.wide), (1, d.wide, f)]
    shapes += [(1, 3 * f, f), (1, f, f), (1, f, f), (n_bias, 1, f), (n_gain, 1, f)]

    def kernel(t, own, got, node, mw1, mw2, mw3, inner, inner_b, outer, uw1, uw2, uw3, bias, gain):
        node[...] = (own[...] + got[...].astype(F32)).astype(BF)
        for ref, at in ((mw1, 0), (mw2, 3 * f), (mw3, 4 * f), (outer, d.at_outer)):
            ref[0] = t[at : at + ref.shape[1], :].astype(F32)
        for ref, at in ((uw1, m), (uw2, m + 3 * f), (uw3, m + 4 * f)):
            ref[0] = t[at : at + ref.shape[1], :].astype(F32)
        inner[0] = t[d.at_inner : d.at_inner + d.wide, :].astype(F32).T
        small = t[d.at_small : d.at_small + SMALL, :].astype(F32)
        other = t[m + 5 * f : m + 5 * f + SMALL, :].astype(F32)
        both = small + other
        for i in range(n_bias):
            bias[i] = both[i : i + 1]
        for i in range(n_gain):
            gain[i] = both[n_bias + i : n_bias + i + 1]
        for i in range(d.wide // f):
            inner_b[0, :, i * f : (i + 1) * f] = small[16 + i : 17 + i]

    vm = pl.BlockSpec(memory_space=pltpu.VMEM)
    out = [jax.ShapeDtypeStruct(dn_own.shape, BF)] + [jax.ShapeDtypeStruct(s, F32) for s in shapes]
    return pl.pallas_call(kernel, in_specs=[vm] * 3, out_specs=[vm] * len(out), out_shape=out, name="unpack")(
        total, dn_own, dn_got
    )


def per_device(
    node_input,
    edge_input,
    neighbors,
    residue_mask,
    decode_order,
    node_cotangent,
    edge_cotangent,
    message_w1,
    message_w2,
    message_w3,
    inner_w,
    inner_bias,
    outer_w,
    update_w1,
    update_w2,
    update_w3,
    biases,
    norm_gains,
):
    parts, half, near, feat = edge_input.shape
    length = neighbors.shape[1]
    wide = inner_w.shape[2]
    res = BLOCK_RES
    rows = res * near
    blocks = half // res
    at_outer = 5 * feat
    at_inner = at_outer + wide
    at_small = at_inner + wide
    d = types.SimpleNamespace(
        parts=parts, half=half, near=near, feat=feat, length=length, wide=wide, res=res, rows=rows, blocks=blocks,
        at_outer=at_outer, at_inner=at_inner, at_small=at_small, msg_rows=at_small + SMALL,
        upd_rows=5 * feat + SMALL, devices=lax.axis_size(AXIS_D),
    )
    weights = dict(
        mw1=message_w1[0], mw2=message_w2[0], mw3=message_w3[0], inner=inner_w[0], inner_b=inner_bias, outer=outer_w[0],
        uw1=update_w1[0], uw2=update_w2[0], uw3=update_w3[0],
        bias=biases.transpose(1, 0, 2), gain=norm_gains.transpose(1, 0, 2),
    )
    sums = np.zeros((128, rows), np.float32)
    sums[np.arange(rows) // near, np.arange(rows)] = 1.0
    pick = (np.arange(rows)[None, :] % near == np.arange(near)[:, None]).astype(np.float32)
    consts = types.SimpleNamespace(sums=jnp.asarray(sums, BF), pick=jnp.asarray(pick, BF))
    fa = encoder_message(
        d, edge_input, node_input, neighbors.transpose(0, 2, 1), residue_mask, decode_order, weights, consts
    )
    consts.idx, consts.mask = fa.idx, fa.mask
    st = types.SimpleNamespace(**{n: getattr(fa, W_OUT + n) for n in weights})
    fb = encoder_update(d, edge_input, st, fa, consts)
    fd = decoder_update(d, st, fb, edge_cotangent, consts)
    fe = middle_backward(d, edge_input, st, fa, fb, fd, node_cotangent, consts)
    ff = encoder_message_back(d, edge_input, st, fa, fe, node_input, fa.nodes_got, consts)
    total, got = reduce_grads(d, ff.msg, fe.upd, fe.msg, fd.upd, ff.dn_far)
    node_grad, mw1, mw2, mw3, inner, inner_b, outer, uw1, uw2, uw3, bias, gain = unpack(
        d, total, ff.dn_own, got, biases.shape[1], norm_gains.shape[1]
    )
    return (
        fd.nodes, fd.decoded, node_grad, ff.edge_grad, mw1, mw2, mw3, inner, inner_b[:, 0], outer,
        uw1, uw2, uw3, bias.transpose(1, 0, 2), gain.transpose(1, 0, 2),
    )


def solution(mesh):
    def split(*axes):
        return P(*axes)

    by_part = split(AXIS_D)
    by_half = split(AXIS_D, AXIS_S)
    by_layer = split(AXIS_S)
    in_specs = (by_half, by_half, by_part, by_part, by_part, by_half, by_half) + (by_layer,) * 11
    out_specs = (by_half,) * 4 + (by_layer,) * 11
    return jax.shard_map(per_device, mesh=mesh, in_specs=in_specs, out_specs=out_specs, check_vma=False)
```

```python
import types

import jax
import jax.numpy as jnp
import numpy as np
from jax import lax
from jax.experimental import pallas as pl
from jax.experimental.pallas import tpu as pltpu
from jax.sharding import PartitionSpec as P

BF = jnp.bfloat16
F32 = jnp.float32
C1 = 0.7978845608
C2 = C1 * 0.044715
EPS = 1e-5
BLOCK_RES = 96
EXTRA = 16
SMALL = 32
MESH = pl.DeviceIdType.MESH


def mm(a, b, ca=1, cb=0):
    return lax.dot_general(a, b, (((ca,), (cb,)), ((), ())), preferred_element_type=F32)


def mm_exact(a, b, ca=1, cb=0):
    return lax.dot_general(
        a, b, (((ca,), (cb,)), ((), ())), precision=lax.Precision.HIGHEST, preferred_element_type=F32
    )


def gelu_pair(x):
    x = x.astype(BF)
    w = x * x * BF(C2)
    h = jnp.tanh(x * (w + BF(C1))) + BF(1.0)
    g = x * h
    d = h + g * (BF(2.0) - h) * (w * BF(3.0) + BF(C1))
    return g, d


def gelu_pair_wide(x):
    x2 = x * x
    h = 0.5 * jnp.tanh(x * (x2 * C2 + C1)) + 0.5
    g = x * h
    d = h + (g * (1.0 - h)) * (x2 * (6 * C2) + 2 * C1)
    return g, d


def lane_sum(x):
    total = x[:, :128]
    for at in range(128, x.shape[1], 128):
        total = total + x[:, at : at + 128]
    return total


def to_row(acc):
    return mm_exact(jnp.ones((8, acc.shape[1]), F32), acc, 1, 1)[0:1]


def norm_rows(r):
    c = r - jnp.mean(r, axis=-1, keepdims=True)
    rs = lax.rsqrt(jnp.mean(c * c, axis=-1, keepdims=True) + EPS)
    return c * rs, rs


def norm_back_rows(dxh, xh, rs):
    m1 = jnp.mean(dxh, axis=-1, keepdims=True)
    m2 = jnp.mean(dxh * xh, axis=-1, keepdims=True)
    return (dxh - m1 - xh * m2) * rs


def norm_back(dy, xh, rs, gain_col):
    dxh = dy * gain_col
    m1 = jnp.mean(dxh, axis=0, keepdims=True)
    m2 = jnp.mean(dxh * xh, axis=0, keepdims=True)
    return (dxh - m1 - xh * m2) * rs


class Phase:
    def __init__(self, dims, collective_id=None):
        self.d = dims
        self.collective_id = collective_id
        self.ins, self.outs, self.temps, self.kinds, self.wholes, self.later = [], [], [], {}, {}, ()

    def whole_spec(self, shape):
        rank = len(shape)
        return pl.BlockSpec(tuple(shape), lambda p, b: (0,) * rank)

    def whole(self, **arrays):
        self.raw(**arrays)
        self.wholes.update({n: pltpu.VMEM(a.shape, a.dtype) for n, a in arrays.items()})

    def raw(self, **arrays):
        self.ins += [(n, a, pl.BlockSpec(memory_space=pl.ANY)) for n, a in arrays.items()]

    def stream(self, **arrays):
        self.raw(**arrays)
        self.kinds.update({n: (False, False, a.shape[2:], a.dtype) for n, a in arrays.items()})

    def stream_top(self, rows, **arrays):
        self.raw(**arrays)
        self.kinds.update({n: (False, False, (rows,) + a.shape[3:], a.dtype) for n, a in arrays.items()})

    def edges(self, **arrays):
        self.raw(**arrays)
        block = (self.d.res, self.d.near, self.d.feat)
        self.kinds.update({n: (False, True, block, a.dtype) for n, a in arrays.items()})

    def out_whole(self, dtype, **shapes):
        self.outs += [(n, jax.ShapeDtypeStruct(s, dtype), self.whole_spec(s)) for n, s in shapes.items()]

    def out_raw(self, dtype, **shapes):
        spec = pl.BlockSpec(memory_space=pl.ANY)
        self.outs += [(n, jax.ShapeDtypeStruct(s, dtype), spec) for n, s in shapes.items()]

    def out_stream(self, dtype, **shapes):
        self.out_raw(dtype, **shapes)
        self.kinds.update({n: (True, False, s[2:], dtype) for n, s in shapes.items()})

    def out_edges(self, **shapes):
        self.out_raw(BF, **shapes)
        block = (self.d.res, self.d.near, self.d.feat)
        self.kinds.update({n: (True, True, block, BF) for n in shapes})

    def temp(self, dtype, **shapes):
        self.temps += [(n, pltpu.VMEM(s, dtype)) for n, s in shapes.items()]

    def sems(self, **counts):
        self.temps += [(n, pltpu.SemaphoreType.DMA((c,))) for n, c in counts.items()]

    def call(self, name, body):
        d = self.d
        names = [n for n, _, _ in self.ins] + [n for n, _, _ in self.outs] + [n for n, _ in self.temps]
        steps = d.parts * d.blocks
        buffers = [pltpu.VMEM((2,) + tuple(block), dtype) for _, _, block, dtype in self.kinds.values()]
        count = len(self.kinds)

        def kernel(*refs):
            refs, rest = refs[: len(names)], refs[len(names) :]
            slots, sems, kept = rest[:count], rest[count : 2 * count], rest[2 * count : -1]
            plain = dict(zip(names, refs))
            step = pl.program_id(0) * d.blocks + pl.program_id(1)
            now = lax.rem(step, 2)

            def copy(i, n, at, slot):
                out, edges, block, _ = self.kinds[n]
                p, b = at // d.blocks, lax.rem(at, d.blocks)
                if edges:
                    far = plain[n].at[p, pl.ds(pl.multiple_of(b * d.res, d.res), d.res)]
                elif block[0] < plain[n].shape[2]:
                    far = plain[n].at[p, b, pl.ds(0, block[0])]
                else:
                    far = plain[n].at[p, b]
                near = slots[i].at[slot]
                return pltpu.make_async_copy(*((near, far) if out else (far, near)), sems[i].at[slot])

            into = [(i, n) for i, n in enumerate(self.kinds) if not self.kinds[n][0]]
            outof = [(i, n) for i, n in enumerate(self.kinds) if self.kinds[n][0]]

            def loads():
                return [
                    pltpu.make_async_copy(plain[n], kept[i], rest[-1].at[i]) for i, n in enumerate(self.wholes)
                ]

            def load(*later):
                for item, n in zip(loads(), self.wholes):
                    if (n in later) if later else (n not in self.later):
                        item.wait()

            @pl.when(step == 0)
            def _():
                for item in loads():
                    item.start()
                for i, n in into:
                    copy(i, n, step, now).start()

            @pl.when(step + 1 < steps)
            def _():
                for i, n in into:
                    copy(i, n, step + 1, 1 - now).start()

            @pl.when(step >= 2)
            def _():
                for i, n in outof:
                    copy(i, n, step - 2, now).wait()

            def ready():
                for i, n in into:
                    copy(i, n, step, now).wait()

            def flush():
                for i, n in outof:
                    copy(i, n, step, now).start()

            plain_or_slot = dict(plain, ready=ready, flush=flush, load=load)
            plain_or_slot.update(zip(self.wholes, kept))
            plain_or_slot.update({n: slots[i].at[now] for i, n in enumerate(self.kinds)})
            body(types.SimpleNamespace(**plain_or_slot))

            @pl.when(step == steps - 1)
            def _():
                for i, n in outof:
                    if steps > 1:
                        copy(i, n, step - 1, 1 - now).wait()
                    copy(i, n, step, now).wait()

        results = pl.pallas_call(
            kernel,
            grid=(d.parts, d.blocks),
            in_specs=[s for _, _, s in self.ins],
            out_specs=[s for _, _, s in self.outs],
            out_shape=[s for _, s, _ in self.outs],
            scratch_shapes=[s for _, s in self.temps] + buffers
            + [pltpu.SemaphoreType.DMA((2,))] * count
            + list(self.wholes.values())
            + [pltpu.SemaphoreType.DMA((len(self.wholes),))],
            compiler_params=pltpu.CompilerParams(
                dimension_semantics=(pltpu.ARBITRARY,) * 2,
                vmem_limit_bytes=60 << 20,
                collective_id=self.collective_id,
                has_side_effects=self.collective_id is not None,
            ),
            name=name,
        )(*[a for _, a, _ in self.ins])
        return types.SimpleNamespace(**dict(zip([n for n, _, _ in self.outs], results)))


def other_section():
    return {AXIS_S: 1 - lax.axis_index(AXIS_S)}


AXIS_S = "section"
AXIS_D = "dp"


def greet_partner():
    barrier = pltpu.get_barrier_semaphore()
    pl.semaphore_signal(barrier, inc=1, device_id=other_section(), device_id_type=MESH)
    pl.semaphore_wait(barrier, 1)


def to_partner(src, dst, send, recv):
    return pltpu.make_async_remote_copy(
        src_ref=src, dst_ref=dst, send_sem=send, recv_sem=recv, device_id=other_section(), device_id_type=MESH
    )


def put_one_hot(d, ref, at, idx):
    idx = idx.astype(jnp.int16)
    place = lax.broadcasted_iota(jnp.int16, (d.length, d.rows), 0)
    ref[at : at + d.length, :] = jnp.where(place == idx, jnp.ones((), BF), jnp.zeros((), BF))


def put_one_hot_rows(d, ref, idx):
    centre = d.length // 2
    idx = jnp.broadcast_to((idx - centre).astype(F32).astype(BF), (128, d.rows)).T
    place = lax.broadcasted_iota(jnp.int32, (d.rows, 128), 1)
    for at in range(0, d.length, 128):
        there = (place + (at - centre)).astype(F32).astype(BF)
        ref[:, at : at + 128] = jnp.where(idx == there, jnp.ones((), BF), jnp.zeros((), BF))


def weight_args(w, *names):
    return {n: getattr(w, n) for n in names}


def load_cols(r, layer, aux, cols):
    n_bias, n_gain = r.bias.shape[1], r.gain.shape[1]
    aux[...] = jnp.zeros(aux.shape, F32)
    for i in range(n_bias):
        aux[i : i + 1] = r.bias[layer, i]
    for i in range(n_gain):
        aux[n_bias + i : n_bias + i + 1] = r.gain[layer, i]
    cols[...] = aux[...].T


def put_table(d, lhs, at, left, n_cat, w1):
    lhs[at : at + d.feat, left : left + d.length] = mm(w1[2 * d.feat :, :].T, n_cat[...], 1, 1).astype(BF)


def put_own(d, lhs, at, left, w1, n_blk, bias_col):
    own = mm(w1[0 : d.feat, :].T, n_blk, 1, 1) + bias_col
    lhs[at : at + d.feat, left + d.length :] = own.astype(BF)


def message_part(a1, w2t, b2, att, kept):
    g1, d1 = gelu_pair(a1)
    a2 = mm(w2t, g1) + b2
    g2, d2 = gelu_pair(a2)
    attb = att.astype(BF)
    feat, rows = g2.shape
    kept[:feat] = g2 * attb
    kept[feat:] = jnp.broadcast_to(attb, (16, rows))
    return g1, d1, d2 * attb


def add_node_outs(ph, d):
    ph.out_whole(BF, node_out=(d.parts, d.half, d.feat))
    shape = (d.parts, d.half, d.feat)
    ph.out_whole(F32, r1=shape, ip=(d.parts, d.half, d.wide), r2=shape, big=shape, cnt=shape)


def node_step(d, r, p, b):
    sums = mm(r.rt[: d.res], r.kept[...], 1, 1)
    at = pl.ds(pl.multiple_of(b * d.res, d.res), d.res)
    r.big[p, at, :] = sums[:, : d.feat] * 0.5
    r.cnt[p, at, :] = jnp.broadcast_to(sums[:, d.feat : d.feat + 1], (d.res, d.feat))


def node_forward(r, p, n_own, layer, aux):
    big = r.big[p]
    hi = big.astype(BF)
    lo = (big - hi.astype(F32)).astype(BF)
    w3 = r.mw3[layer]
    upd = (mm(hi, w3) + mm(lo, w3) + r.cnt[p] * aux[2:3]) / 30.0
    r1 = n_own.astype(F32) + upd
    xh1, _ = norm_rows(r1)
    normed = xh1 * aux[10:11] + aux[7:8]
    ip = mm(normed.astype(BF), r.inner[layer]) + r.inner_b[layer]
    hid = gelu_pair_wide(ip)[0].astype(BF)
    r2 = normed + (mm(hid, r.outer[layer]) + aux[3:4])
    xh2, _ = norm_rows(r2)
    out = ((xh2 * aux[11:12] + aux[8:9]) * r.mask[p]).astype(BF)
    r.node_out[p] = out
    r.r1[p] = r1
    r.ip[p] = ip
    r.r2[p] = r2
    return out


def node_backward(d, r, p, layer, aux, dn):
    def rows_of(ref):
        return ref[...].reshape(-1, ref.shape[2]) if p is None else ref[p]

    r1, ip, r2, big, cnt = rows_of(r.r1), rows_of(r.ip), rows_of(r.r2), rows_of(r.big), rows_of(r.cnt)
    xh1, rs1 = norm_rows(r1)
    normed = xh1 * aux[10:11] + aux[7:8]
    xh2, rs2 = norm_rows(r2)
    dy2 = dn * rows_of(r.mask)
    dr2 = norm_back_rows(dy2 * aux[11:12], xh2, rs2)
    low_outer = dr2.astype(BF)
    hid, slope = gelu_pair_wide(ip)
    dip = mm(low_outer, r.outer[layer], 1, 1) * slope
    low_inner = dip.astype(BF)
    at = d.at_outer
    r.msg[at : at + d.wide] += mm(hid.astype(BF), low_outer, 0, 0)
    at = d.at_inner
    r.msg[at : at + d.wide] += mm(low_inner, normed.astype(BF), 0, 0)
    dnormed = dr2 + mm(low_inner, r.inner[layer], 1, 1)
    dr1 = norm_back_rows(dnormed * aux[10:11], xh1, rs1)
    du = dr1 / 30.0
    dub = du.astype(BF)
    r.msg[4 * d.feat : 5 * d.feat] += mm(big.astype(BF), dub, 0, 0)
    dib = jnp.sum(dip, axis=0, keepdims=True)
    rows = {
        2: jnp.sum(cnt * du, axis=0, keepdims=True),
        3: jnp.sum(dr2, axis=0, keepdims=True),
        7: jnp.sum(dnormed, axis=0, keepdims=True),
        8: jnp.sum(dy2, axis=0, keepdims=True),
        10: jnp.sum(dnormed * xh1, axis=0, keepdims=True),
        11: jnp.sum(dy2 * xh2, axis=0, keepdims=True),
    }
    for i in range(d.wide // d.feat):
        rows[16 + i] = dib[:, i * d.feat : (i + 1) * d.feat]
    for row, value in rows.items():
        r.msg[d.at_small + row : d.at_small + row + 1] += value
    if p is None:
        r.dr1[...] = dr1.reshape(r.dr1.shape)
        r.dub[...] = dub.reshape(r.dub.shape)
    else:
        r.dr1[p] = dr1
        r.dub[p] = dub


def own_first(d, row):
    row = row.astype(F32)
    if row.shape[0] == 1:
        row = jnp.broadcast_to(row, (8, d.length))
    return jnp.where(lax.axis_index(AXIS_S) == 0, row, pltpu.roll(row, d.half, 1))


def put_positions(d, r):
    section = lax.axis_index(AXIS_S)
    centre = d.length // 2
    line = lax.broadcasted_iota(jnp.int32, (8, d.length), 0)
    for p in range(d.parts):
        live = own_first(d, r.live[p : p + 1, :])
        order = own_first(d, r.order[p : p + 1, :]) - centre
        code = jnp.where(live > 0.5, order, float(centre))
        r.codes[p, :8] = jnp.where(line == 0, live, jnp.where(line == 1, code, 0.0)).astype(BF)
        r.codes[p, 8:] = jnp.zeros((EXTRA - 8, d.length), BF)
        ids = own_first(d, r.near[p]) - float(d.half) * section.astype(F32)
        ids = jnp.where(ids < 0.0, ids + float(d.length), ids) - float(centre)
        r.mask[p] = jnp.broadcast_to(live[0:1], (d.feat, d.length)).T[: d.half]
        for b in range(d.blocks):
            own = pltpu.roll(order, (d.length - b * d.res) % d.length, 1) if b else order
            r.owns[p, b, :8] = jnp.where(line == 1, -own, 0.0)[:, : d.res].astype(BF)
            r.owns[p, b, 8:] = jnp.zeros((EXTRA - 8, d.res), BF)
            block = pltpu.roll(ids, (d.length - b * d.res) % d.length, 1) if b else ids
            spread = mm(block[:, : d.res].astype(BF), r.rt[: d.res])
            row = jnp.sum(spread * r.pick[...].astype(F32), axis=0, keepdims=True)
            r.idx[p, b] = row.astype(jnp.int32) + centre


def encoder_message(d, edge_input, node_input, neighbors, residue_mask, decode_order, weights, consts):
    ph = Phase(d, 2)
    ph.raw(n_far=node_input)
    ph.whole(n_own=node_input, rt=consts.sums, pick=consts.pick, near=neighbors, live=residue_mask, order=decode_order)
    ph.whole(edge=edge_input)
    ph.later = (EDGE,)
    ph.out_whole(jnp.int32, idx=(d.parts, d.blocks, 1, d.rows))
    ph.out_whole(F32, mask=(d.parts, d.half, d.feat))
    ph.temp(BF, codes=(d.parts, EXTRA, d.length), owns=(d.parts, d.blocks, EXTRA, d.res))
    names = tuple(weights)
    own = {W_IN + n: a for n, a in weights.items()}
    ph.raw(**own)
    act = (d.parts, d.blocks, d.feat, d.rows)
    ph.out_stream(BF, g1=with_ones(d), d1=act, d2=act)
    ph.out_whole(F32, att=(d.parts, d.blocks, 1, d.rows))
    add_node_outs(ph, d)
    ph.out_raw(BF, got=(d.half, d.feat), nodes_got=node_input.shape)
    for n, a in weights.items():
        ph.out_raw(a.dtype, **{W_OUT + n: (2,) + a.shape})
        ph.temp(a.dtype, **{n: (2,) + a.shape})
    sq = (d.feat, d.feat)
    wide = d.feat + d.length + d.res
    ph.temp(BF, n_cat=(d.length, d.feat), lhs=(d.feat + EXTRA, wide), w2t=sq, tt=(d.parts * d.blocks, wide, d.rows))
    ph.temp(BF, leave=(d.half, d.feat), arrive=node_input.shape, kept=(d.feat + 16, d.rows))
    ph.temp(F32, aux=sq, cols=sq)
    count = len(names)
    ph.sems(send=count + 1 + d.parts, recv=count + 1 + d.parts, local=count, back=2 * count + 1)

    def body(r):
        p, b = pl.program_id(0), pl.program_id(1)
        first, last = b == 0, b == d.blocks - 1
        section = lax.axis_index(AXIS_S)
        job = to_partner(r.leave, r.got, r.send.at[count], r.recv.at[count])
        nodes = [
            to_partner(r.n_far.at[q], r.arrive.at[q], r.send.at[count + 1 + q], r.recv.at[count + 1 + q])
            for q in range(d.parts)
        ]

        def swaps(group):
            out = []
            for n in group:
                i = names.index(n)
                dst = getattr(r, n).at[section]
                out.append(to_partner(getattr(r, W_IN + n), dst, r.send.at[i], r.recv.at[i]))
            return out

        def own_copies():
            return [
                pltpu.make_async_copy(getattr(r, W_IN + n), getattr(r, n).at[section], r.local.at[i])
                for i, n in enumerate(names)
            ]

        def returns(group):
            out = [pltpu.make_async_copy(r.arrive, r.nodes_got, r.back.at[2 * count])] if group == GROUP_ONE else []
            for n in group:
                i = names.index(n)
                src, dst = getattr(r, n), getattr(r, W_OUT + n)
                for layer in range(2):
                    sem = r.back.at[2 * i + layer]
                    out.append(pltpu.make_async_copy(src.at[layer], dst.at[layer], sem))
            return out

        begin = first & (p == 0)
        middle = (p == 1) & (b == 1)
        at_end = last & (p == d.parts - 1)

        @pl.when(begin)
        def _():
            greet_partner()
            for item in nodes[:1] + swaps(GROUP_ONE) + own_copies() + nodes[1:]:
                item.start()
            r.load()
            put_positions(d, r)
            r.load(EDGE)
            for q in range(d.parts):

                @pl.loop(0, d.blocks)
                def _(c, q=q):
                    table = r.tt.at[q * d.blocks + c]
                    put_one_hot(d, table, d.feat, r.idx[q, c])
                    table[d.feat + d.length :, :] = r.rt[: d.res]
                    own = r.edge[q, pl.ds(pl.multiple_of(c * d.res, d.res), d.res)]
                    table[: d.feat, :] = own.reshape(d.rows, d.feat).T

            for item in nodes[:1] + swaps(GROUP_ONE) + own_copies():
                item.wait()
            for item in swaps(GROUP_TWO) + swaps(GROUP_THREE):
                item.start()
            r.lhs[: d.feat, : d.feat] = r.mw1[0, d.feat : 2 * d.feat, :].T
            r.lhs[d.feat :, : d.feat] = jnp.zeros((EXTRA, d.feat), BF)
            r.w2t[...] = half_of(r.mw2[0]).T
            load_cols(r, 0, r.aux, r.cols)

        for q in range(1, d.parts):

            @pl.when(first & (p == q))
            def _(q=q):
                nodes[q].wait()

        @pl.when(first)
        def _():
            r.n_cat[: d.half] = r.n_own[p]
            r.n_cat[d.half :] = r.arrive[p]
            put_table(d, r.lhs, 0, d.feat, r.n_cat, r.mw1.at[0])

        n_blk = r.n_own[p, pl.ds(pl.multiple_of(b * d.res, d.res), d.res), :]
        r.ready()
        put_own(d, r.lhs, 0, d.feat, r.mw1.at[0], n_blk, r.cols[:, 0:1])
        r.lhs[d.feat :, d.feat : d.feat + d.length] = r.codes[p]
        r.lhs[d.feat :, d.feat + d.length :] = r.owns[p, b]
        out = mm(r.lhs[...], r.tt[p * d.blocks + b])
        att = out[d.feat : d.feat + 1]
        r.att[p, b] = jnp.where(out[d.feat + 1 : d.feat + 2] < 0.0, 1.0, 0.0)
        g1, r.d1[...], r.d2[...] = message_part(out[: d.feat], r.w2t[...], r.cols[:, 1:2], att, r.kept)
        put_ones(r.g1, g1)
        node_step(d, r, p, b)
        r.flush()

        @pl.when(middle)
        def _():
            for item in swaps(GROUP_TWO) + swaps(GROUP_THREE):
                item.wait()
            for item in returns(GROUP_ONE) + returns(GROUP_TWO) + returns(GROUP_THREE):
                item.start()
            r.leave[...] = node_forward(r, 0, r.n_own[0], 0, r.aux[...])
            job.start()

        @pl.when(at_end)
        def _():
            node_forward(r, d.parts - 1, r.n_own[d.parts - 1], 0, r.aux[...])
            for item in returns(GROUP_ONE) + returns(GROUP_TWO) + returns(GROUP_THREE):
                item.wait()
            job.wait()

    return ph.call("enc_message", body)


W_IN, W_OUT = "i_", "o_"
EDGE = "edge"
GROUP_ONE = ("mw1", "mw2", "bias", "gain")
GROUP_TWO = ("mw3", "inner", "inner_b", "outer")
GROUP_THREE = ("uw1", "uw2", "uw3")
NODE_W = ("mw3", "inner", "inner_b", "outer", "bias", "gain")
MSG_W = ("mw1", "mw2")
UPD_W = ("uw1", "uw2", "uw3")


def with_ones(d):
    return (d.parts, d.blocks, d.feat + 16, d.rows)


def put_ones(ref, g):
    feat, rows = g.shape
    ref[:feat] = g
    ref[feat:] = jnp.ones((16, rows), BF)


def half_of(w):
    return w * BF(0.5)


def update_forward(d, a1, w2t, w3c, b5, b6c, pair, cols):
    f = d.feat
    g1, d1 = gelu_pair(a1)
    a2 = mm(w2t, g1) + b5
    g2, d2 = gelu_pair(a2)
    pair[f : 2 * f] = g2
    cent = mm(w3c[...], pair[: 2 * f]) + b6c
    var = jnp.mean(cent * cent, axis=0, keepdims=True)
    rs = lax.rsqrt(var + EPS)
    xh = cent.astype(BF) * rs.astype(BF)
    y = xh * cols[:, 12:13].astype(BF) + cols[:, 9:10].astype(BF)
    return g1, d1, g2, d2, xh, rs, y


def centre_weights(w3, cols, w3c, b6c):
    feat = w3.shape[0]
    eye = lax.broadcasted_iota(jnp.int32, w3.shape, 0) == lax.broadcasted_iota(jnp.int32, w3.shape, 1)
    w3f = w3.astype(F32)
    w3c[:, feat:] = (0.5 * (w3f - jnp.mean(w3f, axis=1, keepdims=True))).T.astype(BF)
    w3c[:, :feat] = (eye.astype(F32) - 1.0 / feat).astype(BF)
    b6 = cols[:, 6:7]
    b6c[...] = jnp.broadcast_to(b6 - jnp.mean(b6, axis=0, keepdims=True), b6c.shape)


def encoder_update(d, edge_input, st, fa, consts):
    ph = Phase(d, 3)
    ph.raw(n_far=fa.node_out)
    ph.whole(n_own=fa.node_out, got_a=fa.got, idx=consts.idx, rt=consts.sums, mask=consts.mask, att=fa.att)
    ph.edges(edge=edge_input)
    ph.whole(**weight_args(st, *NODE_W, *MSG_W, *UPD_W))
    act = (d.parts, d.blocks, d.feat, d.rows)
    two = (d.parts, d.blocks, 2 * d.feat + 16, d.rows)
    ph.out_stream(BF, ugs=two, ud1=act, ud2=act, uxh=act, e2g=two, d1=act, d2=act)
    ph.out_whole(F32, urs=(d.parts, d.blocks, 1, d.rows))
    add_node_outs(ph, d)
    ph.out_whole(BF, got_in=(d.half, d.feat))
    ph.out_raw(BF, got=(d.parts, d.half, d.feat))
    sq = (d.feat, d.feat)
    wide = d.feat + d.length + d.res
    ph.temp(BF, n_cat=(d.length, d.feat), lhs=(2 * d.feat, wide), tt=(wide, d.rows))
    ph.temp(BF, uw2t=sq, mw2t=sq, w3c=(d.feat, 2 * d.feat), pair=(2 * d.feat, d.rows))
    ph.temp(BF, kept=(d.feat + 16, d.rows), leave=(d.parts, d.half, d.feat), arrive=(d.half, d.feat))
    ph.temp(F32, w3c_b=sq, e_aux=sq, e_cols=sq, d_aux=sq, d_cols=sq)
    ph.sems(send=d.parts + 1, recv=d.parts + 1)

    def body(r):
        p, b = pl.program_id(0), pl.program_id(1)
        first, last = b == 0, b == d.blocks - 1
        early = to_partner(r.n_far.at[d.parts - 1], r.arrive, r.send.at[d.parts], r.recv.at[d.parts])
        jobs = [to_partner(r.leave.at[i], r.got.at[i], r.send.at[i], r.recv.at[i]) for i in range(d.parts)]

        @pl.when(first & (p == 0))
        def _():
            greet_partner()
            early.start()
            r.load()
            r.tt[d.feat + d.length :, :] = r.rt[: d.res]
            r.lhs[: d.feat, : d.feat] = r.uw1[0, d.feat : 2 * d.feat, :].T
            r.lhs[d.feat :, : d.feat] = r.mw1[1, d.feat : 2 * d.feat, :].T
            r.uw2t[...] = half_of(r.uw2[0]).T
            r.mw2t[...] = half_of(r.mw2[1]).T
            load_cols(r, 0, r.e_aux, r.e_cols)
            load_cols(r, 1, r.d_aux, r.d_cols)
            centre_weights(r.uw3[0], r.e_cols[...], r.w3c, r.w3c_b)
            r.n_cat[d.half :] = r.got_a[...]

        @pl.when(first & (p == 1))
        def _():
            early.wait()
            r.n_cat[d.half :] = r.arrive[...]
            r.got_in[...] = r.arrive[...]

        @pl.when(first)
        def _():
            r.n_cat[: d.half] = r.n_own[p]
            put_table(d, r.lhs, 0, d.feat, r.n_cat, r.uw1.at[0])
            put_table(d, r.lhs, d.feat, d.feat, r.n_cat, r.mw1.at[1])

        r.ready()
        n_blk = r.n_own[p, pl.ds(pl.multiple_of(b * d.res, d.res), d.res), :]
        put_own(d, r.lhs, 0, d.feat, r.uw1.at[0], n_blk, r.e_cols[:, 4:5])
        put_own(d, r.lhs, d.feat, d.feat, r.mw1.at[1], n_blk, r.d_cols[:, 0:1])
        put_one_hot(d, r.tt, d.feat, r.idx[p, b])
        edge_t = r.edge[...].reshape(d.rows, d.feat).T
        r.tt[: d.feat, :] = edge_t
        r.pair[: d.feat] = edge_t
        g1, d1, g2, d2, xh, rs, e2 = update_forward(
            d, mm(r.lhs[: d.feat], r.tt[...]), r.uw2t[...], r.w3c, r.e_cols[:, 5:6], r.w3c_b[:, 0:1], r.pair, r.e_cols
        )
        f = d.feat
        r.ugs[:f] = g2
        put_ones(r.ugs.at[f:], g1)
        r.ud1[...], r.ud2[...], r.uxh[...], r.urs[p, b], r.e2g[:f] = d1, d2, xh, rs, e2
        att = r.att[p, b]
        r.tt[:f] = e2
        a1 = mm(r.lhs[f:], r.tt[...])
        g1, r.d1[...], r.d2[...] = message_part(a1, r.mw2t[...], r.d_cols[:, 1:2], att, r.kept)
        put_ones(r.e2g.at[f:], g1)
        node_step(d, r, p, b)
        r.flush()

        @pl.when(last)
        def _():
            r.leave[p] = node_forward(r, p, r.n_own[p], 1, r.d_aux[...])
            for i in range(d.parts):

                @pl.when(p == i)
                def _(i=i):
                    jobs[i].start()

            @pl.when(p == d.parts - 1)
            def _():
                for job in jobs:
                    job.wait()

    return ph.call("enc_update", body)


def spread_nodes(d, acc, sumk, w1, n_cat, grad, grad_at):
    s = acc.astype(BF)
    sk = jnp.concatenate([x[:, : d.res] for x in sumk], axis=1)
    skb = sk.astype(BF)
    far = mm(s, w1[2 * d.feat :].T, 0, 0)
    own = mm(skb, w1[: d.feat].T, 0, 0)
    grad[grad_at + 2 * d.feat : grad_at + 3 * d.feat, :] += mm(n_cat, s, 0, 1)
    grad[grad_at : grad_at + d.feat, :] += mm(n_cat[: d.half], skb, 0, 1)
    return own + far[: d.half], far[d.half :], to_row(sk)


def lane_total(x):
    size = x.shape[1] // 4
    x = (x[:, :size] + x[:, size : 2 * size]) + (x[:, 2 * size : 3 * size] + x[:, 3 * size :])
    return lane_sum(x.astype(F32))


def norm_backward(d, r, dy, xh, rs, gain_mat):
    r.a_b9[...] += lane_total(dy)
    r.a_g2[...] += lane_total(dy * xh)
    z = mm(gain_mat, dy).astype(BF)
    m2 = jnp.mean((z * xh).astype(F32), axis=0, keepdims=True)
    return (z - xh * m2.astype(BF)) * rs.astype(BF)


def gain_matrix(cols):
    feat = cols.shape[0]
    shape = (feat, feat)
    eye = lax.broadcasted_iota(jnp.int32, shape, 0) == lax.broadcasted_iota(jnp.int32, shape, 1)
    scaled = jnp.where(eye, jnp.broadcast_to(cols[:, 12:13], shape), 0.0)
    return (scaled - jnp.mean(scaled, axis=0, keepdims=True)).astype(BF)


def update_backward(d, r, dr3, gs, d1, d2, w2, w3, low, da1):
    f = d.feat
    low[:f] = dr3
    low[f:] = mm(w3, dr3).astype(BF) * d2
    r.a_w23[...] += mm(gs, low[...], 1, 1)
    da1[...] = mm(w2, low[f:]).astype(BF) * d1


def update_small(d, r, b4):
    f = d.feat
    at = 5 * f
    r.upd[at + 4 : at + 5] += b4

    @pl.when(pl.program_id(0) == d.parts - 1)
    def _():
        r.upd[3 * f : 4 * f] = 0.5 * r.a_w23[f : 2 * f, f:]
        r.upd[4 * f : 5 * f] = 0.5 * r.a_w23[:f, :f]
        r.upd[at + 5 : at + 6] = r.a_w23[2 * f : 2 * f + 1, f:]
        r.upd[at + 6 : at + 7] = r.a_w23[2 * f : 2 * f + 1, :f]
        r.upd[at + 9 : at + 10] = to_row(r.a_b9[...])
        r.upd[at + 12 : at + 13] = to_row(r.a_g2[...])


def block_before(d):
    step = jnp.maximum(pl.program_id(0) * d.blocks + pl.program_id(1) - 1, 0)
    return step // d.blocks, lax.rem(step, d.blocks)


def put_spread(d, r, q, c, spread):
    r.a_s[q] += spread[:, : d.length]
    r.a_k[q, c] = spread[:, d.length :]


def zero(*refs):
    for ref in refs:
        ref[...] = jnp.zeros(ref.shape, ref.dtype)


def decoder_update(d, st, fb, cot, consts):
    ph = Phase(d)
    ph.whole(n_own=fb.node_out, n_got=fb.got, idx=consts.idx, rt=consts.sums)
    ph.stream_top(d.feat, e2=fb.e2g)
    ph.edges(cot=cot)
    ph.whole(**weight_args(st, *UPD_W, *AUX_W))
    ph.out_edges(decoded=cot.shape)
    ph.out_stream(BF, part=(d.parts, d.blocks, d.feat, d.rows))
    ph.out_whole(F32, upd=(d.upd_rows, d.feat), dn_own=(d.parts, d.half, d.feat))
    ph.out_whole(BF, dn_far=(d.parts, d.half, d.feat), nodes=(d.parts, d.half, d.feat))
    sq = (d.feat, d.feat)
    wide = d.length + d.res
    ph.temp(BF, n_cat=(d.length, d.feat), lhs=(d.feat, wide), w1bt=sq, w2t=sq, w2h=sq, w3h=sq)
    ph.temp(BF, tt=(wide, d.rows), tn=(d.rows, d.length + 128), da1=(d.feat, d.rows))
    ph.temp(BF, w3c=(d.feat, 2 * d.feat), gain_mat=sq, pair=(3 * d.feat + 16, d.rows), low=(2 * d.feat, d.rows))
    ph.temp(F32, w3c_b=sq, aux=sq, cols=sq, a_w23=(2 * d.feat + 16, 2 * d.feat), a_b9=sq, a_g2=sq)
    ph.temp(F32, a_s=(d.feat, d.length), a_k=(d.blocks, d.feat, 128))

    def body(r):
        p, b = pl.program_id(0), pl.program_id(1)
        first, last = b == 0, b == d.blocks - 1

        @pl.when(first & (p == 0))
        def _():
            r.load()
            r.nodes[...] = r.n_own[...]
            r.w1bt[...] = r.uw1[1, d.feat : 2 * d.feat, :].T
            r.w2h[...] = half_of(r.uw2[1])
            r.w2t[...] = r.w2h[...].T
            r.w3h[...] = half_of(r.uw3[1])
            load_cols(r, 1, r.aux, r.cols)
            centre_weights(r.uw3[1], r.cols[...], r.w3c, r.w3c_b)
            r.gain_mat[...] = gain_matrix(r.cols[...])
            zero(r.upd, r.a_w23, r.a_b9, r.a_g2)
            r.pair[3 * d.feat :] = jnp.ones((16, d.rows), BF)
            r.tt[d.length :, :] = r.rt[: d.res]
            r.tn[:, d.length :] = r.rt[...].T

        @pl.when(first)
        def _():
            r.n_cat[: d.half] = r.n_own[p]
            r.n_cat[d.half :] = r.n_got[p]
            put_table(d, r.lhs, 0, 0, r.n_cat, r.uw1.at[1])
            zero(r.a_s)

        r.ready()
        f = d.feat
        n_blk = r.n_own[p, pl.ds(pl.multiple_of(b * d.res, d.res), d.res), :]
        put_own(d, r.lhs, 0, 0, r.uw1.at[1], n_blk, r.cols[:, 4:5])
        idx = r.idx[p, b]
        put_one_hot(d, r.tt, 0, idx)
        put_one_hot_rows(d, r.tn, idx)
        e2 = r.e2[...]
        r.pair[:f] = e2
        a1 = mm(r.lhs[...], r.tt[...]) + mm(r.w1bt[...], e2)
        g1, d1, _, d2, xh, rs, y = update_forward(
            d, a1, r.w2t[...], r.w3c, r.cols[:, 5:6], r.w3c_b[:, 0:1], r.pair, r.cols
        )
        r.pair[2 * f : 3 * f] = g1
        r.decoded[...] = y.T.reshape(d.res, d.near, f)
        dy = r.cot[...].reshape(d.rows, f).T
        dr3 = norm_backward(d, r, dy, xh, rs, r.gain_mat[...])
        update_backward(d, r, dr3, r.pair[f:], d1, d2, r.w2h[...], r.w3h[...], r.low, r.da1)
        r.upd[f : 2 * f] += mm(e2, r.da1[...], 1, 1)
        r.part[...] = (mm(r.uw1[1, f : 2 * f, :], r.da1[...]) + dr3.astype(F32)).astype(BF)
        spread = mm(r.da1[...], r.tn[...])
        r.a_s[...] += spread[:, : d.length]
        r.a_k[b] = spread[:, d.length :]
        r.flush()

        @pl.when(last)
        def _():
            own, far, b4 = spread_nodes(
                d, r.a_s[...], [r.a_k[i] for i in range(d.blocks)], r.uw1[1], r.n_cat[...], r.upd, 0
            )
            r.dn_own[p] = own
            r.dn_far[p] = far.astype(BF)
            update_small(d, r, b4)

    return ph.call("dec_update", body)


AUX_W = ("bias", "gain")


def message_backward(d, r, b, layer, low):
    at = pl.ds(pl.multiple_of(b * d.res, d.res), d.res)
    v = (mm(r.mw3[layer], r.dub[pl.program_id(0), at, :], 1, 1) * 0.5).astype(BF)
    f = d.feat
    low[:f] = mm(v, r.rt[: d.res]).astype(BF) * r.d2[...]
    low[f:] = mm(r.mw2h[...], low[:f]).astype(BF) * r.d1[...]


def message_small(d, r, b0):
    r.msg[d.at_small : d.at_small + 1] += b0


def middle_backward(d, edge_input, st, fa, fb, fd, cot_n, consts):
    ph = Phase(d, 4)
    ph.raw(dn_far_in=fd.dn_far)
    ph.whole(cot_n=cot_n, dn_a=fd.dn_own, n_own=fa.node_out, got_a=fa.got, got_b=fb.got_in)
    ph.whole(mask=consts.mask, rt=consts.sums, r1=fb.r1, ip=fb.ip, r2=fb.r2, big=fb.big, cnt=fb.cnt)
    ph.whole(urs=fb.urs, idx=consts.idx)
    ph.stream(d2=fb.d2, d1=fb.d1, e2g=fb.e2g, dec_part=fd.part, uxh=fb.uxh, ugs=fb.ugs, ud2=fb.ud2, ud1=fb.ud1)
    ph.edges(edge=edge_input)
    ph.whole(**weight_args(st, *NODE_W, *MSG_W, *UPD_W))
    ph.out_stream(BF, part=(d.parts, d.blocks, d.feat, d.rows))
    ph.out_whole(F32, msg=(d.msg_rows, d.feat), upd=(d.upd_rows, d.feat), dn_own=(d.parts, d.half, d.feat))
    ph.out_raw(BF, got=(d.parts, d.half, d.feat))
    sq = (d.feat, d.feat)
    ph.temp(BF, n_cat=(d.length, d.feat), dub=(d.parts, d.half, d.feat), tt=(d.length + d.res, d.rows))
    ph.temp(BF, tri=(3 * d.feat, d.rows), low=(2 * d.feat, d.rows), w2h=sq, w3h=sq, mw2h=sq, gain_mat=sq)
    ph.temp(BF, leave=(d.parts, d.half, d.feat), arrive=(d.parts, d.half, d.feat))
    ph.temp(F32, dr1=(d.parts, d.half, d.feat), e_aux=sq, e_cols=sq, d_aux=sq, d_cols=sq)
    tall = (2 * d.feat + 16, 2 * d.feat)
    ph.temp(F32, m_w12=tall, a_w23=tall, a_b9=sq, a_g2=sq, a_w1=sq)
    ph.temp(F32, a_s=(2 * d.feat, d.length), a_k=(d.blocks, 2 * d.feat, 128))
    ph.sems(send=2 * d.parts, recv=2 * d.parts)

    def body(r):
        p, b = pl.program_id(0), pl.program_id(1)
        first, last = b == 0, b == d.blocks - 1
        n = d.parts
        early = [to_partner(r.dn_far_in.at[i], r.arrive.at[i], r.send.at[n + i], r.recv.at[n + i]) for i in range(n)]
        jobs = [to_partner(r.leave.at[i], r.got.at[i], r.send.at[i], r.recv.at[i]) for i in range(n)]

        @pl.when(first & (p == 0))
        def _():
            greet_partner()
            for job in early:
                job.start()
            r.load()
            load_cols(r, 0, r.e_aux, r.e_cols)
            load_cols(r, 1, r.d_aux, r.d_cols)
            r.tt[d.length :, :] = r.rt[: d.res]
            r.w2h[...] = half_of(r.uw2[0])
            r.w3h[...] = half_of(r.uw3[0])
            r.mw2h[...] = half_of(r.mw2[1])
            r.gain_mat[...] = gain_matrix(r.e_cols[...])
            zero(r.msg, r.upd, r.m_w12, r.a_w23, r.a_b9, r.a_g2, r.a_w1)
            r.n_cat[d.half :] = r.got_a[...]

        @pl.when(first & (p == 1))
        def _():
            r.n_cat[d.half :] = r.got_b[...]

        for i in range(n):

            @pl.when(first & (p == i))
            def _(i=i):
                early[i].wait()

        @pl.when(first)
        def _():
            r.n_cat[: d.half] = r.n_own[p]
            zero(r.a_s)
            dn = r.cot_n[p].astype(F32) + r.dn_a[p] + r.arrive[p].astype(F32)
            node_backward(d, r, p, 1, r.d_aux[...], dn)

        f = d.feat
        r.ready()
        put_one_hot(d, r.tt, 0, r.idx[p, b])
        message_backward(d, r, b, 1, r.tri.at[: 2 * f])
        r.m_w12[...] += mm(r.e2g[...], r.tri[: 2 * f], 1, 1)
        de = mm(r.mw1[1, f : 2 * f, :], r.tri[f : 2 * f])
        dy = (de + r.dec_part[...].astype(F32)).astype(BF)
        dr3 = norm_backward(d, r, dy, r.uxh[...], r.urs[p, b], r.gain_mat[...])
        da1 = r.tri.at[2 * f :]
        update_backward(d, r, dr3, r.ugs[...], r.ud1[...], r.ud2[...], r.w2h[...], r.w3h[...], r.low, da1)
        r.a_w1[...] += mm(da1[...], r.edge[...].reshape(d.rows, f))
        r.part[...] = (mm(r.uw1[0, f : 2 * f, :], da1[...]) + dr3.astype(F32)).astype(BF)
        spread = mm(r.tri[f:], r.tt[...], 1, 1)
        r.a_s[...] += spread[:, : d.length]
        r.a_k[b, :, : d.res] = spread[:, d.length :]
        r.flush()

        @pl.when(last)
        def _():
            n_cat = r.n_cat[...]
            a_k = [r.a_k[i] for i in range(d.blocks)]
            own_m, far_m, b0 = spread_nodes(
                d, r.a_s[: d.feat], [x[: d.feat] for x in a_k], r.mw1[1], n_cat, r.msg, 0
            )
            own_u, far_u, b4 = spread_nodes(
                d, r.a_s[d.feat :], [x[d.feat :] for x in a_k], r.uw1[0], n_cat, r.upd, 0
            )
            r.dn_own[p] = own_m + own_u + r.dr1[p]
            r.leave[p] = (far_m + far_u).astype(BF)
            for i in range(n):

                @pl.when(p == i)
                def _(i=i):
                    jobs[i].start()

            message_small(d, r, b0)
            update_small(d, r, b4)

            @pl.when(p == n - 1)
            def _():
                f, at = d.feat, d.at_small
                r.upd[f : 2 * f] = r.a_w1[...].T
                r.msg[f : 2 * f] = r.m_w12[:f, f:]
                r.msg[3 * f : 4 * f] = 0.5 * r.m_w12[f : 2 * f, :f]
                r.msg[at + 1 : at + 2] = r.m_w12[2 * f : 2 * f + 1, :f]
                for job in jobs:
                    job.wait()

    return ph.call("dec_message_back", body)


def encoder_message_back(d, edge_input, st, fa, fe, n_own, n_got, consts):
    ph = Phase(d)
    ph.whole(dn_a=fe.dn_own, dn_b=fe.got, n_own=n_own, n_got=n_got)
    ph.whole(mask=consts.mask, rt=consts.sums, r1=fa.r1, ip=fa.ip, r2=fa.r2, big=fa.big, cnt=fa.cnt)
    ph.whole(idx=consts.idx)
    ph.stream(d2=fa.d2, g1=fa.g1, d1=fa.d1, up_part=fe.part)
    ph.edges(edge=edge_input)
    ph.whole(**weight_args(st, *NODE_W, *MSG_W))
    ph.out_edges(edge_grad=edge_input.shape)
    ph.out_whole(F32, msg=(d.msg_rows, d.feat), dn_own=(d.parts, d.half, d.feat))
    ph.out_whole(BF, dn_far=(d.parts, d.half, d.feat))
    sq = (d.feat, d.feat)
    ph.temp(BF, dub=(d.parts, d.half, d.feat), tn=(d.rows, d.length + 128))
    ph.temp(BF, low=(2 * d.feat, d.rows), mw2h=sq)
    ph.temp(F32, dr1=(d.parts, d.half, d.feat), aux=sq, cols=sq, a_w1=sq, m_w2=(d.feat + 16, d.feat))
    ph.temp(F32, a_s=(d.parts, d.feat, d.length), a_k=(d.parts, d.blocks, d.feat, 128))

    def body(r):
        p, b = pl.program_id(0), pl.program_id(1)

        @pl.when((b == 0) & (p == 0))
        def _():
            zero(r.a_s, r.low, r.tn)
            r.load()
            load_cols(r, 0, r.aux, r.cols)
            r.tn[:, d.length :] = r.rt[...].T
            r.mw2h[...] = half_of(r.mw2[0])
            zero(r.msg, r.m_w2, r.a_w1)
            dn = r.dn_a[...] + r.dn_b[...].astype(F32)
            node_backward(d, r, None, 0, r.aux[...], dn.reshape(-1, d.feat))

        f = d.feat
        r.ready()
        put_spread(d, r, *block_before(d), mm(r.low[f:], r.tn[...]))
        put_one_hot_rows(d, r.tn, r.idx[p, b])
        message_backward(d, r, b, 0, r.low)
        da1 = r.low.at[f:]
        r.m_w2[...] += mm(r.g1[...], r.low[:f], 1, 1)
        r.a_w1[...] += mm(da1[...], r.edge[...].reshape(d.rows, f))
        de = mm(r.mw1[0, f : 2 * f, :], da1[...])
        de = (de + r.up_part[...].astype(F32)).astype(BF)
        r.edge_grad[...] = de.T.reshape(d.res, d.near, f)
        r.flush()

        @pl.when((b == d.blocks - 1) & (p == d.parts - 1))
        def _():
            put_spread(d, r, p, b, mm(da1[...], r.tn[...]))
            for q in range(d.parts):
                nodes = jnp.concatenate([r.n_own[q], r.n_got[q]], axis=0)
                sums = [r.a_k[q, i] for i in range(d.blocks)]
                own, far, b0 = spread_nodes(d, r.a_s[q], sums, r.mw1[0], nodes, r.msg, 0)
                r.dn_own[q] = own + r.dr1[q]
                r.dn_far[q] = far.astype(BF)
                message_small(d, r, b0)
            at = d.at_small
            r.msg[f : 2 * f] = r.a_w1[...].T
            r.msg[3 * f : 4 * f] = 0.5 * r.m_w2[:f]
            r.msg[at + 1 : at + 2] = r.m_w2[f : f + 1]

    return ph.call("enc_message_back", body)


class Reducer:
    def __init__(self, devices, feat, shares):
        self.feat = feat
        self.bits = bits = devices.bit_length() - 1
        self.groups = [16 * devices * share for share in shares]
        self.rows = sum(self.groups)
        self.bases = [sum(self.groups[:i]) for i in range(len(shares))]
        pairs, top = [], bits
        while top > 1:
            low = max(1, top - 2)
            pairs.insert(0, (low, top - low))
            top = low
        dims = [ACROSS] + pairs
        turn = min(3, len(dims))
        self.plans = []
        for g, size in enumerate(self.groups):
            head = dims[:turn]
            order = ([(0, 1)] if bits else []) + head[g % turn :] + head[: g % turn] + dims[turn:]
            both, plan = True, []
            for dim in order:
                if dim == ACROSS:
                    both = False
                else:
                    size >>= dim[1]
                plan.append((dim, size, both))
            self.plans.append(plan)
        self.backs = [[step for step in reversed(plan) if step[0] != ACROSS] for plan in self.plans]
        self.halving = len(self.plans[0])
        self.stages = self.halving + len(self.backs[0])
        self.dims = ([(0, 1)] if bits else []) + dims
        self.sem_at, self.buffer_at, self.shapes = {}, {}, []
        for g, plan in enumerate(self.plans):
            for k, (dim, size, both) in enumerate(plan):
                for o in self.offsets(dim):
                    self.sem_at[(g, k, o)] = len(self.sem_at)
                    self.buffer_at[(g, k, o)] = len(self.shapes)
                    self.shapes += [(2, size, feat) if both else (size, feat)] * 2
            for k, (dim, _, _) in enumerate(self.backs[g]):
                for o in self.offsets(dim):
                    self.sem_at[(g, self.halving + k, o)] = len(self.sem_at)

    def scratch(self):
        temps = [pltpu.VMEM((2, self.rows, self.feat), F32), pltpu.VMEM((self.rows, self.feat), BF)]
        temps += [pltpu.VMEM(shape, BF) for shape in self.shapes]
        return temps + [pltpu.SemaphoreType.DMA((len(self.sem_at),))] * 2

    def bind(self, refs):
        self.acc, self.gathered = refs[:2]
        self.buffers, (self.send, self.recv) = refs[2:-2], refs[-2:]

    def offsets(self, dim):
        return range(1, 2 if dim == ACROSS else 1 << dim[1])

    def code(self, dim):
        return lax.rem(lax.axis_index(AXIS_D) // (1 << dim[0]), 1 << dim[1])

    def peer(self, dim, o):
        if dim == ACROSS:
            return other_section()
        code = self.code(dim)
        other = lax.rem(code + o, 1 << dim[1])
        return {AXIS_D: lax.axis_index(AXIS_D) + (other - code) * (1 << dim[0])}

    def greet(self):
        barrier = pltpu.get_barrier_semaphore()
        count = 0
        for dim in self.dims:
            for o in self.offsets(dim):
                pl.semaphore_signal(barrier, inc=1, device_id=self.peer(dim, o), device_id_type=MESH)
                count += 1
        pl.semaphore_wait(barrier, count)

    def begin(self, g, k):
        start = self.bases[g]
        for dim, size, _ in self.plans[g][:k]:
            if dim != ACROSS:
                start = start + self.code(dim) * size
        return start

    def span(self, start, size):
        return pl.ds(pl.multiple_of(start, 16), size)

    def job(self, src, dst, key, dim):
        at = self.sem_at[key]
        return pltpu.make_async_remote_copy(
            src_ref=src, dst_ref=dst, send_sem=self.send.at[at], recv_sem=self.recv.at[at],
            device_id=self.peer(dim, key[2]), device_id_type=MESH,
        )

    def jobs(self, g, k):
        plan = self.plans[g]
        if k < self.halving:
            out = []
            for o in self.offsets(plan[k][0]):
                at = self.buffer_at[(g, k, o)]
                out.append(self.job(self.buffers[at], self.buffers[at + 1], (g, k, o), plan[k][0]))
            return out
        dim, size, _ = self.backs[g][k - self.halving]
        start = self.begin(g, [step[0] for step in plan].index(dim) + 1)
        part = self.gathered.at[self.span(start, size), :]
        return [self.job(part, part, (g, k, o), dim) for o in self.offsets(dim)]

    def start(self, g, k):
        section = lax.axis_index(AXIS_S)
        plan = self.plans[g]
        if k < self.halving:
            dim, size, both = plan[k]
            start = self.begin(g, k)
            for o in self.offsets(dim):
                out = self.buffers[self.buffer_at[(g, k, o)]]
                if dim == ACROSS:
                    out[...] = self.acc[1 - section, self.span(start, size), :].astype(BF)
                    continue
                give = self.span(start + lax.rem(self.code(dim) + o, 1 << dim[1]) * size, size)
                if both:
                    out[...] = self.acc[:, give, :].astype(BF)
                else:
                    out[...] = self.acc[section, give, :].astype(BF)
        elif k == self.halving:
            keep = self.span(self.begin(g, self.halving), plan[-1][1])
            self.gathered[keep, :] = self.acc[section, keep, :].astype(BF)
        for job in self.jobs(g, k):
            job.start()

    def finish(self, g, k):
        section = lax.axis_index(AXIS_S)
        for job in self.jobs(g, k):
            job.wait()
        if k >= self.halving:
            return
        dim, size, both = self.plans[g][k]
        keep = self.span(self.begin(g, k + 1), size)
        for o in self.offsets(dim):
            into = self.buffers[self.buffer_at[(g, k, o)] + 1]
            if both:
                self.acc[:, keep, :] += into[...].astype(F32)
            else:
                self.acc[section, keep, :] += into[...].astype(F32)

    def run(self):
        count = len(self.plans)
        for g in range(count):
            self.start(g, 0)
        for k in range(self.stages):
            for g in range(count):
                self.finish(g, k)
                if k + 1 < self.stages:
                    self.start(g, k + 1)
        if self.stages == self.halving:
            self.gathered[...] = self.acc[lax.axis_index(AXIS_S)].astype(BF)


ACROSS = (-1, 0)


def reduce_grads(d, enc_msg, enc_upd, dec_msg, dec_upd, dn_far):
    m, u = d.msg_rows, d.upd_rows
    units = -(-(m + u) // (16 * d.devices))
    red = Reducer(d.devices, d.feat, [2] * (units // 2) + [1] * (units % 2))

    def kernel(em, eu, dm, du, far, res, got, far_sems, load_sems, *refs):
        red.bind(refs)
        loads = []
        for layer, (msg, upd) in enumerate(((em, eu), (dm, du))):
            spots = (red.acc.at[layer, pl.ds(0, m)], red.acc.at[layer, pl.ds(m, u)])
            for i, (src, dst) in enumerate(zip((msg, upd), spots)):
                loads.append(pltpu.make_async_copy(src, dst, load_sems.at[2 * layer + i]))
        for item in loads:
            item.start()
        if red.rows > m + u:
            red.acc[:, m + u :] = jnp.zeros((2, red.rows - m - u, d.feat), F32)
        red.greet()
        nodes = to_partner(far, got, far_sems.at[0], far_sems.at[1])
        nodes.start()
        for item in loads:
            item.wait()
        red.run()
        res[...] = red.gathered[...]
        nodes.wait()

    vm, anywhere = pl.BlockSpec(memory_space=pltpu.VMEM), pl.BlockSpec(memory_space=pl.ANY)
    return pl.pallas_call(
        kernel,
        in_specs=[anywhere] * 5,
        out_specs=[vm, anywhere],
        out_shape=[jax.ShapeDtypeStruct((red.rows, d.feat), BF), jax.ShapeDtypeStruct(dn_far.shape, BF)],
        scratch_shapes=[pltpu.SemaphoreType.DMA((2,)), pltpu.SemaphoreType.DMA((4,))] + red.scratch(),
        compiler_params=pltpu.CompilerParams(vmem_limit_bytes=58 << 20, collective_id=5, has_side_effects=True),
        name="reduce",
    )(enc_msg, enc_upd, dec_msg, dec_upd, dn_far)


def unpack(d, total, dn_own, dn_got, n_bias, n_gain):
    f = d.feat
    m = d.msg_rows
    shapes = [(1, 3 * f, f), (1, f, f), (1, f, f), (1, f, d.wide), (1, 1, d.wide), (1, d.wide, f)]
    shapes += [(1, 3 * f, f), (1, f, f), (1, f, f), (n_bias, 1, f), (n_gain, 1, f)]

    def kernel(t, own, got, node, mw1, mw2, mw3, inner, inner_b, outer, uw1, uw2, uw3, bias, gain):
        node[...] = (own[...] + got[...].astype(F32)).astype(BF)
        for ref, at in ((mw1, 0), (mw2, 3 * f), (mw3, 4 * f), (outer, d.at_outer)):
            ref[0] = t[at : at + ref.shape[1], :].astype(F32)
        for ref, at in ((uw1, m), (uw2, m + 3 * f), (uw3, m + 4 * f)):
            ref[0] = t[at : at + ref.shape[1], :].astype(F32)
        inner[0] = t[d.at_inner : d.at_inner + d.wide, :].astype(F32).T
        small = t[d.at_small : d.at_small + SMALL, :].astype(F32)
        other = t[m + 5 * f : m + 5 * f + SMALL, :].astype(F32)
        both = small + other
        for i in range(n_bias):
            bias[i] = both[i : i + 1]
        for i in range(n_gain):
            gain[i] = both[n_bias + i : n_bias + i + 1]
        for i in range(d.wide // f):
            inner_b[0, :, i * f : (i + 1) * f] = small[16 + i : 17 + i]

    vm = pl.BlockSpec(memory_space=pltpu.VMEM)
    out = [jax.ShapeDtypeStruct(dn_own.shape, BF)] + [jax.ShapeDtypeStruct(s, F32) for s in shapes]
    return pl.pallas_call(kernel, in_specs=[vm] * 3, out_specs=[vm] * len(out), out_shape=out, name="unpack")(
        total, dn_own, dn_got
    )


def per_device(
    node_input,
    edge_input,
    neighbors,
    residue_mask,
    decode_order,
    node_cotangent,
    edge_cotangent,
    message_w1,
    message_w2,
    message_w3,
    inner_w,
    inner_bias,
    outer_w,
    update_w1,
    update_w2,
    update_w3,
    biases,
    norm_gains,
):
    parts, half, near, feat = edge_input.shape
    length = neighbors.shape[1]
    wide = inner_w.shape[2]
    res = BLOCK_RES
    rows = res * near
    blocks = half // res
    at_outer = 5 * feat
    at_inner = at_outer + wide
    at_small = at_inner + wide
    d = types.SimpleNamespace(
        parts=parts, half=half, near=near, feat=feat, length=length, wide=wide, res=res, rows=rows, blocks=blocks,
        at_outer=at_outer, at_inner=at_inner, at_small=at_small, msg_rows=at_small + SMALL,
        upd_rows=5 * feat + SMALL, devices=lax.axis_size(AXIS_D),
    )
    weights = dict(
        mw1=message_w1[0], mw2=message_w2[0], mw3=message_w3[0], inner=inner_w[0], inner_b=inner_bias, outer=outer_w[0],
        uw1=update_w1[0], uw2=update_w2[0], uw3=update_w3[0],
        bias=biases.transpose(1, 0, 2), gain=norm_gains.transpose(1, 0, 2),
    )
    sums = np.zeros((128, rows), np.float32)
    sums[np.arange(rows) // near, np.arange(rows)] = 1.0
    pick = (np.arange(rows)[None, :] % near == np.arange(near)[:, None]).astype(np.float32)
    consts = types.SimpleNamespace(sums=jnp.asarray(sums, BF), pick=jnp.asarray(pick, BF))
    fa = encoder_message(
        d, edge_input, node_input, neighbors.transpose(0, 2, 1), residue_mask, decode_order, weights, consts
    )
    consts.idx, consts.mask = fa.idx, fa.mask
    st = types.SimpleNamespace(**{n: getattr(fa, W_OUT + n) for n in weights})
    fb = encoder_update(d, edge_input, st, fa, consts)
    fd = decoder_update(d, st, fb, edge_cotangent, consts)
    fe = middle_backward(d, edge_input, st, fa, fb, fd, node_cotangent, consts)
    ff = encoder_message_back(d, edge_input, st, fa, fe, node_input, fa.nodes_got, consts)
    total, got = reduce_grads(d, ff.msg, fe.upd, fe.msg, fd.upd, ff.dn_far)
    node_grad, mw1, mw2, mw3, inner, inner_b, outer, uw1, uw2, uw3, bias, gain = unpack(
        d, total, ff.dn_own, got, biases.shape[1], norm_gains.shape[1]
    )
    return (
        fd.nodes, fd.decoded, node_grad, ff.edge_grad, mw1, mw2, mw3, inner, inner_b[:, 0], outer,
        uw1, uw2, uw3, bias.transpose(1, 0, 2), gain.transpose(1, 0, 2),
    )


def solution(mesh):
    def split(*axes):
        return P(*axes)

    by_part = split(AXIS_D)
    by_half = split(AXIS_D, AXIS_S)
    by_layer = split(AXIS_S)
    in_specs = (by_half, by_half, by_part, by_part, by_part, by_half, by_half) + (by_layer,) * 11
    out_specs = (by_half,) * 4 + (by_layer,) * 11
    return jax.shard_map(per_device, mesh=mesh, in_specs=in_specs, out_specs=out_specs, check_vma=False)
```

```python
import types

import jax
import jax.numpy as jnp
import numpy as np
from jax import lax
from jax.experimental import pallas as pl
from jax.experimental.pallas import tpu as pltpu
from jax.sharding import PartitionSpec as P

BF = jnp.bfloat16
F32 = jnp.float32
C1 = 0.7978845608
C2 = C1 * 0.044715
EPS = 1e-5
BLOCK_RES = 96
EXTRA = 16
SMALL = 32
MESH = pl.DeviceIdType.MESH


def mm(a, b, ca=1, cb=0):
    return lax.dot_general(a, b, (((ca,), (cb,)), ((), ())), preferred_element_type=F32)


def mm_exact(a, b, ca=1, cb=0):
    return lax.dot_general(
        a, b, (((ca,), (cb,)), ((), ())), precision=lax.Precision.HIGHEST, preferred_element_type=F32
    )


def gelu_pair(x):
    x = x.astype(BF)
    w = x * x * BF(C2)
    h = jnp.tanh(x * (w + BF(C1))) + BF(1.0)
    g = x * h
    d = h + g * (BF(2.0) - h) * (w * BF(3.0) + BF(C1))
    return g, d


def gelu_pair_wide(x):
    x2 = x * x
    h = 0.5 * jnp.tanh(x * (x2 * C2 + C1)) + 0.5
    g = x * h
    d = h + (g * (1.0 - h)) * (x2 * (6 * C2) + 2 * C1)
    return g, d


def lane_sum(x):
    total = x[:, :128]
    for at in range(128, x.shape[1], 128):
        total = total + x[:, at : at + 128]
    return total


def to_row(acc):
    return mm_exact(jnp.ones((8, acc.shape[1]), F32), acc, 1, 1)[0:1]


def norm_rows(r):
    c = r - jnp.mean(r, axis=-1, keepdims=True)
    rs = lax.rsqrt(jnp.mean(c * c, axis=-1, keepdims=True) + EPS)
    return c * rs, rs


def norm_back_rows(dxh, xh, rs):
    m1 = jnp.mean(dxh, axis=-1, keepdims=True)
    m2 = jnp.mean(dxh * xh, axis=-1, keepdims=True)
    return (dxh - m1 - xh * m2) * rs


def norm_back(dy, xh, rs, gain_col):
    dxh = dy * gain_col
    m1 = jnp.mean(dxh, axis=0, keepdims=True)
    m2 = jnp.mean(dxh * xh, axis=0, keepdims=True)
    return (dxh - m1 - xh * m2) * rs


class Phase:
    def __init__(self, dims, collective_id=None):
        self.d = dims
        self.collective_id = collective_id
        self.ins, self.outs, self.temps, self.kinds, self.wholes, self.later = [], [], [], {}, {}, ()

    def whole_spec(self, shape):
        rank = len(shape)
        return pl.BlockSpec(tuple(shape), lambda p, b: (0,) * rank)

    def whole(self, **arrays):
        self.raw(**arrays)
        self.wholes.update({n: pltpu.VMEM(a.shape, a.dtype) for n, a in arrays.items()})

    def raw(self, **arrays):
        self.ins += [(n, a, pl.BlockSpec(memory_space=pl.ANY)) for n, a in arrays.items()]

    def stream(self, **arrays):
        self.raw(**arrays)
        self.kinds.update({n: (False, False, a.shape[2:], a.dtype) for n, a in arrays.items()})

    def stream_top(self, rows, **arrays):
        self.raw(**arrays)
        self.kinds.update({n: (False, False, (rows,) + a.shape[3:], a.dtype) for n, a in arrays.items()})

    def edges(self, **arrays):
        self.raw(**arrays)
        block = (self.d.res, self.d.near, self.d.feat)
        self.kinds.update({n: (False, True, block, a.dtype) for n, a in arrays.items()})

    def out_whole(self, dtype, **shapes):
        self.outs += [(n, jax.ShapeDtypeStruct(s, dtype), self.whole_spec(s)) for n, s in shapes.items()]

    def out_raw(self, dtype, **shapes):
        spec = pl.BlockSpec(memory_space=pl.ANY)
        self.outs += [(n, jax.ShapeDtypeStruct(s, dtype), spec) for n, s in shapes.items()]

    def out_stream(self, dtype, **shapes):
        self.out_raw(dtype, **shapes)
        self.kinds.update({n: (True, False, s[2:], dtype) for n, s in shapes.items()})

    def out_edges(self, **shapes):
        self.out_raw(BF, **shapes)
        block = (self.d.res, self.d.near, self.d.feat)
        self.kinds.update({n: (True, True, block, BF) for n in shapes})

    def temp(self, dtype, **shapes):
        self.temps += [(n, pltpu.VMEM(s, dtype)) for n, s in shapes.items()]

    def sems(self, **counts):
        self.temps += [(n, pltpu.SemaphoreType.DMA((c,))) for n, c in counts.items()]

    def call(self, name, body):
        d = self.d
        names = [n for n, _, _ in self.ins] + [n for n, _, _ in self.outs] + [n for n, _ in self.temps]
        steps = d.parts * d.blocks
        buffers = [pltpu.VMEM((2,) + tuple(block), dtype) for _, _, block, dtype in self.kinds.values()]
        count = len(self.kinds)

        def kernel(*refs):
            refs, rest = refs[: len(names)], refs[len(names) :]
            slots, sems, kept = rest[:count], rest[count : 2 * count], rest[2 * count : -1]
            plain = dict(zip(names, refs))
            step = pl.program_id(0) * d.blocks + pl.program_id(1)
            now = lax.rem(step, 2)

            def copy(i, n, at, slot):
                out, edges, block, _ = self.kinds[n]
                p, b = at // d.blocks, lax.rem(at, d.blocks)
                if edges:
                    far = plain[n].at[p, pl.ds(pl.multiple_of(b * d.res, d.res), d.res)]
                elif block[0] < plain[n].shape[2]:
                    far = plain[n].at[p, b, pl.ds(0, block[0])]
                else:
                    far = plain[n].at[p, b]
                near = slots[i].at[slot]
                return pltpu.make_async_copy(*((near, far) if out else (far, near)), sems[i].at[slot])

            into = [(i, n) for i, n in enumerate(self.kinds) if not self.kinds[n][0]]
            outof = [(i, n) for i, n in enumerate(self.kinds) if self.kinds[n][0]]

            def loads():
                return [
                    pltpu.make_async_copy(plain[n], kept[i], rest[-1].at[i]) for i, n in enumerate(self.wholes)
                ]

            def load(*later):
                for item, n in zip(loads(), self.wholes):
                    if (n in later) if later else (n not in self.later):
                        item.wait()

            @pl.when(step == 0)
            def _():
                for item in loads():
                    item.start()
                for i, n in into:
                    copy(i, n, step, now).start()

            @pl.when(step >= 2)
            def _():
                for i, n in outof:
                    copy(i, n, step - 2, now).wait()

            def ready():
                for i, n in into:
                    copy(i, n, step, now).wait()

                @pl.when(step + 1 < steps)
                def _():
                    for i, n in into:
                        copy(i, n, step + 1, 1 - now).start()

            def flush():
                for i, n in outof:
                    copy(i, n, step, now).start()

            plain_or_slot = dict(plain, ready=ready, flush=flush, load=load)
            plain_or_slot.update(zip(self.wholes, kept))
            plain_or_slot.update({n: slots[i].at[now] for i, n in enumerate(self.kinds)})
            body(types.SimpleNamespace(**plain_or_slot))

            @pl.when(step == steps - 1)
            def _():
                for i, n in outof:
                    if steps > 1:
                        copy(i, n, step - 1, 1 - now).wait()
                    copy(i, n, step, now).wait()

        results = pl.pallas_call(
            kernel,
            grid=(d.parts, d.blocks),
            in_specs=[s for _, _, s in self.ins],
            out_specs=[s for _, _, s in self.outs],
            out_shape=[s for _, s, _ in self.outs],
            scratch_shapes=[s for _, s in self.temps] + buffers
            + [pltpu.SemaphoreType.DMA((2,))] * count
            + list(self.wholes.values())
            + [pltpu.SemaphoreType.DMA((len(self.wholes),))],
            compiler_params=pltpu.CompilerParams(
                dimension_semantics=(pltpu.ARBITRARY,) * 2,
                vmem_limit_bytes=60 << 20,
                collective_id=self.collective_id,
                has_side_effects=self.collective_id is not None,
            ),
            name=name,
        )(*[a for _, a, _ in self.ins])
        return types.SimpleNamespace(**dict(zip([n for n, _, _ in self.outs], results)))


def other_section():
    return {AXIS_S: 1 - lax.axis_index(AXIS_S)}


AXIS_S = "section"
AXIS_D = "dp"


def greet_partner():
    barrier = pltpu.get_barrier_semaphore()
    pl.semaphore_signal(barrier, inc=1, device_id=other_section(), device_id_type=MESH)
    pl.semaphore_wait(barrier, 1)


def to_partner(src, dst, send, recv):
    return pltpu.make_async_remote_copy(
        src_ref=src, dst_ref=dst, send_sem=send, recv_sem=recv, device_id=other_section(), device_id_type=MESH
    )


def put_one_hot(d, ref, at, idx):
    idx = idx.astype(jnp.int16)
    place = lax.broadcasted_iota(jnp.int16, (d.length, d.rows), 0)
    ref[at : at + d.length, :] = jnp.where(place == idx, jnp.ones((), BF), jnp.zeros((), BF))


def put_one_hot_rows(d, ref, idx):
    centre = d.length // 2
    idx = jnp.broadcast_to((idx - centre).astype(F32).astype(BF), (128, d.rows)).T
    place = lax.broadcasted_iota(jnp.int32, (d.rows, 128), 1)
    for at in range(0, d.length, 128):
        there = (place + (at - centre)).astype(F32).astype(BF)
        ref[:, at : at + 128] = jnp.where(idx == there, jnp.ones((), BF), jnp.zeros((), BF))


def weight_args(w, *names):
    return {n: getattr(w, n) for n in names}


def load_cols(r, layer, aux, cols):
    n_bias, n_gain = r.bias.shape[1], r.gain.shape[1]
    aux[...] = jnp.zeros(aux.shape, F32)
    for i in range(n_bias):
        aux[i : i + 1] = r.bias[layer, i]
    for i in range(n_gain):
        aux[n_bias + i : n_bias + i + 1] = r.gain[layer, i]
    cols[...] = aux[...].T


def put_table(d, lhs, at, left, n_cat, w1):
    lhs[at : at + d.feat, left : left + d.length] = mm(w1[2 * d.feat :, :].T, n_cat[...], 1, 1).astype(BF)


def put_own(d, lhs, at, left, w1, n_blk, bias_col):
    own = mm(w1[0 : d.feat, :].T, n_blk, 1, 1) + bias_col
    lhs[at : at + d.feat, left + d.length :] = own.astype(BF)


def message_part(a1, w2t, b2, att, kept):
    g1, d1 = gelu_pair(a1)
    a2 = mm(w2t, g1) + b2
    g2, d2 = gelu_pair(a2)
    attb = att.astype(BF)
    feat, rows = g2.shape
    kept[:feat] = g2 * attb
    kept[feat:] = jnp.broadcast_to(attb, (16, rows))
    return g1, d1, d2 * attb


def add_node_outs(ph, d):
    ph.out_whole(BF, node_out=(d.parts, d.half, d.feat))
    shape = (d.parts, d.half, d.feat)
    ph.out_whole(F32, r1=shape, ip=(d.parts, d.half, d.wide), r2=shape, big=shape, cnt=shape)


def node_step(d, r, p, b):
    sums = mm(r.rt[: d.res], r.kept[...], 1, 1)
    at = pl.ds(pl.multiple_of(b * d.res, d.res), d.res)
    r.big[p, at, :] = sums[:, : d.feat] * 0.5
    r.cnt[p, at, :] = jnp.broadcast_to(sums[:, d.feat : d.feat + 1], (d.res, d.feat))


def node_forward(r, p, n_own, layer, aux):
    big = r.big[p]
    hi = big.astype(BF)
    lo = (big - hi.astype(F32)).astype(BF)
    w3 = r.mw3[layer]
    upd = (mm(hi, w3) + mm(lo, w3) + r.cnt[p] * aux[2:3]) / 30.0
    r1 = n_own.astype(F32) + upd
    xh1, _ = norm_rows(r1)
    normed = xh1 * aux[10:11] + aux[7:8]
    ip = mm(normed.astype(BF), r.inner[layer]) + r.inner_b[layer]
    hid = gelu_pair_wide(ip)[0].astype(BF)
    r2 = normed + (mm(hid, r.outer[layer]) + aux[3:4])
    xh2, _ = norm_rows(r2)
    out = ((xh2 * aux[11:12] + aux[8:9]) * r.mask[p]).astype(BF)
    r.node_out[p] = out
    r.r1[p] = r1
    r.ip[p] = ip
    r.r2[p] = r2
    return out


def node_backward(d, r, p, layer, aux, dn):
    def rows_of(ref):
        return ref[...].reshape(-1, ref.shape[2]) if p is None else ref[p]

    r1, ip, r2, big, cnt = rows_of(r.r1), rows_of(r.ip), rows_of(r.r2), rows_of(r.big), rows_of(r.cnt)
    xh1, rs1 = norm_rows(r1)
    normed = xh1 * aux[10:11] + aux[7:8]
    xh2, rs2 = norm_rows(r2)
    dy2 = dn * rows_of(r.mask)
    dr2 = norm_back_rows(dy2 * aux[11:12], xh2, rs2)
    low_outer = dr2.astype(BF)
    hid, slope = gelu_pair_wide(ip)
    dip = mm(low_outer, r.outer[layer], 1, 1) * slope
    low_inner = dip.astype(BF)
    at = d.at_outer
    r.msg[at : at + d.wide] += mm(hid.astype(BF), low_outer, 0, 0)
    at = d.at_inner
    r.msg[at : at + d.wide] += mm(low_inner, normed.astype(BF), 0, 0)
    dnormed = dr2 + mm(low_inner, r.inner[layer], 1, 1)
    dr1 = norm_back_rows(dnormed * aux[10:11], xh1, rs1)
    du = dr1 / 30.0
    dub = du.astype(BF)
    r.msg[4 * d.feat : 5 * d.feat] += mm(big.astype(BF), dub, 0, 0)
    dib = jnp.sum(dip, axis=0, keepdims=True)
    rows = {
        2: jnp.sum(cnt * du, axis=0, keepdims=True),
        3: jnp.sum(dr2, axis=0, keepdims=True),
        7: jnp.sum(dnormed, axis=0, keepdims=True),
        8: jnp.sum(dy2, axis=0, keepdims=True),
        10: jnp.sum(dnormed * xh1, axis=0, keepdims=True),
        11: jnp.sum(dy2 * xh2, axis=0, keepdims=True),
    }
    for i in range(d.wide // d.feat):
        rows[16 + i] = dib[:, i * d.feat : (i + 1) * d.feat]
    for row, value in rows.items():
        r.msg[d.at_small + row : d.at_small + row + 1] += value
    if p is None:
        r.dr1[...] = dr1.reshape(r.dr1.shape)
        r.dub[...] = dub.reshape(r.dub.shape)
    else:
        r.dr1[p] = dr1
        r.dub[p] = dub


def own_first(d, row):
    row = row.astype(F32)
    if row.shape[0] == 1:
        row = jnp.broadcast_to(row, (8, d.length))
    return jnp.where(lax.axis_index(AXIS_S) == 0, row, pltpu.roll(row, d.half, 1))


def put_positions(d, r):
    section = lax.axis_index(AXIS_S)
    centre = d.length // 2
    line = lax.broadcasted_iota(jnp.int32, (8, d.length), 0)
    for p in range(d.parts):
        live = own_first(d, r.live[p : p + 1, :])
        order = own_first(d, r.order[p : p + 1, :]) - centre
        code = jnp.where(live > 0.5, order, float(centre))
        r.codes[p, :8] = jnp.where(line == 0, live, jnp.where(line == 1, code, 0.0)).astype(BF)
        r.codes[p, 8:] = jnp.zeros((EXTRA - 8, d.length), BF)
        ids = own_first(d, r.near[p]) - float(d.half) * section.astype(F32)
        ids = jnp.where(ids < 0.0, ids + float(d.length), ids) - float(centre)
        r.mask[p] = jnp.broadcast_to(live[0:1], (d.feat, d.length)).T[: d.half]
        for b in range(d.blocks):
            own = pltpu.roll(order, (d.length - b * d.res) % d.length, 1) if b else order
            r.owns[p, b, :8] = jnp.where(line == 1, -own, 0.0)[:, : d.res].astype(BF)
            r.owns[p, b, 8:] = jnp.zeros((EXTRA - 8, d.res), BF)
            block = pltpu.roll(ids, (d.length - b * d.res) % d.length, 1) if b else ids
            spread = mm(block[:, : d.res].astype(BF), r.rt[: d.res])
            row = jnp.sum(spread * r.pick[...].astype(F32), axis=0, keepdims=True)
            r.idx[p, b] = row.astype(jnp.int32) + centre


def encoder_message(d, edge_input, node_input, neighbors, residue_mask, decode_order, weights, consts):
    ph = Phase(d, 2)
    ph.raw(n_far=node_input)
    ph.whole(n_own=node_input, rt=consts.sums, pick=consts.pick, near=neighbors, live=residue_mask, order=decode_order)
    ph.whole(edge=edge_input)
    ph.later = (EDGE,)
    ph.out_whole(jnp.int32, idx=(d.parts, d.blocks, 1, d.rows))
    ph.out_whole(F32, mask=(d.parts, d.half, d.feat))
    ph.temp(BF, codes=(d.parts, EXTRA, d.length), owns=(d.parts, d.blocks, EXTRA, d.res))
    names = tuple(weights)
    own = {W_IN + n: a for n, a in weights.items()}
    ph.raw(**own)
    act = (d.parts, d.blocks, d.feat, d.rows)
    ph.out_stream(BF, g1=with_ones(d), d1=act, d2=act)
    ph.out_whole(F32, att=(d.parts, d.blocks, 1, d.rows))
    add_node_outs(ph, d)
    ph.out_raw(BF, got=(d.half, d.feat), nodes_got=node_input.shape)
    for n, a in weights.items():
        ph.out_raw(a.dtype, **{W_OUT + n: (2,) + a.shape})
        ph.temp(a.dtype, **{n: (2,) + a.shape})
    sq = (d.feat, d.feat)
    wide = d.feat + d.length + d.res
    ph.temp(BF, n_cat=(d.length, d.feat), lhs=(d.feat + EXTRA, wide), w2t=sq, tt=(d.parts * d.blocks, wide, d.rows))
    ph.temp(BF, leave=(d.half, d.feat), arrive=node_input.shape, kept=(d.feat + 16, d.rows))
    ph.temp(F32, aux=sq, cols=sq)
    count = len(names)
    ph.sems(send=count + 1 + d.parts, recv=count + 1 + d.parts, local=count, back=2 * count + 1)

    def body(r):
        p, b = pl.program_id(0), pl.program_id(1)
        first, last = b == 0, b == d.blocks - 1
        section = lax.axis_index(AXIS_S)
        job = to_partner(r.leave, r.got, r.send.at[count], r.recv.at[count])
        nodes = [
            to_partner(r.n_far.at[q], r.arrive.at[q], r.send.at[count + 1 + q], r.recv.at[count + 1 + q])
            for q in range(d.parts)
        ]

        def swaps(group):
            out = []
            for n in group:
                i = names.index(n)
                dst = getattr(r, n).at[section]
                out.append(to_partner(getattr(r, W_IN + n), dst, r.send.at[i], r.recv.at[i]))
            return out

        def own_copies():
            return [
                pltpu.make_async_copy(getattr(r, W_IN + n), getattr(r, n).at[section], r.local.at[i])
                for i, n in enumerate(names)
            ]

        def returns(group):
            out = [pltpu.make_async_copy(r.arrive, r.nodes_got, r.back.at[2 * count])] if group == GROUP_ONE else []
            for n in group:
                i = names.index(n)
                src, dst = getattr(r, n), getattr(r, W_OUT + n)
                for layer in range(2):
                    sem = r.back.at[2 * i + layer]
                    out.append(pltpu.make_async_copy(src.at[layer], dst.at[layer], sem))
            return out

        begin = first & (p == 0)
        middle = (p == 1) & (b == 1)
        at_end = last & (p == d.parts - 1)

        @pl.when(begin)
        def _():
            greet_partner()
            for item in nodes[:1] + swaps(GROUP_ONE) + own_copies() + nodes[1:]:
                item.start()
            r.load()
            put_positions(d, r)
            r.load(EDGE)
            for q in range(d.parts):

                @pl.loop(0, d.blocks)
                def _(c, q=q):
                    table = r.tt.at[q * d.blocks + c]
                    put_one_hot(d, table, d.feat, r.idx[q, c])
                    table[d.feat + d.length :, :] = r.rt[: d.res]
                    own = r.edge[q, pl.ds(pl.multiple_of(c * d.res, d.res), d.res)]
                    table[: d.feat, :] = own.reshape(d.rows, d.feat).T

            for item in nodes[:1] + swaps(GROUP_ONE) + own_copies():
                item.wait()
            for item in swaps(GROUP_TWO) + swaps(GROUP_THREE):
                item.start()
            r.lhs[: d.feat, : d.feat] = r.mw1[0, d.feat : 2 * d.feat, :].T
            r.lhs[d.feat :, : d.feat] = jnp.zeros((EXTRA, d.feat), BF)
            r.w2t[...] = half_of(r.mw2[0]).T
            load_cols(r, 0, r.aux, r.cols)

        for q in range(1, d.parts):

            @pl.when(first & (p == q))
            def _(q=q):
                nodes[q].wait()

        @pl.when(first)
        def _():
            r.n_cat[: d.half] = r.n_own[p]
            r.n_cat[d.half :] = r.arrive[p]
            put_table(d, r.lhs, 0, d.feat, r.n_cat, r.mw1.at[0])

        n_blk = r.n_own[p, pl.ds(pl.multiple_of(b * d.res, d.res), d.res), :]
        r.ready()
        put_own(d, r.lhs, 0, d.feat, r.mw1.at[0], n_blk, r.cols[:, 0:1])
        r.lhs[d.feat :, d.feat : d.feat + d.length] = r.codes[p]
        r.lhs[d.feat :, d.feat + d.length :] = r.owns[p, b]
        out = mm(r.lhs[...], r.tt[p * d.blocks + b])
        att = out[d.feat : d.feat + 1]
        r.att[p, b] = jnp.where(out[d.feat + 1 : d.feat + 2] < 0.0, 1.0, 0.0)
        g1, r.d1[...], r.d2[...] = message_part(out[: d.feat], r.w2t[...], r.cols[:, 1:2], att, r.kept)
        put_ones(r.g1, g1)
        node_step(d, r, p, b)
        r.flush()

        @pl.when(middle)
        def _():
            for item in swaps(GROUP_TWO) + swaps(GROUP_THREE):
                item.wait()
            for item in returns(GROUP_ONE) + returns(GROUP_TWO) + returns(GROUP_THREE):
                item.start()
            r.leave[...] = node_forward(r, 0, r.n_own[0], 0, r.aux[...])
            job.start()

        @pl.when(at_end)
        def _():
            node_forward(r, d.parts - 1, r.n_own[d.parts - 1], 0, r.aux[...])
            for item in returns(GROUP_ONE) + returns(GROUP_TWO) + returns(GROUP_THREE):
                item.wait()
            job.wait()

    return ph.call("enc_message", body)


W_IN, W_OUT = "i_", "o_"
EDGE = "edge"
GROUP_ONE = ("mw1", "mw2", "bias", "gain")
GROUP_TWO = ("mw3", "inner", "inner_b", "outer")
GROUP_THREE = ("uw1", "uw2", "uw3")
NODE_W = ("mw3", "inner", "inner_b", "outer", "bias", "gain")
MSG_W = ("mw1", "mw2")
UPD_W = ("uw1", "uw2", "uw3")


def with_ones(d):
    return (d.parts, d.blocks, d.feat + 16, d.rows)


def put_ones(ref, g):
    feat, rows = g.shape
    ref[:feat] = g
    ref[feat:] = jnp.ones((16, rows), BF)


def half_of(w):
    return w * BF(0.5)


def update_forward(d, a1, w2t, w3c, b5, b6c, pair, cols):
    f = d.feat
    g1, d1 = gelu_pair(a1)
    a2 = mm(w2t, g1) + b5
    g2, d2 = gelu_pair(a2)
    pair[f : 2 * f] = g2
    cent = mm(w3c[...], pair[: 2 * f]) + b6c
    var = jnp.mean(cent * cent, axis=0, keepdims=True)
    rs = lax.rsqrt(var + EPS)
    xh = cent.astype(BF) * rs.astype(BF)
    y = xh * cols[:, 12:13].astype(BF) + cols[:, 9:10].astype(BF)
    return g1, d1, g2, d2, xh, rs, y


def centre_weights(w3, cols, w3c, b6c):
    feat = w3.shape[0]
    eye = lax.broadcasted_iota(jnp.int32, w3.shape, 0) == lax.broadcasted_iota(jnp.int32, w3.shape, 1)
    w3f = w3.astype(F32)
    w3c[:, feat:] = (0.5 * (w3f - jnp.mean(w3f, axis=1, keepdims=True))).T.astype(BF)
    w3c[:, :feat] = (eye.astype(F32) - 1.0 / feat).astype(BF)
    b6 = cols[:, 6:7]
    b6c[...] = jnp.broadcast_to(b6 - jnp.mean(b6, axis=0, keepdims=True), b6c.shape)


def encoder_update(d, edge_input, st, fa, consts):
    ph = Phase(d, 3)
    ph.raw(n_far=fa.node_out)
    ph.whole(n_own=fa.node_out, got_a=fa.got, idx=consts.idx, rt=consts.sums, mask=consts.mask, att=fa.att)
    ph.edges(edge=edge_input)
    ph.whole(**weight_args(st, *NODE_W, *MSG_W, *UPD_W))
    act = (d.parts, d.blocks, d.feat, d.rows)
    two = (d.parts, d.blocks, 2 * d.feat + 16, d.rows)
    ph.out_stream(BF, ugs=two, ud1=act, ud2=act, uxh=act, e2g=two, d1=act, d2=act)
    ph.out_whole(F32, urs=(d.parts, d.blocks, 1, d.rows))
    add_node_outs(ph, d)
    ph.out_whole(BF, got_in=(d.half, d.feat))
    ph.out_raw(BF, got=(d.parts, d.half, d.feat))
    sq = (d.feat, d.feat)
    wide = d.feat + d.length + d.res
    ph.temp(BF, n_cat=(d.length, d.feat), lhs=(2 * d.feat, wide), tt=(wide, d.rows))
    ph.temp(BF, uw2t=sq, mw2t=sq, w3c=(d.feat, 2 * d.feat), pair=(2 * d.feat, d.rows))
    ph.temp(BF, kept=(d.feat + 16, d.rows), leave=(d.parts, d.half, d.feat), arrive=(d.half, d.feat))
    ph.temp(F32, w3c_b=sq, e_aux=sq, e_cols=sq, d_aux=sq, d_cols=sq)
    ph.sems(send=d.parts + 1, recv=d.parts + 1)

    def body(r):
        p, b = pl.program_id(0), pl.program_id(1)
        first, last = b == 0, b == d.blocks - 1
        early = to_partner(r.n_far.at[d.parts - 1], r.arrive, r.send.at[d.parts], r.recv.at[d.parts])
        jobs = [to_partner(r.leave.at[i], r.got.at[i], r.send.at[i], r.recv.at[i]) for i in range(d.parts)]

        @pl.when(first & (p == 0))
        def _():
            greet_partner()
            early.start()
            r.load()
            r.tt[d.feat + d.length :, :] = r.rt[: d.res]
            r.lhs[: d.feat, : d.feat] = r.uw1[0, d.feat : 2 * d.feat, :].T
            r.lhs[d.feat :, : d.feat] = r.mw1[1, d.feat : 2 * d.feat, :].T
            r.uw2t[...] = half_of(r.uw2[0]).T
            r.mw2t[...] = half_of(r.mw2[1]).T
            load_cols(r, 0, r.e_aux, r.e_cols)
            load_cols(r, 1, r.d_aux, r.d_cols)
            centre_weights(r.uw3[0], r.e_cols[...], r.w3c, r.w3c_b)
            r.n_cat[d.half :] = r.got_a[...]

        @pl.when(first & (p == 1))
        def _():
            early.wait()
            r.n_cat[d.half :] = r.arrive[...]
            r.got_in[...] = r.arrive[...]

        @pl.when(first)
        def _():
            r.n_cat[: d.half] = r.n_own[p]
            put_table(d, r.lhs, 0, d.feat, r.n_cat, r.uw1.at[0])
            put_table(d, r.lhs, d.feat, d.feat, r.n_cat, r.mw1.at[1])

        r.ready()
        n_blk = r.n_own[p, pl.ds(pl.multiple_of(b * d.res, d.res), d.res), :]
        put_own(d, r.lhs, 0, d.feat, r.uw1.at[0], n_blk, r.e_cols[:, 4:5])
        put_own(d, r.lhs, d.feat, d.feat, r.mw1.at[1], n_blk, r.d_cols[:, 0:1])
        put_one_hot(d, r.tt, d.feat, r.idx[p, b])
        edge_t = r.edge[...].reshape(d.rows, d.feat).T
        r.tt[: d.feat, :] = edge_t
        r.pair[: d.feat] = edge_t
        g1, d1, g2, d2, xh, rs, e2 = update_forward(
            d, mm(r.lhs[: d.feat], r.tt[...]), r.uw2t[...], r.w3c, r.e_cols[:, 5:6], r.w3c_b[:, 0:1], r.pair, r.e_cols
        )
        f = d.feat
        r.ugs[:f] = g2
        put_ones(r.ugs.at[f:], g1)
        r.ud1[...], r.ud2[...], r.uxh[...], r.urs[p, b], r.e2g[:f] = d1, d2, xh, rs, e2
        att = r.att[p, b]
        r.tt[:f] = e2
        a1 = mm(r.lhs[f:], r.tt[...])
        g1, r.d1[...], r.d2[...] = message_part(a1, r.mw2t[...], r.d_cols[:, 1:2], att, r.kept)
        put_ones(r.e2g.at[f:], g1)
        node_step(d, r, p, b)
        r.flush()

        @pl.when(last)
        def _():
            r.leave[p] = node_forward(r, p, r.n_own[p], 1, r.d_aux[...])
            for i in range(d.parts):

                @pl.when(p == i)
                def _(i=i):
                    jobs[i].start()

            @pl.when(p == d.parts - 1)
            def _():
                for job in jobs:
                    job.wait()

    return ph.call("enc_update", body)


def spread_nodes(d, acc, sumk, w1, n_cat, grad, grad_at):
    s = acc.astype(BF)
    sk = jnp.concatenate([x[:, : d.res] for x in sumk], axis=1)
    skb = sk.astype(BF)
    far = mm(s, w1[2 * d.feat :].T, 0, 0)
    own = mm(skb, w1[: d.feat].T, 0, 0)
    grad[grad_at + 2 * d.feat : grad_at + 3 * d.feat, :] += mm(n_cat, s, 0, 1)
    grad[grad_at : grad_at + d.feat, :] += mm(n_cat[: d.half], skb, 0, 1)
    return own + far[: d.half], far[d.half :], to_row(sk)


def lane_total(x):
    size = x.shape[1] // 4
    x = (x[:, :size] + x[:, size : 2 * size]) + (x[:, 2 * size : 3 * size] + x[:, 3 * size :])
    return lane_sum(x.astype(F32))


def norm_backward(d, r, dy, xh, rs, gain_mat):
    r.a_b9[...] += lane_total(dy)
    r.a_g2[...] += lane_total(dy * xh)
    z = mm(gain_mat, dy).astype(BF)
    m2 = jnp.mean((z * xh).astype(F32), axis=0, keepdims=True)
    return (z - xh * m2.astype(BF)) * rs.astype(BF)


def gain_matrix(cols):
    feat = cols.shape[0]
    shape = (feat, feat)
    eye = lax.broadcasted_iota(jnp.int32, shape, 0) == lax.broadcasted_iota(jnp.int32, shape, 1)
    scaled = jnp.where(eye, jnp.broadcast_to(cols[:, 12:13], shape), 0.0)
    return (scaled - jnp.mean(scaled, axis=0, keepdims=True)).astype(BF)


def update_backward(d, r, dr3, gs, d1, d2, w2, w3, low, da1):
    f = d.feat
    low[:f] = dr3
    low[f:] = mm(w3, dr3).astype(BF) * d2
    r.a_w23[...] += mm(gs, low[...], 1, 1)
    da1[...] = mm(w2, low[f:]).astype(BF) * d1


def update_small(d, r, b4):
    f = d.feat
    at = 5 * f
    r.upd[at + 4 : at + 5] += b4

    @pl.when(pl.program_id(0) == d.parts - 1)
    def _():
        r.upd[3 * f : 4 * f] = 0.5 * r.a_w23[f : 2 * f, f:]
        r.upd[4 * f : 5 * f] = 0.5 * r.a_w23[:f, :f]
        r.upd[at + 5 : at + 6] = r.a_w23[2 * f : 2 * f + 1, f:]
        r.upd[at + 6 : at + 7] = r.a_w23[2 * f : 2 * f + 1, :f]
        r.upd[at + 9 : at + 10] = to_row(r.a_b9[...])
        r.upd[at + 12 : at + 13] = to_row(r.a_g2[...])


def block_before(d):
    step = jnp.maximum(pl.program_id(0) * d.blocks + pl.program_id(1) - 1, 0)
    return step // d.blocks, lax.rem(step, d.blocks)


def put_spread(d, r, q, c, spread):
    r.a_s[q] += spread[:, : d.length]
    r.a_k[q, c] = spread[:, d.length :]


def zero(*refs):
    for ref in refs:
        ref[...] = jnp.zeros(ref.shape, ref.dtype)


def decoder_update(d, st, fb, cot, consts):
    ph = Phase(d)
    ph.whole(n_own=fb.node_out, n_got=fb.got, idx=consts.idx, rt=consts.sums)
    ph.stream_top(d.feat, e2=fb.e2g)
    ph.edges(cot=cot)
    ph.whole(**weight_args(st, *UPD_W, *AUX_W))
    ph.out_edges(decoded=cot.shape)
    ph.out_stream(BF, part=(d.parts, d.blocks, d.feat, d.rows))
    ph.out_whole(F32, upd=(d.upd_rows, d.feat), dn_own=(d.parts, d.half, d.feat))
    ph.out_whole(BF, dn_far=(d.parts, d.half, d.feat), nodes=(d.parts, d.half, d.feat))
    sq = (d.feat, d.feat)
    wide = d.length + d.res
    ph.temp(BF, n_cat=(d.length, d.feat), lhs=(d.feat, wide), w1bt=sq, w2t=sq, w2h=sq, w3h=sq)
    ph.temp(BF, tt=(wide, d.rows), tn=(d.rows, d.length + 128), da1=(d.feat, d.rows))
    ph.temp(BF, w3c=(d.feat, 2 * d.feat), gain_mat=sq, pair=(3 * d.feat + 16, d.rows), low=(2 * d.feat, d.rows))
    ph.temp(F32, w3c_b=sq, aux=sq, cols=sq, a_w23=(2 * d.feat + 16, 2 * d.feat), a_b9=sq, a_g2=sq)
    ph.temp(F32, a_s=(d.parts, d.feat, d.length), a_k=(d.parts, d.blocks, d.feat, 128))

    def body(r):
        p, b = pl.program_id(0), pl.program_id(1)
        first = b == 0

        @pl.when(first & (p == 0))
        def _():
            r.load()
            r.nodes[...] = r.n_own[...]
            r.w1bt[...] = r.uw1[1, d.feat : 2 * d.feat, :].T
            r.w2h[...] = half_of(r.uw2[1])
            r.w2t[...] = r.w2h[...].T
            r.w3h[...] = half_of(r.uw3[1])
            load_cols(r, 1, r.aux, r.cols)
            centre_weights(r.uw3[1], r.cols[...], r.w3c, r.w3c_b)
            r.gain_mat[...] = gain_matrix(r.cols[...])
            zero(r.upd, r.a_w23, r.a_b9, r.a_g2, r.a_s)
            r.pair[3 * d.feat :] = jnp.ones((16, d.rows), BF)
            r.tt[d.length :, :] = r.rt[: d.res]
            r.tn[:, d.length :] = r.rt[...].T

        @pl.when(first)
        def _():
            r.n_cat[: d.half] = r.n_own[p]
            r.n_cat[d.half :] = r.n_got[p]
            put_table(d, r.lhs, 0, 0, r.n_cat, r.uw1.at[1])

        r.ready()
        f = d.feat
        n_blk = r.n_own[p, pl.ds(pl.multiple_of(b * d.res, d.res), d.res), :]
        put_own(d, r.lhs, 0, 0, r.uw1.at[1], n_blk, r.cols[:, 4:5])
        idx = r.idx[p, b]
        put_one_hot(d, r.tt, 0, idx)
        put_one_hot_rows(d, r.tn, idx)
        e2 = r.e2[...]
        r.pair[:f] = e2
        a1 = mm(r.lhs[...], r.tt[...]) + mm(r.w1bt[...], e2)
        g1, d1, _, d2, xh, rs, y = update_forward(
            d, a1, r.w2t[...], r.w3c, r.cols[:, 5:6], r.w3c_b[:, 0:1], r.pair, r.cols
        )
        r.pair[2 * f : 3 * f] = g1
        r.decoded[...] = y.T.reshape(d.res, d.near, f)
        dy = r.cot[...].reshape(d.rows, f).T
        dr3 = norm_backward(d, r, dy, xh, rs, r.gain_mat[...])
        update_backward(d, r, dr3, r.pair[f:], d1, d2, r.w2h[...], r.w3h[...], r.low, r.da1)
        r.upd[f : 2 * f] += mm(e2, r.da1[...], 1, 1)
        r.part[...] = (mm(r.uw1[1, f : 2 * f, :], r.da1[...]) + dr3.astype(F32)).astype(BF)
        put_spread(d, r, p, b, mm(r.da1[...], r.tn[...]))
        r.flush()

        @pl.when((b == d.blocks - 1) & (p == d.parts - 1))
        def _():
            total = jnp.zeros((1, f), F32)
            for q in range(d.parts):
                nodes = jnp.concatenate([r.n_own[q], r.n_got[q]], axis=0)
                sums = [r.a_k[q, i] for i in range(d.blocks)]
                own, far, b4 = spread_nodes(d, r.a_s[q], sums, r.uw1[1], nodes, r.upd, 0)
                r.dn_own[q] = own
                r.dn_far[q] = far.astype(BF)
                total = total + b4
            update_small(d, r, total)

    return ph.call("dec_update", body)


AUX_W = ("bias", "gain")


def message_backward(d, r, b, layer, low):
    at = pl.ds(pl.multiple_of(b * d.res, d.res), d.res)
    v = (mm(r.mw3[layer], r.dub[pl.program_id(0), at, :], 1, 1) * 0.5).astype(BF)
    f = d.feat
    low[:f] = mm(v, r.rt[: d.res]).astype(BF) * r.d2[...]
    low[f:] = mm(r.mw2h[...], low[:f]).astype(BF) * r.d1[...]


def message_small(d, r, b0):
    r.msg[d.at_small : d.at_small + 1] += b0


def middle_backward(d, edge_input, st, fa, fb, fd, cot_n, consts):
    ph = Phase(d, 4)
    ph.raw(dn_far_in=fd.dn_far)
    ph.whole(cot_n=cot_n, dn_a=fd.dn_own, n_own=fa.node_out, got_a=fa.got, got_b=fb.got_in)
    ph.whole(mask=consts.mask, rt=consts.sums, r1=fb.r1, ip=fb.ip, r2=fb.r2, big=fb.big, cnt=fb.cnt)
    ph.whole(urs=fb.urs, idx=consts.idx)
    ph.stream(d2=fb.d2, d1=fb.d1, e2g=fb.e2g, dec_part=fd.part, uxh=fb.uxh, ugs=fb.ugs, ud2=fb.ud2, ud1=fb.ud1)
    ph.edges(edge=edge_input)
    ph.whole(**weight_args(st, *NODE_W, *MSG_W, *UPD_W))
    ph.out_stream(BF, part=(d.parts, d.blocks, d.feat, d.rows))
    ph.out_whole(F32, msg=(d.msg_rows, d.feat), upd=(d.upd_rows, d.feat), dn_own=(d.parts, d.half, d.feat))
    ph.out_raw(BF, got=(d.parts, d.half, d.feat))
    sq = (d.feat, d.feat)
    ph.temp(BF, n_cat=(d.length, d.feat), dub=(d.parts, d.half, d.feat), tt=(d.length + d.res, d.rows))
    ph.temp(BF, tri=(3 * d.feat, d.rows), low=(2 * d.feat, d.rows), w2h=sq, w3h=sq, mw2h=sq, gain_mat=sq)
    ph.temp(BF, leave=(d.parts, d.half, d.feat), arrive=(d.parts, d.half, d.feat))
    ph.temp(F32, dr1=(d.parts, d.half, d.feat), e_aux=sq, e_cols=sq, d_aux=sq, d_cols=sq)
    tall = (2 * d.feat + 16, 2 * d.feat)
    ph.temp(F32, m_w12=tall, a_w23=tall, a_b9=sq, a_g2=sq, a_w1=sq)
    ph.temp(F32, a_s=(2 * d.feat, d.length), a_k=(d.blocks, 2 * d.feat, 128))
    ph.sems(send=2 * d.parts, recv=2 * d.parts)

    def body(r):
        p, b = pl.program_id(0), pl.program_id(1)
        first, last = b == 0, b == d.blocks - 1
        n = d.parts
        early = [to_partner(r.dn_far_in.at[i], r.arrive.at[i], r.send.at[n + i], r.recv.at[n + i]) for i in range(n)]
        jobs = [to_partner(r.leave.at[i], r.got.at[i], r.send.at[i], r.recv.at[i]) for i in range(n)]

        @pl.when(first & (p == 0))
        def _():
            greet_partner()
            for job in early:
                job.start()
            r.load()
            load_cols(r, 0, r.e_aux, r.e_cols)
            load_cols(r, 1, r.d_aux, r.d_cols)
            r.tt[d.length :, :] = r.rt[: d.res]
            r.w2h[...] = half_of(r.uw2[0])
            r.w3h[...] = half_of(r.uw3[0])
            r.mw2h[...] = half_of(r.mw2[1])
            r.gain_mat[...] = gain_matrix(r.e_cols[...])
            zero(r.msg, r.upd, r.m_w12, r.a_w23, r.a_b9, r.a_g2, r.a_w1)
            r.n_cat[d.half :] = r.got_a[...]

        @pl.when(first & (p == 1))
        def _():
            r.n_cat[d.half :] = r.got_b[...]

        for i in range(n):

            @pl.when(first & (p == i))
            def _(i=i):
                early[i].wait()

        @pl.when(first)
        def _():
            r.n_cat[: d.half] = r.n_own[p]
            zero(r.a_s)
            dn = r.cot_n[p].astype(F32) + r.dn_a[p] + r.arrive[p].astype(F32)
            node_backward(d, r, p, 1, r.d_aux[...], dn)

        f = d.feat
        r.ready()
        put_one_hot(d, r.tt, 0, r.idx[p, b])
        message_backward(d, r, b, 1, r.tri.at[: 2 * f])
        r.m_w12[...] += mm(r.e2g[...], r.tri[: 2 * f], 1, 1)
        de = mm(r.mw1[1, f : 2 * f, :], r.tri[f : 2 * f])
        dy = (de + r.dec_part[...].astype(F32)).astype(BF)
        dr3 = norm_backward(d, r, dy, r.uxh[...], r.urs[p, b], r.gain_mat[...])
        da1 = r.tri.at[2 * f :]
        update_backward(d, r, dr3, r.ugs[...], r.ud1[...], r.ud2[...], r.w2h[...], r.w3h[...], r.low, da1)
        r.a_w1[...] += mm(da1[...], r.edge[...].reshape(d.rows, f))
        r.part[...] = (mm(r.uw1[0, f : 2 * f, :], da1[...]) + dr3.astype(F32)).astype(BF)
        spread = mm(r.tri[f:], r.tt[...], 1, 1)
        r.a_s[...] += spread[:, : d.length]
        r.a_k[b, :, : d.res] = spread[:, d.length :]
        r.flush()

        @pl.when(last)
        def _():
            n_cat = r.n_cat[...]
            a_k = [r.a_k[i] for i in range(d.blocks)]
            own_m, far_m, b0 = spread_nodes(
                d, r.a_s[: d.feat], [x[: d.feat] for x in a_k], r.mw1[1], n_cat, r.msg, 0
            )
            own_u, far_u, b4 = spread_nodes(
                d, r.a_s[d.feat :], [x[d.feat :] for x in a_k], r.uw1[0], n_cat, r.upd, 0
            )
            r.dn_own[p] = own_m + own_u + r.dr1[p]
            r.leave[p] = (far_m + far_u).astype(BF)
            for i in range(n):

                @pl.when(p == i)
                def _(i=i):
                    jobs[i].start()

            message_small(d, r, b0)
            update_small(d, r, b4)

            @pl.when(p == n - 1)
            def _():
                f, at = d.feat, d.at_small
                r.upd[f : 2 * f] = r.a_w1[...].T
                r.msg[f : 2 * f] = r.m_w12[:f, f:]
                r.msg[3 * f : 4 * f] = 0.5 * r.m_w12[f : 2 * f, :f]
                r.msg[at + 1 : at + 2] = r.m_w12[2 * f : 2 * f + 1, :f]
                for job in jobs:
                    job.wait()

    return ph.call("dec_message_back", body)


def encoder_message_back(d, edge_input, st, fa, fe, n_own, n_got, consts):
    ph = Phase(d)
    ph.whole(dn_a=fe.dn_own, dn_b=fe.got, n_own=n_own, n_got=n_got)
    ph.whole(mask=consts.mask, rt=consts.sums, r1=fa.r1, ip=fa.ip, r2=fa.r2, big=fa.big, cnt=fa.cnt)
    ph.whole(idx=consts.idx)
    ph.stream(d2=fa.d2, g1=fa.g1, d1=fa.d1, up_part=fe.part)
    ph.edges(edge=edge_input)
    ph.whole(**weight_args(st, *NODE_W, *MSG_W))
    ph.out_edges(edge_grad=edge_input.shape)
    ph.out_whole(F32, msg=(d.msg_rows, d.feat), dn_own=(d.parts, d.half, d.feat))
    ph.out_whole(BF, dn_far=(d.parts, d.half, d.feat))
    sq = (d.feat, d.feat)
    ph.temp(BF, dub=(d.parts, d.half, d.feat), tn=(d.rows, d.length + 128))
    ph.temp(BF, low=(2 * d.feat, d.rows), mw2h=sq)
    ph.temp(F32, dr1=(d.parts, d.half, d.feat), aux=sq, cols=sq, a_w1=sq, m_w2=(d.feat + 16, d.feat))
    ph.temp(F32, a_s=(d.parts, d.feat, d.length), a_k=(d.parts, d.blocks, d.feat, 128))

    def body(r):
        p, b = pl.program_id(0), pl.program_id(1)

        @pl.when((b == 0) & (p == 0))
        def _():
            zero(r.a_s, r.low, r.tn)
            r.load()
            load_cols(r, 0, r.aux, r.cols)
            r.tn[:, d.length :] = r.rt[...].T
            r.mw2h[...] = half_of(r.mw2[0])
            zero(r.msg, r.m_w2, r.a_w1)
            dn = r.dn_a[...] + r.dn_b[...].astype(F32)
            node_backward(d, r, None, 0, r.aux[...], dn.reshape(-1, d.feat))

        f = d.feat
        r.ready()
        put_spread(d, r, *block_before(d), mm(r.low[f:], r.tn[...]))
        put_one_hot_rows(d, r.tn, r.idx[p, b])
        message_backward(d, r, b, 0, r.low)
        da1 = r.low.at[f:]
        r.m_w2[...] += mm(r.g1[...], r.low[:f], 1, 1)
        r.a_w1[...] += mm(da1[...], r.edge[...].reshape(d.rows, f))
        de = mm(r.mw1[0, f : 2 * f, :], da1[...])
        de = (de + r.up_part[...].astype(F32)).astype(BF)
        r.edge_grad[...] = de.T.reshape(d.res, d.near, f)
        r.flush()

        @pl.when((b == d.blocks - 1) & (p == d.parts - 1))
        def _():
            put_spread(d, r, p, b, mm(da1[...], r.tn[...]))
            for q in range(d.parts):
                nodes = jnp.concatenate([r.n_own[q], r.n_got[q]], axis=0)
                sums = [r.a_k[q, i] for i in range(d.blocks)]
                own, far, b0 = spread_nodes(d, r.a_s[q], sums, r.mw1[0], nodes, r.msg, 0)
                r.dn_own[q] = own + r.dr1[q]
                r.dn_far[q] = far.astype(BF)
                message_small(d, r, b0)
            at = d.at_small
            r.msg[f : 2 * f] = r.a_w1[...].T
            r.msg[3 * f : 4 * f] = 0.5 * r.m_w2[:f]
            r.msg[at + 1 : at + 2] = r.m_w2[f : f + 1]

    return ph.call("enc_message_back", body)


class Reducer:
    def __init__(self, devices, feat, shares):
        self.feat = feat
        self.bits = bits = devices.bit_length() - 1
        self.groups = [16 * devices * share for share in shares]
        self.rows = sum(self.groups)
        self.bases = [sum(self.groups[:i]) for i in range(len(shares))]
        pairs, top = [], bits
        while top > 1:
            low = max(1, top - 2)
            pairs.insert(0, (low, top - low))
            top = low
        dims = [ACROSS] + pairs
        turn = min(3, len(dims))
        self.plans = []
        for g, size in enumerate(self.groups):
            head = dims[:turn]
            order = ([(0, 1)] if bits else []) + head[g % turn :] + head[: g % turn] + dims[turn:]
            both, plan = True, []
            for dim in order:
                if dim == ACROSS:
                    both = False
                else:
                    size >>= dim[1]
                plan.append((dim, size, both))
            self.plans.append(plan)
        self.backs = [[step for step in reversed(plan) if step[0] != ACROSS] for plan in self.plans]
        self.halving = len(self.plans[0])
        self.stages = self.halving + len(self.backs[0])
        self.dims = ([(0, 1)] if bits else []) + dims
        self.sem_at, self.buffer_at, self.shapes = {}, {}, []
        for g, plan in enumerate(self.plans):
            for k, (dim, size, both) in enumerate(plan):
                for o in self.offsets(dim):
                    self.sem_at[(g, k, o)] = len(self.sem_at)
                    self.buffer_at[(g, k, o)] = len(self.shapes)
                    self.shapes += [(2, size, feat) if both else (size, feat)] * 2
            for k, (dim, _, _) in enumerate(self.backs[g]):
                for o in self.offsets(dim):
                    self.sem_at[(g, self.halving + k, o)] = len(self.sem_at)

    def scratch(self):
        temps = [pltpu.VMEM((2, self.rows, self.feat), F32), pltpu.VMEM((self.rows, self.feat), BF)]
        temps += [pltpu.VMEM(shape, BF) for shape in self.shapes]
        return temps + [pltpu.SemaphoreType.DMA((len(self.sem_at),))] * 2

    def bind(self, refs):
        self.acc, self.gathered = refs[:2]
        self.buffers, (self.send, self.recv) = refs[2:-2], refs[-2:]

    def offsets(self, dim):
        return range(1, 2 if dim == ACROSS else 1 << dim[1])

    def code(self, dim):
        return lax.rem(lax.axis_index(AXIS_D) // (1 << dim[0]), 1 << dim[1])

    def peer(self, dim, o):
        if dim == ACROSS:
            return other_section()
        code = self.code(dim)
        other = lax.rem(code + o, 1 << dim[1])
        return {AXIS_D: lax.axis_index(AXIS_D) + (other - code) * (1 << dim[0])}

    def greet(self):
        barrier = pltpu.get_barrier_semaphore()
        count = 0
        for dim in self.dims:
            for o in self.offsets(dim):
                pl.semaphore_signal(barrier, inc=1, device_id=self.peer(dim, o), device_id_type=MESH)
                count += 1
        pl.semaphore_wait(barrier, count)

    def begin(self, g, k):
        start = self.bases[g]
        for dim, size, _ in self.plans[g][:k]:
            if dim != ACROSS:
                start = start + self.code(dim) * size
        return start

    def span(self, start, size):
        return pl.ds(pl.multiple_of(start, 16), size)

    def job(self, src, dst, key, dim):
        at = self.sem_at[key]
        return pltpu.make_async_remote_copy(
            src_ref=src, dst_ref=dst, send_sem=self.send.at[at], recv_sem=self.recv.at[at],
            device_id=self.peer(dim, key[2]), device_id_type=MESH,
        )

    def jobs(self, g, k):
        plan = self.plans[g]
        if k < self.halving:
            out = []
            for o in self.offsets(plan[k][0]):
                at = self.buffer_at[(g, k, o)]
                out.append(self.job(self.buffers[at], self.buffers[at + 1], (g, k, o), plan[k][0]))
            return out
        dim, size, _ = self.backs[g][k - self.halving]
        start = self.begin(g, [step[0] for step in plan].index(dim) + 1)
        part = self.gathered.at[self.span(start, size), :]
        return [self.job(part, part, (g, k, o), dim) for o in self.offsets(dim)]

    def start(self, g, k):
        section = lax.axis_index(AXIS_S)
        plan = self.plans[g]
        if k < self.halving:
            dim, size, both = plan[k]
            start = self.begin(g, k)
            for o in self.offsets(dim):
                out = self.buffers[self.buffer_at[(g, k, o)]]
                if dim == ACROSS:
                    out[...] = self.acc[1 - section, self.span(start, size), :].astype(BF)
                    continue
                give = self.span(start + lax.rem(self.code(dim) + o, 1 << dim[1]) * size, size)
                if both:
                    out[...] = self.acc[:, give, :].astype(BF)
                else:
                    out[...] = self.acc[section, give, :].astype(BF)
        elif k == self.halving:
            keep = self.span(self.begin(g, self.halving), plan[-1][1])
            self.gathered[keep, :] = self.acc[section, keep, :].astype(BF)
        for job in self.jobs(g, k):
            job.start()

    def finish(self, g, k):
        section = lax.axis_index(AXIS_S)
        for job in self.jobs(g, k):
            job.wait()
        if k >= self.halving:
            return
        dim, size, both = self.plans[g][k]
        keep = self.span(self.begin(g, k + 1), size)
        for o in self.offsets(dim):
            into = self.buffers[self.buffer_at[(g, k, o)] + 1]
            if both:
                self.acc[:, keep, :] += into[...].astype(F32)
            else:
                self.acc[section, keep, :] += into[...].astype(F32)

    def run(self):
        count = len(self.plans)
        for g in range(count):
            self.start(g, 0)
        for k in range(self.stages):
            for g in range(count):
                self.finish(g, k)
                if k + 1 < self.stages:
                    self.start(g, k + 1)
        if self.stages == self.halving:
            self.gathered[...] = self.acc[lax.axis_index(AXIS_S)].astype(BF)


ACROSS = (-1, 0)


def reduce_grads(d, enc_msg, enc_upd, dec_msg, dec_upd, dn_far):
    m, u = d.msg_rows, d.upd_rows
    units = -(-(m + u) // (16 * d.devices))
    red = Reducer(d.devices, d.feat, [2] * (units // 2) + [1] * (units % 2))

    def kernel(em, eu, dm, du, far, res, got, far_sems, load_sems, *refs):
        red.bind(refs)
        loads = []
        for layer, (msg, upd) in enumerate(((em, eu), (dm, du))):
            spots = (red.acc.at[layer, pl.ds(0, m)], red.acc.at[layer, pl.ds(m, u)])
            for i, (src, dst) in enumerate(zip((msg, upd), spots)):
                loads.append(pltpu.make_async_copy(src, dst, load_sems.at[2 * layer + i]))
        for item in loads:
            item.start()
        if red.rows > m + u:
            red.acc[:, m + u :] = jnp.zeros((2, red.rows - m - u, d.feat), F32)
        red.greet()
        nodes = to_partner(far, got, far_sems.at[0], far_sems.at[1])
        nodes.start()
        for item in loads:
            item.wait()
        red.run()
        res[...] = red.gathered[...]
        nodes.wait()

    vm, anywhere = pl.BlockSpec(memory_space=pltpu.VMEM), pl.BlockSpec(memory_space=pl.ANY)
    return pl.pallas_call(
        kernel,
        in_specs=[anywhere] * 5,
        out_specs=[vm, anywhere],
        out_shape=[jax.ShapeDtypeStruct((red.rows, d.feat), BF), jax.ShapeDtypeStruct(dn_far.shape, BF)],
        scratch_shapes=[pltpu.SemaphoreType.DMA((2,)), pltpu.SemaphoreType.DMA((4,))] + red.scratch(),
        compiler_params=pltpu.CompilerParams(vmem_limit_bytes=58 << 20, collective_id=5, has_side_effects=True),
        name="reduce",
    )(enc_msg, enc_upd, dec_msg, dec_upd, dn_far)


def unpack(d, total, dn_own, dn_got, n_bias, n_gain):
    f = d.feat
    m = d.msg_rows
    shapes = [(1, 3 * f, f), (1, f, f), (1, f, f), (1, f, d.wide), (1, 1, d.wide), (1, d.wide, f)]
    shapes += [(1, 3 * f, f), (1, f, f), (1, f, f), (n_bias, 1, f), (n_gain, 1, f)]

    def kernel(t, own, got, node, mw1, mw2, mw3, inner, inner_b, outer, uw1, uw2, uw3, bias, gain):
        node[...] = (own[...] + got[...].astype(F32)).astype(BF)
        for ref, at in ((mw1, 0), (mw2, 3 * f), (mw3, 4 * f), (outer, d.at_outer)):
            ref[0] = t[at : at + ref.shape[1], :].astype(F32)
        for ref, at in ((uw1, m), (uw2, m + 3 * f), (uw3, m + 4 * f)):
            ref[0] = t[at : at + ref.shape[1], :].astype(F32)
        inner[0] = t[d.at_inner : d.at_inner + d.wide, :].astype(F32).T
        small = t[d.at_small : d.at_small + SMALL, :].astype(F32)
        other = t[m + 5 * f : m + 5 * f + SMALL, :].astype(F32)
        both = small + other
        for i in range(n_bias):
            bias[i] = both[i : i + 1]
        for i in range(n_gain):
            gain[i] = both[n_bias + i : n_bias + i + 1]
        for i in range(d.wide // f):
            inner_b[0, :, i * f : (i + 1) * f] = small[16 + i : 17 + i]

    vm = pl.BlockSpec(memory_space=pltpu.VMEM)
    out = [jax.ShapeDtypeStruct(dn_own.shape, BF)] + [jax.ShapeDtypeStruct(s, F32) for s in shapes]
    return pl.pallas_call(kernel, in_specs=[vm] * 3, out_specs=[vm] * len(out), out_shape=out, name="unpack")(
        total, dn_own, dn_got
    )


def per_device(
    node_input,
    edge_input,
    neighbors,
    residue_mask,
    decode_order,
    node_cotangent,
    edge_cotangent,
    message_w1,
    message_w2,
    message_w3,
    inner_w,
    inner_bias,
    outer_w,
    update_w1,
    update_w2,
    update_w3,
    biases,
    norm_gains,
):
    parts, half, near, feat = edge_input.shape
    length = neighbors.shape[1]
    wide = inner_w.shape[2]
    res = BLOCK_RES
    rows = res * near
    blocks = half // res
    at_outer = 5 * feat
    at_inner = at_outer + wide
    at_small = at_inner + wide
    d = types.SimpleNamespace(
        parts=parts, half=half, near=near, feat=feat, length=length, wide=wide, res=res, rows=rows, blocks=blocks,
        at_outer=at_outer, at_inner=at_inner, at_small=at_small, msg_rows=at_small + SMALL,
        upd_rows=5 * feat + SMALL, devices=lax.axis_size(AXIS_D),
    )
    weights = dict(
        mw1=message_w1[0], mw2=message_w2[0], mw3=message_w3[0], inner=inner_w[0], inner_b=inner_bias, outer=outer_w[0],
        uw1=update_w1[0], uw2=update_w2[0], uw3=update_w3[0],
        bias=biases.transpose(1, 0, 2), gain=norm_gains.transpose(1, 0, 2),
    )
    sums = np.zeros((128, rows), np.float32)
    sums[np.arange(rows) // near, np.arange(rows)] = 1.0
    pick = (np.arange(rows)[None, :] % near == np.arange(near)[:, None]).astype(np.float32)
    consts = types.SimpleNamespace(sums=jnp.asarray(sums, BF), pick=jnp.asarray(pick, BF))
    fa = encoder_message(
        d, edge_input, node_input, neighbors.transpose(0, 2, 1), residue_mask, decode_order, weights, consts
    )
    consts.idx, consts.mask = fa.idx, fa.mask
    st = types.SimpleNamespace(**{n: getattr(fa, W_OUT + n) for n in weights})
    fb = encoder_update(d, edge_input, st, fa, consts)
    fd = decoder_update(d, st, fb, edge_cotangent, consts)
    fe = middle_backward(d, edge_input, st, fa, fb, fd, node_cotangent, consts)
    ff = encoder_message_back(d, edge_input, st, fa, fe, node_input, fa.nodes_got, consts)
    total, got = reduce_grads(d, ff.msg, fe.upd, fe.msg, fd.upd, ff.dn_far)
    node_grad, mw1, mw2, mw3, inner, inner_b, outer, uw1, uw2, uw3, bias, gain = unpack(
        d, total, ff.dn_own, got, biases.shape[1], norm_gains.shape[1]
    )
    return (
        fd.nodes, fd.decoded, node_grad, ff.edge_grad, mw1, mw2, mw3, inner, inner_b[:, 0], outer,
        uw1, uw2, uw3, bias.transpose(1, 0, 2), gain.transpose(1, 0, 2),
    )


def solution(mesh):
    def split(*axes):
        return P(*axes)

    by_part = split(AXIS_D)
    by_half = split(AXIS_D, AXIS_S)
    by_layer = split(AXIS_S)
    in_specs = (by_half, by_half, by_part, by_part, by_part, by_half, by_half) + (by_layer,) * 11
    out_specs = (by_half,) * 4 + (by_layer,) * 11
    return jax.shard_map(per_device, mesh=mesh, in_specs=in_specs, out_specs=out_specs, check_vma=False)
```

```python
import types

import jax
import jax.numpy as jnp
import numpy as np
from jax import lax
from jax.experimental import pallas as pl
from jax.experimental.pallas import tpu as pltpu
from jax.sharding import PartitionSpec as P

BF = jnp.bfloat16
F32 = jnp.float32
C1 = 0.7978845608
C2 = C1 * 0.044715
EPS = 1e-5
BLOCK_RES = 96
EXTRA = 16
SMALL = 32
MESH = pl.DeviceIdType.MESH


def mm(a, b, ca=1, cb=0):
    return lax.dot_general(a, b, (((ca,), (cb,)), ((), ())), preferred_element_type=F32)


def mm_exact(a, b, ca=1, cb=0):
    return lax.dot_general(
        a, b, (((ca,), (cb,)), ((), ())), precision=lax.Precision.HIGHEST, preferred_element_type=F32
    )


def gelu_pair(x):
    x = x.astype(BF)
    w = x * x * BF(C2)
    h = jnp.tanh(x * (w + BF(C1))) + BF(1.0)
    g = x * h
    d = h + g * (BF(2.0) - h) * (w * BF(3.0) + BF(C1))
    return g, d


def gelu_pair_wide(x):
    x2 = x * x
    h = 0.5 * jnp.tanh(x * (x2 * C2 + C1)) + 0.5
    g = x * h
    d = h + (g * (1.0 - h)) * (x2 * (6 * C2) + 2 * C1)
    return g, d


def lane_sum(x):
    total = x[:, :128]
    for at in range(128, x.shape[1], 128):
        total = total + x[:, at : at + 128]
    return total


def to_row(acc):
    return mm_exact(jnp.ones((8, acc.shape[1]), F32), acc, 1, 1)[0:1]


def norm_rows(r):
    c = r - jnp.mean(r, axis=-1, keepdims=True)
    rs = lax.rsqrt(jnp.mean(c * c, axis=-1, keepdims=True) + EPS)
    return c * rs, rs


def norm_back_rows(dxh, xh, rs):
    m1 = jnp.mean(dxh, axis=-1, keepdims=True)
    m2 = jnp.mean(dxh * xh, axis=-1, keepdims=True)
    return (dxh - m1 - xh * m2) * rs


def norm_back(dy, xh, rs, gain_col):
    dxh = dy * gain_col
    m1 = jnp.mean(dxh, axis=0, keepdims=True)
    m2 = jnp.mean(dxh * xh, axis=0, keepdims=True)
    return (dxh - m1 - xh * m2) * rs


class Phase:
    def __init__(self, dims, collective_id=None):
        self.d = dims
        self.collective_id = collective_id
        self.ins, self.outs, self.temps, self.kinds, self.wholes, self.later = [], [], [], {}, {}, ()
        self.only = {}

    def whole_spec(self, shape):
        rank = len(shape)
        return pl.BlockSpec(tuple(shape), lambda p, b: (0,) * rank)

    def whole(self, **arrays):
        self.raw(**arrays)
        self.wholes.update({n: pltpu.VMEM(a.shape, a.dtype) for n, a in arrays.items()})

    def raw(self, **arrays):
        self.ins += [(n, a, pl.BlockSpec(memory_space=pl.ANY)) for n, a in arrays.items()]

    def stream(self, **arrays):
        self.raw(**arrays)
        self.kinds.update({n: (False, False, a.shape[2:], a.dtype) for n, a in arrays.items()})

    def stream_top(self, rows, **arrays):
        self.raw(**arrays)
        self.kinds.update({n: (False, False, (rows,) + a.shape[3:], a.dtype) for n, a in arrays.items()})

    def edges(self, **arrays):
        self.raw(**arrays)
        block = (self.d.res, self.d.near, self.d.feat)
        self.kinds.update({n: (False, True, block, a.dtype) for n, a in arrays.items()})

    def out_whole(self, dtype, **shapes):
        self.outs += [(n, jax.ShapeDtypeStruct(s, dtype), self.whole_spec(s)) for n, s in shapes.items()]

    def out_raw(self, dtype, **shapes):
        spec = pl.BlockSpec(memory_space=pl.ANY)
        self.outs += [(n, jax.ShapeDtypeStruct(s, dtype), spec) for n, s in shapes.items()]

    def out_stream(self, dtype, **shapes):
        self.out_raw(dtype, **shapes)
        self.kinds.update({n: (True, False, s[2:], dtype) for n, s in shapes.items()})

    def out_edges(self, **shapes):
        self.out_raw(BF, **shapes)
        block = (self.d.res, self.d.near, self.d.feat)
        self.kinds.update({n: (True, True, block, BF) for n in shapes})

    def temp(self, dtype, **shapes):
        self.temps += [(n, pltpu.VMEM(s, dtype)) for n, s in shapes.items()]

    def sems(self, **counts):
        self.temps += [(n, pltpu.SemaphoreType.DMA((c,))) for n, c in counts.items()]

    def call(self, name, body):
        d = self.d
        names = [n for n, _, _ in self.ins] + [n for n, _, _ in self.outs] + [n for n, _ in self.temps]
        steps = d.parts * d.blocks
        buffers = [pltpu.VMEM((2,) + tuple(block), dtype) for _, _, block, dtype in self.kinds.values()]
        count = len(self.kinds)

        def kernel(*refs):
            refs, rest = refs[: len(names)], refs[len(names) :]
            slots, sems, kept = rest[:count], rest[count : 2 * count], rest[2 * count : -1]
            plain = dict(zip(names, refs))
            step = pl.program_id(0) * d.blocks + pl.program_id(1)
            now = lax.rem(step, 2)

            def copy(i, n, at, slot):
                out, edges, block, _ = self.kinds[n]
                p, b = at // d.blocks, lax.rem(at, d.blocks)
                if edges:
                    far = plain[n].at[p, pl.ds(pl.multiple_of(b * d.res, d.res), d.res)]
                elif block[0] < plain[n].shape[2]:
                    far = plain[n].at[p, b, pl.ds(0, block[0])]
                else:
                    far = plain[n].at[p, b]
                near = slots[i].at[slot]
                return pltpu.make_async_copy(*((near, far) if out else (far, near)), sems[i].at[slot])

            into = [(i, n) for i, n in enumerate(self.kinds) if not self.kinds[n][0]]
            outof = [(i, n) for i, n in enumerate(self.kinds) if self.kinds[n][0]]

            def loads():
                out = []
                for i, n in enumerate(self.wholes):
                    src, dst = plain[n], kept[i]
                    if n in self.only:
                        src, dst = src.at[self.only[n]], dst.at[self.only[n]]
                    out.append(pltpu.make_async_copy(src, dst, rest[-1].at[i]))
                return out

            def load(*later):
                for item, n in zip(loads(), self.wholes):
                    if (n in later) if later else (n not in self.later):
                        item.wait()

            @pl.when(step == 0)
            def _():
                for item in loads():
                    item.start()
                for i, n in into:
                    copy(i, n, step, now).start()

            @pl.when(step >= 2)
            def _():
                for i, n in outof:
                    copy(i, n, step - 2, now).wait()

            def ready():
                for i, n in into:
                    copy(i, n, step, now).wait()

                @pl.when(step + 1 < steps)
                def _():
                    for i, n in into:
                        copy(i, n, step + 1, 1 - now).start()

            def flush():
                for i, n in outof:
                    copy(i, n, step, now).start()

            plain_or_slot = dict(plain, ready=ready, flush=flush, load=load)
            plain_or_slot.update(zip(self.wholes, kept))
            plain_or_slot.update({n: slots[i].at[now] for i, n in enumerate(self.kinds)})
            body(types.SimpleNamespace(**plain_or_slot))

            @pl.when(step == steps - 1)
            def _():
                for i, n in outof:
                    if steps > 1:
                        copy(i, n, step - 1, 1 - now).wait()
                    copy(i, n, step, now).wait()

        results = pl.pallas_call(
            kernel,
            grid=(d.parts, d.blocks),
            in_specs=[s for _, _, s in self.ins],
            out_specs=[s for _, _, s in self.outs],
            out_shape=[s for _, s, _ in self.outs],
            scratch_shapes=[s for _, s in self.temps] + buffers
            + [pltpu.SemaphoreType.DMA((2,))] * count
            + list(self.wholes.values())
            + [pltpu.SemaphoreType.DMA((len(self.wholes),))],
            compiler_params=pltpu.CompilerParams(
                dimension_semantics=(pltpu.ARBITRARY,) * 2,
                vmem_limit_bytes=60 << 20,
                collective_id=self.collective_id,
                has_side_effects=self.collective_id is not None,
            ),
            name=name,
        )(*[a for _, a, _ in self.ins])
        return types.SimpleNamespace(**dict(zip([n for n, _, _ in self.outs], results)))


def other_section():
    return {AXIS_S: 1 - lax.axis_index(AXIS_S)}


AXIS_S = "section"
AXIS_D = "dp"


def greet_partner():
    barrier = pltpu.get_barrier_semaphore()
    pl.semaphore_signal(barrier, inc=1, device_id=other_section(), device_id_type=MESH)
    pl.semaphore_wait(barrier, 1)


def to_partner(src, dst, send, recv):
    return pltpu.make_async_remote_copy(
        src_ref=src, dst_ref=dst, send_sem=send, recv_sem=recv, device_id=other_section(), device_id_type=MESH
    )


def put_one_hot(d, ref, at, idx):
    idx = idx.astype(jnp.int16)
    place = lax.broadcasted_iota(jnp.int16, (d.length, d.rows), 0)
    ref[at : at + d.length, :] = jnp.where(place == idx, jnp.ones((), BF), jnp.zeros((), BF))


def put_one_hot_rows(d, ref, idx):
    centre = d.length // 2
    idx = jnp.broadcast_to((idx - centre).astype(F32).astype(BF), (128, d.rows)).T
    place = lax.broadcasted_iota(jnp.int32, (d.rows, 128), 1)
    for at in range(0, d.length, 128):
        there = (place + (at - centre)).astype(F32).astype(BF)
        ref[:, at : at + 128] = jnp.where(idx == there, jnp.ones((), BF), jnp.zeros((), BF))


def weight_args(w, *names):
    return {n: getattr(w, n) for n in names}


def load_cols(r, layer, aux, cols):
    n_bias, n_gain = r.bias.shape[1], r.gain.shape[1]
    aux[...] = jnp.zeros(aux.shape, F32)
    for i in range(n_bias):
        aux[i : i + 1] = r.bias[layer, i]
    for i in range(n_gain):
        aux[n_bias + i : n_bias + i + 1] = r.gain[layer, i]
    cols[...] = aux[...].T


def put_table(d, lhs, at, left, n_cat, w1):
    lhs[at : at + d.feat, left : left + d.length] = mm(w1[2 * d.feat :, :].T, n_cat[...], 1, 1).astype(BF)


def put_own(d, lhs, at, left, w1, n_blk, bias_col):
    own = mm(w1[0 : d.feat, :].T, n_blk, 1, 1) + bias_col
    lhs[at : at + d.feat, left + d.length :] = own.astype(BF)


def message_part(a1, w2t, b2, att, kept):
    g1, d1 = gelu_pair(a1)
    a2 = mm(w2t, g1) + b2
    g2, d2 = gelu_pair(a2)
    attb = att.astype(BF)
    feat, rows = g2.shape
    kept[:feat] = g2 * attb
    kept[feat:] = jnp.broadcast_to(attb, (16, rows))
    return g1, d1, d2 * attb


def add_node_outs(ph, d):
    ph.out_whole(BF, node_out=(d.parts, d.half, d.feat))
    shape = (d.parts, d.half, d.feat)
    ph.out_whole(F32, r1=shape, ip=(d.parts, d.half, d.wide), r2=shape, big=shape, cnt=shape)


def node_step(d, r, p, b):
    sums = mm(r.rt[: d.res], r.kept[...], 1, 1)
    at = pl.ds(pl.multiple_of(b * d.res, d.res), d.res)
    r.big[p, at, :] = sums[:, : d.feat] * 0.5
    r.cnt[p, at, :] = jnp.broadcast_to(sums[:, d.feat : d.feat + 1], (d.res, d.feat))


def node_forward(r, p, n_own, layer, aux):
    big = r.big[p]
    hi = big.astype(BF)
    lo = (big - hi.astype(F32)).astype(BF)
    w3 = r.mw3[layer]
    upd = (mm(hi, w3) + mm(lo, w3) + r.cnt[p] * aux[2:3]) / 30.0
    r1 = n_own.astype(F32) + upd
    xh1, _ = norm_rows(r1)
    normed = xh1 * aux[10:11] + aux[7:8]
    ip = mm(normed.astype(BF), r.inner[layer]) + r.inner_b[layer]
    hid = gelu_pair_wide(ip)[0].astype(BF)
    r2 = normed + (mm(hid, r.outer[layer]) + aux[3:4])
    xh2, _ = norm_rows(r2)
    out = ((xh2 * aux[11:12] + aux[8:9]) * r.mask[p]).astype(BF)
    r.node_out[p] = out
    r.r1[p] = r1
    r.ip[p] = ip
    r.r2[p] = r2
    return out


def node_backward(d, r, p, layer, aux, dn):
    def rows_of(ref):
        return ref[...].reshape(-1, ref.shape[2]) if p is None else ref[p]

    r1, ip, r2, big, cnt = rows_of(r.r1), rows_of(r.ip), rows_of(r.r2), rows_of(r.big), rows_of(r.cnt)
    xh1, rs1 = norm_rows(r1)
    normed = xh1 * aux[10:11] + aux[7:8]
    xh2, rs2 = norm_rows(r2)
    dy2 = dn * rows_of(r.mask)
    dr2 = norm_back_rows(dy2 * aux[11:12], xh2, rs2)
    low_outer = dr2.astype(BF)
    hid, slope = gelu_pair_wide(ip)
    dip = mm(low_outer, r.outer[layer], 1, 1) * slope
    low_inner = dip.astype(BF)
    at = d.at_outer
    r.msg[at : at + d.wide] += mm(hid.astype(BF), low_outer, 0, 0)
    at = d.at_inner
    r.msg[at : at + d.wide] += mm(low_inner, normed.astype(BF), 0, 0)
    dnormed = dr2 + mm(low_inner, r.inner[layer], 1, 1)
    dr1 = norm_back_rows(dnormed * aux[10:11], xh1, rs1)
    du = dr1 / 30.0
    dub = du.astype(BF)
    r.msg[4 * d.feat : 5 * d.feat] += mm(big.astype(BF), dub, 0, 0)
    dib = jnp.sum(dip, axis=0, keepdims=True)
    rows = {
        2: jnp.sum(cnt * du, axis=0, keepdims=True),
        3: jnp.sum(dr2, axis=0, keepdims=True),
        7: jnp.sum(dnormed, axis=0, keepdims=True),
        8: jnp.sum(dy2, axis=0, keepdims=True),
        10: jnp.sum(dnormed * xh1, axis=0, keepdims=True),
        11: jnp.sum(dy2 * xh2, axis=0, keepdims=True),
    }
    for i in range(d.wide // d.feat):
        rows[16 + i] = dib[:, i * d.feat : (i + 1) * d.feat]
    for row, value in rows.items():
        r.msg[d.at_small + row : d.at_small + row + 1] += value
    if p is None:
        r.dr1[...] = dr1.reshape(r.dr1.shape)
        r.dub[...] = dub.reshape(r.dub.shape)
    else:
        r.dr1[p] = dr1
        r.dub[p] = dub


def own_first(d, row):
    row = row.astype(F32)
    if row.shape[0] == 1:
        row = jnp.broadcast_to(row, (8, d.length))
    return jnp.where(lax.axis_index(AXIS_S) == 0, row, pltpu.roll(row, d.half, 1))


def put_positions(d, r):
    section = lax.axis_index(AXIS_S)
    centre = d.length // 2
    line = lax.broadcasted_iota(jnp.int32, (8, d.length), 0)
    for p in range(d.parts):
        live = own_first(d, r.live[p : p + 1, :])
        order = own_first(d, r.order[p : p + 1, :]) - centre
        code = jnp.where(live > 0.5, order, float(centre))
        r.codes[p, :8] = jnp.where(line == 0, live, jnp.where(line == 1, code, 0.0)).astype(BF)
        r.codes[p, 8:] = jnp.zeros((EXTRA - 8, d.length), BF)
        ids = own_first(d, r.near[p]) - float(d.half) * section.astype(F32)
        ids = jnp.where(ids < 0.0, ids + float(d.length), ids) - float(centre)
        r.mask[p] = jnp.broadcast_to(live[0:1], (d.feat, d.length)).T[: d.half]
        for b in range(d.blocks):
            own = pltpu.roll(order, (d.length - b * d.res) % d.length, 1) if b else order
            r.owns[p, b, :8] = jnp.where(line == 1, -own, 0.0)[:, : d.res].astype(BF)
            r.owns[p, b, 8:] = jnp.zeros((EXTRA - 8, d.res), BF)
            block = pltpu.roll(ids, (d.length - b * d.res) % d.length, 1) if b else ids
            spread = mm(block[:, : d.res].astype(BF), r.rt[: d.res])
            row = jnp.sum(spread * r.pick[...].astype(F32), axis=0, keepdims=True)
            r.idx[p, b] = row.astype(jnp.int32) + centre


def encoder_message(d, edge_input, node_input, neighbors, residue_mask, decode_order, weights, consts):
    ph = Phase(d, 2)
    ph.raw(n_far=node_input)
    ph.whole(n_own=node_input, rt=consts.sums, pick=consts.pick, near=neighbors, live=residue_mask, order=decode_order)
    ph.whole(edge=edge_input)
    ph.later = (EDGE,)
    ph.out_whole(jnp.int32, idx=(d.parts, d.blocks, 1, d.rows))
    ph.out_whole(F32, mask=(d.parts, d.half, d.feat))
    ph.temp(BF, codes=(d.parts, EXTRA, d.length), owns=(d.parts, d.blocks, EXTRA, d.res))
    names = tuple(weights)
    own = {W_IN + n: a for n, a in weights.items()}
    ph.raw(**own)
    act = (d.parts, d.blocks, d.feat, d.rows)
    ph.out_stream(BF, g1=with_ones(d), d1=act, d2=act)
    ph.out_whole(F32, att=(d.parts, d.blocks, 1, d.rows))
    add_node_outs(ph, d)
    ph.out_raw(BF, got=(d.half, d.feat), nodes_got=node_input.shape)
    for n, a in weights.items():
        ph.out_raw(a.dtype, **{W_OUT + n: (2,) + a.shape})
        ph.temp(a.dtype, **{n: (2,) + a.shape})
    sq = (d.feat, d.feat)
    wide = d.feat + d.length + d.res
    ph.temp(BF, n_cat=(d.length, d.feat), lhs=(d.feat + EXTRA, wide), w2t=sq, tt=(d.parts * d.blocks, wide, d.rows))
    ph.temp(BF, leave=(d.half, d.feat), arrive=node_input.shape, kept=(d.feat + 16, d.rows))
    ph.temp(F32, aux=sq, cols=sq)
    count = len(names)
    ph.sems(send=count + 1 + d.parts, recv=count + 1 + d.parts, local=count, back=2 * count + 1)

    def body(r):
        p, b = pl.program_id(0), pl.program_id(1)
        first, last = b == 0, b == d.blocks - 1
        section = lax.axis_index(AXIS_S)
        job = to_partner(r.leave, r.got, r.send.at[count], r.recv.at[count])
        nodes = [
            to_partner(r.n_far.at[q], r.arrive.at[q], r.send.at[count + 1 + q], r.recv.at[count + 1 + q])
            for q in range(d.parts)
        ]

        def swaps(group):
            out = []
            for n in group:
                i = names.index(n)
                dst = getattr(r, n).at[section]
                out.append(to_partner(getattr(r, W_IN + n), dst, r.send.at[i], r.recv.at[i]))
            return out

        def own_copies():
            return [
                pltpu.make_async_copy(getattr(r, W_IN + n), getattr(r, n).at[section], r.local.at[i])
                for i, n in enumerate(names)
            ]

        def returns(group):
            out = [pltpu.make_async_copy(r.arrive, r.nodes_got, r.back.at[2 * count])] if group == GROUP_ONE else []
            for n in group:
                i = names.index(n)
                src, dst = getattr(r, n), getattr(r, W_OUT + n)
                for layer in range(2):
                    sem = r.back.at[2 * i + layer]
                    out.append(pltpu.make_async_copy(src.at[layer], dst.at[layer], sem))
            return out

        begin = first & (p == 0)
        middle = (p == 1) & (b == 1)
        at_end = last & (p == d.parts - 1)

        @pl.when(begin)
        def _():
            greet_partner()
            for item in nodes[:1] + swaps(GROUP_ONE) + own_copies() + nodes[1:]:
                item.start()
            r.load()
            put_positions(d, r)
            r.load(EDGE)
            for q in range(d.parts):

                @pl.loop(0, d.blocks)
                def _(c, q=q):
                    table = r.tt.at[q * d.blocks + c]
                    put_one_hot(d, table, d.feat, r.idx[q, c])
                    table[d.feat + d.length :, :] = r.rt[: d.res]
                    own = r.edge[q, pl.ds(pl.multiple_of(c * d.res, d.res), d.res)]
                    table[: d.feat, :] = own.reshape(d.rows, d.feat).T

            for item in nodes[:1] + swaps(GROUP_ONE) + own_copies():
                item.wait()
            for item in swaps(GROUP_TWO) + swaps(GROUP_THREE):
                item.start()
            r.lhs[: d.feat, : d.feat] = r.mw1[0, d.feat : 2 * d.feat, :].T
            r.lhs[d.feat :, : d.feat] = jnp.zeros((EXTRA, d.feat), BF)
            r.w2t[...] = half_of(r.mw2[0]).T
            load_cols(r, 0, r.aux, r.cols)

        for q in range(1, d.parts):

            @pl.when(first & (p == q))
            def _(q=q):
                nodes[q].wait()

        @pl.when(first)
        def _():
            r.n_cat[: d.half] = r.n_own[p]
            r.n_cat[d.half :] = r.arrive[p]
            put_table(d, r.lhs, 0, d.feat, r.n_cat, r.mw1.at[0])

        n_blk = r.n_own[p, pl.ds(pl.multiple_of(b * d.res, d.res), d.res), :]
        r.ready()
        put_own(d, r.lhs, 0, d.feat, r.mw1.at[0], n_blk, r.cols[:, 0:1])
        r.lhs[d.feat :, d.feat : d.feat + d.length] = r.codes[p]
        r.lhs[d.feat :, d.feat + d.length :] = r.owns[p, b]
        out = mm(r.lhs[...], r.tt[p * d.blocks + b])
        att = out[d.feat : d.feat + 1]
        r.att[p, b] = jnp.where(out[d.feat + 1 : d.feat + 2] < 0.0, 1.0, 0.0)
        g1, r.d1[...], r.d2[...] = message_part(out[: d.feat], r.w2t[...], r.cols[:, 1:2], att, r.kept)
        put_ones(r.g1, g1)
        node_step(d, r, p, b)
        r.flush()

        @pl.when(middle)
        def _():
            for item in swaps(GROUP_TWO) + swaps(GROUP_THREE):
                item.wait()
            for item in returns(GROUP_ONE) + returns(GROUP_TWO) + returns(GROUP_THREE):
                item.start()
            r.leave[...] = node_forward(r, 0, r.n_own[0], 0, r.aux[...])
            job.start()

        @pl.when(at_end)
        def _():
            node_forward(r, d.parts - 1, r.n_own[d.parts - 1], 0, r.aux[...])
            for item in returns(GROUP_ONE) + returns(GROUP_TWO) + returns(GROUP_THREE):
                item.wait()
            job.wait()

    return ph.call("enc_message", body)


W_IN, W_OUT = "i_", "o_"
EDGE = "edge"
GROUP_ONE = ("mw1", "mw2", "bias", "gain")
GROUP_TWO = ("mw3", "inner", "inner_b", "outer")
GROUP_THREE = ("uw1", "uw2", "uw3")
NODE_W = ("mw3", "inner", "inner_b", "outer", "bias", "gain")
MSG_W = ("mw1", "mw2")
UPD_W = ("uw1", "uw2", "uw3")


def with_ones(d):
    return (d.parts, d.blocks, d.feat + 16, d.rows)


def put_ones(ref, g):
    feat, rows = g.shape
    ref[:feat] = g
    ref[feat:] = jnp.ones((16, rows), BF)


def half_of(w):
    return w * BF(0.5)


def update_forward(d, a1, w2t, w3c, b5, b6c, pair, cols):
    f = d.feat
    g1, d1 = gelu_pair(a1)
    a2 = mm(w2t, g1) + b5
    g2, d2 = gelu_pair(a2)
    pair[f : 2 * f] = g2
    cent = mm(w3c[...], pair[: 2 * f]) + b6c
    var = jnp.mean(cent * cent, axis=0, keepdims=True)
    rs = lax.rsqrt(var + EPS)
    xh = cent.astype(BF) * rs.astype(BF)
    y = xh * cols[:, 12:13].astype(BF) + cols[:, 9:10].astype(BF)
    return g1, d1, g2, d2, xh, rs, y


def centre_weights(w3, cols, w3c, b6c):
    feat = w3.shape[0]
    eye = lax.broadcasted_iota(jnp.int32, w3.shape, 0) == lax.broadcasted_iota(jnp.int32, w3.shape, 1)
    w3f = w3.astype(F32)
    w3c[:, feat:] = (0.5 * (w3f - jnp.mean(w3f, axis=1, keepdims=True))).T.astype(BF)
    w3c[:, :feat] = (eye.astype(F32) - 1.0 / feat).astype(BF)
    b6 = cols[:, 6:7]
    b6c[...] = jnp.broadcast_to(b6 - jnp.mean(b6, axis=0, keepdims=True), b6c.shape)


def encoder_update(d, edge_input, st, fa, consts):
    ph = Phase(d, 3)
    ph.raw(n_far=fa.node_out)
    ph.whole(n_own=fa.node_out, got_a=fa.got, idx=consts.idx, rt=consts.sums, mask=consts.mask, att=fa.att)
    ph.edges(edge=edge_input)
    ph.whole(**weight_args(st, *NODE_W, *MSG_W, *UPD_W))
    act = (d.parts, d.blocks, d.feat, d.rows)
    two = (d.parts, d.blocks, 2 * d.feat + 16, d.rows)
    ph.out_stream(BF, ugs=two, ud1=act, ud2=act, uxh=act, e2g=two, d1=act, d2=act)
    ph.out_whole(F32, urs=(d.parts, d.blocks, 1, d.rows))
    add_node_outs(ph, d)
    ph.out_whole(BF, got_in=(d.half, d.feat))
    ph.out_raw(BF, got=(d.parts, d.half, d.feat))
    sq = (d.feat, d.feat)
    wide = d.feat + d.length + d.res
    ph.temp(BF, n_cat=(d.length, d.feat), lhs=(2 * d.feat, wide), tt=(wide, d.rows))
    ph.temp(BF, uw2t=sq, mw2t=sq, w3c=(d.feat, 2 * d.feat), pair=(2 * d.feat, d.rows))
    ph.temp(BF, kept=(d.feat + 16, d.rows), leave=(d.parts, d.half, d.feat), arrive=(d.half, d.feat))
    ph.temp(F32, w3c_b=sq, e_aux=sq, e_cols=sq, d_aux=sq, d_cols=sq)
    ph.sems(send=d.parts + 1, recv=d.parts + 1)

    ph.only = dict(mw1=1, mw2=1, mw3=1, inner=1, inner_b=1, outer=1, uw1=0, uw2=0, uw3=0)

    def body(r):
        p, b = pl.program_id(0), pl.program_id(1)
        first, last = b == 0, b == d.blocks - 1
        early = to_partner(r.n_far.at[d.parts - 1], r.arrive, r.send.at[d.parts], r.recv.at[d.parts])
        jobs = [to_partner(r.leave.at[i], r.got.at[i], r.send.at[i], r.recv.at[i]) for i in range(d.parts)]

        @pl.when(first & (p == 0))
        def _():
            greet_partner()
            early.start()
            r.load()
            r.tt[d.feat + d.length :, :] = r.rt[: d.res]
            r.lhs[: d.feat, : d.feat] = r.uw1[0, d.feat : 2 * d.feat, :].T
            r.lhs[d.feat :, : d.feat] = r.mw1[1, d.feat : 2 * d.feat, :].T
            r.uw2t[...] = half_of(r.uw2[0]).T
            r.mw2t[...] = half_of(r.mw2[1]).T
            load_cols(r, 0, r.e_aux, r.e_cols)
            load_cols(r, 1, r.d_aux, r.d_cols)
            centre_weights(r.uw3[0], r.e_cols[...], r.w3c, r.w3c_b)
            r.n_cat[d.half :] = r.got_a[...]

        @pl.when(first & (p == 1))
        def _():
            early.wait()
            r.n_cat[d.half :] = r.arrive[...]
            r.got_in[...] = r.arrive[...]

        @pl.when(first)
        def _():
            r.n_cat[: d.half] = r.n_own[p]
            put_table(d, r.lhs, 0, d.feat, r.n_cat, r.uw1.at[0])
            put_table(d, r.lhs, d.feat, d.feat, r.n_cat, r.mw1.at[1])

        r.ready()
        n_blk = r.n_own[p, pl.ds(pl.multiple_of(b * d.res, d.res), d.res), :]
        put_own(d, r.lhs, 0, d.feat, r.uw1.at[0], n_blk, r.e_cols[:, 4:5])
        put_own(d, r.lhs, d.feat, d.feat, r.mw1.at[1], n_blk, r.d_cols[:, 0:1])
        put_one_hot(d, r.tt, d.feat, r.idx[p, b])
        edge_t = r.edge[...].reshape(d.rows, d.feat).T
        r.tt[: d.feat, :] = edge_t
        r.pair[: d.feat] = edge_t
        g1, d1, g2, d2, xh, rs, e2 = update_forward(
            d, mm(r.lhs[: d.feat], r.tt[...]), r.uw2t[...], r.w3c, r.e_cols[:, 5:6], r.w3c_b[:, 0:1], r.pair, r.e_cols
        )
        f = d.feat
        r.ugs[:f] = g2
        put_ones(r.ugs.at[f:], g1)
        r.ud1[...], r.ud2[...], r.uxh[...], r.urs[p, b], r.e2g[:f] = d1, d2, xh, rs, e2
        att = r.att[p, b]
        r.tt[:f] = e2
        a1 = mm(r.lhs[f:], r.tt[...])
        g1, r.d1[...], r.d2[...] = message_part(a1, r.mw2t[...], r.d_cols[:, 1:2], att, r.kept)
        put_ones(r.e2g.at[f:], g1)
        node_step(d, r, p, b)
        r.flush()

        @pl.when(last)
        def _():
            r.leave[p] = node_forward(r, p, r.n_own[p], 1, r.d_aux[...])
            for i in range(d.parts):

                @pl.when(p == i)
                def _(i=i):
                    jobs[i].start()

            @pl.when(p == d.parts - 1)
            def _():
                for job in jobs:
                    job.wait()

    return ph.call("enc_update", body)


def spread_nodes(d, acc, sumk, w1, n_cat, grad, grad_at):
    s = acc.astype(BF)
    sk = jnp.concatenate([x[:, : d.res] for x in sumk], axis=1)
    skb = sk.astype(BF)
    far = mm(s, w1[2 * d.feat :].T, 0, 0)
    own = mm(skb, w1[: d.feat].T, 0, 0)
    grad[grad_at + 2 * d.feat : grad_at + 3 * d.feat, :] += mm(n_cat, s, 0, 1)
    grad[grad_at : grad_at + d.feat, :] += mm(n_cat[: d.half], skb, 0, 1)
    return own + far[: d.half], far[d.half :], to_row(sk)


def lane_total(x):
    size = x.shape[1] // 4
    x = (x[:, :size] + x[:, size : 2 * size]) + (x[:, 2 * size : 3 * size] + x[:, 3 * size :])
    return lane_sum(x.astype(F32))


def norm_backward(d, r, dy, xh, rs, gain_mat):
    r.a_b9[...] += lane_total(dy)
    r.a_g2[...] += lane_total(dy * xh)
    z = mm(gain_mat, dy).astype(BF)
    m2 = jnp.mean((z * xh).astype(F32), axis=0, keepdims=True)
    return (z - xh * m2.astype(BF)) * rs.astype(BF)


def gain_matrix(cols):
    feat = cols.shape[0]
    shape = (feat, feat)
    eye = lax.broadcasted_iota(jnp.int32, shape, 0) == lax.broadcasted_iota(jnp.int32, shape, 1)
    scaled = jnp.where(eye, jnp.broadcast_to(cols[:, 12:13], shape), 0.0)
    return (scaled - jnp.mean(scaled, axis=0, keepdims=True)).astype(BF)


def update_backward(d, r, dr3, gs, d1, d2, w2, w3, low, da1):
    f = d.feat
    low[:f] = dr3
    low[f:] = mm(w3, dr3).astype(BF) * d2
    r.a_w23[...] += mm(gs, low[...], 1, 1)
    da1[...] = mm(w2, low[f:]).astype(BF) * d1


def update_small(d, r, b4):
    f = d.feat
    at = 5 * f
    r.upd[at + 4 : at + 5] += b4

    @pl.when(pl.program_id(0) == d.parts - 1)
    def _():
        r.upd[3 * f : 4 * f] = 0.5 * r.a_w23[f : 2 * f, f:]
        r.upd[4 * f : 5 * f] = 0.5 * r.a_w23[:f, :f]
        r.upd[at + 5 : at + 6] = r.a_w23[2 * f : 2 * f + 1, f:]
        r.upd[at + 6 : at + 7] = r.a_w23[2 * f : 2 * f + 1, :f]
        r.upd[at + 9 : at + 10] = to_row(r.a_b9[...])
        r.upd[at + 12 : at + 13] = to_row(r.a_g2[...])


def block_before(d):
    step = jnp.maximum(pl.program_id(0) * d.blocks + pl.program_id(1) - 1, 0)
    return step // d.blocks, lax.rem(step, d.blocks)


def put_spread(d, r, q, c, spread):
    r.a_s[q] += spread[:, : d.length]
    r.a_k[q, c] = spread[:, d.length :]


def zero(*refs):
    for ref in refs:
        ref[...] = jnp.zeros(ref.shape, ref.dtype)


def decoder_update(d, st, fb, cot, consts):
    ph = Phase(d)
    ph.whole(n_own=fb.node_out, n_got=fb.got, idx=consts.idx, rt=consts.sums)
    ph.stream_top(d.feat, e2=fb.e2g)
    ph.edges(cot=cot)
    ph.whole(**weight_args(st, *UPD_W, *AUX_W))
    ph.out_edges(decoded=cot.shape)
    ph.out_stream(BF, part=(d.parts, d.blocks, d.feat, d.rows))
    ph.out_whole(F32, upd=(d.upd_rows, d.feat), dn_own=(d.parts, d.half, d.feat))
    ph.out_whole(BF, dn_far=(d.parts, d.half, d.feat), nodes=(d.parts, d.half, d.feat))
    sq = (d.feat, d.feat)
    wide = d.length + d.res
    ph.temp(BF, n_cat=(d.length, d.feat), lhs=(d.feat, wide), w1bt=sq, w2t=sq, w2h=sq, w3h=sq)
    ph.temp(BF, tt=(wide, d.rows), tn=(d.rows, d.length + 128), da1=(d.feat, d.rows))
    ph.temp(BF, w3c=(d.feat, 2 * d.feat), gain_mat=sq, pair=(3 * d.feat + 16, d.rows), low=(2 * d.feat, d.rows))
    ph.temp(F32, w3c_b=sq, aux=sq, cols=sq, a_w23=(2 * d.feat + 16, 2 * d.feat), a_b9=sq, a_g2=sq)
    ph.temp(F32, a_s=(d.parts, d.feat, d.length), a_k=(d.parts, d.blocks, d.feat, 128))

    ph.only = dict(uw1=1, uw2=1, uw3=1)

    def body(r):
        p, b = pl.program_id(0), pl.program_id(1)
        first = b == 0

        @pl.when(first & (p == 0))
        def _():
            r.load()
            r.nodes[...] = r.n_own[...]
            r.w1bt[...] = r.uw1[1, d.feat : 2 * d.feat, :].T
            r.w2h[...] = half_of(r.uw2[1])
            r.w2t[...] = r.w2h[...].T
            r.w3h[...] = half_of(r.uw3[1])
            load_cols(r, 1, r.aux, r.cols)
            centre_weights(r.uw3[1], r.cols[...], r.w3c, r.w3c_b)
            r.gain_mat[...] = gain_matrix(r.cols[...])
            zero(r.upd, r.a_w23, r.a_b9, r.a_g2, r.a_s)
            r.pair[3 * d.feat :] = jnp.ones((16, d.rows), BF)
            r.tt[d.length :, :] = r.rt[: d.res]
            r.tn[:, d.length :] = r.rt[...].T

        @pl.when(first)
        def _():
            r.n_cat[: d.half] = r.n_own[p]
            r.n_cat[d.half :] = r.n_got[p]
            put_table(d, r.lhs, 0, 0, r.n_cat, r.uw1.at[1])

        r.ready()
        f = d.feat
        n_blk = r.n_own[p, pl.ds(pl.multiple_of(b * d.res, d.res), d.res), :]
        put_own(d, r.lhs, 0, 0, r.uw1.at[1], n_blk, r.cols[:, 4:5])
        idx = r.idx[p, b]
        put_one_hot(d, r.tt, 0, idx)
        put_one_hot_rows(d, r.tn, idx)
        e2 = r.e2[...]
        r.pair[:f] = e2
        a1 = mm(r.lhs[...], r.tt[...]) + mm(r.w1bt[...], e2)
        g1, d1, _, d2, xh, rs, y = update_forward(
            d, a1, r.w2t[...], r.w3c, r.cols[:, 5:6], r.w3c_b[:, 0:1], r.pair, r.cols
        )
        r.pair[2 * f : 3 * f] = g1
        r.decoded[...] = y.T.reshape(d.res, d.near, f)
        dy = r.cot[...].reshape(d.rows, f).T
        dr3 = norm_backward(d, r, dy, xh, rs, r.gain_mat[...])
        update_backward(d, r, dr3, r.pair[f:], d1, d2, r.w2h[...], r.w3h[...], r.low, r.da1)
        r.upd[f : 2 * f] += mm(e2, r.da1[...], 1, 1)
        r.part[...] = (mm(r.uw1[1, f : 2 * f, :], r.da1[...]) + dr3.astype(F32)).astype(BF)
        put_spread(d, r, p, b, mm(r.da1[...], r.tn[...]))
        r.flush()

        @pl.when((b == d.blocks - 1) & (p == d.parts - 1))
        def _():
            total = jnp.zeros((1, f), F32)
            for q in range(d.parts):
                nodes = jnp.concatenate([r.n_own[q], r.n_got[q]], axis=0)
                sums = [r.a_k[q, i] for i in range(d.blocks)]
                own, far, b4 = spread_nodes(d, r.a_s[q], sums, r.uw1[1], nodes, r.upd, 0)
                r.dn_own[q] = own
                r.dn_far[q] = far.astype(BF)
                total = total + b4
            update_small(d, r, total)

    return ph.call("dec_update", body)


AUX_W = ("bias", "gain")


def message_backward(d, r, b, layer, low):
    at = pl.ds(pl.multiple_of(b * d.res, d.res), d.res)
    v = (mm(r.mw3[layer], r.dub[pl.program_id(0), at, :], 1, 1) * 0.5).astype(BF)
    f = d.feat
    low[:f] = mm(v, r.rt[: d.res]).astype(BF) * r.d2[...]
    low[f:] = mm(r.mw2h[...], low[:f]).astype(BF) * r.d1[...]


def message_small(d, r, b0):
    r.msg[d.at_small : d.at_small + 1] += b0


def middle_backward(d, edge_input, st, fa, fb, fd, cot_n, consts):
    ph = Phase(d, 4)
    ph.raw(dn_far_in=fd.dn_far)
    ph.whole(cot_n=cot_n, dn_a=fd.dn_own, n_own=fa.node_out, got_a=fa.got, got_b=fb.got_in)
    ph.whole(mask=consts.mask, rt=consts.sums, r1=fb.r1, ip=fb.ip, r2=fb.r2, big=fb.big, cnt=fb.cnt)
    ph.whole(urs=fb.urs, idx=consts.idx)
    ph.stream(d2=fb.d2, d1=fb.d1, e2g=fb.e2g, dec_part=fd.part, uxh=fb.uxh, ugs=fb.ugs, ud2=fb.ud2, ud1=fb.ud1)
    ph.edges(edge=edge_input)
    ph.whole(**weight_args(st, *NODE_W, *MSG_W, *UPD_W))
    ph.out_stream(BF, part=(d.parts, d.blocks, d.feat, d.rows))
    ph.out_whole(F32, msg=(d.msg_rows, d.feat), upd=(d.upd_rows, d.feat), dn_own=(d.parts, d.half, d.feat))
    ph.out_raw(BF, got=(d.parts, d.half, d.feat))
    sq = (d.feat, d.feat)
    ph.temp(BF, n_cat=(d.length, d.feat), dub=(d.parts, d.half, d.feat), tt=(d.length + d.res, d.rows))
    ph.temp(BF, tri=(3 * d.feat, d.rows), low=(2 * d.feat, d.rows), w2h=sq, w3h=sq, mw2h=sq, gain_mat=sq)
    ph.temp(BF, leave=(d.parts, d.half, d.feat), arrive=(d.parts, d.half, d.feat))
    ph.temp(F32, dr1=(d.parts, d.half, d.feat), e_aux=sq, e_cols=sq, d_aux=sq, d_cols=sq)
    tall = (2 * d.feat + 16, 2 * d.feat)
    ph.temp(F32, m_w12=tall, a_w23=tall, a_b9=sq, a_g2=sq, a_w1=sq)
    ph.temp(F32, a_s=(2 * d.feat, d.length), a_k=(d.blocks, 2 * d.feat, 128))
    ph.sems(send=2 * d.parts, recv=2 * d.parts)

    ph.only = dict(mw1=1, mw2=1, mw3=1, inner=1, inner_b=1, outer=1, uw1=0, uw2=0, uw3=0)

    def body(r):
        p, b = pl.program_id(0), pl.program_id(1)
        first, last = b == 0, b == d.blocks - 1
        n = d.parts
        early = [to_partner(r.dn_far_in.at[i], r.arrive.at[i], r.send.at[n + i], r.recv.at[n + i]) for i in range(n)]
        jobs = [to_partner(r.leave.at[i], r.got.at[i], r.send.at[i], r.recv.at[i]) for i in range(n)]

        @pl.when(first & (p == 0))
        def _():
            greet_partner()
            for job in early:
                job.start()
            r.load()
            load_cols(r, 0, r.e_aux, r.e_cols)
            load_cols(r, 1, r.d_aux, r.d_cols)
            r.tt[d.length :, :] = r.rt[: d.res]
            r.w2h[...] = half_of(r.uw2[0])
            r.w3h[...] = half_of(r.uw3[0])
            r.mw2h[...] = half_of(r.mw2[1])
            r.gain_mat[...] = gain_matrix(r.e_cols[...])
            zero(r.msg, r.upd, r.m_w12, r.a_w23, r.a_b9, r.a_g2, r.a_w1)
            r.n_cat[d.half :] = r.got_a[...]

        @pl.when(first & (p == 1))
        def _():
            r.n_cat[d.half :] = r.got_b[...]

        for i in range(n):

            @pl.when(first & (p == i))
            def _(i=i):
                early[i].wait()

        @pl.when(first)
        def _():
            r.n_cat[: d.half] = r.n_own[p]
            zero(r.a_s)
            dn = r.cot_n[p].astype(F32) + r.dn_a[p] + r.arrive[p].astype(F32)
            node_backward(d, r, p, 1, r.d_aux[...], dn)

        f = d.feat
        r.ready()
        put_one_hot(d, r.tt, 0, r.idx[p, b])
        message_backward(d, r, b, 1, r.tri.at[: 2 * f])
        r.m_w12[...] += mm(r.e2g[...], r.tri[: 2 * f], 1, 1)
        de = mm(r.mw1[1, f : 2 * f, :], r.tri[f : 2 * f])
        dy = (de + r.dec_part[...].astype(F32)).astype(BF)
        dr3 = norm_backward(d, r, dy, r.uxh[...], r.urs[p, b], r.gain_mat[...])
        da1 = r.tri.at[2 * f :]
        update_backward(d, r, dr3, r.ugs[...], r.ud1[...], r.ud2[...], r.w2h[...], r.w3h[...], r.low, da1)
        r.a_w1[...] += mm(da1[...], r.edge[...].reshape(d.rows, f))
        r.part[...] = (mm(r.uw1[0, f : 2 * f, :], da1[...]) + dr3.astype(F32)).astype(BF)
        spread = mm(r.tri[f:], r.tt[...], 1, 1)
        r.a_s[...] += spread[:, : d.length]
        r.a_k[b, :, : d.res] = spread[:, d.length :]
        r.flush()

        @pl.when(last)
        def _():
            n_cat = r.n_cat[...]
            a_k = [r.a_k[i] for i in range(d.blocks)]
            own_m, far_m, b0 = spread_nodes(
                d, r.a_s[: d.feat], [x[: d.feat] for x in a_k], r.mw1[1], n_cat, r.msg, 0
            )
            own_u, far_u, b4 = spread_nodes(
                d, r.a_s[d.feat :], [x[d.feat :] for x in a_k], r.uw1[0], n_cat, r.upd, 0
            )
            r.dn_own[p] = own_m + own_u + r.dr1[p]
            r.leave[p] = (far_m + far_u).astype(BF)
            for i in range(n):

                @pl.when(p == i)
                def _(i=i):
                    jobs[i].start()

            message_small(d, r, b0)
            update_small(d, r, b4)

            @pl.when(p == n - 1)
            def _():
                f, at = d.feat, d.at_small
                r.upd[f : 2 * f] = r.a_w1[...].T
                r.msg[f : 2 * f] = r.m_w12[:f, f:]
                r.msg[3 * f : 4 * f] = 0.5 * r.m_w12[f : 2 * f, :f]
                r.msg[at + 1 : at + 2] = r.m_w12[2 * f : 2 * f + 1, :f]
                for job in jobs:
                    job.wait()

    return ph.call("dec_message_back", body)


def encoder_message_back(d, edge_input, st, fa, fe, n_own, n_got, consts):
    ph = Phase(d)
    ph.whole(dn_a=fe.dn_own, dn_b=fe.got, n_own=n_own, n_got=n_got)
    ph.whole(mask=consts.mask, rt=consts.sums, r1=fa.r1, ip=fa.ip, r2=fa.r2, big=fa.big, cnt=fa.cnt)
    ph.whole(idx=consts.idx)
    ph.stream(d2=fa.d2, g1=fa.g1, d1=fa.d1, up_part=fe.part)
    ph.edges(edge=edge_input)
    ph.whole(**weight_args(st, *NODE_W, *MSG_W))
    ph.out_edges(edge_grad=edge_input.shape)
    ph.out_whole(F32, msg=(d.msg_rows, d.feat), dn_own=(d.parts, d.half, d.feat))
    ph.out_whole(BF, dn_far=(d.parts, d.half, d.feat))
    sq = (d.feat, d.feat)
    ph.temp(BF, dub=(d.parts, d.half, d.feat), tn=(d.rows, d.length + 128))
    ph.temp(BF, low=(2 * d.feat, d.rows), mw2h=sq)
    ph.temp(F32, dr1=(d.parts, d.half, d.feat), aux=sq, cols=sq, a_w1=sq, m_w2=(d.feat + 16, d.feat))
    ph.temp(F32, a_s=(d.parts, d.feat, d.length), a_k=(d.parts, d.blocks, d.feat, 128))

    ph.only = dict(mw1=0, mw2=0, mw3=0, inner=0, inner_b=0, outer=0)

    def body(r):
        p, b = pl.program_id(0), pl.program_id(1)

        @pl.when((b == 0) & (p == 0))
        def _():
            zero(r.a_s, r.low, r.tn)
            r.load()
            load_cols(r, 0, r.aux, r.cols)
            r.tn[:, d.length :] = r.rt[...].T
            r.mw2h[...] = half_of(r.mw2[0])
            zero(r.msg, r.m_w2, r.a_w1)
            dn = r.dn_a[...] + r.dn_b[...].astype(F32)
            node_backward(d, r, None, 0, r.aux[...], dn.reshape(-1, d.feat))

        f = d.feat
        r.ready()
        put_spread(d, r, *block_before(d), mm(r.low[f:], r.tn[...]))
        put_one_hot_rows(d, r.tn, r.idx[p, b])
        message_backward(d, r, b, 0, r.low)
        da1 = r.low.at[f:]
        r.m_w2[...] += mm(r.g1[...], r.low[:f], 1, 1)
        r.a_w1[...] += mm(da1[...], r.edge[...].reshape(d.rows, f))
        de = mm(r.mw1[0, f : 2 * f, :], da1[...])
        de = (de + r.up_part[...].astype(F32)).astype(BF)
        r.edge_grad[...] = de.T.reshape(d.res, d.near, f)
        r.flush()

        @pl.when((b == d.blocks - 1) & (p == d.parts - 1))
        def _():
            put_spread(d, r, p, b, mm(da1[...], r.tn[...]))
            for q in range(d.parts):
                nodes = jnp.concatenate([r.n_own[q], r.n_got[q]], axis=0)
                sums = [r.a_k[q, i] for i in range(d.blocks)]
                own, far, b0 = spread_nodes(d, r.a_s[q], sums, r.mw1[0], nodes, r.msg, 0)
                r.dn_own[q] = own + r.dr1[q]
                r.dn_far[q] = far.astype(BF)
                message_small(d, r, b0)
            at = d.at_small
            r.msg[f : 2 * f] = r.a_w1[...].T
            r.msg[3 * f : 4 * f] = 0.5 * r.m_w2[:f]
            r.msg[at + 1 : at + 2] = r.m_w2[f : f + 1]

    return ph.call("enc_message_back", body)


class Reducer:
    def __init__(self, devices, feat, shares):
        self.feat = feat
        self.bits = bits = devices.bit_length() - 1
        self.groups = [16 * devices * share for share in shares]
        self.rows = sum(self.groups)
        self.bases = [sum(self.groups[:i]) for i in range(len(shares))]
        pairs, top = [], bits
        while top > 1:
            low = max(1, top - 2)
            pairs.insert(0, (low, top - low))
            top = low
        dims = [ACROSS] + pairs
        turn = min(3, len(dims))
        self.plans = []
        for g, size in enumerate(self.groups):
            head = dims[:turn]
            order = ([(0, 1)] if bits else []) + head[g % turn :] + head[: g % turn] + dims[turn:]
            both, plan = True, []
            for dim in order:
                if dim == ACROSS:
                    both = False
                else:
                    size >>= dim[1]
                plan.append((dim, size, both))
            self.plans.append(plan)
        self.backs = [[step for step in reversed(plan) if step[0] != ACROSS] for plan in self.plans]
        self.halving = len(self.plans[0])
        self.stages = self.halving + len(self.backs[0])
        self.dims = ([(0, 1)] if bits else []) + dims
        self.sem_at, self.buffer_at, self.shapes = {}, {}, []
        for g, plan in enumerate(self.plans):
            for k, (dim, size, both) in enumerate(plan):
                for o in self.offsets(dim):
                    self.sem_at[(g, k, o)] = len(self.sem_at)
                    self.buffer_at[(g, k, o)] = len(self.shapes)
                    self.shapes += [(2, size, feat) if both else (size, feat)] * 2
            for k, (dim, _, _) in enumerate(self.backs[g]):
                for o in self.offsets(dim):
                    self.sem_at[(g, self.halving + k, o)] = len(self.sem_at)

    def scratch(self):
        temps = [pltpu.VMEM((2, self.rows, self.feat), F32), pltpu.VMEM((self.rows, self.feat), BF)]
        temps += [pltpu.VMEM(shape, BF) for shape in self.shapes]
        return temps + [pltpu.SemaphoreType.DMA((len(self.sem_at),))] * 2

    def bind(self, refs):
        self.acc, self.gathered = refs[:2]
        self.buffers, (self.send, self.recv) = refs[2:-2], refs[-2:]

    def offsets(self, dim):
        return range(1, 2 if dim == ACROSS else 1 << dim[1])

    def code(self, dim):
        return lax.rem(lax.axis_index(AXIS_D) // (1 << dim[0]), 1 << dim[1])

    def peer(self, dim, o):
        if dim == ACROSS:
            return other_section()
        code = self.code(dim)
        other = lax.rem(code + o, 1 << dim[1])
        return {AXIS_D: lax.axis_index(AXIS_D) + (other - code) * (1 << dim[0])}

    def greet(self):
        barrier = pltpu.get_barrier_semaphore()
        count = 0
        for dim in self.dims:
            for o in self.offsets(dim):
                pl.semaphore_signal(barrier, inc=1, device_id=self.peer(dim, o), device_id_type=MESH)
                count += 1
        pl.semaphore_wait(barrier, count)

    def begin(self, g, k):
        start = self.bases[g]
        for dim, size, _ in self.plans[g][:k]:
            if dim != ACROSS:
                start = start + self.code(dim) * size
        return start

    def span(self, start, size):
        return pl.ds(pl.multiple_of(start, 16), size)

    def job(self, src, dst, key, dim):
        at = self.sem_at[key]
        return pltpu.make_async_remote_copy(
            src_ref=src, dst_ref=dst, send_sem=self.send.at[at], recv_sem=self.recv.at[at],
            device_id=self.peer(dim, key[2]), device_id_type=MESH,
        )

    def jobs(self, g, k):
        plan = self.plans[g]
        if k < self.halving:
            out = []
            for o in self.offsets(plan[k][0]):
                at = self.buffer_at[(g, k, o)]
                out.append(self.job(self.buffers[at], self.buffers[at + 1], (g, k, o), plan[k][0]))
            return out
        dim, size, _ = self.backs[g][k - self.halving]
        start = self.begin(g, [step[0] for step in plan].index(dim) + 1)
        part = self.gathered.at[self.span(start, size), :]
        return [self.job(part, part, (g, k, o), dim) for o in self.offsets(dim)]

    def start(self, g, k):
        section = lax.axis_index(AXIS_S)
        plan = self.plans[g]
        if k < self.halving:
            dim, size, both = plan[k]
            start = self.begin(g, k)
            for o in self.offsets(dim):
                out = self.buffers[self.buffer_at[(g, k, o)]]
                if dim == ACROSS:
                    out[...] = self.acc[1 - section, self.span(start, size), :].astype(BF)
                    continue
                give = self.span(start + lax.rem(self.code(dim) + o, 1 << dim[1]) * size, size)
                if both:
                    out[...] = self.acc[:, give, :].astype(BF)
                else:
                    out[...] = self.acc[section, give, :].astype(BF)
        elif k == self.halving:
            keep = self.span(self.begin(g, self.halving), plan[-1][1])
            self.gathered[keep, :] = self.acc[section, keep, :].astype(BF)
        for job in self.jobs(g, k):
            job.start()

    def finish(self, g, k):
        section = lax.axis_index(AXIS_S)
        for job in self.jobs(g, k):
            job.wait()
        if k >= self.halving:
            return
        dim, size, both = self.plans[g][k]
        keep = self.span(self.begin(g, k + 1), size)
        for o in self.offsets(dim):
            into = self.buffers[self.buffer_at[(g, k, o)] + 1]
            if both:
                self.acc[:, keep, :] += into[...].astype(F32)
            else:
                self.acc[section, keep, :] += into[...].astype(F32)

    def run(self):
        count = len(self.plans)
        for g in range(count):
            self.start(g, 0)
        for k in range(self.stages):
            for g in range(count):
                self.finish(g, k)
                if k + 1 < self.stages:
                    self.start(g, k + 1)
        if self.stages == self.halving:
            self.gathered[...] = self.acc[lax.axis_index(AXIS_S)].astype(BF)


ACROSS = (-1, 0)


def reduce_grads(d, enc_msg, enc_upd, dec_msg, dec_upd, dn_far):
    m, u = d.msg_rows, d.upd_rows
    units = -(-(m + u) // (16 * d.devices))
    red = Reducer(d.devices, d.feat, [2] * (units // 2) + [1] * (units % 2))

    def kernel(em, eu, dm, du, far, res, got, far_sems, load_sems, *refs):
        red.bind(refs)
        loads = []
        for layer, (msg, upd) in enumerate(((em, eu), (dm, du))):
            spots = (red.acc.at[layer, pl.ds(0, m)], red.acc.at[layer, pl.ds(m, u)])
            for i, (src, dst) in enumerate(zip((msg, upd), spots)):
                loads.append(pltpu.make_async_copy(src, dst, load_sems.at[2 * layer + i]))
        for item in loads:
            item.start()
        if red.rows > m + u:
            red.acc[:, m + u :] = jnp.zeros((2, red.rows - m - u, d.feat), F32)
        red.greet()
        nodes = to_partner(far, got, far_sems.at[0], far_sems.at[1])
        nodes.start()
        for item in loads:
            item.wait()
        red.run()
        res[...] = red.gathered[...]
        nodes.wait()

    vm, anywhere = pl.BlockSpec(memory_space=pltpu.VMEM), pl.BlockSpec(memory_space=pl.ANY)
    return pl.pallas_call(
        kernel,
        in_specs=[anywhere] * 5,
        out_specs=[vm, anywhere],
        out_shape=[jax.ShapeDtypeStruct((red.rows, d.feat), BF), jax.ShapeDtypeStruct(dn_far.shape, BF)],
        scratch_shapes=[pltpu.SemaphoreType.DMA((2,)), pltpu.SemaphoreType.DMA((4,))] + red.scratch(),
        compiler_params=pltpu.CompilerParams(vmem_limit_bytes=58 << 20, collective_id=5, has_side_effects=True),
        name="reduce",
    )(enc_msg, enc_upd, dec_msg, dec_upd, dn_far)


def unpack(d, total, dn_own, dn_got, n_bias, n_gain):
    f = d.feat
    m = d.msg_rows
    shapes = [(1, 3 * f, f), (1, f, f), (1, f, f), (1, f, d.wide), (1, 1, d.wide), (1, d.wide, f)]
    shapes += [(1, 3 * f, f), (1, f, f), (1, f, f), (n_bias, 1, f), (n_gain, 1, f)]

    def kernel(t, own, got, node, mw1, mw2, mw3, inner, inner_b, outer, uw1, uw2, uw3, bias, gain):
        node[...] = (own[...] + got[...].astype(F32)).astype(BF)
        for ref, at in ((mw1, 0), (mw2, 3 * f), (mw3, 4 * f), (outer, d.at_outer)):
            ref[0] = t[at : at + ref.shape[1], :].astype(F32)
        for ref, at in ((uw1, m), (uw2, m + 3 * f), (uw3, m + 4 * f)):
            ref[0] = t[at : at + ref.shape[1], :].astype(F32)
        inner[0] = t[d.at_inner : d.at_inner + d.wide, :].astype(F32).T
        small = t[d.at_small : d.at_small + SMALL, :].astype(F32)
        other = t[m + 5 * f : m + 5 * f + SMALL, :].astype(F32)
        both = small + other
        for i in range(n_bias):
            bias[i] = both[i : i + 1]
        for i in range(n_gain):
            gain[i] = both[n_bias + i : n_bias + i + 1]
        for i in range(d.wide // f):
            inner_b[0, :, i * f : (i + 1) * f] = small[16 + i : 17 + i]

    vm = pl.BlockSpec(memory_space=pltpu.VMEM)
    out = [jax.ShapeDtypeStruct(dn_own.shape, BF)] + [jax.ShapeDtypeStruct(s, F32) for s in shapes]
    return pl.pallas_call(kernel, in_specs=[vm] * 3, out_specs=[vm] * len(out), out_shape=out, name="unpack")(
        total, dn_own, dn_got
    )


def per_device(
    node_input,
    edge_input,
    neighbors,
    residue_mask,
    decode_order,
    node_cotangent,
    edge_cotangent,
    message_w1,
    message_w2,
    message_w3,
    inner_w,
    inner_bias,
    outer_w,
    update_w1,
    update_w2,
    update_w3,
    biases,
    norm_gains,
):
    parts, half, near, feat = edge_input.shape
    length = neighbors.shape[1]
    wide = inner_w.shape[2]
    res = BLOCK_RES
    rows = res * near
    blocks = half // res
    at_outer = 5 * feat
    at_inner = at_outer + wide
    at_small = at_inner + wide
    d = types.SimpleNamespace(
        parts=parts, half=half, near=near, feat=feat, length=length, wide=wide, res=res, rows=rows, blocks=blocks,
        at_outer=at_outer, at_inner=at_inner, at_small=at_small, msg_rows=at_small + SMALL,
        upd_rows=5 * feat + SMALL, devices=lax.axis_size(AXIS_D),
    )
    weights = dict(
        mw1=message_w1[0], mw2=message_w2[0], mw3=message_w3[0], inner=inner_w[0], inner_b=inner_bias, outer=outer_w[0],
        uw1=update_w1[0], uw2=update_w2[0], uw3=update_w3[0],
        bias=biases.transpose(1, 0, 2), gain=norm_gains.transpose(1, 0, 2),
    )
    sums = np.zeros((128, rows), np.float32)
    sums[np.arange(rows) // near, np.arange(rows)] = 1.0
    pick = (np.arange(rows)[None, :] % near == np.arange(near)[:, None]).astype(np.float32)
    consts = types.SimpleNamespace(sums=jnp.asarray(sums, BF), pick=jnp.asarray(pick, BF))
    fa = encoder_message(
        d, edge_input, node_input, neighbors.transpose(0, 2, 1), residue_mask, decode_order, weights, consts
    )
    consts.idx, consts.mask = fa.idx, fa.mask
    st = types.SimpleNamespace(**{n: getattr(fa, W_OUT + n) for n in weights})
    fb = encoder_update(d, edge_input, st, fa, consts)
    fd = decoder_update(d, st, fb, edge_cotangent, consts)
    fe = middle_backward(d, edge_input, st, fa, fb, fd, node_cotangent, consts)
    ff = encoder_message_back(d, edge_input, st, fa, fe, node_input, fa.nodes_got, consts)
    total, got = reduce_grads(d, ff.msg, fe.upd, fe.msg, fd.upd, ff.dn_far)
    node_grad, mw1, mw2, mw3, inner, inner_b, outer, uw1, uw2, uw3, bias, gain = unpack(
        d, total, ff.dn_own, got, biases.shape[1], norm_gains.shape[1]
    )
    return (
        fd.nodes, fd.decoded, node_grad, ff.edge_grad, mw1, mw2, mw3, inner, inner_b[:, 0], outer,
        uw1, uw2, uw3, bias.transpose(1, 0, 2), gain.transpose(1, 0, 2),
    )


def solution(mesh):
    def split(*axes):
        return P(*axes)

    by_part = split(AXIS_D)
    by_half = split(AXIS_D, AXIS_S)
    by_layer = split(AXIS_S)
    in_specs = (by_half, by_half, by_part, by_part, by_part, by_half, by_half) + (by_layer,) * 11
    out_specs = (by_half,) * 4 + (by_layer,) * 11
    return jax.shard_map(per_device, mesh=mesh, in_specs=in_specs, out_specs=out_specs, check_vma=False)
```
